32 devices in a mesh: dp: 8 (over y, x, core), tensor: 4 (over z).
Axes of the slice: x: 2, y: 2, z: 4, core: 2. Of those that a mesh axis runs over, the one named last changes fastest.
Arguments:
- patches: bfloat16 [768, 8, 768], P('tensor', 'dp'), may hold values from -64 to 64
- mask: int32 [768, 8], P('tensor', 'dp'), may hold values 0 or 1
- edge: float32 [2, 768, 768], P(None, ('dp', 'tensor')), may hold values from -0.21875 to 0.21875
- attn_w: float32 [2, 768, 4, 768], P(None, 'dp', None, 'tensor'), may hold values from -3 to 3
- mlp_w: float32 [2, 768, 2, 3072], P(None, 'dp', None, 'tensor'), may hold values from -0.21875 to 0.21875
- vecs: float32 [12, 768], P(None, ('dp', 'tensor')), may hold values from -4 to 4
- edge_m: float32 [2, 768, 768], P(None, ('dp', 'tensor')), may hold values from -1.25 to 1.25
- edge_v: float32 [2, 768, 768], P(None, ('dp', 'tensor')), may hold values from 0.001 to 0.02
- attn_m: float32 [2, 768, 4, 768], P(None, 'dp', None, 'tensor'), may hold values from -1.25 to 1.25
- attn_v: float32 [2, 768, 4, 768], P(None, 'dp', None, 'tensor'), may hold values from 0.001 to 0.02
- mlp_m: float32 [2, 768, 2, 3072], P(None, 'dp', None, 'tensor'), may hold values from -1.25 to 1.25
- mlp_v: float32 [2, 768, 2, 3072], P(None, 'dp', None, 'tensor'), may hold values from 0.001 to 0.02
- vecs_m: float32 [12, 768], P(None, ('dp', 'tensor')), may hold values from -1.25 to 1.25
- vecs_v: float32 [12, 768], P(None, ('dp', 'tensor')), may hold values from 0.001 to 0.02
- teacher_edge: float32 [2, 768, 768], P(None, ('dp', 'tensor')), may hold values from -0.21875 to 0.21875
- teacher_attn: float32 [2, 768, 4, 768], P(None, 'dp', None, 'tensor'), may hold values from -3 to 3
- teacher_mlp: float32 [2, 768, 2, 3072], P(None, 'dp', None, 'tensor'), may hold values from -0.21875 to 0.21875
- teacher_vecs: float32 [12, 768], P(None, ('dp', 'tensor')), may hold values from -4 to 4
Outputs:
- loss: float32 [], replicated
- norms: float32 [2, 14], replicated
- new_edge: float32 [2, 768, 768], P(None, ('dp', 'tensor'))
- new_attn: float32 [2, 768, 4, 768], P(None, 'dp', None, 'tensor')
- new_mlp: float32 [2, 768, 2, 3072], P(None, 'dp', None, 'tensor')
- new_vecs: float32 [12, 768], P(None, ('dp', 'tensor'))
- edge_m_new: float32 [2, 768, 768], P(None, ('dp', 'tensor'))
- patch_second: float32 [768, 768], P(('dp', 'tensor'))
- head_second: float32 [768, 768], P(('dp', 'tensor'))
- attn_m_new: float32 [2, 768, 4, 768], P(None, 'dp', None, 'tensor')
- inward_second: float32 [2, 768, 3, 768], P(None, 'dp', None, 'tensor')
- outward_second: float32 [2, 768, 768], P(None, 'dp', 'tensor')
- mlp_m_new: float32 [2, 768, 2, 3072], P(None, 'dp', None, 'tensor')
- mlp_v_new: float32 [2, 768, 2, 3072], P(None, 'dp', None, 'tensor')
- vecs_m_new: float32 [12, 768], P(None, ('dp', 'tensor'))
- vecs_v_new: float32 [12, 768], P(None, ('dp', 'tensor'))
- teacher_edge_move: float32 [2, 768, 768], P(None, ('dp', 'tensor'))
- teacher_attn_move: float32 [2, 768, 4, 768], P(None, 'dp', None, 'tensor')
- teacher_mlp_move: float32 [2, 768, 2, 3072], P(None, 'dp', None, 'tensor')
- teacher_vecs_move: float32 [12, 768], P(None, ('dp', 'tensor'))
- edge_low: bfloat16 [2, 768, 768], P(None, ('dp', 'tensor'))
- attn_low: bfloat16 [2, 768, 4, 768], P(None, 'dp', None, 'tensor')
- mlp_low: bfloat16 [2, 768, 2, 3072], P(None, 'dp', None, 'tensor')
- vecs_low: bfloat16 [12, 768], P(None, ('dp', 'tensor'))
The draws below stay inside these ranges and needn't reach their ends.
All inputs are finite; a program needn't handle non-finite values. No bound on the sum of `mask` on one device may be relied on, other than what follows from the above.
Results may differ from the reference program's by a relative error of at most 0.019.
Values may be sent and summed in bfloat16 or wider, within the bound.
A program may use at most 192 MiB of HBM per device.

```python
import math
import jax
import jax.numpy as jnp
from jax import lax

HEADS = 12
HEAD = 64
D = 768
FF = 3072
LAYERS = 2
SEQ = 768
CLIPS = 8
TOKENS = 6144
NVEC = 12


def layer_draw(key):
    base = jax.random.truncated_normal(key, -4.0, 4.0, (LAYERS, D, 4, D), jnp.float32)
    factor = jnp.where(jnp.arange(4) == 3, (SEQ / 3.0) ** 0.5, 1.0)
    return base * factor[None, None, :, None] * D ** (-0.5)


def vector_draw(key):
    base = jax.random.truncated_normal(key, -4.0, 4.0, (4 * LAYERS + 4, D), jnp.float32)
    row_index = jnp.arange(4 * LAYERS + 4)
    gain_row = (row_index % 2 == 0) & (row_index < 4 * LAYERS) | (row_index == 4 * LAYERS)
    embed_row = row_index == 4 * LAYERS + 2
    factor = jnp.where(gain_row, 0.2, jnp.where(embed_row, 1.0, 0.3))
    offset = jnp.where(gain_row, 1.0, 0.0)
    return offset[:, None] + factor[:, None] * base


def draw_patches(key, part):
    position = jnp.arange(SEQ, dtype=jnp.float32) / max(SEQ - 1, 1)
    base = jax.random.truncated_normal(jax.random.fold_in(key, 61), -6.0, 6.0, (SEQ, CLIPS, D), jnp.float32)
    rise = 1.0 + 3.0 * position
    return (base * rise[:, None, None]).astype(jnp.bfloat16)


def draw_attn_w(key, part):
    return layer_draw(jax.random.fold_in(key, 11))


def draw_teacher_attn(key, part):
    return layer_draw(jax.random.fold_in(key, 23))


def draw_vecs(key, part):
    return vector_draw(jax.random.fold_in(key, 37))


def draw_teacher_vecs(key, part):
    return vector_draw(jax.random.fold_in(key, 53))


def plant(array, own_key, least, high):
    longest = array.shape.index(max(array.shape))
    spots = []
    for shift in (0, 1):
        where = [jax.random.randint(jax.random.fold_in(own_key, axis), (), 0, length) for axis, length in enumerate(array.shape)]
        where[longest] = (where[longest] + shift) % array.shape[longest]
        spots.append(tuple(where))
    return array.at[spots[0]].set(least).at[spots[1]].set(high)


def levels(key, shape, shards, low, top_value):
    def one(axis_at, blocks):
        draws = jax.random.uniform(jax.random.fold_in(jax.random.fold_in(key, 6), axis_at), (blocks,), jnp.float32, low / len(shards), top_value / len(shards))
        return jnp.repeat(jnp.exp(draws), shape[axis_at] // blocks).reshape((-1,) + (1,) * (len(shape) - axis_at - 1))

    level = one(*shards[0])
    for cut in shards[1:]:
        level = level * one(*cut)
    return level


def bell_draw(own_key, shape, scale, limit, pieces=(), kind=jnp.bfloat16):
    result = scale * jax.random.normal(own_key, shape, jnp.float32)
    if pieces:
        result = result * levels(own_key, shape, pieces, -0.22, 0.18)
    return jnp.clip(result, -limit, limit).astype(kind)


def setup_inputs(seed: int = 0) -> dict:
    key_list = jax.random.split(jax.random.key(seed), 19)
    patches = draw_patches(jax.random.fold_in(key_list[18], 71), 0)
    mask = plant((jax.random.randint(key_list[1], (SEQ, CLIPS), 0, 5) < 3).astype(jnp.int32), jax.random.fold_in(key_list[1], 1), 0, 1)
    edge = bell_draw(key_list[2], (2, D, D), D ** -0.5, 0.21875, ((1, 32),), jnp.float32)
    attn_w = draw_attn_w(jax.random.fold_in(key_list[18], 71), 0)
    mlp_w = bell_draw(key_list[4], (LAYERS, D, 2, FF), D ** -0.5, 0.21875, ((1, 8), (3, 4)), jnp.float32)
    vecs = draw_vecs(jax.random.fold_in(key_list[18], 71), 0)
    edge_m = bell_draw(key_list[6], (2, D, D), 0.2, 1.25, ((1, 32),), jnp.float32)
    edge_v = jnp.clip(jnp.exp(math.log(0.02) - 2.9957322 * jax.random.uniform(key_list[7], (2, D, D), jnp.float32) ** levels(key_list[7], (2, D, D), ((1, 32),), -0.2, 0.2)), 0.001, 0.02)
    attn_m = bell_draw(key_list[8], (LAYERS, D, 4, D), 0.2, 1.25, ((1, 8), (3, 4)), jnp.float32)
    attn_v = jnp.clip(jnp.exp(math.log(0.02) - 2.9957322 * jax.random.uniform(key_list[9], (LAYERS, D, 4, D), jnp.float32) ** levels(key_list[9], (LAYERS, D, 4, D), ((1, 8), (3, 4)), -0.2, 0.2)), 0.001, 0.02)
    mlp_m = bell_draw(key_list[10], (LAYERS, D, 2, FF), 0.2, 1.25, ((1, 8), (3, 4)), jnp.float32)
    mlp_v = jnp.clip(jnp.exp(math.log(0.02) - 2.9957322 * jax.random.uniform(key_list[11], (LAYERS, D, 2, FF), jnp.float32) ** levels(key_list[11], (LAYERS, D, 2, FF), ((1, 8), (3, 4)), -0.2, 0.2)), 0.001, 0.02)
    vecs_m = bell_draw(key_list[12], (NVEC, D), 0.2, 1.25, ((1, 32),), jnp.float32)
    vecs_v = jnp.clip(jnp.exp(math.log(0.02) - 2.9957322 * jax.random.uniform(key_list[13], (NVEC, D), jnp.float32) ** levels(key_list[13], (NVEC, D), ((1, 32),), -0.2, 0.2)), 0.001, 0.02)
    teacher_edge = bell_draw(key_list[14], (2, D, D), D ** -0.5, 0.21875, ((1, 32),), jnp.float32)
    teacher_attn = draw_teacher_attn(jax.random.fold_in(key_list[18], 71), 0)
    teacher_mlp = bell_draw(key_list[16], (LAYERS, D, 2, FF), D ** -0.5, 0.21875, ((1, 8), (3, 4)), jnp.float32)
    teacher_vecs = draw_teacher_vecs(jax.random.fold_in(key_list[18], 71), 0)
    return dict(patches=patches, mask=mask, edge=edge, attn_w=attn_w, mlp_w=mlp_w, vecs=vecs, edge_m=edge_m, edge_v=edge_v, attn_m=attn_m, attn_v=attn_v, mlp_m=mlp_m, mlp_v=mlp_v, vecs_m=vecs_m, vecs_v=vecs_v, teacher_edge=teacher_edge, teacher_attn=teacher_attn, teacher_mlp=teacher_mlp, teacher_vecs=teacher_vecs)


norm_epsilon = 1e-06
inst_epsilon = 1e-05
first_decay = 0.9
second_decay = 0.999
adam_epsilon = 1e-06
weight_decay = 0.01
learn_rate = 0.3
teacher_decay = 0.999
step_count = 10
group_clips = 4
highest = lax.Precision.HIGHEST

@jax.custom_vjp
def low(v):
    return lax.optimization_barrier(v.astype(jnp.bfloat16)).astype(jnp.float32)

@jax.custom_vjp
def low_back(v):
    return v

def low_keep(v):
    return (low(v), None)

def low_pass(kept, grad):
    return (grad,)

def back_keep(v):
    return (v, None)

def back_low(kept, grad):
    return (low(grad),)
low.defvjp(low_keep, low_pass)
low_back.defvjp(back_keep, back_low)

def product(left, right):
    return jnp.einsum('...k,kn->...n', left, right, precision=highest)

def norm_rows(values, gain, shift):
    average = lax.optimization_barrier(jnp.mean(values, axis=-1, keepdims=True))
    centered = values - average
    spread = lax.optimization_barrier(jnp.mean(centered * centered, axis=-1, keepdims=True))
    return centered * lax.rsqrt(spread + norm_epsilon) * gain + shift

def attend(parts):
    queries, keys_in, values_in = parts
    scores = low_back(jnp.einsum('shd,thd->hst', queries, keys_in, precision=highest) * HEAD ** (-0.5))
    weights = low(jax.nn.softmax(scores, axis=-1))
    return jnp.einsum('hst,thd->shd', weights, values_in, precision=highest)

def block(stream, attn_layer, mlp_layer, gains):
    clip_count = stream.shape[0]
    normed = low(norm_rows(stream, gains[0], gains[1]))
    attn_round = low(attn_layer)
    mlp_round = low(mlp_layer)
    joined = low(low_back(product(normed, attn_round[:, 0:3].reshape(D, 3 * D))))
    split_heads = joined.reshape(clip_count, SEQ, 3, HEADS, HEAD)
    context = lax.map(jax.checkpoint(attend), (split_heads[:, :, 0], split_heads[:, :, 1], split_heads[:, :, 2]))
    context = low(low_back(context.reshape(clip_count, SEQ, D)))
    middle = stream + low_back(product(context, attn_round[:, 3].T))
    hidden = low(norm_rows(middle, gains[2], gains[3]))
    upward = low_back(product(hidden, mlp_round[:, 0]))
    active = low(jax.nn.gelu(upward, approximate=False))
    return middle + low_back(product(active, mlp_round[:, 1].T))

def embed_rows(patch_rows, edge):
    return low_back(product(patch_rows, low(edge[0])))

def teacher_targets(patch_rows, edge, attn_w, mlp_w, vecs):
    stream = embed_rows(patch_rows, edge)
    summed = jnp.zeros_like(stream)
    for layer_index in range(LAYERS):
        stream = block(stream, attn_w[layer_index], mlp_w[layer_index], vecs[4 * layer_index:4 * layer_index + 4])
        average = lax.optimization_barrier(jnp.mean(stream, axis=1, keepdims=True))
        spread = lax.optimization_barrier(jnp.mean(stream * stream, axis=1, keepdims=True)) - average * average
        summed = summed + (stream - average) * lax.rsqrt(spread + inst_epsilon)
    return summed / LAYERS

def student_loss(params, patch_rows, mask_rows, target):
    edge, attn_w, mlp_w, vecs = params
    masked = mask_rows[..., None]
    stream = embed_rows(patch_rows, edge) * (1.0 - masked) + masked * vecs[4 * LAYERS + 2]
    for layer_index in range(LAYERS):
        stream = block(stream, attn_w[layer_index], mlp_w[layer_index], vecs[4 * layer_index:4 * layer_index + 4])
    final = low(norm_rows(stream, vecs[4 * LAYERS], vecs[4 * LAYERS + 1]))
    predicted = low_back(product(final, low(edge[1]))) + vecs[4 * LAYERS + 3]
    offset = predicted - target
    size_abs = jnp.abs(offset)
    smooth = jnp.where(size_abs < 1.0, 0.5 * offset * offset, size_abs - 0.5)
    return jnp.sum(smooth * masked) / D ** 0.5

def direction(weight, grad, first, second):
    bias_one = 1.0 - first_decay ** step_count
    bias_two = 1.0 - second_decay ** step_count
    first_new = first_decay * first + (1.0 - first_decay) * grad
    second_new = second_decay * second + (1.0 - second_decay) * grad * grad
    update = first_new / bias_one / (jnp.sqrt(second_new / bias_two) + adam_epsilon) + weight_decay * weight
    return (first_new, second_new, update)

def matrix_squares(edge_part, attn_part, mlp_part):
    layer_part = jnp.concatenate([lax.optimization_barrier(jnp.sum(attn_part * attn_part, axis=(1, 3))), lax.optimization_barrier(jnp.sum(mlp_part * mlp_part, axis=(1, 3)))], axis=1)
    return jnp.concatenate([lax.optimization_barrier(jnp.sum(edge_part * edge_part, axis=(1, 2))), layer_part.reshape(-1)])

def reference(patches, mask, edge, attn_w, mlp_w, vecs, edge_m, edge_v, attn_m, attn_v, mlp_m, mlp_v, vecs_m, vecs_v, teacher_edge, teacher_attn, teacher_mlp, teacher_vecs):
    groups = CLIPS // group_clips
    patch_groups = jnp.transpose(patches.astype(jnp.float32), (1, 0, 2)).reshape(groups, group_clips, SEQ, D)
    mask_groups = jnp.transpose(mask, (1, 0)).astype(jnp.float32).reshape(groups, group_clips, SEQ)
    params = (edge, attn_w, mlp_w, vecs)

    def accumulate(carry, item):
        grads, loss_sum = carry
        patch_rows, mask_rows = item
        target = teacher_targets(patch_rows, teacher_edge, teacher_attn, teacher_mlp, teacher_vecs)
        value, pull = jax.vjp(lambda weights: student_loss(weights, patch_rows, mask_rows, target), params)
        step_grads, = pull(jnp.ones_like(value))
        return ((jax.tree.map(jnp.add, grads, step_grads), loss_sum + value), None)
    start = (jax.tree.map(jnp.zeros_like, params), jnp.zeros((), jnp.float32))
    (grads, loss_sum), unused = lax.scan(accumulate, start, (patch_groups, mask_groups))
    edge_first, edge_second, edge_update = direction(edge, grads[0], edge_m, edge_v)
    attn_first, attn_second, attn_update = direction(attn_w, grads[1], attn_m, attn_v)
    mlp_first, mlp_second, mlp_update = direction(mlp_w, grads[2], mlp_m, mlp_v)
    vecs_first, vecs_second, vecs_update = direction(vecs, grads[3], vecs_m, vecs_v)
    weight_norm = jnp.sqrt(matrix_squares(edge, attn_w, mlp_w))
    update_norm = jnp.sqrt(matrix_squares(edge_update, attn_update, mlp_update))
    trust = weight_norm / (update_norm + adam_epsilon)
    edge_trust = trust[0:2]
    layer_trust = trust[2:].reshape(LAYERS, 6)
    new_edge = edge - learn_rate * edge_trust[:, None, None] * edge_update
    new_attn = attn_w - learn_rate * layer_trust[:, None, 0:4, None] * attn_update
    new_mlp = mlp_w - learn_rate * layer_trust[:, None, 4:6, None] * mlp_update
    new_vecs = vecs - learn_rate * vecs_update
    keep_share = 1.0 - teacher_decay
    return (loss_sum / TOKENS, jnp.stack([weight_norm, update_norm]), new_edge, new_attn, new_mlp, new_vecs, edge_first, edge_second[0], edge_second[1], attn_first, attn_second[:, :, 0:3], attn_second[:, :, 3], mlp_first, mlp_second, vecs_first, vecs_second, keep_share * (new_edge - teacher_edge), keep_share * (new_attn - teacher_attn), keep_share * (new_mlp - teacher_mlp), keep_share * (new_vecs - teacher_vecs), new_edge.astype(jnp.bfloat16), new_attn.astype(jnp.bfloat16), new_mlp.astype(jnp.bfloat16), new_vecs.astype(jnp.bfloat16))
```

```python
import jax
import jax.numpy as jnp
from jax import lax
from jax.experimental import pallas as pl
from jax.experimental.pallas import tpu as pltpu
from jax.sharding import PartitionSpec as P

HEAD = 64


norm_epsilon = 1e-06
inst_epsilon = 1e-05
first_decay = 0.9
second_decay = 0.999
adam_epsilon = 1e-06
weight_decay = 0.01
learn_rate = 0.3
teacher_decay = 0.999
step_count = 10


def norm_rows(values, gain, shift):
    average = jnp.mean(values, axis=-1, keepdims=True)
    centered = values - average
    spread = jnp.mean(centered * centered, axis=-1, keepdims=True)
    return centered * lax.rsqrt(spread + norm_epsilon) * gain + shift


def exact_gelu(values):
    return jax.nn.gelu(values, approximate=False)


def fetch_edges(edge_part, vector_part):
    return (
        lax.all_gather(edge_part, ("dp", "tensor"), axis=1, tiled=True),
        lax.all_gather(vector_part, ("dp", "tensor"), axis=1, tiled=True),
    )


def fetch_layer(attn_part, mlp_part):
    return (
        lax.all_gather(attn_part.astype(jnp.bfloat16), "dp", axis=0, tiled=True),
        lax.all_gather(mlp_part.astype(jnp.bfloat16), "dp", axis=0, tiled=True),
    )


def fetch_again(attn_part, mlp_part):
    return (
        lax.all_gather(attn_part.astype(jnp.bfloat16), "dp", axis=0, tiled=True),
        lax.all_gather(mlp_part.astype(jnp.bfloat16), "dp", axis=0, tiled=True),
    )


def gather_rows(local_part):
    return lax.all_gather(local_part, "tensor", axis=0, tiled=True)


def gather_grads(local_part):
    return lax.all_gather(local_part, "tensor", axis=0, tiled=True)


def project_term(full_rows, weight):
    return jnp.einsum("sck,dk->scd", full_rows, weight, preferred_element_type=jnp.float32)


def scatter_rows(full_rows, weight):
    return lax.psum_scatter(
        project_term(full_rows, weight).astype(jnp.bfloat16),
        "tensor",
        scatter_dimension=0,
        tiled=True,
    ).astype(jnp.float32)


def scatter_grads(full_rows, weight):
    return lax.psum_scatter(
        project_term(full_rows, weight).astype(jnp.bfloat16),
        "tensor",
        scatter_dimension=0,
        tiled=True,
    ).astype(jnp.float32)


def attend_forward(parts):
    queries, keys_in, values_in = parts
    scores = jnp.einsum(
        "shd,thd->hst", queries, keys_in, preferred_element_type=jnp.float32
    ) * HEAD ** (-0.5)
    peak = jnp.max(scores, axis=-1, keepdims=True)
    raised = jnp.exp(scores - peak)
    summed = jnp.sum(raised, axis=-1, keepdims=True)
    weights = (raised / summed).astype(jnp.bfloat16)
    context = jnp.einsum("hst,thd->shd", weights, values_in, preferred_element_type=jnp.float32)
    return (context.astype(jnp.bfloat16), (peak + jnp.log(summed))[..., 0])


def attend_backward(parts):
    queries, keys_in, values_in, log_total, grad_context = parts
    scale = HEAD ** (-0.5)
    scores = (
        jnp.einsum("shd,thd->hst", queries, keys_in, preferred_element_type=jnp.float32) * scale
    )
    probs = jnp.exp(scores - log_total[..., None])
    probs_low = probs.astype(jnp.bfloat16)
    grad_values = jnp.einsum(
        "hst,shd->thd", probs_low, grad_context, preferred_element_type=jnp.float32
    )
    grad_probs = jnp.einsum(
        "shd,thd->hst", grad_context, values_in, preferred_element_type=jnp.float32
    )
    grad_scores = (
        probs * (grad_probs - jnp.sum(probs * grad_probs, axis=-1, keepdims=True))
    ).astype(jnp.bfloat16)
    grad_queries = (
        jnp.einsum("hst,thd->shd", grad_scores, keys_in, preferred_element_type=jnp.float32) * scale
    )
    grad_keys = (
        jnp.einsum("hst,shd->thd", grad_scores, queries, preferred_element_type=jnp.float32) * scale
    )
    return (grad_queries, grad_keys, grad_values)


def run_block(stream, attn_full, mlp_full, gains):
    model_width = stream.shape[2]
    head_width = attn_full.shape[2]
    normed = norm_rows(stream, gains[0], gains[1]).astype(jnp.bfloat16)
    normed_full = gather_rows(normed)
    seq_len = normed_full.shape[0]
    clip_count = normed_full.shape[1]
    weight_in = attn_full[:, 0:3].reshape(model_width, 3 * head_width)
    joined = jnp.einsum(
        "scd,dk->sck", normed_full, weight_in, preferred_element_type=jnp.float32
    ).astype(jnp.bfloat16)
    split_heads = jnp.moveaxis(
        joined.reshape(seq_len, clip_count, 3, head_width // HEAD, HEAD), 1, 0
    )
    context, log_total = lax.map(
        attend_forward, (split_heads[:, :, 0], split_heads[:, :, 1], split_heads[:, :, 2])
    )
    context_rows = jnp.moveaxis(context, 0, 1).reshape(seq_len, clip_count, head_width)
    middle = stream + scatter_rows(context_rows, attn_full[:, 3])
    hidden = norm_rows(middle, gains[2], gains[3]).astype(jnp.bfloat16)
    hidden_full = gather_rows(hidden)
    upward = jnp.einsum(
        "scd,df->scf", hidden_full, mlp_full[:, 0], preferred_element_type=jnp.float32
    )
    active = exact_gelu(upward).astype(jnp.bfloat16)
    result = middle + scatter_rows(active, mlp_full[:, 1])
    return (
        result,
        (
            stream,
            normed_full,
            split_heads,
            log_total,
            context_rows,
            middle,
            hidden_full,
            upward,
            active,
        ),
    )


def back_block(grad_stream, saved, attn_full, mlp_full, gains):
    (
        stream,
        normed_full,
        split_heads,
        log_total,
        context_rows,
        middle,
        hidden_full,
        upward,
        active,
    ) = saved
    model_width = stream.shape[2]
    head_width = attn_full.shape[2]
    seq_len = normed_full.shape[0]
    clip_count = normed_full.shape[1]
    grad_ffn = gather_grads(grad_stream.astype(jnp.bfloat16))
    grad_down = jnp.einsum("scd,scf->df", grad_ffn, active, preferred_element_type=jnp.float32)
    grad_active = jnp.einsum(
        "scd,df->scf", grad_ffn, mlp_full[:, 1], preferred_element_type=jnp.float32
    )
    unused, gelu_pull = jax.vjp(exact_gelu, upward)
    grad_upward = gelu_pull(grad_active)[0].astype(jnp.bfloat16)
    grad_up = jnp.einsum(
        "scd,scf->df", hidden_full, grad_upward, preferred_element_type=jnp.float32
    )
    grad_hidden = scatter_grads(grad_upward, mlp_full[:, 0])
    unused, second_pull = jax.vjp(norm_rows, middle, gains[2], gains[3])
    grad_middle_norm, grad_gain_two, grad_shift_two = second_pull(grad_hidden)
    grad_middle = grad_stream + grad_middle_norm
    grad_attn = gather_grads(grad_middle.astype(jnp.bfloat16))
    grad_outward = jnp.einsum(
        "scd,sck->dk", grad_attn, context_rows, preferred_element_type=jnp.float32
    )
    grad_context = jnp.einsum(
        "scd,dk->sck", grad_attn, attn_full[:, 3], preferred_element_type=jnp.float32
    ).astype(jnp.bfloat16)
    grad_context = jnp.moveaxis(
        grad_context.reshape(seq_len, clip_count, head_width // HEAD, HEAD), 1, 0
    )
    grad_queries, grad_keys, grad_values = lax.map(
        attend_backward,
        (split_heads[:, :, 0], split_heads[:, :, 1], split_heads[:, :, 2], log_total, grad_context),
    )
    grad_joined = jnp.moveaxis(jnp.stack((grad_queries, grad_keys, grad_values), axis=2), 0, 1)
    grad_joined = grad_joined.reshape(seq_len, clip_count, 3 * head_width).astype(jnp.bfloat16)
    weight_in = attn_full[:, 0:3].reshape(model_width, 3 * head_width)
    grad_inward = jnp.einsum(
        "scd,sck->dk", normed_full, grad_joined, preferred_element_type=jnp.float32
    ).reshape(model_width, 3, head_width)
    grad_normed = scatter_grads(grad_joined, weight_in)
    unused, first_pull = jax.vjp(norm_rows, stream, gains[0], gains[1])
    grad_stream_norm, grad_gain_one, grad_shift_one = first_pull(grad_normed)
    attn_grad = jnp.concatenate([grad_inward, grad_outward[:, None]], axis=1)
    mlp_grad = jnp.stack([grad_up, grad_down], axis=1)
    layer_attn, layer_mlp = (
        lax.psum_scatter(attn_grad, "dp", scatter_dimension=0, tiled=True),
        lax.psum_scatter(mlp_grad, "dp", scatter_dimension=0, tiled=True),
    )
    vector_grads = jnp.stack([grad_gain_one, grad_shift_one, grad_gain_two, grad_shift_two])
    return (grad_middle + grad_stream_norm, layer_attn, layer_mlp, vector_grads)


def direction(weight, grad, first, second):
    bias_one = 1.0 - first_decay**step_count
    bias_two = 1.0 - second_decay**step_count
    first_new = first_decay * first + (1.0 - first_decay) * grad
    second_new = second_decay * second + (1.0 - second_decay) * grad * grad
    update = (
        first_new / bias_one / (jnp.sqrt(second_new / bias_two) + adam_epsilon)
        + weight_decay * weight
    )
    return (first_new, second_new, update)


def matrix_squares(edge_part, attn_part, mlp_part):
    layer_part = jnp.concatenate(
        [jnp.sum(attn_part * attn_part, axis=(1, 3)), jnp.sum(mlp_part * mlp_part, axis=(1, 3))],
        axis=1,
    )
    return jnp.concatenate([jnp.sum(edge_part * edge_part, axis=(1, 2)), layer_part.reshape(-1)])


def per_device_general(
    patches,
    mask,
    edge,
    attn_w,
    mlp_w,
    vecs,
    edge_m,
    edge_v,
    attn_m,
    attn_v,
    mlp_m,
    mlp_v,
    vecs_m,
    vecs_v,
    teacher_edge,
    teacher_attn,
    teacher_mlp,
    teacher_vecs,
):
    layer_count = attn_w.shape[0]
    local_count = patches.shape[0]
    clip_count = patches.shape[1]
    model_width = patches.shape[2]
    last_row = 4 * layer_count
    student_edge, student_vecs = fetch_edges(edge, vecs)
    teach_edge, teach_vecs = fetch_edges(teacher_edge, teacher_vecs)
    seq_total = local_count * lax.axis_size("tensor")
    stream = jnp.einsum(
        "scp,pd->scd",
        patches,
        teach_edge[0].astype(jnp.bfloat16),
        preferred_element_type=jnp.float32,
    )
    summed = jnp.zeros_like(stream)
    for layer_index in range(layer_count):
        attn_full, mlp_full = fetch_layer(teacher_attn[layer_index], teacher_mlp[layer_index])
        stream, unused = run_block(
            stream, attn_full, mlp_full, teach_vecs[4 * layer_index : 4 * layer_index + 4]
        )
        first_sum, square_sum = lax.psum(
            (jnp.sum(stream, axis=0), jnp.sum(stream * stream, axis=0)), "tensor"
        )
        average = first_sum / seq_total
        spread = square_sum / seq_total - average * average
        summed = summed + (stream - average) * lax.rsqrt(spread + inst_epsilon)
    target = summed / layer_count
    masked = mask.astype(jnp.float32)[..., None]
    embedded = jnp.einsum(
        "scp,pd->scd",
        patches,
        student_edge[0].astype(jnp.bfloat16),
        preferred_element_type=jnp.float32,
    )
    stream = embedded * (1.0 - masked) + masked * student_vecs[last_row + 2]
    saved_list = []
    weight_list = []
    for layer_index in range(layer_count):
        attn_full, mlp_full = fetch_layer(attn_w[layer_index], mlp_w[layer_index])
        stream, saved = run_block(
            stream, attn_full, mlp_full, student_vecs[4 * layer_index : 4 * layer_index + 4]
        )
        saved_list.append(saved)
        weight_list.append((attn_full, mlp_full))
    final_low = norm_rows(stream, student_vecs[last_row], student_vecs[last_row + 1]).astype(
        jnp.bfloat16
    )
    head_low = student_edge[1].astype(jnp.bfloat16)
    predicted = (
        jnp.einsum("scd,de->sce", final_low, head_low, preferred_element_type=jnp.float32)
        + student_vecs[last_row + 3]
    )
    offset = predicted - target
    size_abs = jnp.abs(offset)
    loss_part = (
        jnp.sum(jnp.where(size_abs < 1.0, 0.5 * offset * offset, size_abs - 0.5) * masked)
        / model_width**0.5
    )
    grad_pred = jnp.clip(offset, -1.0, 1.0) * masked / model_width**0.5
    grad_low = grad_pred.astype(jnp.bfloat16)
    grad_head = jnp.einsum("scd,sce->de", final_low, grad_low, preferred_element_type=jnp.float32)
    grad_bias = jnp.sum(grad_pred, axis=(0, 1))
    grad_final = jnp.einsum("sce,de->scd", grad_low, head_low, preferred_element_type=jnp.float32)
    unused, final_pull = jax.vjp(
        norm_rows, stream, student_vecs[last_row], student_vecs[last_row + 1]
    )
    grad_stream, grad_final_gain, grad_final_shift = final_pull(grad_final)
    attn_grads = []
    mlp_grads = []
    vector_rows = []
    for layer_index in reversed(range(layer_count)):
        attn_full, mlp_full = fetch_again(attn_w[layer_index], mlp_w[layer_index])
        grad_stream, layer_attn, layer_mlp, vector_grads = back_block(
            grad_stream,
            saved_list[layer_index],
            attn_full,
            mlp_full,
            student_vecs[4 * layer_index : 4 * layer_index + 4],
        )
        attn_grads.insert(0, layer_attn)
        mlp_grads.insert(0, layer_mlp)
        vector_rows.insert(0, vector_grads)
    grad_embed = (grad_stream * (1.0 - masked)).astype(jnp.bfloat16)
    grad_mask_vec = jnp.sum(grad_stream * masked, axis=(0, 1))
    grad_patch = jnp.einsum("scp,scd->pd", patches, grad_embed, preferred_element_type=jnp.float32)
    vector_grad = jnp.concatenate(
        vector_rows + [jnp.stack([grad_final_gain, grad_final_shift, grad_mask_vec, grad_bias])],
        axis=0,
    )
    edge_grad, vecs_grad = (
        lax.psum_scatter(
            jnp.stack([grad_patch, grad_head]), ("dp", "tensor"), scatter_dimension=1, tiled=True
        ),
        lax.psum_scatter(vector_grad, ("dp", "tensor"), scatter_dimension=1, tiled=True),
    )
    attn_grad = jnp.stack(attn_grads)
    mlp_grad = jnp.stack(mlp_grads)
    edge_first, edge_second, edge_update = direction(edge, edge_grad, edge_m, edge_v)
    attn_first, attn_second, attn_update = direction(attn_w, attn_grad, attn_m, attn_v)
    mlp_first, mlp_second, mlp_update = direction(mlp_w, mlp_grad, mlp_m, mlp_v)
    vecs_first, vecs_second, vecs_update = direction(vecs, vecs_grad, vecs_m, vecs_v)
    weight_sq, update_sq, loss_total = lax.psum(
        (
            matrix_squares(edge, attn_w, mlp_w),
            matrix_squares(edge_update, attn_update, mlp_update),
            loss_part,
        ),
        ("dp", "tensor"),
    )
    weight_norm = jnp.sqrt(weight_sq)
    update_norm = jnp.sqrt(update_sq)
    trust = weight_norm / (update_norm + adam_epsilon)
    edge_trust = trust[0:2]
    layer_trust = trust[2:].reshape(layer_count, 6)
    new_edge = edge - learn_rate * edge_trust[:, None, None] * edge_update
    new_attn = attn_w - learn_rate * layer_trust[:, None, 0:4, None] * attn_update
    new_mlp = mlp_w - learn_rate * layer_trust[:, None, 4:6, None] * mlp_update
    new_vecs = vecs - learn_rate * vecs_update
    keep_share = 1.0 - teacher_decay
    token_total = seq_total * clip_count * lax.axis_size("dp")
    return (
        loss_total / token_total,
        jnp.stack([weight_norm, update_norm]),
        new_edge,
        new_attn,
        new_mlp,
        new_vecs,
        edge_first,
        edge_second[0],
        edge_second[1],
        attn_first,
        attn_second[:, :, 0:3],
        attn_second[:, :, 3],
        mlp_first,
        mlp_second,
        vecs_first,
        vecs_second,
        keep_share * (new_edge - teacher_edge),
        keep_share * (new_attn - teacher_attn),
        keep_share * (new_mlp - teacher_mlp),
        keep_share * (new_vecs - teacher_vecs),
        new_edge.astype(jnp.bfloat16),
        new_attn.astype(jnp.bfloat16),
        new_mlp.astype(jnp.bfloat16),
        new_vecs.astype(jnp.bfloat16),
    )


MESH = pl.DeviceIdType.MESH
ORDERS = (("z", "x", "y"), ("x", "y", "z"), ("y", "z", "x"))
LOW = jnp.bfloat16
ALL = slice(None)


def coords():
    d = lax.axis_index("dp")
    t = lax.axis_index("tensor")
    return dict(a=t // 2, z=t % 2, y=d // 4, x=(d // 2) % 2, c=d % 2)


def ident(co):
    return (co["y"] * 4 + co["x"] * 2 + co["c"], co["a"] * 2 + co["z"])


def flip(co, k):
    co = dict(co)
    co[k] = 1 - co[k]
    return ident(co)


def place(co, full, rows):
    return tuple(ALL if k in full else co[k] for k in "azyxc") + (rows,)


def gather_kernel(
    attn_mine,
    attn_other,
    mlp_mine,
    mlp_other,
    edge_mine,
    edge_other,
    vec_mine,
    vec_other,
    patch,
    attn_all,
    mlp_all,
    edge_all,
    vec_all,
    patch_all,
    local_sem,
    send_sem,
    recv_sem,
    patch_sem,
):
    co = coords()
    me = ident(co)
    column = co["y"] * 2 + co["x"]
    barrier = pltpu.get_barrier_semaphore()
    for k in range(1, 8):
        to = (column * 2 + (co["c"] + k // 4) % 2, (me[1] + k % 4) % 4)
        pl.semaphore_signal(barrier, inc=1, device_id=to, device_id_type=MESH)
    for k in "xy":
        pl.semaphore_signal(barrier, inc=1, device_id=flip(co, k), device_id_type=MESH)
    pl.semaphore_wait(barrier, 9)
    rows = attn_mine.shape[1]
    items = [
        (edge_mine, edge_other, edge_all, edge_mine.shape[0], 3),
        (vec_mine, vec_other, vec_all, 16, 1),
    ]
    for l in range(2):
        items.append((attn_mine.at[l], attn_other.at[l], attn_all.at[l], rows, 3))
        items.append((mlp_mine.at[l], mlp_other.at[l], mlp_all.at[l], rows, 3))
    sent = []

    def remote(source, target, i, j, k, to):
        copy = pltpu.make_async_remote_copy(
            src_ref=source,
            dst_ref=target,
            send_sem=send_sem.at[i, j, k],
            recv_sem=recv_sem.at[i, j, k],
            device_id=to,
            device_id_type=MESH,
        )
        copy.start()
        sent.append(copy)
        return copy

    def at(ref, index):
        return ref.at[(ALL,) * (len(ref.shape) - 7) + index]

    local = []
    first = []
    for i, (mine, other, full, count, parts) in enumerate(items):
        copy = pltpu.make_async_copy(mine, at(full, place(co, "", ALL)), local_sem.at[i])
        copy.start()
        local.append(copy)
        first.append(remote(other, at(full, place(co, "", ALL)), i, 0, 4, flip(co, "a")))
    for r in range(2):
        to = (column * 2 + co["a"], 2 * r + co["c"])
        same = jnp.logical_and(to[0] == me[0], to[1] == me[1])
        target = patch_all.at[co["z"]]

        @pl.when(same)
        def _():
            pltpu.make_async_copy(patch, target, patch_sem.at[2]).start()

        @pl.when(jnp.logical_not(same))
        def _():
            pltpu.make_async_remote_copy(
                src_ref=patch,
                dst_ref=target,
                send_sem=patch_sem.at[3 + r],
                recv_sem=patch_sem.at[co["z"]],
                device_id=to,
                device_id_type=MESH,
            ).start()

    table = {}
    for wave in range(len(items) + 5):
        for i, (mine, other, full, count, parts) in enumerate(items):
            s = wave - i
            if s < 0 or s > 4:
                continue
            if s == 0:
                local[i].wait()
                first[i].wait_recv()
            else:
                for copy in table[i, s - 1]:
                    copy.wait_recv()
            if s < 3:
                copies = []
                for p in range(parts):
                    order = ORDERS[p]
                    span = ALL if parts == 1 else pl.ds(p * (count // parts), count // parts)
                    ref = at(full, place(co, ("a",) + order[:s], span))
                    copies.append(remote(ref, ref, i, p, s, flip(co, order[s])))
                table[i, s] = copies
            elif s == 3:
                ref = at(full, place(co, "axyz", ALL))
                table[i, s] = [remote(ref, ref, i, 0, 3, flip(co, "c"))]
    for q in range(2):
        origin = (column * 2 + co["z"], co["c"] * 2 + q)
        same = jnp.logical_and(origin[0] == me[0], origin[1] == me[1])

        @pl.when(same)
        def _():
            pltpu.make_async_copy(patch, patch_all.at[q], patch_sem.at[2]).wait()

        @pl.when(jnp.logical_not(same))
        def _():
            pltpu.make_async_remote_copy(
                src_ref=patch,
                dst_ref=patch_all.at[q],
                send_sem=patch_sem.at[3],
                recv_sem=patch_sem.at[q],
                device_id=me,
                device_id_type=MESH,
            ).wait_recv()

    for r in range(2):
        to = (column * 2 + co["a"], 2 * r + co["c"])
        same = jnp.logical_and(to[0] == me[0], to[1] == me[1])

        @pl.when(jnp.logical_not(same))
        def _():
            pltpu.make_async_remote_copy(
                src_ref=patch,
                dst_ref=patch_all.at[0],
                send_sem=patch_sem.at[3 + r],
                recv_sem=patch_sem.at[0],
                device_id=me,
                device_id_type=MESH,
            ).wait_send()

    for copy in sent:
        copy.wait_send()


ANY = pl.BlockSpec(memory_space=pl.ANY)
DMA = pltpu.SemaphoreType.DMA


def shape_of(shape, kind=LOW):
    return jax.ShapeDtypeStruct(shape, kind)


def gather_all(*parts):
    rows, width = parts[0].shape[1:]
    edge_rows = parts[4].shape[0]
    cube = (2, 2, 2, 2, 2)
    return pl.pallas_call(
        gather_kernel,
        out_shape=(
            shape_of((2,) + cube + (rows, width)),
            shape_of((2, 2) + cube + (rows, parts[2].shape[3])),
            shape_of(cube + (edge_rows, width)),
            shape_of(cube + parts[6].shape, jnp.float32),
            shape_of((2,) + parts[8].shape),
        ),
        in_specs=[ANY] * 9,
        out_specs=(ANY,) * 5,
        scratch_shapes=[DMA((6,)), DMA((6, 3, 5)), DMA((6, 3, 5)), DMA((5,))],
        compiler_params=pltpu.CompilerParams(collective_id=0, has_side_effects=True),
    )(*parts)


def scatter_kernel(layout, *refs):
    count = len(layout)
    sources, targets, scratch = refs[:4], refs[4:8], refs[8:-4]
    local_sem, send_sem, recv_sem, out_sem = refs[-4:]
    co = coords()
    barrier = pltpu.get_barrier_semaphore()
    for k in "azyxc":
        pl.semaphore_signal(barrier, inc=1, device_id=flip(co, k), device_id_type=MESH)
    pl.semaphore_wait(barrier, 5)
    sent = []

    def remote(source, target, i, j, k, to):
        copy = pltpu.make_async_remote_copy(
            src_ref=source,
            dst_ref=target,
            send_sem=send_sem.at[i, j, k],
            recv_sem=recv_sem.at[i, j, k],
            device_id=to,
            device_id_type=MESH,
        )
        copy.start()
        sent.append(copy)
        return copy

    def pick(fixed, span):
        return (ALL,) + tuple(fixed.get(k, ALL) for k in "azyx") + (span,)

    items = []
    spot = 0
    for which, layer, lead, rows, cols, kind, parts in layout:
        item = dict(lead=lead, rows=rows, parts=parts, kind=kind)
        source, target = sources[which], targets[which]
        if layer is not None:
            source, target = source.at[layer], target.at[layer]
        item.update(source=source, target=target)
        item.update(mine=scratch[spot], swap=scratch[spot + 1])
        spot += 2
        item["part"] = []
        for p in range(parts):
            item["part"].append(scratch[spot : spot + 3])
            spot += 3
        item["last"] = scratch[spot]
        spot += 1
        items.append(item)

    def span_of(item, p):
        size = item["rows"] // item["parts"]
        return ALL if item["parts"] == 1 else pl.ds(p * size, size)

    def squeeze(item, ref, index):
        if len(item["source"].shape) == 7:
            return ref.at[(0,) + index[1:]]
        return ref.at[index]

    def add_into(item, ref, index, other, index_other):
        total = ref[index].astype(jnp.float32) + other[index_other].astype(jnp.float32)
        ref[index] = total.astype(item["kind"])

    def add_swap(item):
        def body(n, _):
            index = (n // 16, n // 8 % 2, n // 4 % 2, n // 2 % 2, n % 2)
            add_into(item, item["mine"], index, item["swap"], index)
            return 0

        lax.fori_loop(0, item["lead"] * 16, body, 0)

    def add_part(item, p, s):
        done = ORDERS[p][::-1][: s + 1]
        left = [k for k in "azyx" if k not in done]

        def body(n, _):
            at = {}
            for k in reversed(left):
                at[k] = n % 2
                n = n // 2
            there = (n,) + tuple(0 if k in done else at[k] for k in "azyx")
            here = (n,) + tuple(co[k] if k in done else at[k] for k in "azyx")
            add_into(item, item["mine"], here + (span_of(item, p),), item["part"][p][s], there)
            return 0

        lax.fori_loop(0, item["lead"] * 2 ** len(left), body, 0)

    def last_hop(i, item):
        return pltpu.make_async_remote_copy(
            src_ref=item["mine"].at[pick({**own, "a": 1}, ALL)],
            dst_ref=item["last"],
            send_sem=send_sem.at[i, 0, 3],
            recv_sem=recv_sem.at[i, 0, 3],
            device_id=flip(co, "a"),
            device_id_type=MESH,
        )

    own = {q: co[q] for q in "zyx"}
    local = []
    table = {}
    for i, item in enumerate(items):
        source = item["source"]
        lead = (ALL,) * (len(source.shape) - 3)
        copy = pltpu.make_async_copy(
            source.at[lead + (co["c"],)], squeeze(item, item["mine"], (ALL,)), local_sem.at[i]
        )
        copy.start()
        local.append(copy)
        table[i, 0] = [
            remote(
                source.at[lead + (1 - co["c"],)],
                squeeze(item, item["swap"], (ALL,)),
                i,
                0,
                4,
                flip(co, "c"),
            )
        ]
    for wave in range(count + 6):
        for i, item in enumerate(items):
            s = wave - i
            if s < 1 or s > 5:
                continue
            if s == 1:
                local[i].wait()
                table[i, 0][0].wait_recv()
                add_swap(item)
            elif s <= 4:
                for p, copy in enumerate(table[i, s - 1]):
                    copy.wait_recv()
                    add_part(item, p, s - 2)
            if s <= 3:
                copies = []
                for p in range(item["parts"]):
                    order = ORDERS[p][::-1]
                    k = order[s - 1]
                    fixed = {q: co[q] for q in order[: s - 1]}
                    source = item["mine"].at[pick({**fixed, k: 1 - co[k]}, span_of(item, p))]
                    target = item["part"][p][s - 1].at[pick({q: 0 for q in order[:s]}, ALL)]
                    copies.append(remote(source, target, i, p, s - 1, flip(co, k)))
                table[i, s] = copies
            elif s == 4:

                @pl.when(co["a"] == 0)
                def _():
                    last_hop(i, item).start()
                    result = squeeze(item, item["mine"], pick({**own, "a": 0}, ALL))
                    pltpu.make_async_copy(result, item["target"], out_sem.at[i]).start()

            else:
                result = squeeze(item, item["last"], (ALL,))

                @pl.when(co["a"] == 1)
                def _():
                    last_hop(i, item).wait_recv()
                    pltpu.make_async_copy(result, item["target"], out_sem.at[i]).start()

                @pl.when(co["a"] == 0)
                def _():
                    last_hop(i, item).wait_send()

                pltpu.make_async_copy(result, item["target"], out_sem.at[i]).wait()
    for copy in sent:
        copy.wait_send()


def scatter_all(attn, mlp, edge, vec):
    rows, width = attn.shape[-2:]
    hidden = mlp.shape[-1]
    edge_rows = edge.shape[-2]
    layout = (
        (1, 1, 2, rows, hidden, LOW, 3),
        (0, 1, 1, rows, width, LOW, 3),
        (1, 0, 2, rows, hidden, LOW, 3),
        (0, 0, 1, rows, width, LOW, 3),
        (2, None, 1, edge_rows, width, LOW, 3),
        (3, None, 1, vec.shape[-2], vec.shape[-1], jnp.float32, 1),
    )
    scratch = []
    for which, layer, lead, count, cols, kind, parts in layout:
        scratch.append(pltpu.VMEM((lead, 2, 2, 2, 2, count, cols), kind))
        scratch.append(pltpu.VMEM((lead, 2, 2, 2, 2, count, cols), kind))
        for p in range(parts):
            order = ORDERS[p][::-1]
            for s in range(3):
                dims = tuple(1 if k in order[: s + 1] else 2 for k in "azyx")
                scratch.append(pltpu.VMEM((lead,) + dims + (count // parts, cols), kind))
        scratch.append(pltpu.VMEM((lead, count, cols), kind))
    return pl.pallas_call(
        lambda *refs: scatter_kernel(layout, *refs),
        out_shape=(
            shape_of((2, rows, width)),
            shape_of((2, 2, rows, hidden)),
            shape_of((edge_rows, width)),
            shape_of(vec.shape[-2:], jnp.float32),
        ),
        in_specs=[ANY] * 4,
        out_specs=(ANY,) * 4,
        scratch_shapes=scratch + [DMA((6,)), DMA((6, 3, 5)), DMA((6, 3, 5)), DMA((6,))],
        compiler_params=pltpu.CompilerParams(
            collective_id=1, has_side_effects=True, vmem_limit_bytes=60 * 2**20
        ),
    )(attn, mlp, edge, vec)


def total_kernel(value, out, held, send_sem, recv_sem):
    co = coords()
    barrier = pltpu.get_barrier_semaphore()
    for k in "azyxc":
        pl.semaphore_signal(barrier, inc=1, device_id=flip(co, k), device_id_type=MESH)
    pl.semaphore_wait(barrier, 5)
    held[0] = value[...]
    for s, k in enumerate("cxyza"):
        copy = pltpu.make_async_remote_copy(
            src_ref=held.at[2 * s],
            dst_ref=held.at[2 * s + 1],
            send_sem=send_sem.at[s],
            recv_sem=recv_sem.at[s],
            device_id=flip(co, k),
            device_id_type=MESH,
        )
        copy.start()
        copy.wait()
        held[2 * s + 2] = held[2 * s] + held[2 * s + 1]
    out[...] = held[10]


def total_all(value):
    return pl.pallas_call(
        total_kernel,
        out_shape=shape_of(value.shape, jnp.float32),
        in_specs=[pl.BlockSpec(memory_space=pltpu.VMEM)],
        out_specs=pl.BlockSpec(memory_space=pltpu.VMEM),
        scratch_shapes=[pltpu.VMEM((11,) + value.shape, jnp.float32), DMA((5,)), DMA((5,))],
        compiler_params=pltpu.CompilerParams(collective_id=2, has_side_effects=True),
    )(value)


def dot(left, right):
    return jnp.dot(left, right, preferred_element_type=jnp.float32)


def dot_nt(left, right):
    return lax.dot_general(
        left, right, (((1,), (1,)), ((), ())), preferred_element_type=jnp.float32
    )


def dot_tn(left, right):
    return lax.dot_general(
        left, right, (((0,), (0,)), ((), ())), preferred_element_type=jnp.float32
    )


def swap_core(value):
    count = lax.axis_size("dp")
    return lax.ppermute(value, "dp", [(i, i ^ 1) for i in range(count)])


def forward_rows(stream, attn, mlp, gains):
    block = attn.shape[2] // 4
    heads = block // HEAD
    normed = norm_rows(stream, gains[0], gains[1]).astype(LOW)
    joined = [dot(normed, attn[z][:, : 3 * block]).astype(LOW) for z in range(4)]
    queries = jnp.concatenate([j[:, :block] for j in joined], axis=1)
    keyval = jnp.stack(
        [
            jnp.concatenate([j[:, block : 2 * block] for j in joined], axis=1),
            jnp.concatenate([j[:, 2 * block :] for j in joined], axis=1),
        ]
    )
    keyval = jnp.concatenate([keyval, swap_core(keyval)], axis=1)
    split = lambda value: value.reshape(value.shape[0], 4 * heads, HEAD)
    context, log_total = attend_forward((split(queries), split(keyval[0]), split(keyval[1])))
    context = context.reshape(queries.shape)
    middle = stream
    for z in range(4):
        middle = middle + dot_nt(context[:, z * block : (z + 1) * block], attn[z][:, 3 * block :])
    hidden = norm_rows(middle, gains[2], gains[3]).astype(LOW)
    upward = jnp.concatenate([dot(hidden, mlp[0, z]) for z in range(4)], axis=1)
    active = exact_gelu(upward).astype(LOW)
    wide = mlp.shape[3]
    result = middle
    for z in range(4):
        result = result + dot_nt(active[:, z * wide : (z + 1) * wide], mlp[1, z])
    return result, (
        stream,
        normed,
        queries,
        keyval,
        log_total,
        context,
        middle,
        hidden,
        upward,
        active,
    )


def backward_rows(grad, saved, attn, mlp, gains):
    stream, normed, queries, keyval, log_total, context, middle, hidden, upward, active = saved
    block = attn.shape[2] // 4
    heads = block // HEAD
    wide = mlp.shape[3]
    rows = grad.shape[0]
    low_grad = grad.astype(LOW)
    grad_active = jnp.concatenate([dot(low_grad, mlp[1, z]) for z in range(4)], axis=1)
    unused, gelu_pull = jax.vjp(exact_gelu, upward)
    grad_upward = gelu_pull(grad_active)[0].astype(LOW)
    cut = lambda value, z, size: value[:, z * size : (z + 1) * size]
    grad_mlp = jnp.stack(
        [
            jnp.stack([dot_tn(hidden, cut(grad_upward, z, wide)).astype(LOW) for z in range(4)]),
            jnp.stack([dot_tn(low_grad, cut(active, z, wide)).astype(LOW) for z in range(4)]),
        ]
    )
    grad_hidden = sum(dot_nt(cut(grad_upward, z, wide), mlp[0, z]) for z in range(4))
    unused, second_pull = jax.vjp(norm_rows, middle, gains[2], gains[3])
    grad_norm, grad_gain_two, grad_shift_two = second_pull(grad_hidden)
    grad_middle = grad + grad_norm
    low_middle = grad_middle.astype(LOW)
    grad_context = jnp.concatenate(
        [dot(low_middle, attn[z][:, 3 * block :]).astype(LOW) for z in range(4)], axis=1
    )
    split = lambda value: value.reshape(value.shape[0], 4 * heads, HEAD)
    grad_queries, grad_keys, grad_values = attend_backward(
        (split(queries), split(keyval[0]), split(keyval[1]), log_total, split(grad_context))
    )
    grad_keyval = jnp.stack([grad_keys, grad_values]).reshape(keyval.shape)
    other = swap_core(grad_keyval[:, rows:].astype(LOW))
    grad_keyval = (grad_keyval[:, :rows] + other.astype(jnp.float32)).astype(LOW)
    grad_queries = grad_queries.reshape(rows, 4 * block).astype(LOW)
    pieces = []
    grad_normed = 0.0
    for z in range(4):
        joined = jnp.concatenate(
            [
                cut(grad_queries, z, block),
                cut(grad_keyval[0], z, block),
                cut(grad_keyval[1], z, block),
            ],
            axis=1,
        )
        grad_normed = grad_normed + dot_nt(joined, attn[z][:, : 3 * block])
        pieces.append(
            jnp.concatenate(
                [
                    dot_tn(normed, joined).astype(LOW),
                    dot_tn(low_middle, cut(context, z, block)).astype(LOW),
                ],
                axis=1,
            )
        )
    unused, first_pull = jax.vjp(norm_rows, stream, gains[0], gains[1])
    grad_norm, grad_gain_one, grad_shift_one = first_pull(grad_normed)
    vectors = [grad_gain_one, grad_shift_one, grad_gain_two, grad_shift_two]
    return grad_middle + grad_norm, jnp.stack(pieces), grad_mlp, vectors


def per_device(
    patches,
    mask,
    edge,
    attn_w,
    mlp_w,
    vecs,
    edge_m,
    edge_v,
    attn_m,
    attn_v,
    mlp_m,
    mlp_v,
    vecs_m,
    vecs_v,
    teacher_edge,
    teacher_attn,
    teacher_mlp,
    teacher_vecs,
):
    layer_count, rows, kinds, block = attn_w.shape
    wide = mlp_w.shape[3]
    width = patches.shape[2]
    quarter = patches.shape[0]
    edge_rows = edge.shape[1]
    vec_count, vec_cols = vecs.shape
    last_row = 4 * layer_count
    teaching = lax.axis_index("tensor") >= 2
    dp_size = lax.axis_size("dp")

    def pack(own_edge, own_attn, own_mlp, own_vecs):
        return (
            own_attn.astype(LOW).reshape(layer_count, rows, kinds * block),
            jnp.swapaxes(own_mlp.astype(LOW), 1, 2),
            own_edge.astype(LOW).reshape(2 * edge_rows, width),
            jnp.pad(own_vecs, ((0, 16 - vec_count), (0, 128 - vec_cols))),
        )

    student = pack(edge, attn_w, mlp_w, vecs)
    teacher = pack(teacher_edge, teacher_attn, teacher_mlp, teacher_vecs)
    parts = []
    for left, right in zip(student, teacher):
        parts += [jnp.where(teaching, right, left), jnp.where(teaching, left, right)]
    marks = jnp.broadcast_to(mask.astype(LOW), (quarter, 128))
    parts.append(jnp.concatenate([patches.reshape(quarter, width), marks], axis=1))
    attn_all, mlp_all, edge_all, vec_all, patch_all = gather_all(*parts)
    attn_all = attn_all.reshape(layer_count, 4, dp_size * rows, kinds * block)
    mlp_all = mlp_all.reshape(layer_count, 2, 4, dp_size * rows, wide)
    by_owner = (2, 3, 4, 0, 1, 5, 6)
    edge_all = edge_all.transpose(by_owner).reshape(4 * dp_size, 2, edge_rows, width)
    embed_w = edge_all[:, 0].reshape(width, width)
    head_w = edge_all[:, 1].reshape(width, width)
    vec_all = vec_all.transpose(by_owner).reshape(4 * dp_size, 16, 128)
    gains = jnp.moveaxis(vec_all[:, :vec_count, :vec_cols], 0, 1).reshape(vec_count, width)
    patch_all = patch_all.reshape(2 * quarter, width + 128)
    pixels = patch_all[:, :width]
    masked = patch_all[:, width : width + 1].astype(jnp.float32)
    hide = jnp.where(teaching, 0.0, masked)
    stream = dot(pixels, embed_w) * (1.0 - hide) + hide * gains[last_row + 2]
    saved_list = []
    summed = jnp.zeros_like(stream)
    for layer in range(layer_count):
        stream, saved = forward_rows(
            stream, attn_all[layer], mlp_all[layer], gains[4 * layer : 4 * layer + 4]
        )
        saved_list.append(saved)
        sums = jnp.stack([jnp.sum(stream, axis=0), jnp.sum(stream * stream, axis=0)])
        sums = (sums + swap_core(sums)) / (4 * quarter)
        spread = sums[1] - sums[0] * sums[0]
        summed = summed + (stream - sums[0]) * lax.rsqrt(spread + inst_epsilon)
    target = lax.ppermute(
        (summed / layer_count).astype(LOW), "tensor", [(i, i ^ 2) for i in range(4)]
    ).astype(jnp.float32)
    final_low = norm_rows(stream, gains[last_row], gains[last_row + 1]).astype(LOW)
    offset = dot(final_low, head_w) + gains[last_row + 3] - target
    size_abs = jnp.abs(offset)
    loss_part = (
        jnp.sum(jnp.where(size_abs < 1.0, 0.5 * offset * offset, size_abs - 0.5) * masked)
        / width**0.5
    )
    grad_pred = jnp.clip(offset, -1.0, 1.0) * masked / width**0.5
    grad_low = grad_pred.astype(LOW)
    grad_head = dot_tn(final_low, grad_low)
    grad_bias = jnp.sum(grad_pred, axis=0)
    unused, final_pull = jax.vjp(norm_rows, stream, gains[last_row], gains[last_row + 1])
    grad, grad_final_gain, grad_final_shift = final_pull(dot_nt(grad_low, head_w))
    attn_list = []
    mlp_list = []
    vector_rows = []
    for layer in reversed(range(layer_count)):
        grad, layer_attn, layer_mlp, vectors = backward_rows(
            grad,
            saved_list[layer],
            attn_all[layer],
            mlp_all[layer],
            gains[4 * layer : 4 * layer + 4],
        )
        attn_list.insert(0, layer_attn)
        mlp_list.insert(0, layer_mlp)
        vector_rows = vectors + vector_rows
    grad_embed = (grad * (1.0 - masked)).astype(LOW)
    grad_mask = jnp.sum(grad * masked, axis=0)
    grad_patch = dot_tn(pixels, grad_embed)
    cube = (2, 2, 2, 2, 2)
    to_owner = (3, 4, 0, 1, 2)
    attn_send = jnp.stack(attn_list).reshape((layer_count,) + cube + (rows, kinds * block))
    mlp_send = jnp.stack(mlp_list).reshape((layer_count, 2) + cube + (rows, wide))
    edge_send = jnp.stack([grad_patch, grad_head]).astype(LOW)
    edge_send = edge_send.reshape((2,) + cube + (edge_rows, width))
    edge_send = edge_send.transpose(4, 5, 1, 2, 3, 0, 6, 7).reshape(cube + (2 * edge_rows, width))
    loss_row = jnp.full((width,), loss_part)
    vec_send = jnp.stack(
        vector_rows + [grad_final_gain, grad_final_shift, grad_mask, grad_bias, loss_row]
    )
    vec_send = jnp.pad(vec_send, ((0, 15 - vec_count), (0, 0))).reshape((16,) + cube + (vec_cols,))
    vec_send = jnp.pad(
        vec_send.transpose(4, 5, 1, 2, 3, 0, 6), ((0, 0),) * 6 + ((0, 128 - vec_cols),)
    )
    attn_grad, mlp_grad, edge_grad, vecs_grad = scatter_all(
        attn_send, mlp_send, edge_send, vec_send
    )
    attn_grad = attn_grad.astype(jnp.float32).reshape(attn_w.shape)
    mlp_grad = jnp.swapaxes(mlp_grad.astype(jnp.float32), 1, 2)
    edge_grad = edge_grad.astype(jnp.float32).reshape(edge.shape)
    loss_total = vecs_grad[vec_count, 0]
    vecs_grad = vecs_grad[:vec_count, :vec_cols]
    edge_first, edge_second, edge_update = direction(edge, edge_grad, edge_m, edge_v)
    attn_first, attn_second, attn_update = direction(attn_w, attn_grad, attn_m, attn_v)
    mlp_first, mlp_second, mlp_update = direction(mlp_w, mlp_grad, mlp_m, mlp_v)
    vecs_first, vecs_second, vecs_update = direction(vecs, vecs_grad, vecs_m, vecs_v)
    squares = jnp.stack(
        [
            matrix_squares(edge, attn_w, mlp_w),
            matrix_squares(edge_update, attn_update, mlp_update),
        ]
    )
    squares = jnp.pad(squares, ((0, 6), (0, 128 - squares.shape[1])))
    norms = jnp.sqrt(total_all(squares)[:2, : 2 + 6 * layer_count])
    trust = norms[0] / (norms[1] + adam_epsilon)
    edge_trust = trust[0:2]
    layer_trust = trust[2:].reshape(layer_count, 6)
    new_edge = edge - learn_rate * edge_trust[:, None, None] * edge_update
    new_attn = attn_w - learn_rate * layer_trust[:, None, 0:4, None] * attn_update
    new_mlp = mlp_w - learn_rate * layer_trust[:, None, 4:6, None] * mlp_update
    new_vecs = vecs - learn_rate * vecs_update
    keep_share = 1.0 - teacher_decay
    token_total = 4 * quarter * dp_size
    return (
        loss_total / token_total,
        norms,
        new_edge,
        new_attn,
        new_mlp,
        new_vecs,
        edge_first,
        edge_second[0],
        edge_second[1],
        attn_first,
        attn_second[:, :, 0:3],
        attn_second[:, :, 3],
        mlp_first,
        mlp_second,
        vecs_first,
        vecs_second,
        keep_share * (new_edge - teacher_edge),
        keep_share * (new_attn - teacher_attn),
        keep_share * (new_mlp - teacher_mlp),
        keep_share * (new_vecs - teacher_vecs),
        new_edge.astype(LOW),
        new_attn.astype(LOW),
        new_mlp.astype(LOW),
        new_vecs.astype(LOW),
    )


def solution(mesh):
    placed = (
        P("tensor", "dp", None),
        P("tensor", "dp"),
        P(None, ("dp", "tensor"), None),
        P(None, "dp", None, "tensor"),
        P(None, "dp", None, "tensor"),
        P(None, ("dp", "tensor")),
        P(None, ("dp", "tensor"), None),
        P(None, ("dp", "tensor"), None),
        P(None, "dp", None, "tensor"),
        P(None, "dp", None, "tensor"),
        P(None, "dp", None, "tensor"),
        P(None, "dp", None, "tensor"),
        P(None, ("dp", "tensor")),
        P(None, ("dp", "tensor")),
        P(None, ("dp", "tensor"), None),
        P(None, "dp", None, "tensor"),
        P(None, "dp", None, "tensor"),
        P(None, ("dp", "tensor")),
    )
    planned = dict(mesh.shape) == {"dp": 8, "tensor": 4}
    return jax.shard_map(
        per_device if planned else per_device_general,
        mesh=mesh,
        in_specs=placed,
        out_specs=(
            P(),
            P(),
            P(None, ("dp", "tensor"), None),
            P(None, "dp", None, "tensor"),
            P(None, "dp", None, "tensor"),
            P(None, ("dp", "tensor")),
            P(None, ("dp", "tensor"), None),
            P(("dp", "tensor"), None),
            P(("dp", "tensor"), None),
            P(None, "dp", None, "tensor"),
            P(None, "dp", None, "tensor"),
            P(None, "dp", "tensor"),
            P(None, "dp", None, "tensor"),
            P(None, "dp", None, "tensor"),
            P(None, ("dp", "tensor")),
            P(None, ("dp", "tensor")),
            P(None, ("dp", "tensor"), None),
            P(None, "dp", None, "tensor"),
            P(None, "dp", None, "tensor"),
            P(None, ("dp", "tensor")),
            P(None, ("dp", "tensor"), None),
            P(None, "dp", None, "tensor"),
            P(None, "dp", None, "tensor"),
            P(None, ("dp", "tensor")),
        ),
        check_vma=False,
    )
```

```python
import jax
import jax.numpy as jnp
from jax import lax
from jax.experimental import pallas as pl
from jax.experimental.pallas import tpu as pltpu
from jax.sharding import PartitionSpec as P

HEAD = 64


norm_epsilon = 1e-06
inst_epsilon = 1e-05
first_decay = 0.9
second_decay = 0.999
adam_epsilon = 1e-06
weight_decay = 0.01
learn_rate = 0.3
teacher_decay = 0.999
step_count = 10


def norm_rows(values, gain, shift):
    average = jnp.mean(values, axis=-1, keepdims=True)
    centered = values - average
    spread = jnp.mean(centered * centered, axis=-1, keepdims=True)
    return centered * lax.rsqrt(spread + norm_epsilon) * gain + shift


def exact_gelu(values):
    return jax.nn.gelu(values, approximate=False)


def fetch_edges(edge_part, vector_part):
    return (
        lax.all_gather(edge_part, ("dp", "tensor"), axis=1, tiled=True),
        lax.all_gather(vector_part, ("dp", "tensor"), axis=1, tiled=True),
    )


def fetch_layer(attn_part, mlp_part):
    return (
        lax.all_gather(attn_part.astype(jnp.bfloat16), "dp", axis=0, tiled=True),
        lax.all_gather(mlp_part.astype(jnp.bfloat16), "dp", axis=0, tiled=True),
    )


def fetch_again(attn_part, mlp_part):
    return (
        lax.all_gather(attn_part.astype(jnp.bfloat16), "dp", axis=0, tiled=True),
        lax.all_gather(mlp_part.astype(jnp.bfloat16), "dp", axis=0, tiled=True),
    )


def gather_rows(local_part):
    return lax.all_gather(local_part, "tensor", axis=0, tiled=True)


def gather_grads(local_part):
    return lax.all_gather(local_part, "tensor", axis=0, tiled=True)


def project_term(full_rows, weight):
    return jnp.einsum("sck,dk->scd", full_rows, weight, preferred_element_type=jnp.float32)


def scatter_rows(full_rows, weight):
    return lax.psum_scatter(
        project_term(full_rows, weight).astype(jnp.bfloat16),
        "tensor",
        scatter_dimension=0,
        tiled=True,
    ).astype(jnp.float32)


def scatter_grads(full_rows, weight):
    return lax.psum_scatter(
        project_term(full_rows, weight).astype(jnp.bfloat16),
        "tensor",
        scatter_dimension=0,
        tiled=True,
    ).astype(jnp.float32)


def attend_forward(parts):
    queries, keys_in, values_in = parts
    scores = jnp.einsum(
        "shd,thd->hst", queries, keys_in, preferred_element_type=jnp.float32
    ) * HEAD ** (-0.5)
    peak = jnp.max(scores, axis=-1, keepdims=True)
    raised = jnp.exp(scores - peak)
    summed = jnp.sum(raised, axis=-1, keepdims=True)
    weights = (raised / summed).astype(jnp.bfloat16)
    context = jnp.einsum("hst,thd->shd", weights, values_in, preferred_element_type=jnp.float32)
    return (context.astype(jnp.bfloat16), (peak + jnp.log(summed))[..., 0])


def attend_backward(parts):
    queries, keys_in, values_in, log_total, grad_context = parts
    scale = HEAD ** (-0.5)
    scores = (
        jnp.einsum("shd,thd->hst", queries, keys_in, preferred_element_type=jnp.float32) * scale
    )
    probs = jnp.exp(scores - log_total[..., None])
    probs_low = probs.astype(jnp.bfloat16)
    grad_values = jnp.einsum(
        "hst,shd->thd", probs_low, grad_context, preferred_element_type=jnp.float32
    )
    grad_probs = jnp.einsum(
        "shd,thd->hst", grad_context, values_in, preferred_element_type=jnp.float32
    )
    grad_scores = (
        probs * (grad_probs - jnp.sum(probs * grad_probs, axis=-1, keepdims=True))
    ).astype(jnp.bfloat16)
    grad_queries = (
        jnp.einsum("hst,thd->shd", grad_scores, keys_in, preferred_element_type=jnp.float32) * scale
    )
    grad_keys = (
        jnp.einsum("hst,shd->thd", grad_scores, queries, preferred_element_type=jnp.float32) * scale
    )
    return (grad_queries, grad_keys, grad_values)


def run_block(stream, attn_full, mlp_full, gains):
    model_width = stream.shape[2]
    head_width = attn_full.shape[2]
    normed = norm_rows(stream, gains[0], gains[1]).astype(jnp.bfloat16)
    normed_full = gather_rows(normed)
    seq_len = normed_full.shape[0]
    clip_count = normed_full.shape[1]
    weight_in = attn_full[:, 0:3].reshape(model_width, 3 * head_width)
    joined = jnp.einsum(
        "scd,dk->sck", normed_full, weight_in, preferred_element_type=jnp.float32
    ).astype(jnp.bfloat16)
    split_heads = jnp.moveaxis(
        joined.reshape(seq_len, clip_count, 3, head_width // HEAD, HEAD), 1, 0
    )
    context, log_total = lax.map(
        attend_forward, (split_heads[:, :, 0], split_heads[:, :, 1], split_heads[:, :, 2])
    )
    context_rows = jnp.moveaxis(context, 0, 1).reshape(seq_len, clip_count, head_width)
    middle = stream + scatter_rows(context_rows, attn_full[:, 3])
    hidden = norm_rows(middle, gains[2], gains[3]).astype(jnp.bfloat16)
    hidden_full = gather_rows(hidden)
    upward = jnp.einsum(
        "scd,df->scf", hidden_full, mlp_full[:, 0], preferred_element_type=jnp.float32
    )
    active = exact_gelu(upward).astype(jnp.bfloat16)
    result = middle + scatter_rows(active, mlp_full[:, 1])
    return (
        result,
        (
            stream,
            normed_full,
            split_heads,
            log_total,
            context_rows,
            middle,
            hidden_full,
            upward,
            active,
        ),
    )


def back_block(grad_stream, saved, attn_full, mlp_full, gains):
    (
        stream,
        normed_full,
        split_heads,
        log_total,
        context_rows,
        middle,
        hidden_full,
        upward,
        active,
    ) = saved
    model_width = stream.shape[2]
    head_width = attn_full.shape[2]
    seq_len = normed_full.shape[0]
    clip_count = normed_full.shape[1]
    grad_ffn = gather_grads(grad_stream.astype(jnp.bfloat16))
    grad_down = jnp.einsum("scd,scf->df", grad_ffn, active, preferred_element_type=jnp.float32)
    grad_active = jnp.einsum(
        "scd,df->scf", grad_ffn, mlp_full[:, 1], preferred_element_type=jnp.float32
    )
    unused, gelu_pull = jax.vjp(exact_gelu, upward)
    grad_upward = gelu_pull(grad_active)[0].astype(jnp.bfloat16)
    grad_up = jnp.einsum(
        "scd,scf->df", hidden_full, grad_upward, preferred_element_type=jnp.float32
    )
    grad_hidden = scatter_grads(grad_upward, mlp_full[:, 0])
    unused, second_pull = jax.vjp(norm_rows, middle, gains[2], gains[3])
    grad_middle_norm, grad_gain_two, grad_shift_two = second_pull(grad_hidden)
    grad_middle = grad_stream + grad_middle_norm
    grad_attn = gather_grads(grad_middle.astype(jnp.bfloat16))
    grad_outward = jnp.einsum(
        "scd,sck->dk", grad_attn, context_rows, preferred_element_type=jnp.float32
    )
    grad_context = jnp.einsum(
        "scd,dk->sck", grad_attn, attn_full[:, 3], preferred_element_type=jnp.float32
    ).astype(jnp.bfloat16)
    grad_context = jnp.moveaxis(
        grad_context.reshape(seq_len, clip_count, head_width // HEAD, HEAD), 1, 0
    )
    grad_queries, grad_keys, grad_values = lax.map(
        attend_backward,
        (split_heads[:, :, 0], split_heads[:, :, 1], split_heads[:, :, 2], log_total, grad_context),
    )
    grad_joined = jnp.moveaxis(jnp.stack((grad_queries, grad_keys, grad_values), axis=2), 0, 1)
    grad_joined = grad_joined.reshape(seq_len, clip_count, 3 * head_width).astype(jnp.bfloat16)
    weight_in = attn_full[:, 0:3].reshape(model_width, 3 * head_width)
    grad_inward = jnp.einsum(
        "scd,sck->dk", normed_full, grad_joined, preferred_element_type=jnp.float32
    ).reshape(model_width, 3, head_width)
    grad_normed = scatter_grads(grad_joined, weight_in)
    unused, first_pull = jax.vjp(norm_rows, stream, gains[0], gains[1])
    grad_stream_norm, grad_gain_one, grad_shift_one = first_pull(grad_normed)
    attn_grad = jnp.concatenate([grad_inward, grad_outward[:, None]], axis=1)
    mlp_grad = jnp.stack([grad_up, grad_down], axis=1)
    layer_attn, layer_mlp = (
        lax.psum_scatter(attn_grad, "dp", scatter_dimension=0, tiled=True),
        lax.psum_scatter(mlp_grad, "dp", scatter_dimension=0, tiled=True),
    )
    vector_grads = jnp.stack([grad_gain_one, grad_shift_one, grad_gain_two, grad_shift_two])
    return (grad_middle + grad_stream_norm, layer_attn, layer_mlp, vector_grads)


def direction(weight, grad, first, second):
    bias_one = 1.0 - first_decay**step_count
    bias_two = 1.0 - second_decay**step_count
    first_new = first_decay * first + (1.0 - first_decay) * grad
    second_new = second_decay * second + (1.0 - second_decay) * grad * grad
    update = (
        first_new / bias_one / (jnp.sqrt(second_new / bias_two) + adam_epsilon)
        + weight_decay * weight
    )
    return (first_new, second_new, update)


def matrix_squares(edge_part, attn_part, mlp_part):
    layer_part = jnp.concatenate(
        [jnp.sum(attn_part * attn_part, axis=(1, 3)), jnp.sum(mlp_part * mlp_part, axis=(1, 3))],
        axis=1,
    )
    return jnp.concatenate([jnp.sum(edge_part * edge_part, axis=(1, 2)), layer_part.reshape(-1)])


def per_device_general(
    patches,
    mask,
    edge,
    attn_w,
    mlp_w,
    vecs,
    edge_m,
    edge_v,
    attn_m,
    attn_v,
    mlp_m,
    mlp_v,
    vecs_m,
    vecs_v,
    teacher_edge,
    teacher_attn,
    teacher_mlp,
    teacher_vecs,
):
    layer_count = attn_w.shape[0]
    local_count = patches.shape[0]
    clip_count = patches.shape[1]
    model_width = patches.shape[2]
    last_row = 4 * layer_count
    student_edge, student_vecs = fetch_edges(edge, vecs)
    teach_edge, teach_vecs = fetch_edges(teacher_edge, teacher_vecs)
    seq_total = local_count * lax.axis_size("tensor")
    stream = jnp.einsum(
        "scp,pd->scd",
        patches,
        teach_edge[0].astype(jnp.bfloat16),
        preferred_element_type=jnp.float32,
    )
    summed = jnp.zeros_like(stream)
    for layer_index in range(layer_count):
        attn_full, mlp_full = fetch_layer(teacher_attn[layer_index], teacher_mlp[layer_index])
        stream, unused = run_block(
            stream, attn_full, mlp_full, teach_vecs[4 * layer_index : 4 * layer_index + 4]
        )
        first_sum, square_sum = lax.psum(
            (jnp.sum(stream, axis=0), jnp.sum(stream * stream, axis=0)), "tensor"
        )
        average = first_sum / seq_total
        spread = square_sum / seq_total - average * average
        summed = summed + (stream - average) * lax.rsqrt(spread + inst_epsilon)
    target = summed / layer_count
    masked = mask.astype(jnp.float32)[..., None]
    embedded = jnp.einsum(
        "scp,pd->scd",
        patches,
        student_edge[0].astype(jnp.bfloat16),
        preferred_element_type=jnp.float32,
    )
    stream = embedded * (1.0 - masked) + masked * student_vecs[last_row + 2]
    saved_list = []
    weight_list = []
    for layer_index in range(layer_count):
        attn_full, mlp_full = fetch_layer(attn_w[layer_index], mlp_w[layer_index])
        stream, saved = run_block(
            stream, attn_full, mlp_full, student_vecs[4 * layer_index : 4 * layer_index + 4]
        )
        saved_list.append(saved)
        weight_list.append((attn_full, mlp_full))
    final_low = norm_rows(stream, student_vecs[last_row], student_vecs[last_row + 1]).astype(
        jnp.bfloat16
    )
    head_low = student_edge[1].astype(jnp.bfloat16)
    predicted = (
        jnp.einsum("scd,de->sce", final_low, head_low, preferred_element_type=jnp.float32)
        + student_vecs[last_row + 3]
    )
    offset = predicted - target
    size_abs = jnp.abs(offset)
    loss_part = (
        jnp.sum(jnp.where(size_abs < 1.0, 0.5 * offset * offset, size_abs - 0.5) * masked)
        / model_width**0.5
    )
    grad_pred = jnp.clip(offset, -1.0, 1.0) * masked / model_width**0.5
    grad_low = grad_pred.astype(jnp.bfloat16)
    grad_head = jnp.einsum("scd,sce->de", final_low, grad_low, preferred_element_type=jnp.float32)
    grad_bias = jnp.sum(grad_pred, axis=(0, 1))
    grad_final = jnp.einsum("sce,de->scd", grad_low, head_low, preferred_element_type=jnp.float32)
    unused, final_pull = jax.vjp(
        norm_rows, stream, student_vecs[last_row], student_vecs[last_row + 1]
    )
    grad_stream, grad_final_gain, grad_final_shift = final_pull(grad_final)
    attn_grads = []
    mlp_grads = []
    vector_rows = []
    for layer_index in reversed(range(layer_count)):
        attn_full, mlp_full = fetch_again(attn_w[layer_index], mlp_w[layer_index])
        grad_stream, layer_attn, layer_mlp, vector_grads = back_block(
            grad_stream,
            saved_list[layer_index],
            attn_full,
            mlp_full,
            student_vecs[4 * layer_index : 4 * layer_index + 4],
        )
        attn_grads.insert(0, layer_attn)
        mlp_grads.insert(0, layer_mlp)
        vector_rows.insert(0, vector_grads)
    grad_embed = (grad_stream * (1.0 - masked)).astype(jnp.bfloat16)
    grad_mask_vec = jnp.sum(grad_stream * masked, axis=(0, 1))
    grad_patch = jnp.einsum("scp,scd->pd", patches, grad_embed, preferred_element_type=jnp.float32)
    vector_grad = jnp.concatenate(
        vector_rows + [jnp.stack([grad_final_gain, grad_final_shift, grad_mask_vec, grad_bias])],
        axis=0,
    )
    edge_grad, vecs_grad = (
        lax.psum_scatter(
            jnp.stack([grad_patch, grad_head]), ("dp", "tensor"), scatter_dimension=1, tiled=True
        ),
        lax.psum_scatter(vector_grad, ("dp", "tensor"), scatter_dimension=1, tiled=True),
    )
    attn_grad = jnp.stack(attn_grads)
    mlp_grad = jnp.stack(mlp_grads)
    edge_first, edge_second, edge_update = direction(edge, edge_grad, edge_m, edge_v)
    attn_first, attn_second, attn_update = direction(attn_w, attn_grad, attn_m, attn_v)
    mlp_first, mlp_second, mlp_update = direction(mlp_w, mlp_grad, mlp_m, mlp_v)
    vecs_first, vecs_second, vecs_update = direction(vecs, vecs_grad, vecs_m, vecs_v)
    weight_sq, update_sq, loss_total = lax.psum(
        (
            matrix_squares(edge, attn_w, mlp_w),
            matrix_squares(edge_update, attn_update, mlp_update),
            loss_part,
        ),
        ("dp", "tensor"),
    )
    weight_norm = jnp.sqrt(weight_sq)
    update_norm = jnp.sqrt(update_sq)
    trust = weight_norm / (update_norm + adam_epsilon)
    edge_trust = trust[0:2]
    layer_trust = trust[2:].reshape(layer_count, 6)
    new_edge = edge - learn_rate * edge_trust[:, None, None] * edge_update
    new_attn = attn_w - learn_rate * layer_trust[:, None, 0:4, None] * attn_update
    new_mlp = mlp_w - learn_rate * layer_trust[:, None, 4:6, None] * mlp_update
    new_vecs = vecs - learn_rate * vecs_update
    keep_share = 1.0 - teacher_decay
    token_total = seq_total * clip_count * lax.axis_size("dp")
    return (
        loss_total / token_total,
        jnp.stack([weight_norm, update_norm]),
        new_edge,
        new_attn,
        new_mlp,
        new_vecs,
        edge_first,
        edge_second[0],
        edge_second[1],
        attn_first,
        attn_second[:, :, 0:3],
        attn_second[:, :, 3],
        mlp_first,
        mlp_second,
        vecs_first,
        vecs_second,
        keep_share * (new_edge - teacher_edge),
        keep_share * (new_attn - teacher_attn),
        keep_share * (new_mlp - teacher_mlp),
        keep_share * (new_vecs - teacher_vecs),
        new_edge.astype(jnp.bfloat16),
        new_attn.astype(jnp.bfloat16),
        new_mlp.astype(jnp.bfloat16),
        new_vecs.astype(jnp.bfloat16),
    )


MESH = pl.DeviceIdType.MESH
ORDERS = (("z", "x", "y"), ("x", "y", "z"), ("y", "z", "x"))
LOW = jnp.bfloat16
ALL = slice(None)


def coords():
    d = lax.axis_index("dp")
    t = lax.axis_index("tensor")
    return dict(a=t // 2, z=t % 2, y=d // 4, x=(d // 2) % 2, c=d % 2)


def ident(co):
    return (co["y"] * 4 + co["x"] * 2 + co["c"], co["a"] * 2 + co["z"])


def flip(co, k):
    co = dict(co)
    co[k] = 1 - co[k]
    return ident(co)


def place(co, full, rows):
    return tuple(ALL if k in full else co[k] for k in "azyxc") + (rows,)


PACKED = (0, 1, 3, 4, 6, 7, 2, 8, 5, 10, 9, 11)
ANY = pl.BlockSpec(memory_space=pl.ANY)
DMA = pltpu.SemaphoreType.DMA


def shape_of(shape, kind=LOW):
    return jax.ShapeDtypeStruct(shape, kind)


def dot(left, right):
    return jnp.dot(left, right, preferred_element_type=jnp.float32)


def dot_nt(left, right):
    return lax.dot_general(
        left, right, (((1,), (1,)), ((), ())), preferred_element_type=jnp.float32
    )


def dot_tn(left, right):
    return lax.dot_general(
        left, right, (((0,), (0,)), ((), ())), preferred_element_type=jnp.float32
    )


def pack_heads(block):
    lead = block.shape[:-2]
    flat = block.reshape(lead + (12, HEAD))
    return jnp.concatenate([flat[..., i, :] for i in PACKED], axis=-1)


def unpack_heads(packed, kinds):
    lead = packed.shape[:-1]
    flat = packed.reshape(lead + (12, HEAD))
    spots = [PACKED.index(i) for i in range(12)]
    return jnp.concatenate([flat[..., i, :] for i in spots], axis=-1).reshape(lead + (kinds, -1))


def norm_block(values, gain, shift):
    average = jnp.mean(values, axis=-1, keepdims=True)
    centered = values - average
    spread = jnp.mean(centered * centered, axis=-1, keepdims=True)
    return centered * lax.rsqrt(spread + norm_epsilon) * gain + shift


def matrix(value):
    return value.reshape(-1, value.shape[-1])


def low_lanes(shape):
    return lax.broadcasted_iota(jnp.int32, shape, len(shape) - 1) % 128 < HEAD


def forward_kernel(*refs):
    (attn_mine, attn_other, mlp_mine, mlp_other, edge_mine, edge_other) = refs[:6]
    vec_mine, vec_other, patch = refs[6:9]
    (o_attn, o_mlp, o_head, o_vec, o_x, o_mid, o_normed, o_qkv, o_peer, o_ctx) = refs[9:19]
    (o_hid, o_act, o_slope, o_lse, o_last, o_final, o_dlow, o_sums, o_patch) = refs[19:28]
    (w_attn, w_mlp, w_edge, w_vec, pixels, embed_w, head_w, gains, x, mid) = refs[28:38]
    (normed, qkv, peer, ctx, hid, act, slope, lse, work, target, stat, sums) = refs[38:50]
    local_sem, send_sem, recv_sem, patch_sem, peer_sem, stat_sem, save_sem = refs[50:]
    co = coords()
    me = ident(co)
    column = co["y"] * 2 + co["x"]
    teaching = co["a"] == 1
    rows_here = x.shape[0]
    width = x.shape[1]
    layers = attn_mine.shape[0]
    last_row = 4 * layers
    barrier = pltpu.get_barrier_semaphore()
    for k in range(1, 8):
        to = (column * 2 + (co["c"] + k // 4) % 2, (me[1] + k % 4) % 4)
        pl.semaphore_signal(barrier, inc=1, device_id=to, device_id_type=MESH)
    for k in "xy":
        pl.semaphore_signal(barrier, inc=1, device_id=flip(co, k), device_id_type=MESH)
    pl.semaphore_wait(barrier, 9)

    items = [(edge_mine, edge_other, w_edge, 0), (vec_mine, vec_other, w_vec, 0)]
    for l in range(layers):
        items.append((attn_mine.at[l], attn_other.at[l], w_attn.at[l], 3 * l + 1))
        for k in range(2):
            items.append(
                (mlp_mine.at[l, k], mlp_other.at[l, k], w_mlp.at[l, k], 3 * l + 2 + k)
            )
    sent = []
    table = {}

    def remote(source, to_ref, i, j, k, to):
        copy = pltpu.make_async_remote_copy(
            src_ref=source,
            dst_ref=to_ref,
            send_sem=send_sem.at[i, j, k],
            recv_sem=recv_sem.at[i, j, k],
            device_id=to,
            device_id_type=MESH,
        )
        copy.start()
        sent.append(copy)
        return copy

    def begin(slot):
        for i, (mine, other, full, at) in enumerate(items):
            if at == slot:
                spot = full.at[place(co, "", ALL)]
                copy = pltpu.make_async_copy(mine, spot, local_sem.at[i])
                copy.start()
                table[i, -1] = (copy, remote(other, spot, i, 0, 4, flip(co, "a")))

    def step(wave, s):
        for i, (mine, other, full, at) in enumerate(items):
            if wave - at != s:
                continue
            if s == 0:
                table[i, -1][0].wait()
                table[i, -1][1].wait_recv()
            size = mine.shape[0] // 3
            copies = []
            for p in range(3):
                if s > 0:
                    table[i, s - 1][p].wait_recv()
                if s < 4:
                    order = ORDERS[p] + ("c",)
                    full_dims = ("a",) + order[:s]
                    ref = full.at[place(co, full_dims, pl.ds(p * size, size))]
                    copies.append(remote(ref, ref, i, p, s, flip(co, order[s])))
            table[i, s] = copies

    saves = {}
    counter = iter(range(48))

    def save(name, source, to_ref):
        copy = pltpu.make_async_copy(source, to_ref, save_sem.at[next(counter)])
        copy.start()
        saves[name] = copy

    def by_rows(size, body):
        def run(n, _):
            body(pl.ds(pl.multiple_of(n * size, size), size))
            return 0

        lax.fori_loop(0, rows_here // size, run, 0)

    def gain(row):
        return gains[row : row + 1, :]

    def norm_into(source, out, row):
        def body(span):
            out[span, :] = norm_block(source[span, :], gain(row), gain(row + 1)).astype(LOW)

        by_rows(64, body)

    def embed():
        owned = [
            w_vec[t // 2, t % 2, d // 4, d // 2 % 2, d % 2] for d in range(8) for t in range(4)
        ]
        gains[...] = jnp.transpose(jnp.concatenate(owned))[: gains.shape[0]]
        save("vec", gains, o_vec)
        half = edge_mine.shape[0] // 2
        for d in range(8):
            for a in range(2):
                at = (d // 4, d // 2 % 2, d % 2)
                left = w_edge[(a, 0) + at].astype(jnp.float32)
                right = w_edge[(a, 1) + at].astype(jnp.float32)
                spot = pl.ds((2 * d + a) * 2 * half, 2 * half)
                embed_w[spot, :] = jnp.concatenate([left[:half], right[:half]]).astype(LOW)
                head_w[spot, :] = jnp.concatenate([left[half:], right[half:]]).astype(LOW)
        save("head", head_w, o_head)
        for q in range(2):
            origin = (column * 2 + co["z"], co["c"] * 2 + q)
            same = jnp.logical_and(origin[0] == me[0], origin[1] == me[1])

            @pl.when(same)
            def _():
                pltpu.make_async_copy(patch, pixels.at[q], patch_sem.at[2]).wait()

            @pl.when(jnp.logical_not(same))
            def _():
                pltpu.make_async_remote_copy(
                    src_ref=patch,
                    dst_ref=pixels.at[q],
                    send_sem=patch_sem.at[3],
                    recv_sem=patch_sem.at[q],
                    device_id=me,
                    device_id_type=MESH,
                ).wait_recv()

        save("patch", pixels, o_patch)
        quarter = pixels.shape[1]
        for q in range(2):
            hide = pixels[q, :, width : width + 1].astype(jnp.float32)
            hide = jnp.where(teaching, 0.0, hide)
            rows = pl.ds(q * quarter, quarter)
            x[rows, :] = (
                dot(pixels[q, :, :width], embed_w[...]) * (1.0 - hide) + hide * gain(last_row + 2)
            )

    def peer_copy(l, t):
        return pltpu.make_async_remote_copy(
            src_ref=qkv.at[t, :, 128:640],
            dst_ref=peer.at[l, t],
            send_sem=peer_sem.at[0, l, t],
            recv_sem=peer_sem.at[1, l, t],
            device_id=flip(co, "c"),
            device_id_type=MESH,
        )

    def wait_saves(*names):
        for name in names:
            if name in saves:
                saves[name].wait()
                del saves[name]

    def project(l):
        save(("x", l), x, o_x.at[l])
        norm_into(x, normed, 4 * l)
        save(("normed", l), normed, o_normed.at[l])
        for t in range(4):
            weight = matrix(w_attn[l, t // 2, t % 2])
            qkv[t] = dot(normed[...], weight).astype(LOW)
            peer_copy(l, t).start()
            save(("qkv", l, t), qkv.at[t], o_qkv.at[l, t])

    def attend(l, first, last):
        if first == 0:
            for t in range(4):
                peer_copy(l, t).wait_recv()
            lse[...] = jnp.zeros_like(lse)
        size = 128

        def body(n, _):
            t = n // (rows_here // size)
            span = pl.ds(pl.multiple_of(n % (rows_here // size) * size, size), size)
            low = low_lanes((size, 128))
            lane = lax.broadcasted_iota(jnp.int32, (size, 128), 1)
            zero = jnp.zeros((size, 128), LOW)
            outs = []
            total = lse[span, :]
            for j in range(3):
                q_at = 0 if j < 2 else 384
                k_at = 128 if j < 2 else 512
                v_at = 256 if j < 2 else 384
                query = qkv[t, span, q_at : q_at + 128] * jnp.asarray(HEAD**-0.5, LOW)
                query = jnp.where(low, query, zero) if j != 1 else jnp.where(low, zero, query)
                scores = jnp.concatenate(
                    [
                        dot_nt(query, qkv[t, :, k_at : k_at + 128]),
                        dot_nt(query, peer[l, t, :, k_at - 128 : k_at]),
                    ],
                    axis=1,
                )
                peak = jnp.max(scores, axis=1, keepdims=True)
                raised = jnp.exp(scores - peak)
                summed = jnp.sum(raised, axis=1, keepdims=True)
                weights = raised.astype(LOW)
                out = dot(weights[:, :rows_here], qkv[t, :, v_at : v_at + 128])
                out = out + dot(weights[:, rows_here:], peer[l, t, :, v_at - 128 : v_at])
                outs.append(out / summed)
                total = jnp.where(lane == 3 * t + j, peak + jnp.log(summed), total)
            lse[span, :] = total
            ctx[t, span, :128] = jnp.where(low, 0.0, outs[1]).astype(LOW)
            ctx[t, span, 128:] = jnp.where(low, outs[0], outs[2]).astype(LOW)
            return 0

        each = rows_here // size
        lax.fori_loop(first * each, last * each, body, 0)
        if last == 4:
            save(("lse", l), lse, o_lse.at[l])
            save(("ctx", l), ctx, o_ctx.at[l])
            save(("peer", l), peer.at[l], o_peer.at[l])

    def out_project(l):
        mid[...] = x[...]

        def body(t, _):
            weight = matrix(w_attn[l, t // 2, t % 2, :, :, :, :, 512:])
            mid[...] += dot_nt(ctx[t], weight)
            return 0

        lax.fori_loop(0, 4, body, 0)
        save(("mid", l), mid, o_mid.at[l])
        norm_into(mid, hid, 4 * l + 2)
        save(("hid", l), hid, o_hid.at[l])

    def expand(l, first, last):
        def body(n, _):
            t = n // 3
            cols = pl.ds(pl.multiple_of(n % 3 * 256, 256), 256)
            weight = matrix(w_mlp[l, 0, t // 2, t % 2, :, :, :, :, cols])
            upward = dot(hid[...], weight)
            share = 0.5 + 0.5 * lax.erf(upward * 0.5**0.5)
            act[t, :, cols] = (upward * share).astype(LOW)
            bell = jnp.exp(-0.5 * upward * upward) * (2.0 * jnp.pi) ** -0.5
            slope[t, :, cols] = (share + upward * bell).astype(LOW)
            return 0

        lax.fori_loop(3 * first, 3 * last, body, 0)
        if last == 4:
            save(("act", l), act, o_act.at[l])
            save(("slope", l), slope, o_slope.at[l])

    def contract(l, first, last):
        if first == 0:
            wait_saves(("x", l))
            x[...] = mid[...]

        def body(t, _):
            x[...] += dot_nt(act[t], matrix(w_mlp[l, 1, t // 2, t % 2]))
            return 0

        lax.fori_loop(first, last, body, 0)

    def stat_copy(l):
        return pltpu.make_async_remote_copy(
            src_ref=stat.at[l, 0],
            dst_ref=stat.at[l, 1],
            send_sem=stat_sem.at[0, l],
            recv_sem=stat_sem.at[1, l],
            device_id=flip(co, "c"),
            device_id_type=MESH,
        )

    def target_copy():
        return pltpu.make_async_remote_copy(
            src_ref=target,
            dst_ref=target,
            send_sem=stat_sem.at[0, layers],
            recv_sem=stat_sem.at[1, layers],
            device_id=flip(co, "a"),
            device_id_type=MESH,
        )

    def teach(l):
        @pl.when(teaching)
        def _():
            stat[l, 0] = jnp.zeros_like(stat[l, 0])

            def body(span):
                value = x[span, :]
                stat[l, 0, 0:1] += jnp.sum(value, axis=0, keepdims=True)
                stat[l, 0, 1:2] += jnp.sum(value * value, axis=0, keepdims=True)

            by_rows(64, body)
            stat_copy(l).start()
            stat_copy(l).wait()
            both = (stat[l, 0] + stat[l, 1]) / (2 * rows_here)
            average = both[0:1]
            spread = both[1:2] - average * average
            scale = lax.rsqrt(spread + inst_epsilon) / layers

            def mix(span):
                value = (x[span, :] - average) * scale
                if l > 0:
                    value = value + work[span, :]
                if l < layers - 1:
                    work[span, :] = value
                else:
                    target[span, :] = value.astype(LOW)

            by_rows(64, mix)
            if l == layers - 1:
                target_copy().start()
                target_copy().wait_send()

    def finish():
        save("last", x, o_last)
        wait_saves(("normed", layers - 1))
        sums[...] = jnp.zeros_like(sums)

        @pl.when(jnp.logical_not(teaching))
        def _():
            norm_into(x, normed, last_row)
            work[...] = dot(normed[...], head_w[...])
            target_copy().wait_recv()

            quarter = pixels.shape[1]

            def body(n, _):
                span = pl.ds(pl.multiple_of(n * 64, 64), 64)
                part = pl.ds(pl.multiple_of(n % 3 * 64, 64), 64)
                masked = pixels[n // 3, part, width : width + 1].astype(jnp.float32)
                offset = work[span, :] + gain(last_row + 3) - target[span, :].astype(jnp.float32)
                size = jnp.abs(offset)
                loss = jnp.where(size < 1.0, 0.5 * offset * offset, size - 0.5) * masked
                pull = jnp.clip(offset, -1.0, 1.0) * masked * width**-0.5
                sums[0:1] += jnp.sum(pull, axis=0, keepdims=True)
                sums[1:2] += jnp.sum(loss, axis=0, keepdims=True)
                target[span, :] = pull.astype(LOW)
                return 0

            lax.fori_loop(0, rows_here // 64, body, 0)

        save("final", normed, o_final)
        save("dlow", target, o_dlow)
        save("sums", sums, o_sums)

    for r in range(2):
        to = (column * 2 + co["a"], 2 * r + co["c"])
        same = jnp.logical_and(to[0] == me[0], to[1] == me[1])
        spot = pixels.at[co["z"]]

        @pl.when(same)
        def _():
            pltpu.make_async_copy(patch, spot, patch_sem.at[2]).start()

        @pl.when(jnp.logical_not(same))
        def _():
            pltpu.make_async_remote_copy(
                src_ref=patch,
                dst_ref=spot,
                send_sem=patch_sem.at[3 + r],
                recv_sem=patch_sem.at[co["z"]],
                device_id=to,
                device_id_type=MESH,
            ).start()

    def save_weights(slot):
        def run():
            l, k = (slot - 1) // 3, (slot - 1) % 3
            if k == 0:
                save(("attn", l), w_attn.at[l], o_attn.at[l])
            else:
                save(("mlp", l, k), w_mlp.at[l, k - 1], o_mlp.at[l, k - 1])

        return run

    plan = {0: [embed]}
    for l in range(layers):
        repeat = l > 0

        def start(l=l):
            if l > 0:
                for t in range(4):
                    peer_copy(l - 1, t).wait_send()
                wait_saves(("normed", l - 1), *[("qkv", l - 1, t) for t in range(4)])
            project(l)

        def begin_attend(l=l):
            if l > 0:
                wait_saves(("lse", l - 1), ("ctx", l - 1))
            attend(l, 0, 2)

        def begin_out(l=l):
            if l > 0:
                wait_saves(("mid", l - 1), ("hid", l - 1))
            out_project(l)

        def begin_expand(l=l):
            if l > 0:
                wait_saves(("act", l - 1), ("slope", l - 1))
            expand(l, 0, 2)

        plan[3 * l + 1] = [
            save_weights(3 * l + 1),
            start,
            begin_attend,
            lambda l=l: attend(l, 2, 4),
            begin_out,
        ]
        plan[3 * l + 2] = [
            save_weights(3 * l + 2),
            begin_expand,
            lambda l=l: expand(l, 2, 4),
        ]
        plan[3 * l + 3] = [
            save_weights(3 * l + 3),
            lambda l=l: contract(l, 0, 2),
            lambda l=l: contract(l, 2, 4),
            lambda l=l: teach(l),
        ]
    final_slot = 3 * layers
    begin(0)
    begin(1)
    for wave in range(final_slot + 5):
        begin(wave + 2)
        step(wave, 4)
        todo = list(plan.get(wave - 4, []))
        for s in range(4):
            step(wave, s)
            if todo:
                todo.pop(0)()
        while todo:
            todo.pop(0)()
    finish()
    for copy in list(saves.values()):
        copy.wait()
    for t in range(4):
        peer_copy(layers - 1, t).wait_send()
    for r in range(2):
        to = (column * 2 + co["a"], 2 * r + co["c"])
        same = jnp.logical_and(to[0] == me[0], to[1] == me[1])

        @pl.when(jnp.logical_not(same))
        def _():
            pltpu.make_async_remote_copy(
                src_ref=patch,
                dst_ref=pixels.at[0],
                send_sem=patch_sem.at[3 + r],
                recv_sem=patch_sem.at[0],
                device_id=me,
                device_id_type=MESH,
            ).wait_send()

    for copy in sent:
        copy.wait_send()


def forward_all(*parts):
    layers, rows, width = parts[0].shape
    cube = (2, 2, 2, 2, 2)
    here = 2 * parts[8].shape[0]
    f32 = jnp.float32
    attn = (layers,) + cube + (rows, width)
    mlp = (layers, 2) + cube + (rows, width)
    tall = (here, width)
    outs = (
        shape_of(attn),
        shape_of(mlp),
        shape_of((width, width)),
        shape_of((16, width), f32),
        shape_of((layers,) + tall, f32),
        shape_of((layers,) + tall, f32),
        shape_of((layers,) + tall),
        shape_of((layers, 4) + tall),
        shape_of((layers, 4, here, 512)),
        shape_of((layers, 4, here, 256)),
        shape_of((layers,) + tall),
        shape_of((layers, 4) + tall),
        shape_of((layers, 4) + tall),
        shape_of((layers, here, 128), f32),
        shape_of(tall, f32),
        shape_of(tall),
        shape_of(tall),
        shape_of((8, width), f32),
        shape_of((2,) + parts[8].shape),
    )
    scratch = [
        pltpu.VMEM(attn, LOW),
        pltpu.VMEM(mlp, LOW),
        pltpu.VMEM(cube + parts[4].shape, LOW),
        pltpu.VMEM(cube + parts[6].shape, f32),
        pltpu.VMEM((2,) + parts[8].shape, LOW),
        pltpu.VMEM((width, width), LOW),
        pltpu.VMEM((width, width), LOW),
        pltpu.VMEM((16, width), f32),
        pltpu.VMEM(tall, f32),
        pltpu.VMEM(tall, f32),
        pltpu.VMEM(tall, LOW),
        pltpu.VMEM((4,) + tall, LOW),
        pltpu.VMEM((layers, 4, here, 512), LOW),
        pltpu.VMEM((4, here, 256), LOW),
        pltpu.VMEM(tall, LOW),
        pltpu.VMEM((4,) + tall, LOW),
        pltpu.VMEM((4,) + tall, LOW),
        pltpu.VMEM((here, 128), f32),
        pltpu.VMEM(tall, f32),
        pltpu.VMEM(tall, LOW),
        pltpu.VMEM((layers, 2, 8, width), f32),
        pltpu.VMEM((8, width), f32),
    ]
    count = 2 + 3 * layers
    sems = [
        DMA((count,)),
        DMA((count, 3, 5)),
        DMA((count, 3, 5)),
        DMA((5,)),
        DMA((2, layers, 4)),
        DMA((2, layers + 1)),
        DMA((48,)),
    ]
    return pl.pallas_call(
        forward_kernel,
        out_shape=outs,
        in_specs=[ANY] * 9,
        out_specs=(ANY,) * len(outs),
        scratch_shapes=scratch + sems,
        compiler_params=pltpu.CompilerParams(
            collective_id=0, has_side_effects=True, vmem_limit_bytes=60 * 2**20
        ),
    )(*parts)


def scatter_kernel(layout, *refs):
    count = len(layout)
    sources, targets, scratch = refs[:4], refs[4:8], refs[8:-4]
    local_sem, send_sem, recv_sem, out_sem = refs[-4:]
    co = coords()
    barrier = pltpu.get_barrier_semaphore()
    for k in "azyxc":
        pl.semaphore_signal(barrier, inc=1, device_id=flip(co, k), device_id_type=MESH)
    pl.semaphore_wait(barrier, 5)
    sent = []

    def remote(source, target, i, j, k, to):
        copy = pltpu.make_async_remote_copy(
            src_ref=source,
            dst_ref=target,
            send_sem=send_sem.at[i, j, k],
            recv_sem=recv_sem.at[i, j, k],
            device_id=to,
            device_id_type=MESH,
        )
        copy.start()
        sent.append(copy)
        return copy

    def pick(fixed, span):
        return (ALL,) + tuple(fixed.get(k, ALL) for k in "azyx") + (span,)

    items = []
    spot = 0
    for which, layer, lead, rows, cols, kind, parts in layout:
        item = dict(lead=lead, rows=rows, parts=parts, kind=kind)
        source, target = sources[which], targets[which]
        if layer is not None:
            source, target = source.at[layer], target.at[layer]
        item.update(source=source, target=target)
        item.update(mine=scratch[spot], swap=scratch[spot + 1])
        spot += 2
        item["part"] = []
        for p in range(parts):
            item["part"].append(scratch[spot : spot + 3])
            spot += 3
        item["last"] = scratch[spot]
        spot += 1
        items.append(item)

    def span_of(item, p):
        size = item["rows"] // item["parts"]
        return ALL if item["parts"] == 1 else pl.ds(p * size, size)

    def squeeze(item, ref, index):
        if len(item["source"].shape) == 7:
            return ref.at[(0,) + index[1:]]
        return ref.at[index]

    def add_into(item, ref, index, other, index_other):
        total = ref[index].astype(jnp.float32) + other[index_other].astype(jnp.float32)
        ref[index] = total.astype(item["kind"])

    def add_swap(item):
        def body(n, _):
            index = (n // 16, n // 8 % 2, n // 4 % 2, n // 2 % 2, n % 2)
            add_into(item, item["mine"], index, item["swap"], index)
            return 0

        lax.fori_loop(0, item["lead"] * 16, body, 0)

    def add_part(item, p, s):
        done = ORDERS[p][::-1][: s + 1]
        left = [k for k in "azyx" if k not in done]

        def body(n, _):
            at = {}
            for k in reversed(left):
                at[k] = n % 2
                n = n // 2
            there = (n,) + tuple(0 if k in done else at[k] for k in "azyx")
            here = (n,) + tuple(co[k] if k in done else at[k] for k in "azyx")
            add_into(item, item["mine"], here + (span_of(item, p),), item["part"][p][s], there)
            return 0

        lax.fori_loop(0, item["lead"] * 2 ** len(left), body, 0)

    def last_hop(i, item):
        return pltpu.make_async_remote_copy(
            src_ref=item["mine"].at[pick({**own, "a": 1}, ALL)],
            dst_ref=item["last"],
            send_sem=send_sem.at[i, 0, 3],
            recv_sem=recv_sem.at[i, 0, 3],
            device_id=flip(co, "a"),
            device_id_type=MESH,
        )

    own = {q: co[q] for q in "zyx"}
    local = []
    table = {}
    for i, item in enumerate(items):
        source = item["source"]
        lead = (ALL,) * (len(source.shape) - 3)
        copy = pltpu.make_async_copy(
            source.at[lead + (co["c"],)], squeeze(item, item["mine"], (ALL,)), local_sem.at[i]
        )
        copy.start()
        local.append(copy)
        table[i, 0] = [
            remote(
                source.at[lead + (1 - co["c"],)],
                squeeze(item, item["swap"], (ALL,)),
                i,
                0,
                4,
                flip(co, "c"),
            )
        ]
    for wave in range(count + 6):
        for i, item in enumerate(items):
            s = wave - i
            if s < 1 or s > 5:
                continue
            if s == 1:
                local[i].wait()
                table[i, 0][0].wait_recv()
                add_swap(item)
            elif s <= 4:
                for p, copy in enumerate(table[i, s - 1]):
                    copy.wait_recv()
                    add_part(item, p, s - 2)
            if s <= 3:
                copies = []
                for p in range(item["parts"]):
                    order = ORDERS[p][::-1]
                    k = order[s - 1]
                    fixed = {q: co[q] for q in order[: s - 1]}
                    source = item["mine"].at[pick({**fixed, k: 1 - co[k]}, span_of(item, p))]
                    target = item["part"][p][s - 1].at[pick({q: 0 for q in order[:s]}, ALL)]
                    copies.append(remote(source, target, i, p, s - 1, flip(co, k)))
                table[i, s] = copies
            elif s == 4:

                @pl.when(co["a"] == 0)
                def _():
                    last_hop(i, item).start()
                    result = squeeze(item, item["mine"], pick({**own, "a": 0}, ALL))
                    pltpu.make_async_copy(result, item["target"], out_sem.at[i]).start()

            else:
                result = squeeze(item, item["last"], (ALL,))

                @pl.when(co["a"] == 1)
                def _():
                    last_hop(i, item).wait_recv()
                    pltpu.make_async_copy(result, item["target"], out_sem.at[i]).start()

                @pl.when(co["a"] == 0)
                def _():
                    last_hop(i, item).wait_send()

                pltpu.make_async_copy(result, item["target"], out_sem.at[i]).wait()
    for copy in sent:
        copy.wait_send()


def scatter_all(attn, mlp, edge, vec):
    rows, width = attn.shape[-2:]
    hidden = mlp.shape[-1]
    edge_rows = edge.shape[-2]
    layout = (
        (1, 1, 2, rows, hidden, LOW, 3),
        (0, 1, 1, rows, width, LOW, 3),
        (1, 0, 2, rows, hidden, LOW, 3),
        (0, 0, 1, rows, width, LOW, 3),
        (2, None, 1, edge_rows, width, LOW, 3),
        (3, None, 1, vec.shape[-2], vec.shape[-1], jnp.float32, 1),
    )
    scratch = []
    for which, layer, lead, count, cols, kind, parts in layout:
        scratch.append(pltpu.VMEM((lead, 2, 2, 2, 2, count, cols), kind))
        scratch.append(pltpu.VMEM((lead, 2, 2, 2, 2, count, cols), kind))
        for p in range(parts):
            order = ORDERS[p][::-1]
            for s in range(3):
                dims = tuple(1 if k in order[: s + 1] else 2 for k in "azyx")
                scratch.append(pltpu.VMEM((lead,) + dims + (count // parts, cols), kind))
        scratch.append(pltpu.VMEM((lead, count, cols), kind))
    return pl.pallas_call(
        lambda *refs: scatter_kernel(layout, *refs),
        out_shape=(
            shape_of((2, rows, width)),
            shape_of((2, 2, rows, hidden)),
            shape_of((edge_rows, width)),
            shape_of(vec.shape[-2:], jnp.float32),
        ),
        in_specs=[ANY] * 4,
        out_specs=(ANY,) * 4,
        scratch_shapes=scratch + [DMA((6,)), DMA((6, 3, 5)), DMA((6, 3, 5)), DMA((6,))],
        compiler_params=pltpu.CompilerParams(
            collective_id=1, has_side_effects=True, vmem_limit_bytes=60 * 2**20
        ),
    )(attn, mlp, edge, vec)


def total_kernel(value, out, held, send_sem, recv_sem):
    co = coords()
    barrier = pltpu.get_barrier_semaphore()
    for k in "azyxc":
        pl.semaphore_signal(barrier, inc=1, device_id=flip(co, k), device_id_type=MESH)
    pl.semaphore_wait(barrier, 5)
    held[0] = value[...]
    for s, k in enumerate("cxyza"):
        copy = pltpu.make_async_remote_copy(
            src_ref=held.at[2 * s],
            dst_ref=held.at[2 * s + 1],
            send_sem=send_sem.at[s],
            recv_sem=recv_sem.at[s],
            device_id=flip(co, k),
            device_id_type=MESH,
        )
        copy.start()
        copy.wait()
        held[2 * s + 2] = held[2 * s] + held[2 * s + 1]
    out[...] = held[10]


def total_all(value):
    return pl.pallas_call(
        total_kernel,
        out_shape=shape_of(value.shape, jnp.float32),
        in_specs=[pl.BlockSpec(memory_space=pltpu.VMEM)],
        out_specs=pl.BlockSpec(memory_space=pltpu.VMEM),
        scratch_shapes=[pltpu.VMEM((11,) + value.shape, jnp.float32), DMA((5,)), DMA((5,))],
        compiler_params=pltpu.CompilerParams(collective_id=2, has_side_effects=True),
    )(value)


def swap_core(value):
    count = lax.axis_size("dp")
    return lax.ppermute(value, "dp", [(i, i ^ 1) for i in range(count)])


def backward_rows(grad, saved, attn, mlp, gains):
    stream, normed, own, peer, log_total, context, middle, hidden, active, slope = saved
    rows = grad.shape[0]
    o = own.reshape(4, rows, 12, HEAD)
    p = peer.reshape(4, rows, 8, HEAD)
    pick = lambda value, spots: jnp.moveaxis(
        jnp.stack([value[:, :, i] for i in spots], axis=2), 0, 1
    ).reshape(rows, 12, HEAD)
    queries = pick(o, (0, 1, 6))
    keys = jnp.concatenate([pick(o, (2, 3, 8)), pick(p, (0, 1, 6))])
    values = jnp.concatenate([pick(o, (4, 5, 7)), pick(p, (2, 3, 5))])
    low_grad = grad.astype(LOW)
    grad_upward = jnp.stack([dot(low_grad, mlp[1, z]) * slope[z] for z in range(4)]).astype(LOW)
    grad_mlp = jnp.stack(
        [
            jnp.stack([dot_tn(hidden, grad_upward[z]).astype(LOW) for z in range(4)]),
            jnp.stack([dot_tn(low_grad, active[z]).astype(LOW) for z in range(4)]),
        ]
    )
    grad_hidden = sum(dot_nt(grad_upward[z], mlp[0, z]) for z in range(4))
    unused, second_pull = jax.vjp(norm_rows, middle, gains[2], gains[3])
    grad_norm, grad_gain_two, grad_shift_two = second_pull(grad_hidden)
    grad_middle = grad + grad_norm
    low_middle = grad_middle.astype(LOW)
    grad_context = jnp.stack([dot(low_middle, attn[z][:, 576:]).astype(LOW) for z in range(4)])
    grad_context = pick(grad_context.reshape(4, rows, 3, HEAD), (1, 0, 2))
    grad_queries, grad_keys, grad_values = attend_backward(
        (queries, keys, values, log_total[:, :12].T, grad_context)
    )
    grad_keyval = jnp.stack([grad_keys, grad_values])
    other = swap_core(grad_keyval[:, rows:].astype(LOW))
    grad_keyval = (grad_keyval[:, :rows] + other.astype(jnp.float32)).astype(LOW)
    grad_queries = grad_queries.astype(LOW)
    pieces = []
    grad_normed = 0.0
    for z in range(4):
        q, k, v = (
            value[:, 3 * z : 3 * z + 3] for value in (grad_queries, grad_keyval[0], grad_keyval[1])
        )
        joined = jnp.concatenate(
            [q[:, 0], q[:, 1], k[:, 0], k[:, 1], v[:, 0], v[:, 1], q[:, 2], v[:, 2], k[:, 2]],
            axis=1,
        )
        grad_normed = grad_normed + dot_nt(joined, attn[z][:, :576])
        pieces.append(
            jnp.concatenate(
                [
                    dot_tn(normed, joined).astype(LOW),
                    dot_tn(low_middle, context[z][:, HEAD:]).astype(LOW),
                ],
                axis=1,
            )
        )
    unused, first_pull = jax.vjp(norm_rows, stream, gains[0], gains[1])
    grad_norm, grad_gain_one, grad_shift_one = first_pull(grad_normed)
    vectors = [grad_gain_one, grad_shift_one, grad_gain_two, grad_shift_two]
    return grad_middle + grad_norm, jnp.stack(pieces), grad_mlp, vectors


def per_device(
    patches,
    mask,
    edge,
    attn_w,
    mlp_w,
    vecs,
    edge_m,
    edge_v,
    attn_m,
    attn_v,
    mlp_m,
    mlp_v,
    vecs_m,
    vecs_v,
    teacher_edge,
    teacher_attn,
    teacher_mlp,
    teacher_vecs,
):
    layer_count, rows, kinds, block = attn_w.shape
    wide = mlp_w.shape[3]
    width = patches.shape[2]
    quarter = patches.shape[0]
    edge_rows = edge.shape[1]
    vec_count, vec_cols = vecs.shape
    last_row = 4 * layer_count
    teaching = lax.axis_index("tensor") >= 2
    dp_size = lax.axis_size("dp")

    def pack(own_edge, own_attn, own_mlp, own_vecs):
        return (
            pack_heads(own_attn.astype(LOW)),
            jnp.swapaxes(own_mlp.astype(LOW), 1, 2),
            own_edge.astype(LOW).reshape(2 * edge_rows, width),
            jnp.pad(own_vecs.T, ((0, 0), (0, 128 - vec_count))),
        )

    student = pack(edge, attn_w, mlp_w, vecs)
    teacher = pack(teacher_edge, teacher_attn, teacher_mlp, teacher_vecs)
    parts = []
    for left, right in zip(student, teacher):
        parts += [jnp.where(teaching, right, left), jnp.where(teaching, left, right)]
    marks = jnp.broadcast_to(mask.astype(LOW), (quarter, 128))
    parts.append(jnp.concatenate([patches.reshape(quarter, width), marks], axis=1))
    attn_all, mlp_all, head_w, gains, *kept, stream, final_low, grad_low, sums, patch_all = (
        forward_all(*parts)
    )
    attn_all = attn_all.reshape(layer_count, 4, dp_size * rows, kinds * block)
    mlp_all = mlp_all.reshape(layer_count, 2, 4, dp_size * rows, wide)
    (all_x, all_mid, all_normed, all_qkv, all_peer, all_ctx, all_hid, all_act, all_slope, all_lse) = kept
    saved_list = [
        (
            all_x[layer],
            all_normed[layer],
            all_qkv[layer],
            all_peer[layer],
            all_lse[layer],
            all_ctx[layer],
            all_mid[layer],
            all_hid[layer],
            all_act[layer],
            all_slope[layer],
        )
        for layer in range(layer_count)
    ]
    patch_all = patch_all.reshape(2 * quarter, width + 128)
    pixels = patch_all[:, :width]
    masked = patch_all[:, width : width + 1].astype(jnp.float32)
    grad_bias = sums[0]
    loss_part = jnp.sum(sums[1]) / width**0.5
    grad_head = dot_tn(final_low, grad_low)
    unused, final_pull = jax.vjp(norm_rows, stream, gains[last_row], gains[last_row + 1])
    grad, grad_final_gain, grad_final_shift = final_pull(dot_nt(grad_low, head_w))
    attn_list = []
    mlp_list = []
    vector_rows = []
    for layer in reversed(range(layer_count)):
        grad, layer_attn, layer_mlp, vectors = backward_rows(
            grad,
            saved_list[layer],
            attn_all[layer],
            mlp_all[layer],
            gains[4 * layer : 4 * layer + 4],
        )
        attn_list.insert(0, layer_attn)
        mlp_list.insert(0, layer_mlp)
        vector_rows = vectors + vector_rows
    grad_embed = (grad * (1.0 - masked)).astype(LOW)
    grad_mask = jnp.sum(grad * masked, axis=0)
    grad_patch = dot_tn(pixels, grad_embed)
    cube = (2, 2, 2, 2, 2)
    to_owner = (3, 4, 0, 1, 2)
    attn_send = jnp.stack(attn_list).reshape((layer_count,) + cube + (rows, kinds * block))
    mlp_send = jnp.stack(mlp_list).reshape((layer_count, 2) + cube + (rows, wide))
    edge_send = jnp.stack([grad_patch, grad_head]).astype(LOW)
    edge_send = edge_send.reshape((2,) + cube + (edge_rows, width))
    edge_send = edge_send.transpose(4, 5, 1, 2, 3, 0, 6, 7).reshape(cube + (2 * edge_rows, width))
    loss_row = jnp.full((width,), loss_part)
    vec_send = jnp.stack(
        vector_rows + [grad_final_gain, grad_final_shift, grad_mask, grad_bias, loss_row]
    )
    vec_send = jnp.pad(vec_send, ((0, 15 - vec_count), (0, 0))).reshape((16,) + cube + (vec_cols,))
    vec_send = jnp.pad(
        vec_send.transpose(4, 5, 1, 2, 3, 0, 6), ((0, 0),) * 6 + ((0, 128 - vec_cols),)
    )
    attn_grad, mlp_grad, edge_grad, vecs_grad = scatter_all(
        attn_send, mlp_send, edge_send, vec_send
    )
    attn_grad = unpack_heads(attn_grad, kinds).astype(jnp.float32)
    mlp_grad = jnp.swapaxes(mlp_grad.astype(jnp.float32), 1, 2)
    edge_grad = edge_grad.astype(jnp.float32).reshape(edge.shape)
    loss_total = vecs_grad[vec_count, 0]
    vecs_grad = vecs_grad[:vec_count, :vec_cols]
    edge_first, edge_second, edge_update = direction(edge, edge_grad, edge_m, edge_v)
    attn_first, attn_second, attn_update = direction(attn_w, attn_grad, attn_m, attn_v)
    mlp_first, mlp_second, mlp_update = direction(mlp_w, mlp_grad, mlp_m, mlp_v)
    vecs_first, vecs_second, vecs_update = direction(vecs, vecs_grad, vecs_m, vecs_v)
    squares = jnp.stack(
        [
            matrix_squares(edge, attn_w, mlp_w),
            matrix_squares(edge_update, attn_update, mlp_update),
        ]
    )
    squares = jnp.pad(squares, ((0, 6), (0, 128 - squares.shape[1])))
    norms = jnp.sqrt(total_all(squares)[:2, : 2 + 6 * layer_count])
    trust = norms[0] / (norms[1] + adam_epsilon)
    edge_trust = trust[0:2]
    layer_trust = trust[2:].reshape(layer_count, 6)
    new_edge = edge - learn_rate * edge_trust[:, None, None] * edge_update
    new_attn = attn_w - learn_rate * layer_trust[:, None, 0:4, None] * attn_update
    new_mlp = mlp_w - learn_rate * layer_trust[:, None, 4:6, None] * mlp_update
    new_vecs = vecs - learn_rate * vecs_update
    keep_share = 1.0 - teacher_decay
    token_total = 4 * quarter * dp_size
    return (
        loss_total / token_total,
        norms,
        new_edge,
        new_attn,
        new_mlp,
        new_vecs,
        edge_first,
        edge_second[0],
        edge_second[1],
        attn_first,
        attn_second[:, :, 0:3],
        attn_second[:, :, 3],
        mlp_first,
        mlp_second,
        vecs_first,
        vecs_second,
        keep_share * (new_edge - teacher_edge),
        keep_share * (new_attn - teacher_attn),
        keep_share * (new_mlp - teacher_mlp),
        keep_share * (new_vecs - teacher_vecs),
        new_edge.astype(LOW),
        new_attn.astype(LOW),
        new_mlp.astype(LOW),
        new_vecs.astype(LOW),
    )


def solution(mesh):
    placed = (
        P("tensor", "dp", None),
        P("tensor", "dp"),
        P(None, ("dp", "tensor"), None),
        P(None, "dp", None, "tensor"),
        P(None, "dp", None, "tensor"),
        P(None, ("dp", "tensor")),
        P(None, ("dp", "tensor"), None),
        P(None, ("dp", "tensor"), None),
        P(None, "dp", None, "tensor"),
        P(None, "dp", None, "tensor"),
        P(None, "dp", None, "tensor"),
        P(None, "dp", None, "tensor"),
        P(None, ("dp", "tensor")),
        P(None, ("dp", "tensor")),
        P(None, ("dp", "tensor"), None),
        P(None, "dp", None, "tensor"),
        P(None, "dp", None, "tensor"),
        P(None, ("dp", "tensor")),
    )
    planned = dict(mesh.shape) == {"dp": 8, "tensor": 4}
    return jax.shard_map(
        per_device if planned else per_device_general,
        mesh=mesh,
        in_specs=placed,
        out_specs=(
            P(),
            P(),
            P(None, ("dp", "tensor"), None),
            P(None, "dp", None, "tensor"),
            P(None, "dp", None, "tensor"),
            P(None, ("dp", "tensor")),
            P(None, ("dp", "tensor"), None),
            P(("dp", "tensor"), None),
            P(("dp", "tensor"), None),
            P(None, "dp", None, "tensor"),
            P(None, "dp", None, "tensor"),
            P(None, "dp", "tensor"),
            P(None, "dp", None, "tensor"),
            P(None, "dp", None, "tensor"),
            P(None, ("dp", "tensor")),
            P(None, ("dp", "tensor")),
            P(None, ("dp", "tensor"), None),
            P(None, "dp", None, "tensor"),
            P(None, "dp", None, "tensor"),
            P(None, ("dp", "tensor")),
            P(None, ("dp", "tensor"), None),
            P(None, "dp", None, "tensor"),
            P(None, "dp", None, "tensor"),
            P(None, ("dp", "tensor")),
        ),
        check_vma=False,
    )
```

```python
import jax
import jax.numpy as jnp
from jax import lax
from jax.experimental import pallas as pl
from jax.experimental.layout import Layout, with_layout_constraint
from jax.experimental.pallas import tpu as pltpu
from jax.sharding import PartitionSpec as P

HEAD = 64
DP = "dp"
TENSOR = "tensor"


norm_epsilon = 1e-06
inst_epsilon = 1e-05
first_decay = 0.9
second_decay = 0.999
adam_epsilon = 1e-06
weight_decay = 0.01
learn_rate = 0.3
teacher_decay = 0.999
step_count = 10


def norm_rows(values, gain, shift):
    average = jnp.mean(values, axis=-1, keepdims=True)
    centered = values - average
    spread = jnp.mean(centered * centered, axis=-1, keepdims=True)
    return centered * lax.rsqrt(spread + norm_epsilon) * gain + shift


def exact_gelu(values):
    return jax.nn.gelu(values, approximate=False)


def fetch_edges(edge_part, vector_part):
    return (
        lax.all_gather(edge_part, (DP, TENSOR), axis=1, tiled=True),
        lax.all_gather(vector_part, (DP, TENSOR), axis=1, tiled=True),
    )


def fetch_layer(attn_part, mlp_part):
    return (
        lax.all_gather(attn_part.astype(jnp.bfloat16), DP, axis=0, tiled=True),
        lax.all_gather(mlp_part.astype(jnp.bfloat16), DP, axis=0, tiled=True),
    )


def fetch_again(attn_part, mlp_part):
    return (
        lax.all_gather(attn_part.astype(jnp.bfloat16), DP, axis=0, tiled=True),
        lax.all_gather(mlp_part.astype(jnp.bfloat16), DP, axis=0, tiled=True),
    )


def gather_rows(local_part):
    return lax.all_gather(local_part, TENSOR, axis=0, tiled=True)


def gather_grads(local_part):
    return lax.all_gather(local_part, TENSOR, axis=0, tiled=True)


def project_term(full_rows, weight):
    return jnp.einsum("sck,dk->scd", full_rows, weight, preferred_element_type=jnp.float32)


def scatter_rows(full_rows, weight):
    return lax.psum_scatter(
        project_term(full_rows, weight).astype(jnp.bfloat16),
        TENSOR,
        scatter_dimension=0,
        tiled=True,
    ).astype(jnp.float32)


def scatter_grads(full_rows, weight):
    return lax.psum_scatter(
        project_term(full_rows, weight).astype(jnp.bfloat16),
        TENSOR,
        scatter_dimension=0,
        tiled=True,
    ).astype(jnp.float32)


def attend_forward(parts):
    queries, keys_in, values_in = parts
    scores = jnp.einsum(
        "shd,thd->hst", queries, keys_in, preferred_element_type=jnp.float32
    ) * HEAD ** (-0.5)
    peak = jnp.max(scores, axis=-1, keepdims=True)
    raised = jnp.exp(scores - peak)
    summed = jnp.sum(raised, axis=-1, keepdims=True)
    weights = (raised / summed).astype(jnp.bfloat16)
    context = jnp.einsum("hst,thd->shd", weights, values_in, preferred_element_type=jnp.float32)
    return (context.astype(jnp.bfloat16), (peak + jnp.log(summed))[..., 0])


def attend_backward(parts):
    queries, keys_in, values_in, log_total, grad_context = parts
    scale = HEAD ** (-0.5)
    scores = (
        jnp.einsum("shd,thd->hst", queries, keys_in, preferred_element_type=jnp.float32) * scale
    )
    probs = jnp.exp(scores - log_total[..., None])
    probs_low = probs.astype(jnp.bfloat16)
    grad_values = jnp.einsum(
        "hst,shd->thd", probs_low, grad_context, preferred_element_type=jnp.float32
    )
    grad_probs = jnp.einsum(
        "shd,thd->hst", grad_context, values_in, preferred_element_type=jnp.float32
    )
    grad_scores = (
        probs * (grad_probs - jnp.sum(probs * grad_probs, axis=-1, keepdims=True))
    ).astype(jnp.bfloat16)
    grad_queries = (
        jnp.einsum("hst,thd->shd", grad_scores, keys_in, preferred_element_type=jnp.float32) * scale
    )
    grad_keys = (
        jnp.einsum("hst,shd->thd", grad_scores, queries, preferred_element_type=jnp.float32) * scale
    )
    return (grad_queries, grad_keys, grad_values)


def run_block(stream, attn_full, mlp_full, gains):
    model_width = stream.shape[2]
    head_width = attn_full.shape[2]
    normed = norm_rows(stream, gains[0], gains[1]).astype(jnp.bfloat16)
    normed_full = gather_rows(normed)
    seq_len = normed_full.shape[0]
    clip_count = normed_full.shape[1]
    weight_in = attn_full[:, 0:3].reshape(model_width, 3 * head_width)
    joined = jnp.einsum(
        "scd,dk->sck", normed_full, weight_in, preferred_element_type=jnp.float32
    ).astype(jnp.bfloat16)
    split_heads = jnp.moveaxis(
        joined.reshape(seq_len, clip_count, 3, head_width // HEAD, HEAD), 1, 0
    )
    context, log_total = lax.map(
        attend_forward, (split_heads[:, :, 0], split_heads[:, :, 1], split_heads[:, :, 2])
    )
    context_rows = jnp.moveaxis(context, 0, 1).reshape(seq_len, clip_count, head_width)
    middle = stream + scatter_rows(context_rows, attn_full[:, 3])
    hidden = norm_rows(middle, gains[2], gains[3]).astype(jnp.bfloat16)
    hidden_full = gather_rows(hidden)
    upward = jnp.einsum(
        "scd,df->scf", hidden_full, mlp_full[:, 0], preferred_element_type=jnp.float32
    )
    active = exact_gelu(upward).astype(jnp.bfloat16)
    result = middle + scatter_rows(active, mlp_full[:, 1])
    return (
        result,
        (
            stream,
            normed_full,
            split_heads,
            log_total,
            context_rows,
            middle,
            hidden_full,
            upward,
            active,
        ),
    )


def back_block(grad_stream, saved, attn_full, mlp_full, gains):
    (
        stream,
        normed_full,
        split_heads,
        log_total,
        context_rows,
        middle,
        hidden_full,
        upward,
        active,
    ) = saved
    model_width = stream.shape[2]
    head_width = attn_full.shape[2]
    seq_len = normed_full.shape[0]
    clip_count = normed_full.shape[1]
    grad_ffn = gather_grads(grad_stream.astype(jnp.bfloat16))
    grad_down = jnp.einsum("scd,scf->df", grad_ffn, active, preferred_element_type=jnp.float32)
    grad_active = jnp.einsum(
        "scd,df->scf", grad_ffn, mlp_full[:, 1], preferred_element_type=jnp.float32
    )
    unused, gelu_pull = jax.vjp(exact_gelu, upward)
    grad_upward = gelu_pull(grad_active)[0].astype(jnp.bfloat16)
    grad_up = jnp.einsum(
        "scd,scf->df", hidden_full, grad_upward, preferred_element_type=jnp.float32
    )
    grad_hidden = scatter_grads(grad_upward, mlp_full[:, 0])
    unused, second_pull = jax.vjp(norm_rows, middle, gains[2], gains[3])
    grad_middle_norm, grad_gain_two, grad_shift_two = second_pull(grad_hidden)
    grad_middle = grad_stream + grad_middle_norm
    grad_attn = gather_grads(grad_middle.astype(jnp.bfloat16))
    grad_outward = jnp.einsum(
        "scd,sck->dk", grad_attn, context_rows, preferred_element_type=jnp.float32
    )
    grad_context = jnp.einsum(
        "scd,dk->sck", grad_attn, attn_full[:, 3], preferred_element_type=jnp.float32
    ).astype(jnp.bfloat16)
    grad_context = jnp.moveaxis(
        grad_context.reshape(seq_len, clip_count, head_width // HEAD, HEAD), 1, 0
    )
    grad_queries, grad_keys, grad_values = lax.map(
        attend_backward,
        (split_heads[:, :, 0], split_heads[:, :, 1], split_heads[:, :, 2], log_total, grad_context),
    )
    grad_joined = jnp.moveaxis(jnp.stack((grad_queries, grad_keys, grad_values), axis=2), 0, 1)
    grad_joined = grad_joined.reshape(seq_len, clip_count, 3 * head_width).astype(jnp.bfloat16)
    weight_in = attn_full[:, 0:3].reshape(model_width, 3 * head_width)
    grad_inward = jnp.einsum(
        "scd,sck->dk", normed_full, grad_joined, preferred_element_type=jnp.float32
    ).reshape(model_width, 3, head_width)
    grad_normed = scatter_grads(grad_joined, weight_in)
    unused, first_pull = jax.vjp(norm_rows, stream, gains[0], gains[1])
    grad_stream_norm, grad_gain_one, grad_shift_one = first_pull(grad_normed)
    attn_grad = jnp.concatenate([grad_inward, grad_outward[:, None]], axis=1)
    mlp_grad = jnp.stack([grad_up, grad_down], axis=1)
    layer_attn, layer_mlp = (
        lax.psum_scatter(attn_grad, DP, scatter_dimension=0, tiled=True),
        lax.psum_scatter(mlp_grad, DP, scatter_dimension=0, tiled=True),
    )
    vector_grads = jnp.stack([grad_gain_one, grad_shift_one, grad_gain_two, grad_shift_two])
    return (grad_middle + grad_stream_norm, layer_attn, layer_mlp, vector_grads)


def direction(weight, grad, first, second):
    bias_one = 1.0 - first_decay**step_count
    bias_two = 1.0 - second_decay**step_count
    first_new = first_decay * first + (1.0 - first_decay) * grad
    second_new = second_decay * second + (1.0 - second_decay) * grad * grad
    update = (
        first_new / bias_one / (jnp.sqrt(second_new / bias_two) + adam_epsilon)
        + weight_decay * weight
    )
    return (first_new, second_new, update)


def matrix_squares(edge_part, attn_part, mlp_part):
    layer_part = jnp.concatenate(
        [jnp.sum(attn_part * attn_part, axis=(1, 3)), jnp.sum(mlp_part * mlp_part, axis=(1, 3))],
        axis=1,
    )
    return jnp.concatenate([jnp.sum(edge_part * edge_part, axis=(1, 2)), layer_part.reshape(-1)])


def per_device_general(
    patches,
    mask,
    edge,
    attn_w,
    mlp_w,
    vecs,
    edge_m,
    edge_v,
    attn_m,
    attn_v,
    mlp_m,
    mlp_v,
    vecs_m,
    vecs_v,
    teacher_edge,
    teacher_attn,
    teacher_mlp,
    teacher_vecs,
):
    layer_count = attn_w.shape[0]
    local_count = patches.shape[0]
    clip_count = patches.shape[1]
    model_width = patches.shape[2]
    last_row = 4 * layer_count
    student_edge, student_vecs = fetch_edges(edge, vecs)
    teach_edge, teach_vecs = fetch_edges(teacher_edge, teacher_vecs)
    seq_total = local_count * lax.axis_size(TENSOR)
    stream = jnp.einsum(
        "scp,pd->scd",
        patches,
        teach_edge[0].astype(jnp.bfloat16),
        preferred_element_type=jnp.float32,
    )
    summed = jnp.zeros_like(stream)
    for layer_index in range(layer_count):
        attn_full, mlp_full = fetch_layer(teacher_attn[layer_index], teacher_mlp[layer_index])
        stream, unused = run_block(
            stream, attn_full, mlp_full, teach_vecs[4 * layer_index : 4 * layer_index + 4]
        )
        first_sum, square_sum = lax.psum(
            (jnp.sum(stream, axis=0), jnp.sum(stream * stream, axis=0)), TENSOR
        )
        average = first_sum / seq_total
        spread = square_sum / seq_total - average * average
        summed = summed + (stream - average) * lax.rsqrt(spread + inst_epsilon)
    target = summed / layer_count
    masked = mask.astype(jnp.float32)[..., None]
    embedded = jnp.einsum(
        "scp,pd->scd",
        patches,
        student_edge[0].astype(jnp.bfloat16),
        preferred_element_type=jnp.float32,
    )
    stream = embedded * (1.0 - masked) + masked * student_vecs[last_row + 2]
    saved_list = []
    weight_list = []
    for layer_index in range(layer_count):
        attn_full, mlp_full = fetch_layer(attn_w[layer_index], mlp_w[layer_index])
        stream, saved = run_block(
            stream, attn_full, mlp_full, student_vecs[4 * layer_index : 4 * layer_index + 4]
        )
        saved_list.append(saved)
        weight_list.append((attn_full, mlp_full))
    final_low = norm_rows(stream, student_vecs[last_row], student_vecs[last_row + 1]).astype(
        jnp.bfloat16
    )
    head_low = student_edge[1].astype(jnp.bfloat16)
    predicted = (
        jnp.einsum("scd,de->sce", final_low, head_low, preferred_element_type=jnp.float32)
        + student_vecs[last_row + 3]
    )
    offset = predicted - target
    size_abs = jnp.abs(offset)
    loss_part = (
        jnp.sum(jnp.where(size_abs < 1.0, 0.5 * offset * offset, size_abs - 0.5) * masked)
        / model_width**0.5
    )
    grad_pred = jnp.clip(offset, -1.0, 1.0) * masked / model_width**0.5
    grad_low = grad_pred.astype(jnp.bfloat16)
    grad_head = jnp.einsum("scd,sce->de", final_low, grad_low, preferred_element_type=jnp.float32)
    grad_bias = jnp.sum(grad_pred, axis=(0, 1))
    grad_final = jnp.einsum("sce,de->scd", grad_low, head_low, preferred_element_type=jnp.float32)
    unused, final_pull = jax.vjp(
        norm_rows, stream, student_vecs[last_row], student_vecs[last_row + 1]
    )
    grad_stream, grad_final_gain, grad_final_shift = final_pull(grad_final)
    attn_grads = []
    mlp_grads = []
    vector_rows = []
    for layer_index in reversed(range(layer_count)):
        attn_full, mlp_full = fetch_again(attn_w[layer_index], mlp_w[layer_index])
        grad_stream, layer_attn, layer_mlp, vector_grads = back_block(
            grad_stream,
            saved_list[layer_index],
            attn_full,
            mlp_full,
            student_vecs[4 * layer_index : 4 * layer_index + 4],
        )
        attn_grads.insert(0, layer_attn)
        mlp_grads.insert(0, layer_mlp)
        vector_rows.insert(0, vector_grads)
    grad_embed = (grad_stream * (1.0 - masked)).astype(jnp.bfloat16)
    grad_mask_vec = jnp.sum(grad_stream * masked, axis=(0, 1))
    grad_patch = jnp.einsum("scp,scd->pd", patches, grad_embed, preferred_element_type=jnp.float32)
    vector_grad = jnp.concatenate(
        vector_rows + [jnp.stack([grad_final_gain, grad_final_shift, grad_mask_vec, grad_bias])],
        axis=0,
    )
    edge_grad, vecs_grad = (
        lax.psum_scatter(
            jnp.stack([grad_patch, grad_head]), (DP, TENSOR), scatter_dimension=1, tiled=True
        ),
        lax.psum_scatter(vector_grad, (DP, TENSOR), scatter_dimension=1, tiled=True),
    )
    attn_grad = jnp.stack(attn_grads)
    mlp_grad = jnp.stack(mlp_grads)
    edge_first, edge_second, edge_update = direction(edge, edge_grad, edge_m, edge_v)
    attn_first, attn_second, attn_update = direction(attn_w, attn_grad, attn_m, attn_v)
    mlp_first, mlp_second, mlp_update = direction(mlp_w, mlp_grad, mlp_m, mlp_v)
    vecs_first, vecs_second, vecs_update = direction(vecs, vecs_grad, vecs_m, vecs_v)
    weight_sq, update_sq, loss_total = lax.psum(
        (
            matrix_squares(edge, attn_w, mlp_w),
            matrix_squares(edge_update, attn_update, mlp_update),
            loss_part,
        ),
        (DP, TENSOR),
    )
    weight_norm = jnp.sqrt(weight_sq)
    update_norm = jnp.sqrt(update_sq)
    trust = weight_norm / (update_norm + adam_epsilon)
    edge_trust = trust[0:2]
    layer_trust = trust[2:].reshape(layer_count, 6)
    new_edge = edge - learn_rate * edge_trust[:, None, None] * edge_update
    new_attn = attn_w - learn_rate * layer_trust[:, None, 0:4, None] * attn_update
    new_mlp = mlp_w - learn_rate * layer_trust[:, None, 4:6, None] * mlp_update
    new_vecs = vecs - learn_rate * vecs_update
    keep_share = 1.0 - teacher_decay
    token_total = seq_total * clip_count * lax.axis_size(DP)
    return (
        loss_total / token_total,
        jnp.stack([weight_norm, update_norm]),
        new_edge,
        new_attn,
        new_mlp,
        new_vecs,
        edge_first,
        edge_second[0],
        edge_second[1],
        attn_first,
        attn_second[:, :, 0:3],
        attn_second[:, :, 3],
        mlp_first,
        mlp_second,
        vecs_first,
        vecs_second,
        keep_share * (new_edge - teacher_edge),
        keep_share * (new_attn - teacher_attn),
        keep_share * (new_mlp - teacher_mlp),
        keep_share * (new_vecs - teacher_vecs),
        new_edge.astype(jnp.bfloat16),
        new_attn.astype(jnp.bfloat16),
        new_mlp.astype(jnp.bfloat16),
        new_vecs.astype(jnp.bfloat16),
    )


MESH = pl.DeviceIdType.MESH
ORDERS = (("z", "x", "y"), ("x", "y", "z"), ("y", "z", "x"))
LOW = jnp.bfloat16
ALL = slice(None)


def coords():
    d = lax.axis_index(DP)
    t = lax.axis_index(TENSOR)
    return dict(a=t // 2, z=t % 2, y=d // 4, x=(d // 2) % 2, c=d % 2)


def ident(co):
    return (co["y"] * 4 + co["x"] * 2 + co["c"], co["a"] * 2 + co["z"])


def flip(co, k):
    co = dict(co)
    co[k] = 1 - co[k]
    return ident(co)


def place(co, full, rows):
    return tuple(ALL if k in full else co[k] for k in "azyxc") + (rows,)


ANY = pl.BlockSpec(memory_space=pl.ANY)
DMA = pltpu.SemaphoreType.DMA


def shape_of(shape, kind=LOW):
    return jax.ShapeDtypeStruct(shape, kind)


def dot(left, right):
    return jnp.dot(left, right, preferred_element_type=jnp.float32)


def dot_nt(left, right):
    return lax.dot_general(
        left, right, (((1,), (1,)), ((), ())), preferred_element_type=jnp.float32
    )


def dot_tn(left, right):
    return lax.dot_general(
        left, right, (((0,), (0,)), ((), ())), preferred_element_type=jnp.float32
    )


def pack_heads(block):
    q, k, v, o = (block[..., i, :] for i in range(4))
    two = 2 * HEAD
    pieces = [q[..., :two], k[..., :two], v[..., :two], q[..., two:], v[..., two:], k[..., two:]]
    pieces += [o[..., HEAD:two], o[..., :HEAD], o[..., two:]]
    return jnp.concatenate(pieces, axis=-1)


def unpack_heads(packed):
    cut = lambda *spots: jnp.concatenate(
        [packed[..., HEAD * a : HEAD * b] for a, b in spots], axis=-1
    )
    kinds = [cut((0, 2), (6, 7)), cut((2, 4), (8, 9)), cut((4, 6), (7, 8))]
    kinds.append(cut((10, 11), (9, 10), (11, 12)))
    return jnp.stack(kinds, axis=-2)


def norm_block(values, gain, shift):
    average = jnp.mean(values, axis=-1, keepdims=True)
    centered = values - average
    spread = jnp.mean(centered * centered, axis=-1, keepdims=True)
    return centered * lax.rsqrt(spread + norm_epsilon) * gain + shift


def matrix(value):
    return value.reshape(-1, value.shape[-1])


def low_lanes(shape):
    return lax.broadcasted_iota(jnp.int32, shape, len(shape) - 1) % 128 < HEAD


def forward_kernel(*refs):
    (attn_mine, attn_other, mlp_mine, mlp_other, edge_mine, edge_other) = refs[:6]
    vec_mine, vec_other, patch = refs[6:9]
    (o_attn, o_mlp, o_head, o_vec, o_x, o_mid, o_normed, o_qkv, o_peer, o_ctx) = refs[9:19]
    (o_hid, o_act, o_slope, o_lse, o_last, o_final, o_pixels, o_dlow, o_sums, o_mask) = refs[19:29]
    (w_attn, w_mlp, w_edge, w_vec, pixels, embed_w, head_w, gains, x, mid) = refs[29:39]
    (normed, qkv, peer, ctx, hid, act, slope, lse, work, target, stat, sums, turned) = refs[39:52]
    local_sem, send_sem, recv_sem, patch_sem, peer_sem, stat_sem, save_sem, core_sem = refs[52:]
    co = coords()
    me = ident(co)
    column = co["y"] * 2 + co["x"]
    teaching = co["a"] == 1
    rows_here = x.shape[0]
    width = x.shape[1]
    layers = attn_mine.shape[0]
    last_row = 4 * layers
    barrier = pltpu.get_barrier_semaphore()
    for k in range(1, 8):
        to = (column * 2 + (co["c"] + k // 4) % 2, (me[1] + k % 4) % 4)
        pl.semaphore_signal(barrier, inc=1, device_id=to, device_id_type=MESH)
    for k in "xy":
        pl.semaphore_signal(barrier, inc=1, device_id=flip(co, k), device_id_type=MESH)
    pl.semaphore_wait(barrier, 9)

    items = [(edge_mine, edge_other, w_edge, 0), (vec_mine, vec_other, w_vec, 0)]
    for l in range(layers):
        items.append((attn_mine.at[l], attn_other.at[l], w_attn.at[l], 3 * l + 1))
        for k in range(2):
            items.append(
                (mlp_mine.at[l, k], mlp_other.at[l, k], w_mlp.at[l, k], 3 * l + 2 + k)
            )
    sent = []
    table = {}

    def remote(source, to_ref, i, j, k, to):
        copy = pltpu.make_async_remote_copy(
            src_ref=source,
            dst_ref=to_ref,
            send_sem=send_sem.at[i, j, k],
            recv_sem=recv_sem.at[i, j, k],
            device_id=to,
            device_id_type=MESH,
        )
        copy.start()
        sent.append(copy)
        return copy

    def begin(slot):
        for i, (mine, other, full, at) in enumerate(items):
            if at == slot:
                spot = full.at[place(co, "", ALL)]
                copy = pltpu.make_async_copy(mine, spot, local_sem.at[i])
                copy.start()
                table[i, -1] = (copy, remote(other, spot, i, 0, 4, flip(co, "a")))

    def step(wave, s):
        for i, (mine, other, full, at) in enumerate(items):
            if wave - at != s:
                continue
            if s == 0:
                table[i, -1][0].wait()
                table[i, -1][1].wait_recv()
            size = mine.shape[0] // 3
            copies = []
            for p in range(3):
                if s > 0:
                    table[i, s - 1][p].wait_recv()
                if s < 4:
                    order = ORDERS[p] + ("c",)
                    full_dims = ("a",) + order[:s]
                    ref = full.at[place(co, full_dims, pl.ds(p * size, size))]
                    copies.append(remote(ref, ref, i, p, s, flip(co, order[s])))
            table[i, s] = copies

    saves = {}
    counter = iter(range(48))

    def save(name, source, to_ref):
        copy = pltpu.make_async_copy(source, to_ref, save_sem.at[next(counter)])
        copy.start()
        saves[name] = copy

    shared = {}
    core_counter = iter(range(16))
    own_rows, peer_rows = pl.ds(0, rows_here), pl.ds(rows_here, rows_here)

    def to_core(name, source, to_ref):
        n = next(core_counter)
        shared[name] = pltpu.make_async_remote_copy(
            src_ref=source,
            dst_ref=to_ref,
            send_sem=core_sem.at[0, n],
            recv_sem=core_sem.at[1, n],
            device_id=flip(co, "c"),
            device_id_type=MESH,
        )
        shared[name].start()

    def share(name, source, to_ref, lead):
        save(name, source, to_ref.at[lead + (own_rows,)])
        to_core(name, source, to_ref.at[lead + (peer_rows,)])

    turns = []

    def turn(name, columns, to_ref):
        spot = turned.at[len(turns) % 2]
        if len(turns) >= 2:
            wait_saves(turns[-2])
        turns.append(name)
        for n in range(2):
            spot[n] = jnp.transpose(columns(n)).astype(LOW).reshape(spot.shape[1:])
        save(name, spot.at[:, :, co["c"]], to_ref.at[:, :, :, own_rows])
        to_core(name, spot.at[:, :, 1 - co["c"]], to_ref.at[:, :, :, peer_rows])

    def columns_of(ref):
        return lambda n: ref[:, n * rows_here : (n + 1) * rows_here].astype(jnp.float32)

    def by_rows(size, body):
        def run(n, _):
            body(pl.ds(pl.multiple_of(n * size, size), size))
            return 0

        lax.fori_loop(0, rows_here // size, run, 0)

    def gain(row):
        return gains[row : row + 1, :]

    def norm_into(source, out, row):
        def body(span):
            out[span, :] = norm_block(source[span, :], gain(row), gain(row + 1)).astype(LOW)

        by_rows(64, body)

    def embed():
        owned = [
            w_vec[t // 2, t % 2, d // 4, d // 2 % 2, d % 2] for d in range(8) for t in range(4)
        ]
        gains[...] = jnp.transpose(jnp.concatenate(owned))[: gains.shape[0]]
        save("vec", gains, o_vec)
        half = edge_mine.shape[0] // 2
        for d in range(8):
            for a in range(2):
                at = (d // 4, d // 2 % 2, d % 2)
                left = w_edge[(a, 0) + at].astype(jnp.float32)
                right = w_edge[(a, 1) + at].astype(jnp.float32)
                spot = pl.ds((2 * d + a) * 2 * half, 2 * half)
                embed_w[spot, :] = jnp.concatenate([left[:half], right[:half]]).astype(LOW)
                head_w[spot, :] = jnp.concatenate([left[half:], right[half:]]).astype(LOW)
        save("head", head_w, o_head)
        for q in range(2):
            origin = (column * 2 + co["z"], co["c"] * 2 + q)
            same = jnp.logical_and(origin[0] == me[0], origin[1] == me[1])

            @pl.when(same)
            def _():
                pltpu.make_async_copy(patch, pixels.at[q], patch_sem.at[2]).wait()

            @pl.when(jnp.logical_not(same))
            def _():
                pltpu.make_async_remote_copy(
                    src_ref=patch,
                    dst_ref=pixels.at[q],
                    send_sem=patch_sem.at[3],
                    recv_sem=patch_sem.at[q],
                    device_id=me,
                    device_id_type=MESH,
                ).wait_recv()

        save("mask", pixels.at[:, :, width:], o_mask)
        quarter = pixels.shape[1]

        def pixel_columns(n):
            cols = pixels[:, :, n * rows_here : (n + 1) * rows_here].astype(jnp.float32)
            return cols.reshape(rows_here, rows_here)

        turn("pixels", pixel_columns, o_pixels)
        for q in range(2):
            hide = pixels[q, :, width : width + 1].astype(jnp.float32)
            hide = jnp.where(teaching, 0.0, hide)
            rows = pl.ds(q * quarter, quarter)
            x[rows, :] = (
                dot(pixels[q, :, :width], embed_w[...]) * (1.0 - hide) + hide * gain(last_row + 2)
            )

    def peer_copy(l, t):
        return pltpu.make_async_remote_copy(
            src_ref=qkv.at[t, :, 128:640],
            dst_ref=peer.at[l, t],
            send_sem=peer_sem.at[0, l, t],
            recv_sem=peer_sem.at[1, l, t],
            device_id=flip(co, "c"),
            device_id_type=MESH,
        )

    settled = []

    def wait_saves(*names):
        for name in names:
            if name in saves:
                saves.pop(name).wait()
                if name in shared:
                    shared[name].wait_send()
                    settled.append(shared.pop(name))

    def project(l):
        save(("x", l), x, o_x.at[l])
        norm_into(x, normed, 4 * l)
        for t in range(4):
            weight = matrix(w_attn[l, t // 2, t % 2])
            qkv[t] = dot(normed[...], weight).astype(LOW)
            peer_copy(l, t).start()
            save(("qkv", l, t), qkv.at[t], o_qkv.at[l, t])
        turn(("normed", l), columns_of(normed), o_normed.at[l])

    def attend(l, first, last):
        if first == 0:
            for t in range(4):
                peer_copy(l, t).wait_recv()
            lse[...] = jnp.zeros_like(lse)
        size = rows_here

        def body(n, _):
            t = n // (rows_here // size)
            span = pl.ds(pl.multiple_of(n % (rows_here // size) * size, size), size)
            low = low_lanes((size, 128))
            lane = lax.broadcasted_iota(jnp.int32, (size, 128), 1)
            zero = jnp.zeros((size, 128), LOW)
            outs = []
            total = lse[span, :]
            for j in range(3):
                q_at = 0 if j < 2 else 384
                k_at = 128 if j < 2 else 512
                v_at = 256 if j < 2 else 384
                query = qkv[t, span, q_at : q_at + 128] * jnp.asarray(HEAD**-0.5, LOW)
                query = jnp.where(low, query, zero) if j != 1 else jnp.where(low, zero, query)
                scores = jnp.concatenate(
                    [
                        dot_nt(query, qkv[t, :, k_at : k_at + 128]),
                        dot_nt(query, peer[l, t, :, k_at - 128 : k_at]),
                    ],
                    axis=1,
                )
                peak = jnp.max(scores, axis=1, keepdims=True)
                raised = jnp.exp(scores - peak)
                summed = jnp.sum(raised, axis=1, keepdims=True)
                weights = raised.astype(LOW)
                out = dot(weights[:, :rows_here], qkv[t, :, v_at : v_at + 128])
                out = out + dot(weights[:, rows_here:], peer[l, t, :, v_at - 128 : v_at])
                outs.append(out / summed)
                total = jnp.where(lane == 3 * t + j, peak + jnp.log(summed), total)
            lse[span, :] = total
            ctx[t, span, :128] = jnp.where(low, 0.0, outs[1]).astype(LOW)
            ctx[t, span, 128:] = jnp.where(low, outs[0], outs[2]).astype(LOW)
            return 0

        each = rows_here // size
        lax.fori_loop(first * each, last * each, body, 0)
        if last == 4:
            save(("lse", l), lse, o_lse.at[l])
            share(("ctx", l), ctx, o_ctx.at[l], (ALL,))
            save(("peer", l), peer.at[l], o_peer.at[l])

    def out_project(l):
        mid[...] = x[...]

        def body(t, _):
            weight = matrix(w_attn[l, t // 2, t % 2, :, :, :, :, 512:])
            mid[...] += dot_nt(ctx[t], weight)
            return 0

        lax.fori_loop(0, 4, body, 0)
        save(("mid", l), mid, o_mid.at[l])
        norm_into(mid, hid, 4 * l + 2)
        turn(("hid", l), columns_of(hid), o_hid.at[l])

    def expand(l, first, last):
        def body(n, _):
            t = n // 3
            cols = pl.ds(pl.multiple_of(n % 3 * 256, 256), 256)
            weight = matrix(w_mlp[l, 0, t // 2, t % 2, :, :, :, :, cols])
            upward = dot(hid[...], weight)
            share = 0.5 + 0.5 * lax.erf(upward * 0.5**0.5)
            act[t, :, cols] = (upward * share).astype(LOW)
            bell = jnp.exp(-0.5 * upward * upward) * (2.0 * jnp.pi) ** -0.5
            slope[t, :, cols] = (share + upward * bell).astype(LOW)
            return 0

        lax.fori_loop(3 * first, 3 * last, body, 0)
        if last == 4:
            share(("act", l), act, o_act.at[l], (ALL,))
            save(("slope", l), slope, o_slope.at[l])

    def contract(l, first, last):
        if first == 0:
            wait_saves(("x", l))
            x[...] = mid[...]

        def body(t, _):
            x[...] += dot_nt(act[t], matrix(w_mlp[l, 1, t // 2, t % 2]))
            return 0

        lax.fori_loop(first, last, body, 0)

    def stat_copy(l):
        return pltpu.make_async_remote_copy(
            src_ref=stat.at[l, 0],
            dst_ref=stat.at[l, 1],
            send_sem=stat_sem.at[0, l],
            recv_sem=stat_sem.at[1, l],
            device_id=flip(co, "c"),
            device_id_type=MESH,
        )

    def target_copy():
        return pltpu.make_async_remote_copy(
            src_ref=target,
            dst_ref=target,
            send_sem=stat_sem.at[0, layers],
            recv_sem=stat_sem.at[1, layers],
            device_id=flip(co, "a"),
            device_id_type=MESH,
        )

    def teach(l):
        @pl.when(teaching)
        def _():
            stat[l, 0] = jnp.zeros_like(stat[l, 0])

            def body(span):
                value = x[span, :]
                stat[l, 0, 0:1] += jnp.sum(value, axis=0, keepdims=True)
                stat[l, 0, 1:2] += jnp.sum(value * value, axis=0, keepdims=True)

            by_rows(64, body)
            stat_copy(l).start()
            stat_copy(l).wait()
            both = (stat[l, 0] + stat[l, 1]) / (2 * rows_here)
            average = both[0:1]
            spread = both[1:2] - average * average
            scale = lax.rsqrt(spread + inst_epsilon) / layers

            def mix(span):
                value = (x[span, :] - average) * scale
                if l > 0:
                    value = value + work[span, :]
                if l < layers - 1:
                    work[span, :] = value
                else:
                    target[span, :] = value.astype(LOW)

            by_rows(64, mix)
            if l == layers - 1:
                target_copy().start()
                target_copy().wait_send()

    def finish():
        save("last", x, o_last)
        sums[...] = jnp.zeros_like(sums)

        @pl.when(jnp.logical_not(teaching))
        def _():
            norm_into(x, normed, last_row)
            work[...] = dot(normed[...], head_w[...])
            target_copy().wait_recv()

            quarter = pixels.shape[1]

            def body(n, _):
                span = pl.ds(pl.multiple_of(n * 64, 64), 64)
                part = pl.ds(pl.multiple_of(n % 3 * 64, 64), 64)
                masked = pixels[n // 3, part, width : width + 1].astype(jnp.float32)
                offset = work[span, :] + gain(last_row + 3) - target[span, :].astype(jnp.float32)
                size = jnp.abs(offset)
                loss = jnp.where(size < 1.0, 0.5 * offset * offset, size - 0.5) * masked
                pull = jnp.clip(offset, -1.0, 1.0) * masked * width**-0.5
                sums[0:1] += jnp.sum(pull, axis=0, keepdims=True)
                sums[1:2] += jnp.sum(loss, axis=0, keepdims=True)
                target[span, :] = pull.astype(LOW)
                return 0

            lax.fori_loop(0, rows_here // 64, body, 0)

        turn("final", columns_of(normed), o_final)
        share("dlow", target, o_dlow, ())
        save("sums", sums, o_sums)

    for r in range(2):
        to = (column * 2 + co["a"], 2 * r + co["c"])
        same = jnp.logical_and(to[0] == me[0], to[1] == me[1])
        spot = pixels.at[co["z"]]

        @pl.when(same)
        def _():
            pltpu.make_async_copy(patch, spot, patch_sem.at[2]).start()

        @pl.when(jnp.logical_not(same))
        def _():
            pltpu.make_async_remote_copy(
                src_ref=patch,
                dst_ref=spot,
                send_sem=patch_sem.at[3 + r],
                recv_sem=patch_sem.at[co["z"]],
                device_id=to,
                device_id_type=MESH,
            ).start()

    def save_weights(slot):
        def run():
            l, k = (slot - 1) // 3, (slot - 1) % 3
            if k == 0:
                save(("attn", l), w_attn.at[l], o_attn.at[l])
            else:
                save(("mlp", l, k), w_mlp.at[l, k - 1], o_mlp.at[l, k - 1])

        return run

    plan = {0: [embed]}
    for l in range(layers):
        repeat = l > 0

        def start(l=l):
            if l > 0:
                for t in range(4):
                    peer_copy(l - 1, t).wait_send()
                wait_saves(*[("qkv", l - 1, t) for t in range(4)])
            project(l)

        def begin_attend(l=l):
            if l > 0:
                wait_saves(("lse", l - 1), ("ctx", l - 1))
            attend(l, 0, 2)

        def begin_out(l=l):
            if l > 0:
                wait_saves(("mid", l - 1))
            out_project(l)

        def begin_expand(l=l):
            if l > 0:
                wait_saves(("act", l - 1), ("slope", l - 1))
            expand(l, 0, 2)

        plan[3 * l + 1] = [
            save_weights(3 * l + 1),
            start,
            begin_attend,
            lambda l=l: attend(l, 2, 4),
            begin_out,
        ]
        plan[3 * l + 2] = [
            save_weights(3 * l + 2),
            begin_expand,
            lambda l=l: expand(l, 2, 4),
        ]
        plan[3 * l + 3] = [
            save_weights(3 * l + 3),
            lambda l=l: contract(l, 0, 2),
            lambda l=l: contract(l, 2, 4),
            lambda l=l: teach(l),
        ]
    final_slot = 3 * layers
    begin(0)
    begin(1)
    for wave in range(final_slot + 5):
        begin(wave + 2)
        step(wave, 4)
        todo = list(plan.get(wave - 4, []))
        for s in range(4):
            step(wave, s)
            if todo:
                todo.pop(0)()
        while todo:
            todo.pop(0)()
    finish()
    wait_saves(*list(saves))
    for copy in settled:
        copy.wait_recv()
    for t in range(4):
        peer_copy(layers - 1, t).wait_send()
    for r in range(2):
        to = (column * 2 + co["a"], 2 * r + co["c"])
        same = jnp.logical_and(to[0] == me[0], to[1] == me[1])

        @pl.when(jnp.logical_not(same))
        def _():
            pltpu.make_async_remote_copy(
                src_ref=patch,
                dst_ref=pixels.at[0],
                send_sem=patch_sem.at[3 + r],
                recv_sem=patch_sem.at[0],
                device_id=me,
                device_id_type=MESH,
            ).wait_send()

    for copy in sent:
        copy.wait_send()


def forward_all(*parts):
    layers, rows, width = parts[0].shape
    cube = (2, 2, 2, 2, 2)
    here = 2 * parts[8].shape[0]
    f32 = jnp.float32
    attn = (layers,) + cube + (rows, width)
    mlp = (layers, 2) + cube + (rows, width)
    tall = (here, width)
    turned = (2, 2, rows, 2 * here)
    quarter = parts[8].shape[0]
    outs = (
        shape_of(attn),
        shape_of(mlp),
        shape_of((width, width)),
        shape_of((16, width), f32),
        shape_of((layers,) + tall, f32),
        shape_of((layers,) + tall, f32),
        shape_of((layers,) + turned),
        shape_of((layers, 4) + tall),
        shape_of((layers, 4, here, 512)),
        shape_of((layers, 4, 2 * here, 256)),
        shape_of((layers,) + turned),
        shape_of((layers, 4, 2 * here, width)),
        shape_of((layers, 4) + tall),
        shape_of((layers, here, 128), f32),
        shape_of(tall, f32),
        shape_of(turned),
        shape_of(turned),
        shape_of((2 * here, width)),
        shape_of((8, width), f32),
        shape_of((2, quarter, 128)),
    )
    scratch = [
        pltpu.VMEM(attn, LOW),
        pltpu.VMEM(mlp, LOW),
        pltpu.VMEM(cube + parts[4].shape, LOW),
        pltpu.VMEM(cube + parts[6].shape, f32),
        pltpu.VMEM((2,) + parts[8].shape, LOW),
        pltpu.VMEM((width, width), LOW),
        pltpu.VMEM((width, width), LOW),
        pltpu.VMEM((16, width), f32),
        pltpu.VMEM(tall, f32),
        pltpu.VMEM(tall, f32),
        pltpu.VMEM(tall, LOW),
        pltpu.VMEM((4,) + tall, LOW),
        pltpu.VMEM((layers, 4, here, 512), LOW),
        pltpu.VMEM((4, here, 256), LOW),
        pltpu.VMEM(tall, LOW),
        pltpu.VMEM((4,) + tall, LOW),
        pltpu.VMEM((4,) + tall, LOW),
        pltpu.VMEM((here, 128), f32),
        pltpu.VMEM(tall, f32),
        pltpu.VMEM(tall, LOW),
        pltpu.VMEM((layers, 2, 8, width), f32),
        pltpu.VMEM((8, width), f32),
        pltpu.VMEM((2, 2, 2, 2, rows, here), LOW),
    ]
    count = 2 + 3 * layers
    sems = [
        DMA((count,)),
        DMA((count, 3, 5)),
        DMA((count, 3, 5)),
        DMA((5,)),
        DMA((2, layers, 4)),
        DMA((2, layers + 1)),
        DMA((48,)),
        DMA((2, 16)),
    ]
    return pl.pallas_call(
        forward_kernel,
        out_shape=outs,
        in_specs=[ANY] * 9,
        out_specs=(ANY,) * len(outs),
        scratch_shapes=scratch + sems,
        compiler_params=pltpu.CompilerParams(
            collective_id=0, has_side_effects=True, vmem_limit_bytes=60 * 2**20
        ),
    )(*parts)


def backward_kernel(*refs):
    (w_attn, w_mlp, h_head, h_gains, h_x, h_mid, h_normed, h_qkv, h_peer, h_ctx) = refs[:10]
    (h_hid, h_act, h_slope, h_lse, h_last, h_final, h_pixels, h_dlow, h_sums, h_mask) = refs[10:20]
    o_attn, o_mlp, o_head, o_patch, o_vec = refs[20:25]
    (head, gains, x, normed_t, hid_t, qkv, peer, ctx, lse, attn, act) = refs[25:36]
    (down, up, slope, tall_t, tall, mask, sums, g, acc, low_g, turned, dffn_t) = refs[36:48]
    (datt_t, dup, dctx, dqkv, dkv_out, dkv_in, query, pull, score_row, vec_grad) = refs[48:58]
    vec_turned = refs[58]
    rest = refs[59:]
    co = coords()
    layers = w_attn.shape[0]
    last_row = 4 * layers
    here, width = g.shape
    other_core = flip(co, "c")
    own_rows, peer_rows = pl.ds(0, here), pl.ds(here, here)
    barrier = pltpu.get_barrier_semaphore()
    for k in "azyxc":
        pl.semaphore_signal(barrier, inc=1, device_id=flip(co, k), device_id_type=MESH)
    pl.semaphore_wait(barrier, 5)

    kinds = {}
    spot = 0
    for name, parts in (("D", 3), ("U", 3), ("A", 3), ("H", 2), ("P", 2), ("V", 3)):
        kinds[name] = dict(mine=rest[spot], part=[], parts=parts, name=name)
        spot += 1
        for p in range(parts):
            kinds[name]["part"].append(rest[spot : spot + 3])
            spot += 3
    items = {}
    targets = [("H", 0, o_head)]
    for l in reversed(range(layers)):
        targets += [("D", l, o_mlp.at[l, 1]), ("U", l, o_mlp.at[l, 0]), ("A", l, o_attn.at[l])]
    targets += [("P", 0, o_patch), ("V", 0, o_vec)]
    for n, (name, l, target) in enumerate(targets):
        items[name, l] = dict(kinds[name], n=n, l=l, target=target, last=rest[spot], sent=[])
        spot += 1
    load_sem, send_sem, recv_sem, out_sem, core_sem, credit = rest[spot:]
    own = {q: co[q] for q in "zyx"}

    def pick(fixed, span):
        return tuple(fixed.get(k, ALL) for k in "azyx") + (span,)

    def span_of(item, p):
        size = item["mine"].shape[4] // item["parts"]
        return pl.ds(p * size, size)

    def part_copy(item, p, s):
        order = ORDERS[p][::-1]
        k = order[s]
        fixed = {q: co[q] for q in order[:s]}
        return pltpu.make_async_remote_copy(
            src_ref=item["mine"].at[pick({**fixed, k: 1 - co[k]}, span_of(item, p))],
            dst_ref=item["part"][p][s].at[pick({q: 0 for q in order[: s + 1]}, ALL)],
            send_sem=send_sem.at[item["n"], p, s],
            recv_sem=recv_sem.at[item["n"], p, s],
            device_id=flip(co, k),
            device_id_type=MESH,
        )

    def last_hop(item):
        return pltpu.make_async_remote_copy(
            src_ref=item["mine"].at[pick({**own, "a": 1}, ALL)],
            dst_ref=item["last"],
            send_sem=send_sem.at[item["n"], 0, 3],
            recv_sem=recv_sem.at[item["n"], 0, 3],
            device_id=flip(co, "a"),
            device_id_type=MESH,
        )

    def out_copy(item):
        return pltpu.make_async_copy(
            item["mine"].at[pick({**own, "a": 0}, ALL)], item["target"], out_sem.at[item["n"]]
        )

    def begin(item, s):
        if s == 0 and item["name"] in "DUA" and item["l"] < layers - 1:
            for q in range(3):
                pl.semaphore_wait(credit.at["DUA".index(item["name"]), q], 1)
        for p in range(item["parts"]):
            copy = part_copy(item, p, s)
            copy.start()
            item["sent"].append(copy)

    def gather_in(item, s):
        for p in range(item["parts"]):
            part_copy(item, p, s).wait_recv()
            done = ORDERS[p][::-1][: s + 1]
            left = [k for k in "azyx" if k not in done]
            mine, part, span = item["mine"], item["part"][p][s], span_of(item, p)

            def body(n, _):
                at = {}
                for k in reversed(left):
                    at[k] = n % 2
                    n = n // 2
                there = tuple(0 if k in done else at[k] for k in "azyx")
                spot = tuple(co[k] if k in done else at[k] for k in "azyx") + (span,)
                mine[spot] = mine[spot] + part[there]
                return 0

            lax.fori_loop(0, 2 ** len(left), body, 0)

    def advance(name, l, s):
        item = items[name, l]
        gather_in(item, s)
        if s < 2:
            begin(item, s + 1)
            return
        if name in "DUA" and l > 0:
            for q, k in enumerate("zyx"):
                pl.semaphore_signal(
                    credit.at["DUA".index(name), q],
                    inc=1,
                    device_id=flip(co, k),
                    device_id_type=MESH,
                )
        last_hop(item).start()
        out_copy(item).start()

    def settle(name, l):
        item = items[name, l]
        for copy in item["sent"]:
            copy.wait_send()
        last_hop(item).wait_send()
        out_copy(item).wait()

    loads = {}
    counter = iter(range(96))

    def fetch(name, source, to_ref):
        loads[name] = pltpu.make_async_copy(source, to_ref, load_sem.at[next(counter)])
        loads[name].start()

    def need(*names):
        for name in names:
            loads.pop(name).wait()

    core_counter = iter(range(48))
    core = {}

    def to_core(name, source, to_ref):
        n = next(core_counter)
        core[name] = pltpu.make_async_remote_copy(
            src_ref=source,
            dst_ref=to_ref,
            send_sem=core_sem.at[0, n],
            recv_sem=core_sem.at[1, n],
            device_id=other_core,
            device_id_type=MESH,
        )
        core[name].start()

    def by_rows(size, body):
        def run(n, _):
            body(pl.ds(pl.multiple_of(n * size, size), size))
            return 0

        lax.fori_loop(0, here // size, run, 0)

    def turn(name, source, to_ref):
        for n in range(2):
            cols = source[:, n * here : (n + 1) * here].astype(jnp.float32)
            turned[n] = jnp.transpose(cols).astype(LOW).reshape(turned.shape[1:])
        to_ref[:, :, :, :here] = turned[:, :, co["c"]]
        to_core(name, turned.at[:, :, 1 - co["c"]], to_ref.at[:, :, :, here:])

    def norm_back(values, row):
        gain = gains[row : row + 1, :]

        def body(span):
            value = values[span, :]
            average = jnp.mean(value, axis=-1, keepdims=True)
            centered = value - average
            spread = jnp.mean(centered * centered, axis=-1, keepdims=True)
            scale = lax.rsqrt(spread + norm_epsilon)
            hat = centered * scale
            dy = acc[span, :]
            vec_grad[row : row + 1, :] += jnp.sum(dy * hat, axis=0, keepdims=True)
            vec_grad[row + 1 : row + 2, :] += jnp.sum(dy, axis=0, keepdims=True)
            u = dy * gain
            mean_u = jnp.mean(u, axis=-1, keepdims=True)
            mean_uh = jnp.mean(u * hat, axis=-1, keepdims=True)
            g[span, :] += scale * (u - mean_u - hat * mean_uh)

        by_rows(64, body)

    def attend_back(t):
        low = low_lanes((here, 128))
        zero = jnp.zeros((here, 128), LOW)
        scale = jnp.asarray(HEAD**-0.5, LOW)
        first = qkv[t, :, 0:128] * scale
        query[0] = jnp.where(low, first, zero)
        query[1] = jnp.where(low, zero, first)
        query[2] = jnp.where(low, qkv[t, :, 384:512] * scale, zero)
        pull[0] = jnp.where(low, dctx[:, 128:256], zero)
        pull[1] = jnp.where(low, zero, dctx[:, 0:128])
        pull[2] = jnp.where(low, zero, dctx[:, 128:256])
        one = ctx[t, own_rows, 0:128].astype(jnp.float32)
        two = ctx[t, own_rows, 128:256].astype(jnp.float32)
        lane = lax.broadcasted_iota(jnp.int32, (here, 128), 1)
        dots = jnp.zeros((here, 128), jnp.float32)
        for j, value in enumerate((two, one, two)):
            row_sum = jnp.sum(value * pull[j].astype(jnp.float32), axis=1, keepdims=True)
            dots = jnp.where(lane == j, row_sum, dots)
        dots = jnp.transpose(dots)
        score_row[0:8, :] = dots[0:8]
        logs = jnp.transpose(lse[...])
        log_rows = jnp.zeros((8, here), jnp.float32)
        for u in range(4):
            log_rows = jnp.where(t == u, logs[3 * u : 3 * u + 8], log_rows)
        score_row[8:16, :] = log_rows
        pair = (2 * here, 128)
        groups = (
            (128, 256, query[0:2].reshape(pair), pull[0:2].reshape(pair), (0, 1)),
            (512, 384, query[2], pull[2], (2,)),
        )
        half = lax.broadcasted_iota(jnp.int32, (128, here), 0) < HEAD
        grads = [None, None]
        for source, shift in ((peer, 128), (qkv, 0)):
            outs = []
            for i, (k_at, v_at, asked, pulled, heads) in enumerate(groups):
                key = source[t, :, k_at - shift : k_at - shift + 128]
                value = source[t, :, v_at - shift : v_at - shift + 128]
                logs = jnp.concatenate([score_row[8 + j : 9 + j, :] for j in heads], axis=1)
                dots = jnp.concatenate([score_row[j : j + 1, :] for j in heads], axis=1)
                probs = jnp.exp(dot_nt(key, asked) - logs)
                grad_scores = (probs * (dot_nt(value, pulled) - dots)).astype(LOW)
                outs.append(dot(grad_scores, asked))
                outs.append(dot(probs.astype(LOW), pulled))
                back = dot(jnp.transpose(key.astype(jnp.float32)).astype(LOW), grad_scores)
                grads[i] = back if grads[i] is None else grads[i] + back
            for i, out in zip((0, 1, 3, 2), outs):
                cols = slice(128 * i, 128 * i + 128)
                if shift:
                    dkv_out[t, :, cols] = out.astype(LOW)
                else:
                    dqkv[t, own_rows, 128 * i + 128 : 128 * i + 256] = out.astype(LOW)
        first = jnp.where(half, grads[0][:, :here], grads[0][:, here:])
        dqkv[t, own_rows, 0:128] = (jnp.transpose(first) * HEAD**-0.5).astype(LOW)
        second = jnp.transpose(grads[1]) * HEAD**-0.5
        keep = dqkv[t, own_rows, 384:512].astype(jnp.float32)
        dqkv[t, own_rows, 384:512] = jnp.where(low, second, keep).astype(LOW)

    def blocks(value):
        return value.reshape(2, 2, -1, value.shape[-1])

    def student():
        fetch("dlow", h_dlow, tall)
        fetch("head", h_head, head)
        fetch("last", h_last, x)
        fetch("gains", h_gains, gains)
        fetch("final", h_final, tall_t)
        steps = [(l, t) for l in reversed(range(layers)) for t in range(4)]

        def fetch_act(n):
            if n < len(steps):
                l, t = steps[n]
                fetch(("act", l, t), h_act.at[l, t], act.at[n % 2])

        def fetch_mlp(n):
            if n < len(steps):
                l, t = steps[n]
                fetch(("up", l, t), w_mlp.at[l, 0, t // 2, t % 2], up.at[n % 2])
                fetch(("down", l, t), w_mlp.at[l, 1, t // 2, t % 2], down.at[n % 2])
                fetch(("slope", l, t), h_slope.at[l, t], slope.at[n % 2])

        def fetch_late(l):
            fetch(("qkv", l), h_qkv.at[l], qkv)
            fetch(("peer", l), h_peer.at[l], peer)
            fetch(("ctx", l), h_ctx.at[l], ctx)
            fetch(("lse", l), h_lse.at[l], lse)
            fetch(("attn", l), w_attn.at[l], attn)
            fetch(("normed", l), h_normed.at[l], normed_t)

        def fetch_hid(l):
            fetch(("hid", l), h_hid.at[l], hid_t)
            fetch(("mid", l), h_mid.at[l], x)

        vec_grad[...] = jnp.zeros_like(vec_grad)
        dqkv[...] = jnp.zeros_like(dqkv)
        g[...] = jnp.zeros_like(g)
        need("dlow", "head")
        acc[...] = dot_nt(tall[own_rows, :], head[...])
        fetch_mlp(0)
        fetch_act(0)
        fetch_act(1)
        fetch_mlp(1)
        need("last", "gains")
        norm_back(x, last_row)
        fetch_hid(layers - 1)
        need("final")
        value = blocks(dot(matrix(tall_t[...]), tall[...]))

        def edge_blocks(mine, value):
            size = value.shape[2] // 4
            for t in range(4):
                block = value[:, :, size * t : size * (t + 1)]
                pad = jnp.zeros((2, 2, mine.shape[4] - size, width), jnp.float32)
                mine[t // 2, t % 2] = jnp.concatenate([block, pad], axis=2).astype(LOW)

        edge_blocks(items["H", 0]["mine"], value)
        begin(items["H", 0], 0)
        fetch_late(layers - 1)
        fetch("sums", h_sums, sums)
        fetch("mask", h_mask, mask)
        fetch("pixels", h_pixels, tall_t)

        for l in reversed(range(layers)):
            top = l == layers - 1
            low_g[...] = g[...].astype(LOW)
            if not top:
                core["datt", l + 1].wait_send()
            turn(("dffn", l), low_g, dffn_t)

            def widen(t, l=l):
                n = steps.index((l, t))
                need(("down", l, t), ("slope", l, t), ("up", l, t))
                pulled = dot(low_g[...], matrix(down[n % 2])) * slope[n % 2].astype(jnp.float32)
                dup[t, own_rows, :] = pulled.astype(LOW)
                to_core(("dup", l, t), dup.at[t, own_rows], dup.at[t, peer_rows])
                back = dot_nt(dup[t, own_rows, :], matrix(up[n % 2]))
                acc[...] = back if t == 0 else acc[...] + back
                fetch_mlp(n + 2)

            if not top:
                for t in range(4):
                    core["dup", l + 1, t].wait_send()
            widen(0)
            core["dffn", l].wait_recv()
            if not top:
                settle("D", l + 1)
            for t in range(4):
                n = steps.index((l, t))
                need(("act", l, t))
                value = dot(matrix(dffn_t[...]), act[n % 2])
                items["D", l]["mine"][t // 2, t % 2] = blocks(value).astype(LOW)
                fetch_act(n + 2)
            begin(items["D", l], 0)
            before = ("H", 0) if top else ("A", l + 1)
            advance(*before, 0)
            widen(1)
            widen(2)
            advance(*before, 1)
            widen(3)
            need(("mid", l))
            norm_back(x, 4 * l + 2)
            fetch(("x", l), h_x.at[l], x)
            advance(*before, 2)
            need(("hid", l))
            if not top:
                settle("U", l + 1)
            for t in range(4):
                core["dup", l, t].wait_recv()
                value = dot(matrix(hid_t[...]), dup[t])
                items["U", l]["mine"][t // 2, t % 2] = blocks(value).astype(LOW)
            begin(items["U", l], 0)
            advance("D", l, 0)
            low_g[...] = g[...].astype(LOW)
            core["dffn", l].wait_send()
            turn(("datt", l), low_g, datt_t)
            need(("attn", l), ("qkv", l), ("peer", l), ("ctx", l), ("lse", l))
            if not top:
                for t in range(4):
                    core["dkv", l + 1, t].wait_send()
                    core["dqkv", l + 1, t].wait_send()
            for t in range(4):
                weight = matrix(attn[t // 2, t % 2, :, :, :, :, 512:])
                dctx[...] = dot(low_g[...], weight).astype(LOW)
                attend_back(t)
                to_core(("dkv", l, t), dkv_out.at[t], dkv_in.at[t])
                if t == 0:
                    advance("D", l, 1)
                if t == 1:
                    advance("U", l, 0)
                if t == 2:
                    advance("D", l, 2)
            advance("U", l, 1)
            for t in range(4):
                core["dkv", l, t].wait_recv()
                for i in range(4):
                    cols = slice(128 * i + 128, 128 * i + 256)
                    total = dqkv[t, own_rows, cols].astype(jnp.float32)
                    total = total + dkv_in[t, :, 128 * i : 128 * i + 128].astype(jnp.float32)
                    dqkv[t, own_rows, cols] = total.astype(LOW)
                to_core(("dqkv", l, t), dqkv.at[t, own_rows], dqkv.at[t, peer_rows])
                weight = matrix(attn[t // 2, t % 2, :, :, :, :, :640])
                back = dot_nt(dqkv[t, own_rows, :], weight)
                acc[...] = back if t == 0 else acc[...] + back
            need(("normed", l))
            core["datt", l].wait_recv()
            if not top:
                settle("A", l + 1)
            for t in range(4):
                core["dqkv", l, t].wait_recv()
                inward = dot(matrix(normed_t[...]), dqkv[t])
                outward = dot(matrix(datt_t[...]), ctx[t])
                joint = inward[:, 512:640] + outward[:, :128]
                value = jnp.concatenate([inward[:, :512], joint, outward[:, 128:]], axis=1)
                items["A", l]["mine"][t // 2, t % 2] = blocks(value).astype(LOW)
            begin(items["A", l], 0)
            advance("U", l, 2)
            need(("x", l))
            norm_back(x, 4 * l)
            if l > 0:
                fetch_hid(l - 1)
                fetch_late(l - 1)
        need("mask", "sums", "pixels")

        def embed_back(n, _):
            span = pl.ds(pl.multiple_of(n * 64, 64), 64)
            part = pl.ds(pl.multiple_of(n % 3 * 64, 64), 64)
            hide = mask[n // 3, part, 0:1].astype(jnp.float32)
            value = g[span, :]
            tall[span, :] = (value * (1.0 - hide)).astype(LOW)
            vec_grad[last_row + 2 : last_row + 3, :] += jnp.sum(value * hide, axis=0, keepdims=True)
            return 0

        lax.fori_loop(0, here // 64, embed_back, 0)
        to_core("embed", tall.at[own_rows], tall.at[peer_rows])
        vec_grad[last_row + 3 : last_row + 4, :] = sums[0:1, :]
        loss = jnp.sum(sums[1:2, :], axis=1, keepdims=True) * width**-0.5
        vec_grad[last_row + 4 : last_row + 5, :] = jnp.broadcast_to(loss, (1, width))
        full = jnp.concatenate([vec_grad[...], jnp.zeros((112, width), jnp.float32)])
        full = jnp.transpose(full)
        size = width // 32
        for d in range(8):
            for t in range(4):
                row = (4 * d + t) * size
                vec_turned[d % 2, t // 2, t % 2, d // 4, d // 2 % 2] = full[row : row + size]
        vec = items["V", 0]
        vec_in = vec_turned.at[2]
        to_core("vec", vec_turned.at[1 - co["c"]], vec_in)
        core["embed"].wait_recv()
        edge_blocks(items["P", 0]["mine"], blocks(dot(matrix(tall_t[...]), tall[...])))
        begin(items["P", 0], 0)
        core["vec"].wait_recv()
        vec["mine"][...] = vec_turned[co["c"]] + vec_turned[2]
        begin(vec, 0)
        for s in range(3):
            advance("A", 0, s)
            advance("P", 0, s)
            advance("V", 0, s)
        for name, l, unused in targets:
            if l == 0:
                settle(name, l)
        core["embed"].wait_send()
        core["vec"].wait_send()
        core["datt", 0].wait_send()
        for t in range(4):
            for name in ("dup", "dkv", "dqkv"):
                core[name, 0, t].wait_send()

    @pl.when(co["a"] == 0)
    def _():
        student()

    @pl.when(co["a"] == 1)
    def _():
        for name, l, target in targets:
            item = items[name, l]
            last_hop(item).wait_recv()
            copy = pltpu.make_async_copy(item["last"], target, out_sem.at[item["n"]])
            copy.start()
        for name, l, target in targets:
            item = items[name, l]
            pltpu.make_async_copy(item["last"], target, out_sem.at[item["n"]]).wait()


def backward_all(*parts):
    w_attn, w_mlp = parts[:2]
    layers, rows, width = w_attn.shape[0], w_attn.shape[-2], w_attn.shape[-1]
    here = parts[4].shape[1]
    f32 = jnp.float32
    tall = (here, width)
    turned = (2, 2, rows, 2 * here)
    weight = (2, 2, 2, rows, width)
    edge = 32
    small = width // 32
    scratch = [
        ((width, width), LOW),
        ((16, width), f32),
        (tall, f32),
        (turned, LOW),
        (turned, LOW),
        ((4,) + tall, LOW),
        ((4, here, 512), LOW),
        ((4, 2 * here, 256), LOW),
        ((here, 128), f32),
        ((2, 2) + weight, LOW),
        ((2, 2 * here, width), LOW),
        ((2,) + weight, LOW),
        ((2,) + weight, LOW),
        ((2,) + tall, LOW),
        (turned, LOW),
        ((2 * here, width), LOW),
        (parts[19].shape, LOW),
        ((8, width), f32),
        (tall, f32),
        (tall, f32),
        (tall, LOW),
        ((2, 2, 2, rows, here), LOW),
        (turned, LOW),
        (turned, LOW),
        ((4, 2 * here, width), LOW),
        ((here, 256), LOW),
        ((4, 2 * here, 640), LOW),
        ((4, here, 512), LOW),
        ((4, here, 512), LOW),
        ((3, here, 128), LOW),
        ((3, here, 128), LOW),
        ((16, here), f32),
        ((16, width), f32),
        ((3, 2, 2, 2, 2, small, 128), f32),
    ]
    shapes = dict(
        D=(rows, width, LOW, 3),
        U=(rows, width, LOW, 3),
        A=(rows, width, LOW, 3),
        H=(edge, width, LOW, 2),
        P=(edge, width, LOW, 2),
        V=(small, 128, f32, 3),
    )
    for count, cols, kind, pieces in shapes.values():
        scratch.append(((2, 2, 2, 2, count, cols), kind))
        for p in range(pieces):
            order = ORDERS[p][::-1]
            for s in range(3):
                dims = tuple(1 if k in order[: s + 1] else 2 for k in "azyx")
                scratch.append((dims + (count // pieces, cols), kind))
    names = "H" + "DUA" * layers + "PV"
    for name in names:
        count, cols, kind, pieces = shapes[name]
        scratch.append(((count, cols), kind))
    count = len(names)
    return pl.pallas_call(
        backward_kernel,
        out_shape=(
            shape_of((layers, rows, width)),
            shape_of((layers, 2, rows, width)),
            shape_of((edge, width)),
            shape_of((edge, width)),
            shape_of((small, 128), f32),
        ),
        in_specs=[ANY] * len(parts),
        out_specs=(ANY,) * 5,
        scratch_shapes=[pltpu.VMEM(*s) for s in scratch]
        + [
            DMA((96,)),
            DMA((count, 3, 4)),
            DMA((count, 3, 4)),
            DMA((count,)),
            DMA((2, 48)),
            pltpu.SemaphoreType.REGULAR((3, 3)),
        ],
        compiler_params=pltpu.CompilerParams(
            collective_id=1, has_side_effects=True, vmem_limit_bytes=60 * 2**20
        ),
    )(*parts)


def total_kernel(value, out, held, send_sem, recv_sem):
    co = coords()
    d, t = ident(co)
    near = [(d - d % 2 + (d + k // 4) % 2, (t + k) % 4) for k in range(1, 8)]
    far = [((d + 2 * k) % 8, t) for k in range(1, 4)]
    barrier = pltpu.get_barrier_semaphore()
    for to in near + far:
        pl.semaphore_signal(barrier, inc=1, device_id=to, device_id_type=MESH)
    pl.semaphore_wait(barrier, len(near) + len(far))
    total = value[...]
    n = 0
    for s, group in enumerate((near, far)):
        held[0, s] = total
        copies = []
        for to in group:
            copy = pltpu.make_async_remote_copy(
                src_ref=held.at[0, s],
                dst_ref=held.at[1, n],
                send_sem=send_sem.at[n],
                recv_sem=recv_sem.at[n],
                device_id=to,
                device_id_type=MESH,
            )
            copy.start()
            copies.append((copy, n))
            n += 1
        for copy, spot in copies:
            copy.wait()
            total = total + held[1, spot]
    out[...] = total


def total_all(value):
    return pl.pallas_call(
        total_kernel,
        out_shape=shape_of(value.shape, jnp.float32),
        in_specs=[pl.BlockSpec(memory_space=pltpu.VMEM)],
        out_specs=pl.BlockSpec(memory_space=pltpu.VMEM),
        scratch_shapes=[pltpu.VMEM((2, 10) + value.shape, jnp.float32), DMA((10,)), DMA((10,))],
        compiler_params=pltpu.CompilerParams(collective_id=2, has_side_effects=True),
    )(value)


def per_device(
    patches,
    mask,
    edge,
    attn_w,
    mlp_w,
    vecs,
    edge_m,
    edge_v,
    attn_m,
    attn_v,
    mlp_m,
    mlp_v,
    vecs_m,
    vecs_v,
    teacher_edge,
    teacher_attn,
    teacher_mlp,
    teacher_vecs,
):
    layer_count, rows, kinds, block = attn_w.shape
    wide = mlp_w.shape[3]
    width = patches.shape[2]
    quarter = patches.shape[0]
    edge_rows = edge.shape[1]
    vec_count, vec_cols = vecs.shape
    last_row = 4 * layer_count
    teaching = lax.axis_index(TENSOR) >= 2
    dp_size = lax.axis_size(DP)

    def pack(own_edge, own_attn, own_mlp, own_vecs):
        return (
            pack_heads(own_attn.astype(LOW)),
            jnp.swapaxes(own_mlp.astype(LOW), 1, 2),
            own_edge.astype(LOW).reshape(2 * edge_rows, width),
            jnp.pad(own_vecs.T, ((0, 0), (0, 128 - vec_count))),
        )

    student = (edge, attn_w, mlp_w, vecs)
    teacher = (teacher_edge, teacher_attn, teacher_mlp, teacher_vecs)
    mine = pack(*[jnp.where(teaching, right, left) for left, right in zip(student, teacher)])
    other = pack(*[jnp.where(teaching, left, right) for left, right in zip(student, teacher)])
    parts = [part for pair in zip(mine, other) for part in pair]
    marks = jnp.broadcast_to(mask.astype(LOW), (quarter, 128))
    parts.append(jnp.concatenate([patches.reshape(quarter, width), marks], axis=1))
    attn_grad, mlp_grad, head_grad, patch_grad, vecs_grad = backward_all(*forward_all(*parts))
    by_row = Layout(major_to_minor=(0, 1, 2, 3))
    attn_grad = with_layout_constraint(unpack_heads(attn_grad).astype(jnp.float32), by_row)
    mlp_grad = with_layout_constraint(jnp.swapaxes(mlp_grad.astype(jnp.float32), 1, 2), by_row)
    edge_grad = jnp.stack([patch_grad[:edge_rows], head_grad[:edge_rows]]).astype(jnp.float32)
    loss_total = vecs_grad[0, vec_count]
    vecs_grad = vecs_grad[:, :vec_count].T
    edge_first, edge_second, edge_update = direction(edge, edge_grad, edge_m, edge_v)
    attn_first, attn_second, attn_update = direction(attn_w, attn_grad, attn_m, attn_v)
    mlp_first, mlp_second, mlp_update = direction(mlp_w, mlp_grad, mlp_m, mlp_v)
    vecs_first, vecs_second, vecs_update = direction(vecs, vecs_grad, vecs_m, vecs_v)
    squares = jnp.stack(
        [
            matrix_squares(edge, attn_w, mlp_w),
            matrix_squares(edge_update, attn_update, mlp_update),
        ]
    )
    squares = jnp.pad(squares, ((0, 6), (0, 128 - squares.shape[1])))
    norms = jnp.sqrt(total_all(squares)[:2, : 2 + 6 * layer_count])
    trust = norms[0] / (norms[1] + adam_epsilon)
    edge_trust = trust[0:2]
    layer_trust = trust[2:].reshape(layer_count, 6)
    new_edge = edge - learn_rate * edge_trust[:, None, None] * edge_update
    new_attn = attn_w - learn_rate * layer_trust[:, None, 0:4, None] * attn_update
    new_mlp = mlp_w - learn_rate * layer_trust[:, None, 4:6, None] * mlp_update
    new_vecs = vecs - learn_rate * vecs_update
    keep_share = 1.0 - teacher_decay
    token_total = 4 * quarter * dp_size
    return (
        loss_total / token_total,
        norms,
        new_edge,
        new_attn,
        new_mlp,
        new_vecs,
        edge_first,
        edge_second[0],
        edge_second[1],
        attn_first,
        attn_second[:, :, 0:3],
        attn_second[:, :, 3],
        mlp_first,
        mlp_second,
        vecs_first,
        vecs_second,
        keep_share * (new_edge - teacher_edge),
        keep_share * (new_attn - teacher_attn),
        keep_share * (new_mlp - teacher_mlp),
        keep_share * (new_vecs - teacher_vecs),
        new_edge.astype(LOW),
        new_attn.astype(LOW),
        new_mlp.astype(LOW),
        new_vecs.astype(LOW),
    )


def solution(mesh):
    placed = (
        P(TENSOR, DP, None),
        P(TENSOR, DP),
        P(None, (DP, TENSOR), None),
        P(None, DP, None, TENSOR),
        P(None, DP, None, TENSOR),
        P(None, (DP, TENSOR)),
        P(None, (DP, TENSOR), None),
        P(None, (DP, TENSOR), None),
        P(None, DP, None, TENSOR),
        P(None, DP, None, TENSOR),
        P(None, DP, None, TENSOR),
        P(None, DP, None, TENSOR),
        P(None, (DP, TENSOR)),
        P(None, (DP, TENSOR)),
        P(None, (DP, TENSOR), None),
        P(None, DP, None, TENSOR),
        P(None, DP, None, TENSOR),
        P(None, (DP, TENSOR)),
    )
    planned = dict(mesh.shape) == {DP: 8, TENSOR: 4}
    return jax.shard_map(
        per_device if planned else per_device_general,
        mesh=mesh,
        in_specs=placed,
        out_specs=(
            P(),
            P(),
            P(None, (DP, TENSOR), None),
            P(None, DP, None, TENSOR),
            P(None, DP, None, TENSOR),
            P(None, (DP, TENSOR)),
            P(None, (DP, TENSOR), None),
            P((DP, TENSOR), None),
            P((DP, TENSOR), None),
            P(None, DP, None, TENSOR),
            P(None, DP, None, TENSOR),
            P(None, DP, TENSOR),
            P(None, DP, None, TENSOR),
            P(None, DP, None, TENSOR),
            P(None, (DP, TENSOR)),
            P(None, (DP, TENSOR)),
            P(None, (DP, TENSOR), None),
            P(None, DP, None, TENSOR),
            P(None, DP, None, TENSOR),
            P(None, (DP, TENSOR)),
            P(None, (DP, TENSOR), None),
            P(None, DP, None, TENSOR),
            P(None, DP, None, TENSOR),
            P(None, (DP, TENSOR)),
        ),
        check_vma=False,
    )
```

```python
import jax
import jax.numpy as jnp
from jax import lax
from jax.experimental import pallas as pl
from jax.experimental.layout import Layout, with_layout_constraint
from jax.experimental.pallas import tpu as pltpu
from jax.sharding import PartitionSpec as P

HEAD = 64
DP = "dp"
TENSOR = "tensor"


norm_epsilon = 1e-06
inst_epsilon = 1e-05
first_decay = 0.9
second_decay = 0.999
adam_epsilon = 1e-06
weight_decay = 0.01
learn_rate = 0.3
teacher_decay = 0.999
step_count = 10


def norm_rows(values, gain, shift):
    average = jnp.mean(values, axis=-1, keepdims=True)
    centered = values - average
    spread = jnp.mean(centered * centered, axis=-1, keepdims=True)
    return centered * lax.rsqrt(spread + norm_epsilon) * gain + shift


def exact_gelu(values):
    return jax.nn.gelu(values, approximate=False)


def fetch_edges(edge_part, vector_part):
    return (
        lax.all_gather(edge_part, (DP, TENSOR), axis=1, tiled=True),
        lax.all_gather(vector_part, (DP, TENSOR), axis=1, tiled=True),
    )


def fetch_layer(attn_part, mlp_part):
    return (
        lax.all_gather(attn_part.astype(jnp.bfloat16), DP, axis=0, tiled=True),
        lax.all_gather(mlp_part.astype(jnp.bfloat16), DP, axis=0, tiled=True),
    )


def fetch_again(attn_part, mlp_part):
    return (
        lax.all_gather(attn_part.astype(jnp.bfloat16), DP, axis=0, tiled=True),
        lax.all_gather(mlp_part.astype(jnp.bfloat16), DP, axis=0, tiled=True),
    )


def gather_rows(local_part):
    return lax.all_gather(local_part, TENSOR, axis=0, tiled=True)


def gather_grads(local_part):
    return lax.all_gather(local_part, TENSOR, axis=0, tiled=True)


def project_term(full_rows, weight):
    return jnp.einsum("sck,dk->scd", full_rows, weight, preferred_element_type=jnp.float32)


def scatter_rows(full_rows, weight):
    return lax.psum_scatter(
        project_term(full_rows, weight).astype(jnp.bfloat16),
        TENSOR,
        scatter_dimension=0,
        tiled=True,
    ).astype(jnp.float32)


def scatter_grads(full_rows, weight):
    return lax.psum_scatter(
        project_term(full_rows, weight).astype(jnp.bfloat16),
        TENSOR,
        scatter_dimension=0,
        tiled=True,
    ).astype(jnp.float32)


def attend_forward(parts):
    queries, keys_in, values_in = parts
    scores = jnp.einsum(
        "shd,thd->hst", queries, keys_in, preferred_element_type=jnp.float32
    ) * HEAD ** (-0.5)
    peak = jnp.max(scores, axis=-1, keepdims=True)
    raised = jnp.exp(scores - peak)
    summed = jnp.sum(raised, axis=-1, keepdims=True)
    weights = (raised / summed).astype(jnp.bfloat16)
    context = jnp.einsum("hst,thd->shd", weights, values_in, preferred_element_type=jnp.float32)
    return (context.astype(jnp.bfloat16), (peak + jnp.log(summed))[..., 0])


def attend_backward(parts):
    queries, keys_in, values_in, log_total, grad_context = parts
    scale = HEAD ** (-0.5)
    scores = (
        jnp.einsum("shd,thd->hst", queries, keys_in, preferred_element_type=jnp.float32) * scale
    )
    probs = jnp.exp(scores - log_total[..., None])
    probs_low = probs.astype(jnp.bfloat16)
    grad_values = jnp.einsum(
        "hst,shd->thd", probs_low, grad_context, preferred_element_type=jnp.float32
    )
    grad_probs = jnp.einsum(
        "shd,thd->hst", grad_context, values_in, preferred_element_type=jnp.float32
    )
    grad_scores = (
        probs * (grad_probs - jnp.sum(probs * grad_probs, axis=-1, keepdims=True))
    ).astype(jnp.bfloat16)
    grad_queries = (
        jnp.einsum("hst,thd->shd", grad_scores, keys_in, preferred_element_type=jnp.float32) * scale
    )
    grad_keys = (
        jnp.einsum("hst,shd->thd", grad_scores, queries, preferred_element_type=jnp.float32) * scale
    )
    return (grad_queries, grad_keys, grad_values)


def run_block(stream, attn_full, mlp_full, gains):
    model_width = stream.shape[2]
    head_width = attn_full.shape[2]
    normed = norm_rows(stream, gains[0], gains[1]).astype(jnp.bfloat16)
    normed_full = gather_rows(normed)
    seq_len = normed_full.shape[0]
    clip_count = normed_full.shape[1]
    weight_in = attn_full[:, 0:3].reshape(model_width, 3 * head_width)
    joined = jnp.einsum(
        "scd,dk->sck", normed_full, weight_in, preferred_element_type=jnp.float32
    ).astype(jnp.bfloat16)
    split_heads = jnp.moveaxis(
        joined.reshape(seq_len, clip_count, 3, head_width // HEAD, HEAD), 1, 0
    )
    context, log_total = lax.map(
        attend_forward, (split_heads[:, :, 0], split_heads[:, :, 1], split_heads[:, :, 2])
    )
    context_rows = jnp.moveaxis(context, 0, 1).reshape(seq_len, clip_count, head_width)
    middle = stream + scatter_rows(context_rows, attn_full[:, 3])
    hidden = norm_rows(middle, gains[2], gains[3]).astype(jnp.bfloat16)
    hidden_full = gather_rows(hidden)
    upward = jnp.einsum(
        "scd,df->scf", hidden_full, mlp_full[:, 0], preferred_element_type=jnp.float32
    )
    active = exact_gelu(upward).astype(jnp.bfloat16)
    result = middle + scatter_rows(active, mlp_full[:, 1])
    return (
        result,
        (
            stream,
            normed_full,
            split_heads,
            log_total,
            context_rows,
            middle,
            hidden_full,
            upward,
            active,
        ),
    )


def back_block(grad_stream, saved, attn_full, mlp_full, gains):
    (
        stream,
        normed_full,
        split_heads,
        log_total,
        context_rows,
        middle,
        hidden_full,
        upward,
        active,
    ) = saved
    model_width = stream.shape[2]
    head_width = attn_full.shape[2]
    seq_len = normed_full.shape[0]
    clip_count = normed_full.shape[1]
    grad_ffn = gather_grads(grad_stream.astype(jnp.bfloat16))
    grad_down = jnp.einsum("scd,scf->df", grad_ffn, active, preferred_element_type=jnp.float32)
    grad_active = jnp.einsum(
        "scd,df->scf", grad_ffn, mlp_full[:, 1], preferred_element_type=jnp.float32
    )
    unused, gelu_pull = jax.vjp(exact_gelu, upward)
    grad_upward = gelu_pull(grad_active)[0].astype(jnp.bfloat16)
    grad_up = jnp.einsum(
        "scd,scf->df", hidden_full, grad_upward, preferred_element_type=jnp.float32
    )
    grad_hidden = scatter_grads(grad_upward, mlp_full[:, 0])
    unused, second_pull = jax.vjp(norm_rows, middle, gains[2], gains[3])
    grad_middle_norm, grad_gain_two, grad_shift_two = second_pull(grad_hidden)
    grad_middle = grad_stream + grad_middle_norm
    grad_attn = gather_grads(grad_middle.astype(jnp.bfloat16))
    grad_outward = jnp.einsum(
        "scd,sck->dk", grad_attn, context_rows, preferred_element_type=jnp.float32
    )
    grad_context = jnp.einsum(
        "scd,dk->sck", grad_attn, attn_full[:, 3], preferred_element_type=jnp.float32
    ).astype(jnp.bfloat16)
    grad_context = jnp.moveaxis(
        grad_context.reshape(seq_len, clip_count, head_width // HEAD, HEAD), 1, 0
    )
    grad_queries, grad_keys, grad_values = lax.map(
        attend_backward,
        (split_heads[:, :, 0], split_heads[:, :, 1], split_heads[:, :, 2], log_total, grad_context),
    )
    grad_joined = jnp.moveaxis(jnp.stack((grad_queries, grad_keys, grad_values), axis=2), 0, 1)
    grad_joined = grad_joined.reshape(seq_len, clip_count, 3 * head_width).astype(jnp.bfloat16)
    weight_in = attn_full[:, 0:3].reshape(model_width, 3 * head_width)
    grad_inward = jnp.einsum(
        "scd,sck->dk", normed_full, grad_joined, preferred_element_type=jnp.float32
    ).reshape(model_width, 3, head_width)
    grad_normed = scatter_grads(grad_joined, weight_in)
    unused, first_pull = jax.vjp(norm_rows, stream, gains[0], gains[1])
    grad_stream_norm, grad_gain_one, grad_shift_one = first_pull(grad_normed)
    attn_grad = jnp.concatenate([grad_inward, grad_outward[:, None]], axis=1)
    mlp_grad = jnp.stack([grad_up, grad_down], axis=1)
    layer_attn, layer_mlp = (
        lax.psum_scatter(attn_grad, DP, scatter_dimension=0, tiled=True),
        lax.psum_scatter(mlp_grad, DP, scatter_dimension=0, tiled=True),
    )
    vector_grads = jnp.stack([grad_gain_one, grad_shift_one, grad_gain_two, grad_shift_two])
    return (grad_middle + grad_stream_norm, layer_attn, layer_mlp, vector_grads)


def direction(weight, grad, first, second):
    bias_one = 1.0 - first_decay**step_count
    bias_two = 1.0 - second_decay**step_count
    first_new = first_decay * first + (1.0 - first_decay) * grad
    second_new = second_decay * second + (1.0 - second_decay) * grad * grad
    update = (
        first_new / bias_one / (jnp.sqrt(second_new / bias_two) + adam_epsilon)
        + weight_decay * weight
    )
    return (first_new, second_new, update)


def matrix_squares(edge_part, attn_part, mlp_part):
    layer_part = jnp.concatenate(
        [jnp.sum(attn_part * attn_part, axis=(1, 3)), jnp.sum(mlp_part * mlp_part, axis=(1, 3))],
        axis=1,
    )
    return jnp.concatenate([jnp.sum(edge_part * edge_part, axis=(1, 2)), layer_part.reshape(-1)])


def per_device_general(
    patches,
    mask,
    edge,
    attn_w,
    mlp_w,
    vecs,
    edge_m,
    edge_v,
    attn_m,
    attn_v,
    mlp_m,
    mlp_v,
    vecs_m,
    vecs_v,
    teacher_edge,
    teacher_attn,
    teacher_mlp,
    teacher_vecs,
):
    layer_count = attn_w.shape[0]
    local_count = patches.shape[0]
    clip_count = patches.shape[1]
    model_width = patches.shape[2]
    last_row = 4 * layer_count
    student_edge, student_vecs = fetch_edges(edge, vecs)
    teach_edge, teach_vecs = fetch_edges(teacher_edge, teacher_vecs)
    seq_total = local_count * lax.axis_size(TENSOR)
    stream = jnp.einsum(
        "scp,pd->scd",
        patches,
        teach_edge[0].astype(jnp.bfloat16),
        preferred_element_type=jnp.float32,
    )
    summed = jnp.zeros_like(stream)
    for layer_index in range(layer_count):
        attn_full, mlp_full = fetch_layer(teacher_attn[layer_index], teacher_mlp[layer_index])
        stream, unused = run_block(
            stream, attn_full, mlp_full, teach_vecs[4 * layer_index : 4 * layer_index + 4]
        )
        first_sum, square_sum = lax.psum(
            (jnp.sum(stream, axis=0), jnp.sum(stream * stream, axis=0)), TENSOR
        )
        average = first_sum / seq_total
        spread = square_sum / seq_total - average * average
        summed = summed + (stream - average) * lax.rsqrt(spread + inst_epsilon)
    target = summed / layer_count
    masked = mask.astype(jnp.float32)[..., None]
    embedded = jnp.einsum(
        "scp,pd->scd",
        patches,
        student_edge[0].astype(jnp.bfloat16),
        preferred_element_type=jnp.float32,
    )
    stream = embedded * (1.0 - masked) + masked * student_vecs[last_row + 2]
    saved_list = []
    weight_list = []
    for layer_index in range(layer_count):
        attn_full, mlp_full = fetch_layer(attn_w[layer_index], mlp_w[layer_index])
        stream, saved = run_block(
            stream, attn_full, mlp_full, student_vecs[4 * layer_index : 4 * layer_index + 4]
        )
        saved_list.append(saved)
        weight_list.append((attn_full, mlp_full))
    final_low = norm_rows(stream, student_vecs[last_row], student_vecs[last_row + 1]).astype(
        jnp.bfloat16
    )
    head_low = student_edge[1].astype(jnp.bfloat16)
    predicted = (
        jnp.einsum("scd,de->sce", final_low, head_low, preferred_element_type=jnp.float32)
        + student_vecs[last_row + 3]
    )
    offset = predicted - target
    size_abs = jnp.abs(offset)
    loss_part = (
        jnp.sum(jnp.where(size_abs < 1.0, 0.5 * offset * offset, size_abs - 0.5) * masked)
        / model_width**0.5
    )
    grad_pred = jnp.clip(offset, -1.0, 1.0) * masked / model_width**0.5
    grad_low = grad_pred.astype(jnp.bfloat16)
    grad_head = jnp.einsum("scd,sce->de", final_low, grad_low, preferred_element_type=jnp.float32)
    grad_bias = jnp.sum(grad_pred, axis=(0, 1))
    grad_final = jnp.einsum("sce,de->scd", grad_low, head_low, preferred_element_type=jnp.float32)
    unused, final_pull = jax.vjp(
        norm_rows, stream, student_vecs[last_row], student_vecs[last_row + 1]
    )
    grad_stream, grad_final_gain, grad_final_shift = final_pull(grad_final)
    attn_grads = []
    mlp_grads = []
    vector_rows = []
    for layer_index in reversed(range(layer_count)):
        attn_full, mlp_full = fetch_again(attn_w[layer_index], mlp_w[layer_index])
        grad_stream, layer_attn, layer_mlp, vector_grads = back_block(
            grad_stream,
            saved_list[layer_index],
            attn_full,
            mlp_full,
            student_vecs[4 * layer_index : 4 * layer_index + 4],
        )
        attn_grads.insert(0, layer_attn)
        mlp_grads.insert(0, layer_mlp)
        vector_rows.insert(0, vector_grads)
    grad_embed = (grad_stream * (1.0 - masked)).astype(jnp.bfloat16)
    grad_mask_vec = jnp.sum(grad_stream * masked, axis=(0, 1))
    grad_patch = jnp.einsum("scp,scd->pd", patches, grad_embed, preferred_element_type=jnp.float32)
    vector_grad = jnp.concatenate(
        vector_rows + [jnp.stack([grad_final_gain, grad_final_shift, grad_mask_vec, grad_bias])],
        axis=0,
    )
    edge_grad, vecs_grad = (
        lax.psum_scatter(
            jnp.stack([grad_patch, grad_head]), (DP, TENSOR), scatter_dimension=1, tiled=True
        ),
        lax.psum_scatter(vector_grad, (DP, TENSOR), scatter_dimension=1, tiled=True),
    )
    attn_grad = jnp.stack(attn_grads)
    mlp_grad = jnp.stack(mlp_grads)
    edge_first, edge_second, edge_update = direction(edge, edge_grad, edge_m, edge_v)
    attn_first, attn_second, attn_update = direction(attn_w, attn_grad, attn_m, attn_v)
    mlp_first, mlp_second, mlp_update = direction(mlp_w, mlp_grad, mlp_m, mlp_v)
    vecs_first, vecs_second, vecs_update = direction(vecs, vecs_grad, vecs_m, vecs_v)
    weight_sq, update_sq, loss_total = lax.psum(
        (
            matrix_squares(edge, attn_w, mlp_w),
            matrix_squares(edge_update, attn_update, mlp_update),
            loss_part,
        ),
        (DP, TENSOR),
    )
    weight_norm = jnp.sqrt(weight_sq)
    update_norm = jnp.sqrt(update_sq)
    trust = weight_norm / (update_norm + adam_epsilon)
    edge_trust = trust[0:2]
    layer_trust = trust[2:].reshape(layer_count, 6)
    new_edge = edge - learn_rate * edge_trust[:, None, None] * edge_update
    new_attn = attn_w - learn_rate * layer_trust[:, None, 0:4, None] * attn_update
    new_mlp = mlp_w - learn_rate * layer_trust[:, None, 4:6, None] * mlp_update
    new_vecs = vecs - learn_rate * vecs_update
    keep_share = 1.0 - teacher_decay
    token_total = seq_total * clip_count * lax.axis_size(DP)
    return (
        loss_total / token_total,
        jnp.stack([weight_norm, update_norm]),
        new_edge,
        new_attn,
        new_mlp,
        new_vecs,
        edge_first,
        edge_second[0],
        edge_second[1],
        attn_first,
        attn_second[:, :, 0:3],
        attn_second[:, :, 3],
        mlp_first,
        mlp_second,
        vecs_first,
        vecs_second,
        keep_share * (new_edge - teacher_edge),
        keep_share * (new_attn - teacher_attn),
        keep_share * (new_mlp - teacher_mlp),
        keep_share * (new_vecs - teacher_vecs),
        new_edge.astype(jnp.bfloat16),
        new_attn.astype(jnp.bfloat16),
        new_mlp.astype(jnp.bfloat16),
        new_vecs.astype(jnp.bfloat16),
    )


MESH = pl.DeviceIdType.MESH
ORDERS = (("z", "x", "y"), ("x", "y", "z"), ("y", "z", "x"))
LOW = jnp.bfloat16
ALL = slice(None)


def coords():
    d = lax.axis_index(DP)
    t = lax.axis_index(TENSOR)
    return dict(a=t // 2, z=t % 2, y=d // 4, x=(d // 2) % 2, c=d % 2)


def ident(co):
    return (co["y"] * 4 + co["x"] * 2 + co["c"], co["a"] * 2 + co["z"])


def flip(co, k):
    co = dict(co)
    co[k] = 1 - co[k]
    return ident(co)


def place(co, full, rows):
    return tuple(ALL if k in full else co[k] for k in "azyxc") + (rows,)


ANY = pl.BlockSpec(memory_space=pl.ANY)
DMA = pltpu.SemaphoreType.DMA


def shape_of(shape, kind=LOW):
    return jax.ShapeDtypeStruct(shape, kind)


def dot(left, right):
    return jnp.dot(left, right, preferred_element_type=jnp.float32)


def dot_nt(left, right):
    return lax.dot_general(
        left, right, (((1,), (1,)), ((), ())), preferred_element_type=jnp.float32
    )


def dot_tn(left, right):
    return lax.dot_general(
        left, right, (((0,), (0,)), ((), ())), preferred_element_type=jnp.float32
    )


def pack_heads(block):
    q, k, v, o = (block[..., i, :] for i in range(4))
    two = 2 * HEAD
    pieces = [q[..., :two], k[..., :two], v[..., :two], q[..., two:], v[..., two:], k[..., two:]]
    pieces += [o[..., HEAD:two], o[..., :HEAD], o[..., two:]]
    return jnp.concatenate(pieces, axis=-1)


def unpack_heads(packed):
    cut = lambda *spots: jnp.concatenate(
        [packed[..., HEAD * a : HEAD * b] for a, b in spots], axis=-1
    )
    kinds = [cut((0, 2), (6, 7)), cut((2, 4), (8, 9)), cut((4, 6), (7, 8))]
    kinds.append(cut((10, 11), (9, 10), (11, 12)))
    return jnp.stack(kinds, axis=-2)


def norm_block(values, gain, shift):
    average = jnp.mean(values, axis=-1, keepdims=True)
    centered = values - average
    spread = jnp.mean(centered * centered, axis=-1, keepdims=True)
    return centered * lax.rsqrt(spread + norm_epsilon) * gain + shift


def matrix(value):
    return value.reshape(-1, value.shape[-1])


def low_lanes(shape):
    return lax.broadcasted_iota(jnp.int32, shape, len(shape) - 1) % 128 < HEAD


def forward_kernel(*refs):
    (attn_mine, attn_other, mlp_mine, mlp_other, edge_mine, edge_other) = refs[:6]
    vec_mine, vec_other, patch = refs[6:9]
    (o_attn, o_mlp, o_head, o_vec, o_x, o_mid, o_normed, o_qkv, o_peer, o_ctx) = refs[9:19]
    (o_hid, o_act, o_slope, o_lse, o_last, o_final, o_pixels, o_dlow, o_sums, o_mask) = refs[19:29]
    (w_attn, w_mlp, w_edge, w_vec, pixels, embed_w, head_w, gains, x, mid) = refs[29:39]
    (normed, qkv, peer, ctx, hid, act, slope, lse, work, target, stat, sums, turned) = refs[39:52]
    early, final_stat = refs[52:54]
    local_sem, send_sem, recv_sem, patch_sem, peer_sem, stat_sem, save_sem, core_sem = refs[54:]
    co = coords()
    me = ident(co)
    column = co["y"] * 2 + co["x"]
    teaching = co["a"] == 1
    rows_here = x.shape[0]
    width = x.shape[1]
    layers = attn_mine.shape[0]
    last_row = 4 * layers
    barrier = pltpu.get_barrier_semaphore()
    for k in range(1, 8):
        to = (column * 2 + (co["c"] + k // 4) % 2, (me[1] + k % 4) % 4)
        pl.semaphore_signal(barrier, inc=1, device_id=to, device_id_type=MESH)
    for k in "xy":
        pl.semaphore_signal(barrier, inc=1, device_id=flip(co, k), device_id_type=MESH)
    pl.semaphore_wait(barrier, 9)

    items = [(edge_mine, edge_other, w_edge, 0), (vec_mine, vec_other, w_vec, 0)]
    for l in range(layers):
        items.append((attn_mine.at[l], attn_other.at[l], w_attn.at[l], 3 * l + 1))
        for k in range(2):
            items.append(
                (mlp_mine.at[l, k], mlp_other.at[l, k], w_mlp.at[l, k], 3 * l + 2 + k)
            )
    sent = []
    table = {}

    def remote(source, to_ref, i, j, k, to):
        copy = pltpu.make_async_remote_copy(
            src_ref=source,
            dst_ref=to_ref,
            send_sem=send_sem.at[i, j, k],
            recv_sem=recv_sem.at[i, j, k],
            device_id=to,
            device_id_type=MESH,
        )
        copy.start()
        sent.append(copy)
        return copy

    def begin(slot):
        for i, (mine, other, full, at) in enumerate(items):
            if at == slot:
                spot = full.at[place(co, "", ALL)]
                copy = pltpu.make_async_copy(mine, spot, local_sem.at[i])
                copy.start()
                table[i, -1] = (copy, remote(other, spot, i, 0, 4, flip(co, "a")))

    def step(wave, s):
        for i, (mine, other, full, at) in enumerate(items):
            if wave - at != s:
                continue
            if s == 0:
                table[i, -1][0].wait()
                table[i, -1][1].wait_recv()
            size = mine.shape[0] // 3
            copies = []
            for p in range(3):
                if s > 0:
                    table[i, s - 1][p].wait_recv()
                if s < 4:
                    order = ORDERS[p] + ("c",)
                    full_dims = ("a",) + order[:s]
                    ref = full.at[place(co, full_dims, pl.ds(p * size, size))]
                    copies.append(remote(ref, ref, i, p, s, flip(co, order[s])))
            table[i, s] = copies

    saves = {}
    counter = iter(range(48))

    def save(name, source, to_ref):
        copy = pltpu.make_async_copy(source, to_ref, save_sem.at[next(counter)])
        copy.start()
        saves[name] = copy

    shared = {}
    core_counter = iter(range(16))
    own_rows, peer_rows = pl.ds(0, rows_here), pl.ds(rows_here, rows_here)

    def to_core(name, source, to_ref):
        n = next(core_counter)
        shared[name] = pltpu.make_async_remote_copy(
            src_ref=source,
            dst_ref=to_ref,
            send_sem=core_sem.at[0, n],
            recv_sem=core_sem.at[1, n],
            device_id=flip(co, "c"),
            device_id_type=MESH,
        )
        shared[name].start()

    def share(name, source, to_ref, lead):
        save(name, source, to_ref.at[lead + (own_rows,)])
        to_core(name, source, to_ref.at[lead + (peer_rows,)])

    turns = []

    def turn(name, columns, to_ref):
        spot = turned.at[len(turns) % 2]
        if len(turns) >= 2:
            wait_saves(turns[-2])
        turns.append(name)
        for n in range(2):
            spot[n] = jnp.transpose(columns(n)).astype(LOW).reshape(spot.shape[1:])
        save(name, spot.at[:, :, co["c"]], to_ref.at[:, :, :, own_rows])
        to_core(name, spot.at[:, :, 1 - co["c"]], to_ref.at[:, :, :, peer_rows])

    def columns_of(ref):
        return lambda n: ref[:, n * rows_here : (n + 1) * rows_here].astype(jnp.float32)

    def by_rows(size, body):
        def run(n, _):
            body(pl.ds(pl.multiple_of(n * size, size), size))
            return 0

        lax.fori_loop(0, rows_here // size, run, 0)

    def gain(row):
        return gains[row : row + 1, :]

    def norm_into(source, out, row):
        def body(span):
            out[span, :] = norm_block(source[span, :], gain(row), gain(row + 1)).astype(LOW)

        by_rows(64, body)

    def embed():
        owned = [
            w_vec[t // 2, t % 2, d // 4, d // 2 % 2, d % 2] for d in range(8) for t in range(4)
        ]
        gains[...] = jnp.transpose(jnp.concatenate(owned))[: gains.shape[0]]
        save("vec", gains, o_vec)
        half = edge_mine.shape[0] // 2
        for d in range(8):
            for a in range(2):
                at = (d // 4, d // 2 % 2, d % 2)
                left = w_edge[(a, 0) + at].astype(jnp.float32)
                right = w_edge[(a, 1) + at].astype(jnp.float32)
                spot = pl.ds((2 * d + a) * 2 * half, 2 * half)
                embed_w[spot, :] = jnp.concatenate([left[:half], right[:half]]).astype(LOW)
                head_w[spot, :] = jnp.concatenate([left[half:], right[half:]]).astype(LOW)
        save("head", head_w, o_head)
        for q in range(2):
            origin = (column * 2 + co["z"], co["c"] * 2 + q)
            same = jnp.logical_and(origin[0] == me[0], origin[1] == me[1])

            @pl.when(same)
            def _():
                pltpu.make_async_copy(patch, pixels.at[q], patch_sem.at[2]).wait()

            @pl.when(jnp.logical_not(same))
            def _():
                pltpu.make_async_remote_copy(
                    src_ref=patch,
                    dst_ref=pixels.at[q],
                    send_sem=patch_sem.at[3],
                    recv_sem=patch_sem.at[q],
                    device_id=me,
                    device_id_type=MESH,
                ).wait_recv()

        save("mask", pixels.at[:, :, width:], o_mask)
        quarter = pixels.shape[1]

        def pixel_columns(n):
            cols = pixels[:, :, n * rows_here : (n + 1) * rows_here].astype(jnp.float32)
            return cols.reshape(rows_here, rows_here)

        turn("pixels", pixel_columns, o_pixels)
        for q in range(2):
            hide = pixels[q, :, width : width + 1].astype(jnp.float32)
            hide = jnp.where(teaching, 0.0, hide)
            rows = pl.ds(q * quarter, quarter)
            x[rows, :] = (
                dot(pixels[q, :, :width], embed_w[...]) * (1.0 - hide) + hide * gain(last_row + 2)
            )

    def peer_copy(l, t):
        return pltpu.make_async_remote_copy(
            src_ref=qkv.at[t, :, 128:640],
            dst_ref=peer.at[l, t],
            send_sem=peer_sem.at[0, l, t],
            recv_sem=peer_sem.at[1, l, t],
            device_id=flip(co, "c"),
            device_id_type=MESH,
        )

    settled = []

    def wait_saves(*names):
        for name in names:
            if name in saves:
                saves.pop(name).wait()
                if name in shared:
                    shared[name].wait_send()
                    settled.append(shared.pop(name))

    def project(l):
        save(("x", l), x, o_x.at[l])
        norm_into(x, normed, 4 * l)
        for t in range(4):
            weight = matrix(w_attn[l, t // 2, t % 2])
            qkv[t] = dot(normed[...], weight).astype(LOW)
            peer_copy(l, t).start()
            save(("qkv", l, t), qkv.at[t], o_qkv.at[l, t])
        turn(("normed", l), columns_of(normed), o_normed.at[l])

    def attend(l, first, last):
        if first == 0:
            for t in range(4):
                peer_copy(l, t).wait_recv()
            lse[...] = jnp.zeros_like(lse)
        size = rows_here

        def body(n, _):
            t = n // (rows_here // size)
            span = pl.ds(pl.multiple_of(n % (rows_here // size) * size, size), size)
            low = low_lanes((size, 128))
            lane = lax.broadcasted_iota(jnp.int32, (size, 128), 1)
            zero = jnp.zeros((size, 128), LOW)
            outs = []
            total = lse[span, :]
            for j in range(3):
                q_at = 0 if j < 2 else 384
                k_at = 128 if j < 2 else 512
                v_at = 256 if j < 2 else 384
                query = qkv[t, span, q_at : q_at + 128] * jnp.asarray(HEAD**-0.5, LOW)
                query = jnp.where(low, query, zero) if j != 1 else jnp.where(low, zero, query)
                scores = jnp.concatenate(
                    [
                        dot_nt(query, qkv[t, :, k_at : k_at + 128]),
                        dot_nt(query, peer[l, t, :, k_at - 128 : k_at]),
                    ],
                    axis=1,
                )
                peak = jnp.max(scores, axis=1, keepdims=True)
                raised = jnp.exp(scores - peak)
                summed = jnp.sum(raised, axis=1, keepdims=True)
                weights = raised.astype(LOW)
                out = dot(weights[:, :rows_here], qkv[t, :, v_at : v_at + 128])
                out = out + dot(weights[:, rows_here:], peer[l, t, :, v_at - 128 : v_at])
                outs.append(out / summed)
                total = jnp.where(lane == 3 * t + j, peak + jnp.log(summed), total)
            lse[span, :] = total
            ctx[t, span, :128] = jnp.where(low, 0.0, outs[1]).astype(LOW)
            ctx[t, span, 128:] = jnp.where(low, outs[0], outs[2]).astype(LOW)
            return 0

        each = rows_here // size
        lax.fori_loop(first * each, last * each, body, 0)
        if last == 4:
            save(("lse", l), lse, o_lse.at[l])
            share(("ctx", l), ctx, o_ctx.at[l], (ALL,))
            save(("peer", l), peer.at[l], o_peer.at[l])

    def out_project(l):
        mid[...] = x[...]

        def body(t, _):
            weight = matrix(w_attn[l, t // 2, t % 2, :, :, :, :, 512:])
            mid[...] += dot_nt(ctx[t], weight)
            return 0

        lax.fori_loop(0, 4, body, 0)
        save(("mid", l), mid, o_mid.at[l])
        norm_into(mid, hid, 4 * l + 2)
        turn(("hid", l), columns_of(hid), o_hid.at[l])

    def expand(l, first, last):
        def body(n, _):
            t = n // 3
            cols = pl.ds(pl.multiple_of(n % 3 * 256, 256), 256)
            weight = matrix(w_mlp[l, 0, t // 2, t % 2, :, :, :, :, cols])
            upward = dot(hid[...], weight)
            share = 0.5 + 0.5 * lax.erf(upward * 0.5**0.5)
            act[t, :, cols] = (upward * share).astype(LOW)
            bell = jnp.exp(-0.5 * upward * upward) * (2.0 * jnp.pi) ** -0.5
            slope[t, :, cols] = (share + upward * bell).astype(LOW)
            return 0

        lax.fori_loop(3 * first, 3 * last, body, 0)
        if last == 4:
            share(("act", l), act, o_act.at[l], (ALL,))
            save(("slope", l), slope, o_slope.at[l])

    def contract(l, first, last):
        if first == 0:
            if l < layers - 1:
                wait_saves(("x", l))
            x[...] = mid[...]

        def body(t, _):
            x[...] += dot_nt(act[t], matrix(w_mlp[l, 1, t // 2, t % 2]))
            return 0

        lax.fori_loop(first, last, body, 0)

    def stat_copy(l):
        return pltpu.make_async_remote_copy(
            src_ref=stat.at[l, 0],
            dst_ref=stat.at[l, 1],
            send_sem=stat_sem.at[0, l],
            recv_sem=stat_sem.at[1, l],
            device_id=flip(co, "c"),
            device_id_type=MESH,
        )

    def to_student(n, source, to_ref):
        return pltpu.make_async_remote_copy(
            src_ref=source,
            dst_ref=to_ref,
            send_sem=stat_sem.at[0, layers + n],
            recv_sem=stat_sem.at[1, layers + n],
            device_id=flip(co, "a"),
            device_id_type=MESH,
        )

    spans = [pl.ds(n * (rows_here // 2), rows_here // 2) for n in range(2)]

    def target_copies():
        copies = [to_student(n, target.at[span], target.at[span]) for n, span in enumerate(spans)]
        return copies + [to_student(2, early, early), to_student(3, final_stat, final_stat)]

    def column_sums(ref, spot):
        spot[...] = jnp.zeros_like(spot)

        def body(span):
            value = ref[span, :]
            spot[0:1] += jnp.sum(value, axis=0, keepdims=True)
            spot[1:2] += jnp.sum(value * value, axis=0, keepdims=True)

        by_rows(64, body)

    def normalizer(l):
        stat_copy(l).start()
        stat_copy(l).wait()
        both = (stat[l, 0] + stat[l, 1]) / (2 * rows_here)
        average = both[0:1]
        spread = both[1:2] - average * average
        return average, lax.rsqrt(spread + inst_epsilon) / layers

    def teach(l):
        @pl.when(teaching)
        def _():
            column_sums(x, stat.at[l, 0])
            average, scale = normalizer(l)

            def mix(span):
                value = (x[span, :] - average) * scale
                if l > 0:
                    value = value + work[span, :]
                work[span, :] = value
                if l == layers - 2:
                    early[span, :] = value.astype(LOW)

            by_rows(64, mix)
            if l == layers - 2:
                target_copies()[2].start()

    def center_last():
        @pl.when(teaching)
        def _():
            column_sums(mid, final_stat)
            final_stat[2:3] = final_stat[0:1] / rows_here

    def contract_last():
        l = layers - 1

        @pl.when(teaching)
        def _():
            center = final_stat[2:3]
            for n, span in enumerate(spans):
                value = mid[span, :]
                for t in range(4):
                    value = value + dot_nt(act[t, span], matrix(w_mlp[l, 1, t // 2, t % 2]))
                x[span, :] = value
                target[span, :] = (value - center).astype(LOW)
                target_copies()[n].start()
            column_sums(x, stat.at[l, 0])
            average, scale = normalizer(l)
            final_stat[0:1] = scale
            final_stat[1:2] = (center - average) * scale
            copies = target_copies()
            copies[3].start()
            for copy in copies:
                copy.wait_send()

        @pl.when(jnp.logical_not(teaching))
        def _():
            contract(l, 0, 4)

    def finish():
        save("last", x, o_last)
        sums[...] = jnp.zeros_like(sums)
        norm_into(x, normed, last_row)
        turn("final", columns_of(normed), o_final)

        @pl.when(jnp.logical_not(teaching))
        def _():
            work[...] = dot(normed[...], head_w[...]) + gain(last_row + 3)
            copies = target_copies()
            copies[2].wait_recv()

            def add_early(span):
                work[span, :] = work[span, :] - early[span, :].astype(jnp.float32)

            by_rows(64, add_early)
            copies[0].wait_recv()
            copies[1].wait_recv()
            copies[3].wait_recv()

            def body(n, _):
                span = pl.ds(pl.multiple_of(n * 64, 64), 64)
                part = pl.ds(pl.multiple_of(n % 3 * 64, 64), 64)
                masked = pixels[n // 3, part, width : width + 1].astype(jnp.float32)
                aim = target[span, :].astype(jnp.float32) * final_stat[0:1] + final_stat[1:2]
                offset = work[span, :] - aim
                size = jnp.abs(offset)
                loss = jnp.where(size < 1.0, 0.5 * offset * offset, size - 0.5) * masked
                pull = jnp.clip(offset, -1.0, 1.0) * masked * width**-0.5
                sums[0:1] += jnp.sum(pull, axis=0, keepdims=True)
                sums[1:2] += jnp.sum(loss, axis=0, keepdims=True)
                target[span, :] = pull.astype(LOW)
                return 0

            lax.fori_loop(0, rows_here // 64, body, 0)

        share("dlow", target, o_dlow, ())
        save("sums", sums, o_sums)

    for r in range(2):
        to = (column * 2 + co["a"], 2 * r + co["c"])
        same = jnp.logical_and(to[0] == me[0], to[1] == me[1])
        spot = pixels.at[co["z"]]

        @pl.when(same)
        def _():
            pltpu.make_async_copy(patch, spot, patch_sem.at[2]).start()

        @pl.when(jnp.logical_not(same))
        def _():
            pltpu.make_async_remote_copy(
                src_ref=patch,
                dst_ref=spot,
                send_sem=patch_sem.at[3 + r],
                recv_sem=patch_sem.at[co["z"]],
                device_id=to,
                device_id_type=MESH,
            ).start()

    def save_weights(slot):
        def run():
            l, k = (slot - 1) // 3, (slot - 1) % 3
            if k == 0:
                save(("attn", l), w_attn.at[l], o_attn.at[l])
            else:
                save(("mlp", l, k), w_mlp.at[l, k - 1], o_mlp.at[l, k - 1])

        return run

    plan = {0: [embed]}
    for l in range(layers):
        repeat = l > 0

        def start(l=l):
            if l > 0:
                for t in range(4):
                    peer_copy(l - 1, t).wait_send()
                wait_saves(*[("qkv", l - 1, t) for t in range(4)])
            project(l)

        def begin_attend(l=l):
            if l > 0:
                wait_saves(("lse", l - 1), ("ctx", l - 1))
            attend(l, 0, 2)

        def begin_out(l=l):
            if l > 0:
                wait_saves(("mid", l - 1))
            out_project(l)

        def begin_expand(l=l):
            if l > 0:
                wait_saves(("act", l - 1), ("slope", l - 1))
            expand(l, 0, 2)

        plan[3 * l + 1] = [
            save_weights(3 * l + 1),
            start,
            begin_attend,
            lambda l=l: attend(l, 2, 4),
            begin_out,
        ]
        plan[3 * l + 2] = [
            save_weights(3 * l + 2),
            begin_expand,
            lambda l=l: expand(l, 2, 4),
        ]
        plan[3 * l + 3] = [
            save_weights(3 * l + 3),
            lambda l=l: contract(l, 0, 2),
            lambda l=l: contract(l, 2, 4),
            lambda l=l: teach(l),
        ]
    plan[3 * layers - 1].append(center_last)
    wait_last = lambda: wait_saves(("x", layers - 1))
    plan[3 * layers] = [wait_last, contract_last, save_weights(3 * layers)]
    final_slot = 3 * layers
    begin(0)
    begin(1)
    for wave in range(final_slot + 5):
        begin(wave + 2)
        step(wave, 4)
        todo = list(plan.get(wave - 4, []))
        for s in range(4):
            step(wave, s)
            if todo:
                todo.pop(0)()
        while todo:
            todo.pop(0)()
    finish()
    wait_saves(*list(saves))
    for copy in settled:
        copy.wait_recv()
    for t in range(4):
        peer_copy(layers - 1, t).wait_send()
    for r in range(2):
        to = (column * 2 + co["a"], 2 * r + co["c"])
        same = jnp.logical_and(to[0] == me[0], to[1] == me[1])

        @pl.when(jnp.logical_not(same))
        def _():
            pltpu.make_async_remote_copy(
                src_ref=patch,
                dst_ref=pixels.at[0],
                send_sem=patch_sem.at[3 + r],
                recv_sem=patch_sem.at[0],
                device_id=me,
                device_id_type=MESH,
            ).wait_send()

    for copy in sent:
        copy.wait_send()


def forward_all(*parts):
    layers, rows, width = parts[0].shape
    cube = (2, 2, 2, 2, 2)
    here = 2 * parts[8].shape[0]
    f32 = jnp.float32
    attn = (layers,) + cube + (rows, width)
    mlp = (layers, 2) + cube + (rows, width)
    tall = (here, width)
    turned = (2, 2, rows, 2 * here)
    quarter = parts[8].shape[0]
    outs = (
        shape_of(attn),
        shape_of(mlp),
        shape_of((width, width)),
        shape_of((16, width), f32),
        shape_of((layers,) + tall, f32),
        shape_of((layers,) + tall, f32),
        shape_of((layers,) + turned),
        shape_of((layers, 4) + tall),
        shape_of((layers, 4, here, 512)),
        shape_of((layers, 4, 2 * here, 256)),
        shape_of((layers,) + turned),
        shape_of((layers, 4, 2 * here, width)),
        shape_of((layers, 4) + tall),
        shape_of((layers, here, 128), f32),
        shape_of(tall, f32),
        shape_of(turned),
        shape_of(turned),
        shape_of((2 * here, width)),
        shape_of((8, width), f32),
        shape_of((2, quarter, 128)),
    )
    scratch = [
        pltpu.VMEM(attn, LOW),
        pltpu.VMEM(mlp, LOW),
        pltpu.VMEM(cube + parts[4].shape, LOW),
        pltpu.VMEM(cube + parts[6].shape, f32),
        pltpu.VMEM((2,) + parts[8].shape, LOW),
        pltpu.VMEM((width, width), LOW),
        pltpu.VMEM((width, width), LOW),
        pltpu.VMEM((16, width), f32),
        pltpu.VMEM(tall, f32),
        pltpu.VMEM(tall, f32),
        pltpu.VMEM(tall, LOW),
        pltpu.VMEM((4,) + tall, LOW),
        pltpu.VMEM((layers, 4, here, 512), LOW),
        pltpu.VMEM((4, here, 256), LOW),
        pltpu.VMEM(tall, LOW),
        pltpu.VMEM((4,) + tall, LOW),
        pltpu.VMEM((4,) + tall, LOW),
        pltpu.VMEM((here, 128), f32),
        pltpu.VMEM(tall, f32),
        pltpu.VMEM(tall, LOW),
        pltpu.VMEM((layers, 2, 8, width), f32),
        pltpu.VMEM((8, width), f32),
        pltpu.VMEM((2, 2, 2, 2, rows, here), LOW),
        pltpu.VMEM(tall, LOW),
        pltpu.VMEM((8, width), f32),
    ]
    count = 2 + 3 * layers
    sems = [
        DMA((count,)),
        DMA((count, 3, 5)),
        DMA((count, 3, 5)),
        DMA((5,)),
        DMA((2, layers, 4)),
        DMA((2, layers + 4)),
        DMA((48,)),
        DMA((2, 16)),
    ]
    return pl.pallas_call(
        forward_kernel,
        out_shape=outs,
        in_specs=[ANY] * 9,
        out_specs=(ANY,) * len(outs),
        scratch_shapes=scratch + sems,
        compiler_params=pltpu.CompilerParams(
            collective_id=0, has_side_effects=True, vmem_limit_bytes=60 * 2**20
        ),
    )(*parts)


def backward_kernel(*refs):
    (w_attn, w_mlp, h_head, h_gains, h_x, h_mid, h_normed, h_qkv, h_peer, h_ctx) = refs[:10]
    (h_hid, h_act, h_slope, h_lse, h_last, h_final, h_pixels, h_dlow, h_sums, h_mask) = refs[10:20]
    o_attn, o_mlp, o_head, o_patch, o_vec = refs[20:25]
    (head, gains, x, normed_t, hid_t, qkv, peer, ctx, lse, attn, act) = refs[25:36]
    (down, up, slope, tall_t, tall, mask, sums, g, acc, low_g, turned, dffn_t) = refs[36:48]
    (datt_t, dup, dctx, dqkv, dkv_out, dkv_in, query, pull, score_row, vec_grad) = refs[48:58]
    vec_turned = refs[58]
    rest = refs[59:]
    co = coords()
    layers = w_attn.shape[0]
    last_row = 4 * layers
    here, width = g.shape
    other_core = flip(co, "c")
    own_rows, peer_rows = pl.ds(0, here), pl.ds(here, here)
    barrier = pltpu.get_barrier_semaphore()
    for k in "azyxc":
        pl.semaphore_signal(barrier, inc=1, device_id=flip(co, k), device_id_type=MESH)
    pl.semaphore_wait(barrier, 5)

    kinds = {}
    spot = 0
    for name, parts in (("D", 3), ("U", 3), ("A", 3), ("H", 2), ("P", 2), ("V", 3)):
        kinds[name] = dict(mine=rest[spot], part=[], parts=parts, name=name)
        spot += 1
        for p in range(parts):
            kinds[name]["part"].append(rest[spot : spot + 3])
            spot += 3
    items = {}
    targets = [("H", 0, o_head)]
    for l in reversed(range(layers)):
        targets += [("D", l, o_mlp.at[l, 1]), ("U", l, o_mlp.at[l, 0]), ("A", l, o_attn.at[l])]
    targets += [("P", 0, o_patch), ("V", 0, o_vec)]
    for n, (name, l, target) in enumerate(targets):
        items[name, l] = dict(kinds[name], n=n, l=l, target=target, last=rest[spot], sent=[])
        spot += 1
    load_sem, send_sem, recv_sem, out_sem, core_sem, credit = rest[spot:]
    own = {q: co[q] for q in "zyx"}

    def pick(fixed, span):
        return tuple(fixed.get(k, ALL) for k in "azyx") + (span,)

    def span_of(item, p):
        size = item["mine"].shape[4] // item["parts"]
        return pl.ds(p * size, size)

    def part_copy(item, p, s):
        order = ORDERS[p][::-1]
        k = order[s]
        fixed = {q: co[q] for q in order[:s]}
        return pltpu.make_async_remote_copy(
            src_ref=item["mine"].at[pick({**fixed, k: 1 - co[k]}, span_of(item, p))],
            dst_ref=item["part"][p][s].at[pick({q: 0 for q in order[: s + 1]}, ALL)],
            send_sem=send_sem.at[item["n"], p, s],
            recv_sem=recv_sem.at[item["n"], p, s],
            device_id=flip(co, k),
            device_id_type=MESH,
        )

    def last_hop(item):
        return pltpu.make_async_remote_copy(
            src_ref=item["mine"].at[pick({**own, "a": 1}, ALL)],
            dst_ref=item["last"],
            send_sem=send_sem.at[item["n"], 0, 3],
            recv_sem=recv_sem.at[item["n"], 0, 3],
            device_id=flip(co, "a"),
            device_id_type=MESH,
        )

    def out_copy(item):
        return pltpu.make_async_copy(
            item["mine"].at[pick({**own, "a": 0}, ALL)], item["target"], out_sem.at[item["n"]]
        )

    def begin(item, s):
        if s == 0 and item["name"] in "DUA" and item["l"] < layers - 1:
            for q in range(3):
                pl.semaphore_wait(credit.at["DUA".index(item["name"]), q], 1)
        for p in range(item["parts"]):
            copy = part_copy(item, p, s)
            copy.start()
            item["sent"].append(copy)

    def gather_in(item, s):
        for p in range(item["parts"]):
            part_copy(item, p, s).wait_recv()
            done = ORDERS[p][::-1][: s + 1]
            left = [k for k in "azyx" if k not in done]
            mine, part, span = item["mine"], item["part"][p][s], span_of(item, p)

            def body(n, _):
                at = {}
                for k in reversed(left):
                    at[k] = n % 2
                    n = n // 2
                there = tuple(0 if k in done else at[k] for k in "azyx")
                spot = tuple(co[k] if k in done else at[k] for k in "azyx") + (span,)
                mine[spot] = mine[spot] + part[there]
                return 0

            lax.fori_loop(0, 2 ** len(left), body, 0)

    def advance(name, l, s):
        item = items[name, l]
        gather_in(item, s)
        if s < 2:
            begin(item, s + 1)
            return
        if name in "DUA" and l > 0:
            for q, k in enumerate("zyx"):
                pl.semaphore_signal(
                    credit.at["DUA".index(name), q],
                    inc=1,
                    device_id=flip(co, k),
                    device_id_type=MESH,
                )
        last_hop(item).start()
        out_copy(item).start()

    def settle(name, l):
        item = items[name, l]
        for copy in item["sent"]:
            copy.wait_send()
        last_hop(item).wait_send()
        out_copy(item).wait()

    loads = {}
    counter = iter(range(96))

    def fetch(name, source, to_ref):
        loads[name] = pltpu.make_async_copy(source, to_ref, load_sem.at[next(counter)])
        loads[name].start()

    def need(*names):
        for name in names:
            loads.pop(name).wait()

    core_counter = iter(range(48))
    core = {}

    def to_core(name, source, to_ref):
        n = next(core_counter)
        core[name] = pltpu.make_async_remote_copy(
            src_ref=source,
            dst_ref=to_ref,
            send_sem=core_sem.at[0, n],
            recv_sem=core_sem.at[1, n],
            device_id=other_core,
            device_id_type=MESH,
        )
        core[name].start()

    def by_rows(size, body):
        def run(n, _):
            body(pl.ds(pl.multiple_of(n * size, size), size))
            return 0

        lax.fori_loop(0, here // size, run, 0)

    def turn(name, source, to_ref):
        for n in range(2):
            cols = source[:, n * here : (n + 1) * here].astype(jnp.float32)
            turned[n] = jnp.transpose(cols).astype(LOW).reshape(turned.shape[1:])
        to_ref[:, :, :, :here] = turned[:, :, co["c"]]
        to_core(name, turned.at[:, :, 1 - co["c"]], to_ref.at[:, :, :, here:])

    def norm_back(values, row):
        gain = gains[row : row + 1, :]

        def body(span):
            value = values[span, :]
            average = jnp.mean(value, axis=-1, keepdims=True)
            centered = value - average
            spread = jnp.mean(centered * centered, axis=-1, keepdims=True)
            scale = lax.rsqrt(spread + norm_epsilon)
            hat = centered * scale
            dy = acc[span, :]
            vec_grad[row : row + 1, :] += jnp.sum(dy * hat, axis=0, keepdims=True)
            vec_grad[row + 1 : row + 2, :] += jnp.sum(dy, axis=0, keepdims=True)
            u = dy * gain
            mean_u = jnp.mean(u, axis=-1, keepdims=True)
            mean_uh = jnp.mean(u * hat, axis=-1, keepdims=True)
            g[span, :] += scale * (u - mean_u - hat * mean_uh)

        by_rows(64, body)

    def attend_back(t):
        low = low_lanes((here, 128))
        zero = jnp.zeros((here, 128), LOW)
        scale = jnp.asarray(HEAD**-0.5, LOW)
        first = qkv[t, :, 0:128] * scale
        query[0] = jnp.where(low, first, zero)
        query[1] = jnp.where(low, zero, first)
        query[2] = jnp.where(low, qkv[t, :, 384:512] * scale, zero)
        pull[0] = jnp.where(low, dctx[:, 128:256], zero)
        pull[1] = jnp.where(low, zero, dctx[:, 0:128])
        pull[2] = jnp.where(low, zero, dctx[:, 128:256])
        one = ctx[t, own_rows, 0:128].astype(jnp.float32)
        two = ctx[t, own_rows, 128:256].astype(jnp.float32)
        lane = lax.broadcasted_iota(jnp.int32, (here, 128), 1)
        dots = jnp.zeros((here, 128), jnp.float32)
        for j, value in enumerate((two, one, two)):
            row_sum = jnp.sum(value * pull[j].astype(jnp.float32), axis=1, keepdims=True)
            dots = jnp.where(lane == j, row_sum, dots)
        dots = jnp.transpose(dots)
        score_row[0:8, :] = dots[0:8]
        logs = jnp.transpose(lse[...])
        log_rows = jnp.zeros((8, here), jnp.float32)
        for u in range(4):
            log_rows = jnp.where(t == u, logs[3 * u : 3 * u + 8], log_rows)
        score_row[8:16, :] = log_rows
        pair = (2 * here, 128)
        groups = (
            (128, 256, query[0:2].reshape(pair), pull[0:2].reshape(pair), (0, 1)),
            (512, 384, query[2], pull[2], (2,)),
        )
        half = lax.broadcasted_iota(jnp.int32, (128, here), 0) < HEAD
        grads = [None, None]
        for source, shift in ((peer, 128), (qkv, 0)):
            outs = []
            for i, (k_at, v_at, asked, pulled, heads) in enumerate(groups):
                key = source[t, :, k_at - shift : k_at - shift + 128]
                value = source[t, :, v_at - shift : v_at - shift + 128]
                logs = jnp.concatenate([score_row[8 + j : 9 + j, :] for j in heads], axis=1)
                dots = jnp.concatenate([score_row[j : j + 1, :] for j in heads], axis=1)
                probs = jnp.exp(dot_nt(key, asked) - logs)
                grad_scores = (probs * (dot_nt(value, pulled) - dots)).astype(LOW)
                outs.append(dot(grad_scores, asked))
                outs.append(dot(probs.astype(LOW), pulled))
                back = dot(jnp.transpose(key.astype(jnp.float32)).astype(LOW), grad_scores)
                grads[i] = back if grads[i] is None else grads[i] + back
            for i, out in zip((0, 1, 3, 2), outs):
                cols = slice(128 * i, 128 * i + 128)
                if shift:
                    dkv_out[t, :, cols] = out.astype(LOW)
                else:
                    dqkv[t, own_rows, 128 * i + 128 : 128 * i + 256] = out.astype(LOW)
        first = jnp.where(half, grads[0][:, :here], grads[0][:, here:])
        dqkv[t, own_rows, 0:128] = (jnp.transpose(first) * HEAD**-0.5).astype(LOW)
        second = jnp.transpose(grads[1]) * HEAD**-0.5
        keep = dqkv[t, own_rows, 384:512].astype(jnp.float32)
        dqkv[t, own_rows, 384:512] = jnp.where(low, second, keep).astype(LOW)

    def blocks(value):
        return value.reshape(2, 2, -1, value.shape[-1])

    def student():
        fetch("dlow", h_dlow, tall)
        fetch("head", h_head, head)
        fetch("last", h_last, x)
        fetch("gains", h_gains, gains)
        fetch("final", h_final, tall_t)
        steps = [(l, t) for l in reversed(range(layers)) for t in range(4)]

        def fetch_act(n):
            if n < len(steps):
                l, t = steps[n]
                fetch(("act", l, t), h_act.at[l, t], act.at[n % 2])

        def fetch_mlp(n):
            if n < len(steps):
                l, t = steps[n]
                fetch(("up", l, t), w_mlp.at[l, 0, t // 2, t % 2], up.at[n % 2])
                fetch(("down", l, t), w_mlp.at[l, 1, t // 2, t % 2], down.at[n % 2])
                fetch(("slope", l, t), h_slope.at[l, t], slope.at[n % 2])

        def fetch_late(l):
            fetch(("qkv", l), h_qkv.at[l], qkv)
            fetch(("peer", l), h_peer.at[l], peer)
            fetch(("ctx", l), h_ctx.at[l], ctx)
            fetch(("lse", l), h_lse.at[l], lse)
            fetch(("attn", l), w_attn.at[l], attn)
            fetch(("normed", l), h_normed.at[l], normed_t)

        def fetch_hid(l):
            fetch(("hid", l), h_hid.at[l], hid_t)
            fetch(("mid", l), h_mid.at[l], x)

        vec_grad[...] = jnp.zeros_like(vec_grad)
        dqkv[...] = jnp.zeros_like(dqkv)
        g[...] = jnp.zeros_like(g)
        need("dlow", "head")
        acc[...] = dot_nt(tall[own_rows, :], head[...])
        fetch_mlp(0)
        fetch_act(0)
        fetch_act(1)
        fetch_mlp(1)
        need("last", "gains")
        norm_back(x, last_row)
        fetch_hid(layers - 1)
        need("final")
        value = blocks(dot(matrix(tall_t[...]), tall[...]))

        def edge_blocks(mine, value):
            size = value.shape[2] // 4
            for t in range(4):
                block = value[:, :, size * t : size * (t + 1)]
                pad = jnp.zeros((2, 2, mine.shape[4] - size, width), jnp.float32)
                mine[t // 2, t % 2] = jnp.concatenate([block, pad], axis=2).astype(LOW)

        edge_blocks(items["H", 0]["mine"], value)
        begin(items["H", 0], 0)
        fetch_late(layers - 1)
        fetch("sums", h_sums, sums)
        fetch("mask", h_mask, mask)
        fetch("pixels", h_pixels, tall_t)

        for l in reversed(range(layers)):
            top = l == layers - 1
            low_g[...] = g[...].astype(LOW)
            if not top:
                core["datt", l + 1].wait_send()
            turn(("dffn", l), low_g, dffn_t)

            def widen(t, l=l):
                n = steps.index((l, t))
                need(("down", l, t), ("slope", l, t), ("up", l, t))
                pulled = dot(low_g[...], matrix(down[n % 2])) * slope[n % 2].astype(jnp.float32)
                dup[t, own_rows, :] = pulled.astype(LOW)
                to_core(("dup", l, t), dup.at[t, own_rows], dup.at[t, peer_rows])
                back = dot_nt(dup[t, own_rows, :], matrix(up[n % 2]))
                acc[...] = back if t == 0 else acc[...] + back
                fetch_mlp(n + 2)

            if not top:
                for t in range(4):
                    core["dup", l + 1, t].wait_send()
            widen(0)
            if top:
                advance("H", 0, 0)
            core["dffn", l].wait_recv()
            if not top:
                settle("D", l + 1)
            for t in range(4):
                n = steps.index((l, t))
                need(("act", l, t))
                value = dot(matrix(dffn_t[...]), act[n % 2])
                items["D", l]["mine"][t // 2, t % 2] = blocks(value).astype(LOW)
                fetch_act(n + 2)
            if not top:
                advance("A", l + 1, 0)
            begin(items["D", l], 0)
            widen(1)
            if top:
                advance("H", 0, 1)
            widen(2)
            widen(3)
            need(("mid", l))
            norm_back(x, 4 * l + 2)
            fetch(("x", l), h_x.at[l], x)
            need(("hid", l))
            if not top:
                settle("U", l + 1)
            for t in range(4):
                core["dup", l, t].wait_recv()
                value = dot(matrix(hid_t[...]), dup[t])
                items["U", l]["mine"][t // 2, t % 2] = blocks(value).astype(LOW)
            advance("D", l, 0)
            begin(items["U", l], 0)
            if top:
                advance("H", 0, 2)
            else:
                advance("A", l + 1, 1)
            low_g[...] = g[...].astype(LOW)
            core["dffn", l].wait_send()
            turn(("datt", l), low_g, datt_t)
            need(("attn", l), ("qkv", l), ("peer", l), ("ctx", l), ("lse", l))
            if not top:
                for t in range(4):
                    core["dkv", l + 1, t].wait_send()
                    core["dqkv", l + 1, t].wait_send()
            for t in range(4):
                weight = matrix(attn[t // 2, t % 2, :, :, :, :, 512:])
                dctx[...] = dot(low_g[...], weight).astype(LOW)
                attend_back(t)
                to_core(("dkv", l, t), dkv_out.at[t], dkv_in.at[t])
                if t == 0 and not top:
                    advance("A", l + 1, 2)
                if t == 1:
                    advance("D", l, 1)
                if t == 2:
                    advance("U", l, 0)
                if t == 3:
                    advance("D", l, 2)
            for t in range(4):
                core["dkv", l, t].wait_recv()
                for i in range(4):
                    cols = slice(128 * i + 128, 128 * i + 256)
                    total = dqkv[t, own_rows, cols].astype(jnp.float32)
                    total = total + dkv_in[t, :, 128 * i : 128 * i + 128].astype(jnp.float32)
                    dqkv[t, own_rows, cols] = total.astype(LOW)
                to_core(("dqkv", l, t), dqkv.at[t, own_rows], dqkv.at[t, peer_rows])
                weight = matrix(attn[t // 2, t % 2, :, :, :, :, :640])
                back = dot_nt(dqkv[t, own_rows, :], weight)
                acc[...] = back if t == 0 else acc[...] + back
            need(("normed", l))
            core["datt", l].wait_recv()
            advance("U", l, 1)
            if not top:
                settle("A", l + 1)
            for t in range(4):
                core["dqkv", l, t].wait_recv()
                inward = dot(matrix(normed_t[...]), dqkv[t])
                outward = dot(matrix(datt_t[...]), ctx[t])
                joint = inward[:, 512:640] + outward[:, :128]
                value = jnp.concatenate([inward[:, :512], joint, outward[:, 128:]], axis=1)
                items["A", l]["mine"][t // 2, t % 2] = blocks(value).astype(LOW)
            begin(items["A", l], 0)
            advance("U", l, 2)
            need(("x", l))
            norm_back(x, 4 * l)
            if l > 0:
                fetch_hid(l - 1)
                fetch_late(l - 1)
        need("mask", "sums", "pixels")

        def embed_back(n, _):
            span = pl.ds(pl.multiple_of(n * 64, 64), 64)
            part = pl.ds(pl.multiple_of(n % 3 * 64, 64), 64)
            hide = mask[n // 3, part, 0:1].astype(jnp.float32)
            value = g[span, :]
            tall[span, :] = (value * (1.0 - hide)).astype(LOW)
            vec_grad[last_row + 2 : last_row + 3, :] += jnp.sum(value * hide, axis=0, keepdims=True)
            return 0

        lax.fori_loop(0, here // 64, embed_back, 0)
        to_core("embed", tall.at[own_rows], tall.at[peer_rows])
        vec_grad[last_row + 3 : last_row + 4, :] = sums[0:1, :]
        loss = jnp.sum(sums[1:2, :], axis=1, keepdims=True) * width**-0.5
        vec_grad[last_row + 4 : last_row + 5, :] = jnp.broadcast_to(loss, (1, width))
        full = jnp.concatenate([vec_grad[...], jnp.zeros((112, width), jnp.float32)])
        full = jnp.transpose(full)
        size = width // 32
        for d in range(8):
            for t in range(4):
                row = (4 * d + t) * size
                vec_turned[d % 2, t // 2, t % 2, d // 4, d // 2 % 2] = full[row : row + size]
        vec = items["V", 0]
        vec_in = vec_turned.at[2]
        to_core("vec", vec_turned.at[1 - co["c"]], vec_in)
        core["embed"].wait_recv()
        edge_blocks(items["P", 0]["mine"], blocks(dot(matrix(tall_t[...]), tall[...])))
        begin(items["P", 0], 0)
        core["vec"].wait_recv()
        vec["mine"][...] = vec_turned[co["c"]] + vec_turned[2]
        begin(vec, 0)
        for s in range(3):
            advance("A", 0, s)
            advance("P", 0, s)
            advance("V", 0, s)
        for name, l, unused in targets:
            if l == 0:
                settle(name, l)
        core["embed"].wait_send()
        core["vec"].wait_send()
        core["datt", 0].wait_send()
        for t in range(4):
            for name in ("dup", "dkv", "dqkv"):
                core[name, 0, t].wait_send()

    @pl.when(co["a"] == 0)
    def _():
        student()

    @pl.when(co["a"] == 1)
    def _():
        for name, l, target in targets:
            item = items[name, l]
            last_hop(item).wait_recv()
            copy = pltpu.make_async_copy(item["last"], target, out_sem.at[item["n"]])
            copy.start()
        for name, l, target in targets:
            item = items[name, l]
            pltpu.make_async_copy(item["last"], target, out_sem.at[item["n"]]).wait()


def backward_all(*parts):
    w_attn, w_mlp = parts[:2]
    layers, rows, width = w_attn.shape[0], w_attn.shape[-2], w_attn.shape[-1]
    here = parts[4].shape[1]
    f32 = jnp.float32
    tall = (here, width)
    turned = (2, 2, rows, 2 * here)
    weight = (2, 2, 2, rows, width)
    edge = 32
    small = width // 32
    scratch = [
        ((width, width), LOW),
        ((16, width), f32),
        (tall, f32),
        (turned, LOW),
        (turned, LOW),
        ((4,) + tall, LOW),
        ((4, here, 512), LOW),
        ((4, 2 * here, 256), LOW),
        ((here, 128), f32),
        ((2, 2) + weight, LOW),
        ((2, 2 * here, width), LOW),
        ((2,) + weight, LOW),
        ((2,) + weight, LOW),
        ((2,) + tall, LOW),
        (turned, LOW),
        ((2 * here, width), LOW),
        (parts[19].shape, LOW),
        ((8, width), f32),
        (tall, f32),
        (tall, f32),
        (tall, LOW),
        ((2, 2, 2, rows, here), LOW),
        (turned, LOW),
        (turned, LOW),
        ((4, 2 * here, width), LOW),
        ((here, 256), LOW),
        ((4, 2 * here, 640), LOW),
        ((4, here, 512), LOW),
        ((4, here, 512), LOW),
        ((3, here, 128), LOW),
        ((3, here, 128), LOW),
        ((16, here), f32),
        ((16, width), f32),
        ((3, 2, 2, 2, 2, small, 128), f32),
    ]
    shapes = dict(
        D=(rows, width, LOW, 3),
        U=(rows, width, LOW, 3),
        A=(rows, width, LOW, 3),
        H=(edge, width, LOW, 2),
        P=(edge, width, LOW, 2),
        V=(small, 128, f32, 3),
    )
    for count, cols, kind, pieces in shapes.values():
        scratch.append(((2, 2, 2, 2, count, cols), kind))
        for p in range(pieces):
            order = ORDERS[p][::-1]
            for s in range(3):
                dims = tuple(1 if k in order[: s + 1] else 2 for k in "azyx")
                scratch.append((dims + (count // pieces, cols), kind))
    names = "H" + "DUA" * layers + "PV"
    for name in names:
        count, cols, kind, pieces = shapes[name]
        scratch.append(((count, cols), kind))
    count = len(names)
    return pl.pallas_call(
        backward_kernel,
        out_shape=(
            shape_of((layers, rows, width)),
            shape_of((layers, 2, rows, width)),
            shape_of((edge, width)),
            shape_of((edge, width)),
            shape_of((small, 128), f32),
        ),
        in_specs=[ANY] * len(parts),
        out_specs=(ANY,) * 5,
        scratch_shapes=[pltpu.VMEM(*s) for s in scratch]
        + [
            DMA((96,)),
            DMA((count, 3, 4)),
            DMA((count, 3, 4)),
            DMA((count,)),
            DMA((2, 48)),
            pltpu.SemaphoreType.REGULAR((3, 3)),
        ],
        compiler_params=pltpu.CompilerParams(
            collective_id=1, has_side_effects=True, vmem_limit_bytes=60 * 2**20
        ),
    )(*parts)


def total_kernel(value, out, held, send_sem, recv_sem):
    co = coords()
    d, t = ident(co)
    near = [(d - d % 2 + (d + k // 4) % 2, (t + k) % 4) for k in range(1, 8)]
    far = [((d + 2 * k) % 8, t) for k in range(1, 4)]
    barrier = pltpu.get_barrier_semaphore()
    for to in near + far:
        pl.semaphore_signal(barrier, inc=1, device_id=to, device_id_type=MESH)
    pl.semaphore_wait(barrier, len(near) + len(far))
    total = value[...]
    n = 0
    for s, group in enumerate((near, far)):
        held[0, s] = total
        copies = []
        for to in group:
            copy = pltpu.make_async_remote_copy(
                src_ref=held.at[0, s],
                dst_ref=held.at[1, n],
                send_sem=send_sem.at[n],
                recv_sem=recv_sem.at[n],
                device_id=to,
                device_id_type=MESH,
            )
            copy.start()
            copies.append((copy, n))
            n += 1
        for copy, spot in copies:
            copy.wait()
            total = total + held[1, spot]
    out[...] = total


def total_all(value):
    return pl.pallas_call(
        total_kernel,
        out_shape=shape_of(value.shape, jnp.float32),
        in_specs=[pl.BlockSpec(memory_space=pltpu.VMEM)],
        out_specs=pl.BlockSpec(memory_space=pltpu.VMEM),
        scratch_shapes=[pltpu.VMEM((2, 10) + value.shape, jnp.float32), DMA((10,)), DMA((10,))],
        compiler_params=pltpu.CompilerParams(collective_id=2, has_side_effects=True),
    )(value)


def per_device(
    patches,
    mask,
    edge,
    attn_w,
    mlp_w,
    vecs,
    edge_m,
    edge_v,
    attn_m,
    attn_v,
    mlp_m,
    mlp_v,
    vecs_m,
    vecs_v,
    teacher_edge,
    teacher_attn,
    teacher_mlp,
    teacher_vecs,
):
    layer_count, rows, kinds, block = attn_w.shape
    wide = mlp_w.shape[3]
    width = patches.shape[2]
    quarter = patches.shape[0]
    edge_rows = edge.shape[1]
    vec_count, vec_cols = vecs.shape
    last_row = 4 * layer_count
    teaching = lax.axis_index(TENSOR) >= 2
    dp_size = lax.axis_size(DP)

    def pack(own_edge, own_attn, own_mlp, own_vecs):
        return (
            pack_heads(own_attn.astype(LOW)),
            jnp.swapaxes(own_mlp.astype(LOW), 1, 2),
            own_edge.astype(LOW).reshape(2 * edge_rows, width),
            jnp.pad(own_vecs.T, ((0, 0), (0, 128 - vec_count))),
        )

    student = (edge, attn_w, mlp_w, vecs)
    teacher = (teacher_edge, teacher_attn, teacher_mlp, teacher_vecs)
    mine = pack(*[jnp.where(teaching, right, left) for left, right in zip(student, teacher)])
    other = pack(*[jnp.where(teaching, left, right) for left, right in zip(student, teacher)])
    parts = [part for pair in zip(mine, other) for part in pair]
    marks = jnp.broadcast_to(mask.astype(LOW), (quarter, 128))
    parts.append(jnp.concatenate([patches.reshape(quarter, width), marks], axis=1))
    attn_grad, mlp_grad, head_grad, patch_grad, vecs_grad = backward_all(*forward_all(*parts))
    by_row = Layout(major_to_minor=(0, 1, 2, 3))
    attn_grad = with_layout_constraint(unpack_heads(attn_grad).astype(jnp.float32), by_row)
    mlp_grad = with_layout_constraint(jnp.swapaxes(mlp_grad.astype(jnp.float32), 1, 2), by_row)
    edge_grad = jnp.stack([patch_grad[:edge_rows], head_grad[:edge_rows]]).astype(jnp.float32)
    loss_total = vecs_grad[0, vec_count]
    vecs_grad = vecs_grad[:, :vec_count].T
    edge_first, edge_second, edge_update = direction(edge, edge_grad, edge_m, edge_v)
    attn_first, attn_second, attn_update = direction(attn_w, attn_grad, attn_m, attn_v)
    mlp_first, mlp_second, mlp_update = direction(mlp_w, mlp_grad, mlp_m, mlp_v)
    vecs_first, vecs_second, vecs_update = direction(vecs, vecs_grad, vecs_m, vecs_v)
    squares = jnp.stack(
        [
            matrix_squares(edge, attn_w, mlp_w),
            matrix_squares(edge_update, attn_update, mlp_update),
        ]
    )
    squares = jnp.pad(squares, ((0, 6), (0, 128 - squares.shape[1])))
    norms = jnp.sqrt(total_all(squares)[:2, : 2 + 6 * layer_count])
    trust = norms[0] / (norms[1] + adam_epsilon)
    edge_trust = trust[0:2]
    layer_trust = trust[2:].reshape(layer_count, 6)
    new_edge = edge - learn_rate * edge_trust[:, None, None] * edge_update
    new_attn = attn_w - learn_rate * layer_trust[:, None, 0:4, None] * attn_update
    new_mlp = mlp_w - learn_rate * layer_trust[:, None, 4:6, None] * mlp_update
    new_vecs = vecs - learn_rate * vecs_update
    keep_share = 1.0 - teacher_decay
    token_total = 4 * quarter * dp_size
    return (
        loss_total / token_total,
        norms,
        new_edge,
        new_attn,
        new_mlp,
        new_vecs,
        edge_first,
        edge_second[0],
        edge_second[1],
        attn_first,
        attn_second[:, :, 0:3],
        attn_second[:, :, 3],
        mlp_first,
        mlp_second,
        vecs_first,
        vecs_second,
        keep_share * (new_edge - teacher_edge),
        keep_share * (new_attn - teacher_attn),
        keep_share * (new_mlp - teacher_mlp),
        keep_share * (new_vecs - teacher_vecs),
        new_edge.astype(LOW),
        new_attn.astype(LOW),
        new_mlp.astype(LOW),
        new_vecs.astype(LOW),
    )


def solution(mesh):
    placed = (
        P(TENSOR, DP, None),
        P(TENSOR, DP),
        P(None, (DP, TENSOR), None),
        P(None, DP, None, TENSOR),
        P(None, DP, None, TENSOR),
        P(None, (DP, TENSOR)),
        P(None, (DP, TENSOR), None),
        P(None, (DP, TENSOR), None),
        P(None, DP, None, TENSOR),
        P(None, DP, None, TENSOR),
        P(None, DP, None, TENSOR),
        P(None, DP, None, TENSOR),
        P(None, (DP, TENSOR)),
        P(None, (DP, TENSOR)),
        P(None, (DP, TENSOR), None),
        P(None, DP, None, TENSOR),
        P(None, DP, None, TENSOR),
        P(None, (DP, TENSOR)),
    )
    planned = dict(mesh.shape) == {DP: 8, TENSOR: 4}
    return jax.shard_map(
        per_device if planned else per_device_general,
        mesh=mesh,
        in_specs=placed,
        out_specs=(
            P(),
            P(),
            P(None, (DP, TENSOR), None),
            P(None, DP, None, TENSOR),
            P(None, DP, None, TENSOR),
            P(None, (DP, TENSOR)),
            P(None, (DP, TENSOR), None),
            P((DP, TENSOR), None),
            P((DP, TENSOR), None),
            P(None, DP, None, TENSOR),
            P(None, DP, None, TENSOR),
            P(None, DP, TENSOR),
            P(None, DP, None, TENSOR),
            P(None, DP, None, TENSOR),
            P(None, (DP, TENSOR)),
            P(None, (DP, TENSOR)),
            P(None, (DP, TENSOR), None),
            P(None, DP, None, TENSOR),
            P(None, DP, None, TENSOR),
            P(None, (DP, TENSOR)),
            P(None, (DP, TENSOR), None),
            P(None, DP, None, TENSOR),
            P(None, DP, None, TENSOR),
            P(None, (DP, TENSOR)),
        ),
        check_vma=False,
    )
```

```python
import jax
import jax.numpy as jnp
from jax import lax
from jax.experimental import pallas as pl
from jax.experimental.layout import Layout, with_layout_constraint
from jax.experimental.pallas import tpu as pltpu
from jax.sharding import PartitionSpec as P

HEAD = 64
DP = "dp"
TENSOR = "tensor"


norm_epsilon = 1e-06
inst_epsilon = 1e-05
first_decay = 0.9
second_decay = 0.999
adam_epsilon = 1e-06
weight_decay = 0.01
learn_rate = 0.3
teacher_decay = 0.999
step_count = 10


def norm_rows(values, gain, shift):
    average = jnp.mean(values, axis=-1, keepdims=True)
    centered = values - average
    spread = jnp.mean(centered * centered, axis=-1, keepdims=True)
    return centered * lax.rsqrt(spread + norm_epsilon) * gain + shift


def exact_gelu(values):
    return jax.nn.gelu(values, approximate=False)


def fetch_edges(edge_part, vector_part):
    return (
        lax.all_gather(edge_part, (DP, TENSOR), axis=1, tiled=True),
        lax.all_gather(vector_part, (DP, TENSOR), axis=1, tiled=True),
    )


def fetch_layer(attn_part, mlp_part):
    return (
        lax.all_gather(attn_part.astype(jnp.bfloat16), DP, axis=0, tiled=True),
        lax.all_gather(mlp_part.astype(jnp.bfloat16), DP, axis=0, tiled=True),
    )


def fetch_again(attn_part, mlp_part):
    return (
        lax.all_gather(attn_part.astype(jnp.bfloat16), DP, axis=0, tiled=True),
        lax.all_gather(mlp_part.astype(jnp.bfloat16), DP, axis=0, tiled=True),
    )


def gather_rows(local_part):
    return lax.all_gather(local_part, TENSOR, axis=0, tiled=True)


def gather_grads(local_part):
    return lax.all_gather(local_part, TENSOR, axis=0, tiled=True)


def project_term(full_rows, weight):
    return jnp.einsum("sck,dk->scd", full_rows, weight, preferred_element_type=jnp.float32)


def scatter_rows(full_rows, weight):
    return lax.psum_scatter(
        project_term(full_rows, weight).astype(jnp.bfloat16),
        TENSOR,
        scatter_dimension=0,
        tiled=True,
    ).astype(jnp.float32)


def scatter_grads(full_rows, weight):
    return lax.psum_scatter(
        project_term(full_rows, weight).astype(jnp.bfloat16),
        TENSOR,
        scatter_dimension=0,
        tiled=True,
    ).astype(jnp.float32)


def attend_forward(parts):
    queries, keys_in, values_in = parts
    scores = jnp.einsum(
        "shd,thd->hst", queries, keys_in, preferred_element_type=jnp.float32
    ) * HEAD ** (-0.5)
    peak = jnp.max(scores, axis=-1, keepdims=True)
    raised = jnp.exp(scores - peak)
    summed = jnp.sum(raised, axis=-1, keepdims=True)
    weights = (raised / summed).astype(jnp.bfloat16)
    context = jnp.einsum("hst,thd->shd", weights, values_in, preferred_element_type=jnp.float32)
    return (context.astype(jnp.bfloat16), (peak + jnp.log(summed))[..., 0])


def attend_backward(parts):
    queries, keys_in, values_in, log_total, grad_context = parts
    scale = HEAD ** (-0.5)
    scores = (
        jnp.einsum("shd,thd->hst", queries, keys_in, preferred_element_type=jnp.float32) * scale
    )
    probs = jnp.exp(scores - log_total[..., None])
    probs_low = probs.astype(jnp.bfloat16)
    grad_values = jnp.einsum(
        "hst,shd->thd", probs_low, grad_context, preferred_element_type=jnp.float32
    )
    grad_probs = jnp.einsum(
        "shd,thd->hst", grad_context, values_in, preferred_element_type=jnp.float32
    )
    grad_scores = (
        probs * (grad_probs - jnp.sum(probs * grad_probs, axis=-1, keepdims=True))
    ).astype(jnp.bfloat16)
    grad_queries = (
        jnp.einsum("hst,thd->shd", grad_scores, keys_in, preferred_element_type=jnp.float32) * scale
    )
    grad_keys = (
        jnp.einsum("hst,shd->thd", grad_scores, queries, preferred_element_type=jnp.float32) * scale
    )
    return (grad_queries, grad_keys, grad_values)


def run_block(stream, attn_full, mlp_full, gains):
    model_width = stream.shape[2]
    head_width = attn_full.shape[2]
    normed = norm_rows(stream, gains[0], gains[1]).astype(jnp.bfloat16)
    normed_full = gather_rows(normed)
    seq_len = normed_full.shape[0]
    clip_count = normed_full.shape[1]
    weight_in = attn_full[:, 0:3].reshape(model_width, 3 * head_width)
    joined = jnp.einsum(
        "scd,dk->sck", normed_full, weight_in, preferred_element_type=jnp.float32
    ).astype(jnp.bfloat16)
    split_heads = jnp.moveaxis(
        joined.reshape(seq_len, clip_count, 3, head_width // HEAD, HEAD), 1, 0
    )
    context, log_total = lax.map(
        attend_forward, (split_heads[:, :, 0], split_heads[:, :, 1], split_heads[:, :, 2])
    )
    context_rows = jnp.moveaxis(context, 0, 1).reshape(seq_len, clip_count, head_width)
    middle = stream + scatter_rows(context_rows, attn_full[:, 3])
    hidden = norm_rows(middle, gains[2], gains[3]).astype(jnp.bfloat16)
    hidden_full = gather_rows(hidden)
    upward = jnp.einsum(
        "scd,df->scf", hidden_full, mlp_full[:, 0], preferred_element_type=jnp.float32
    )
    active = exact_gelu(upward).astype(jnp.bfloat16)
    result = middle + scatter_rows(active, mlp_full[:, 1])
    return (
        result,
        (
            stream,
            normed_full,
            split_heads,
            log_total,
            context_rows,
            middle,
            hidden_full,
            upward,
            active,
        ),
    )


def back_block(grad_stream, saved, attn_full, mlp_full, gains):
    (
        stream,
        normed_full,
        split_heads,
        log_total,
        context_rows,
        middle,
        hidden_full,
        upward,
        active,
    ) = saved
    model_width = stream.shape[2]
    head_width = attn_full.shape[2]
    seq_len = normed_full.shape[0]
    clip_count = normed_full.shape[1]
    grad_ffn = gather_grads(grad_stream.astype(jnp.bfloat16))
    grad_down = jnp.einsum("scd,scf->df", grad_ffn, active, preferred_element_type=jnp.float32)
    grad_active = jnp.einsum(
        "scd,df->scf", grad_ffn, mlp_full[:, 1], preferred_element_type=jnp.float32
    )
    unused, gelu_pull = jax.vjp(exact_gelu, upward)
    grad_upward = gelu_pull(grad_active)[0].astype(jnp.bfloat16)
    grad_up = jnp.einsum(
        "scd,scf->df", hidden_full, grad_upward, preferred_element_type=jnp.float32
    )
    grad_hidden = scatter_grads(grad_upward, mlp_full[:, 0])
    unused, second_pull = jax.vjp(norm_rows, middle, gains[2], gains[3])
    grad_middle_norm, grad_gain_two, grad_shift_two = second_pull(grad_hidden)
    grad_middle = grad_stream + grad_middle_norm
    grad_attn = gather_grads(grad_middle.astype(jnp.bfloat16))
    grad_outward = jnp.einsum(
        "scd,sck->dk", grad_attn, context_rows, preferred_element_type=jnp.float32
    )
    grad_context = jnp.einsum(
        "scd,dk->sck", grad_attn, attn_full[:, 3], preferred_element_type=jnp.float32
    ).astype(jnp.bfloat16)
    grad_context = jnp.moveaxis(
        grad_context.reshape(seq_len, clip_count, head_width // HEAD, HEAD), 1, 0
    )
    grad_queries, grad_keys, grad_values = lax.map(
        attend_backward,
        (split_heads[:, :, 0], split_heads[:, :, 1], split_heads[:, :, 2], log_total, grad_context),
    )
    grad_joined = jnp.moveaxis(jnp.stack((grad_queries, grad_keys, grad_values), axis=2), 0, 1)
    grad_joined = grad_joined.reshape(seq_len, clip_count, 3 * head_width).astype(jnp.bfloat16)
    weight_in = attn_full[:, 0:3].reshape(model_width, 3 * head_width)
    grad_inward = jnp.einsum(
        "scd,sck->dk", normed_full, grad_joined, preferred_element_type=jnp.float32
    ).reshape(model_width, 3, head_width)
    grad_normed = scatter_grads(grad_joined, weight_in)
    unused, first_pull = jax.vjp(norm_rows, stream, gains[0], gains[1])
    grad_stream_norm, grad_gain_one, grad_shift_one = first_pull(grad_normed)
    attn_grad = jnp.concatenate([grad_inward, grad_outward[:, None]], axis=1)
    mlp_grad = jnp.stack([grad_up, grad_down], axis=1)
    layer_attn, layer_mlp = (
        lax.psum_scatter(attn_grad, DP, scatter_dimension=0, tiled=True),
        lax.psum_scatter(mlp_grad, DP, scatter_dimension=0, tiled=True),
    )
    vector_grads = jnp.stack([grad_gain_one, grad_shift_one, grad_gain_two, grad_shift_two])
    return (grad_middle + grad_stream_norm, layer_attn, layer_mlp, vector_grads)


def direction(weight, grad, first, second):
    bias_one = 1.0 - first_decay**step_count
    bias_two = 1.0 - second_decay**step_count
    first_new = first_decay * first + (1.0 - first_decay) * grad
    second_new = second_decay * second + (1.0 - second_decay) * grad * grad
    update = (
        first_new / bias_one / (jnp.sqrt(second_new / bias_two) + adam_epsilon)
        + weight_decay * weight
    )
    return (first_new, second_new, update)


def matrix_squares(edge_part, attn_part, mlp_part):
    layer_part = jnp.concatenate(
        [jnp.sum(attn_part * attn_part, axis=(1, 3)), jnp.sum(mlp_part * mlp_part, axis=(1, 3))],
        axis=1,
    )
    return jnp.concatenate([jnp.sum(edge_part * edge_part, axis=(1, 2)), layer_part.reshape(-1)])


def per_device_general(
    patches,
    mask,
    edge,
    attn_w,
    mlp_w,
    vecs,
    edge_m,
    edge_v,
    attn_m,
    attn_v,
    mlp_m,
    mlp_v,
    vecs_m,
    vecs_v,
    teacher_edge,
    teacher_attn,
    teacher_mlp,
    teacher_vecs,
):
    layer_count = attn_w.shape[0]
    local_count = patches.shape[0]
    clip_count = patches.shape[1]
    model_width = patches.shape[2]
    last_row = 4 * layer_count
    student_edge, student_vecs = fetch_edges(edge, vecs)
    teach_edge, teach_vecs = fetch_edges(teacher_edge, teacher_vecs)
    seq_total = local_count * lax.axis_size(TENSOR)
    stream = jnp.einsum(
        "scp,pd->scd",
        patches,
        teach_edge[0].astype(jnp.bfloat16),
        preferred_element_type=jnp.float32,
    )
    summed = jnp.zeros_like(stream)
    for layer_index in range(layer_count):
        attn_full, mlp_full = fetch_layer(teacher_attn[layer_index], teacher_mlp[layer_index])
        stream, unused = run_block(
            stream, attn_full, mlp_full, teach_vecs[4 * layer_index : 4 * layer_index + 4]
        )
        first_sum, square_sum = lax.psum(
            (jnp.sum(stream, axis=0), jnp.sum(stream * stream, axis=0)), TENSOR
        )
        average = first_sum / seq_total
        spread = square_sum / seq_total - average * average
        summed = summed + (stream - average) * lax.rsqrt(spread + inst_epsilon)
    target = summed / layer_count
    masked = mask.astype(jnp.float32)[..., None]
    embedded = jnp.einsum(
        "scp,pd->scd",
        patches,
        student_edge[0].astype(jnp.bfloat16),
        preferred_element_type=jnp.float32,
    )
    stream = embedded * (1.0 - masked) + masked * student_vecs[last_row + 2]
    saved_list = []
    weight_list = []
    for layer_index in range(layer_count):
        attn_full, mlp_full = fetch_layer(attn_w[layer_index], mlp_w[layer_index])
        stream, saved = run_block(
            stream, attn_full, mlp_full, student_vecs[4 * layer_index : 4 * layer_index + 4]
        )
        saved_list.append(saved)
        weight_list.append((attn_full, mlp_full))
    final_low = norm_rows(stream, student_vecs[last_row], student_vecs[last_row + 1]).astype(
        jnp.bfloat16
    )
    head_low = student_edge[1].astype(jnp.bfloat16)
    predicted = (
        jnp.einsum("scd,de->sce", final_low, head_low, preferred_element_type=jnp.float32)
        + student_vecs[last_row + 3]
    )
    offset = predicted - target
    size_abs = jnp.abs(offset)
    loss_part = (
        jnp.sum(jnp.where(size_abs < 1.0, 0.5 * offset * offset, size_abs - 0.5) * masked)
        / model_width**0.5
    )
    grad_pred = jnp.clip(offset, -1.0, 1.0) * masked / model_width**0.5
    grad_low = grad_pred.astype(jnp.bfloat16)
    grad_head = jnp.einsum("scd,sce->de", final_low, grad_low, preferred_element_type=jnp.float32)
    grad_bias = jnp.sum(grad_pred, axis=(0, 1))
    grad_final = jnp.einsum("sce,de->scd", grad_low, head_low, preferred_element_type=jnp.float32)
    unused, final_pull = jax.vjp(
        norm_rows, stream, student_vecs[last_row], student_vecs[last_row + 1]
    )
    grad_stream, grad_final_gain, grad_final_shift = final_pull(grad_final)
    attn_grads = []
    mlp_grads = []
    vector_rows = []
    for layer_index in reversed(range(layer_count)):
        attn_full, mlp_full = fetch_again(attn_w[layer_index], mlp_w[layer_index])
        grad_stream, layer_attn, layer_mlp, vector_grads = back_block(
            grad_stream,
            saved_list[layer_index],
            attn_full,
            mlp_full,
            student_vecs[4 * layer_index : 4 * layer_index + 4],
        )
        attn_grads.insert(0, layer_attn)
        mlp_grads.insert(0, layer_mlp)
        vector_rows.insert(0, vector_grads)
    grad_embed = (grad_stream * (1.0 - masked)).astype(jnp.bfloat16)
    grad_mask_vec = jnp.sum(grad_stream * masked, axis=(0, 1))
    grad_patch = jnp.einsum("scp,scd->pd", patches, grad_embed, preferred_element_type=jnp.float32)
    vector_grad = jnp.concatenate(
        vector_rows + [jnp.stack([grad_final_gain, grad_final_shift, grad_mask_vec, grad_bias])],
        axis=0,
    )
    edge_grad, vecs_grad = (
        lax.psum_scatter(
            jnp.stack([grad_patch, grad_head]), (DP, TENSOR), scatter_dimension=1, tiled=True
        ),
        lax.psum_scatter(vector_grad, (DP, TENSOR), scatter_dimension=1, tiled=True),
    )
    attn_grad = jnp.stack(attn_grads)
    mlp_grad = jnp.stack(mlp_grads)
    edge_first, edge_second, edge_update = direction(edge, edge_grad, edge_m, edge_v)
    attn_first, attn_second, attn_update = direction(attn_w, attn_grad, attn_m, attn_v)
    mlp_first, mlp_second, mlp_update = direction(mlp_w, mlp_grad, mlp_m, mlp_v)
    vecs_first, vecs_second, vecs_update = direction(vecs, vecs_grad, vecs_m, vecs_v)
    weight_sq, update_sq, loss_total = lax.psum(
        (
            matrix_squares(edge, attn_w, mlp_w),
            matrix_squares(edge_update, attn_update, mlp_update),
            loss_part,
        ),
        (DP, TENSOR),
    )
    weight_norm = jnp.sqrt(weight_sq)
    update_norm = jnp.sqrt(update_sq)
    trust = weight_norm / (update_norm + adam_epsilon)
    edge_trust = trust[0:2]
    layer_trust = trust[2:].reshape(layer_count, 6)
    new_edge = edge - learn_rate * edge_trust[:, None, None] * edge_update
    new_attn = attn_w - learn_rate * layer_trust[:, None, 0:4, None] * attn_update
    new_mlp = mlp_w - learn_rate * layer_trust[:, None, 4:6, None] * mlp_update
    new_vecs = vecs - learn_rate * vecs_update
    keep_share = 1.0 - teacher_decay
    token_total = seq_total * clip_count * lax.axis_size(DP)
    return (
        loss_total / token_total,
        jnp.stack([weight_norm, update_norm]),
        new_edge,
        new_attn,
        new_mlp,
        new_vecs,
        edge_first,
        edge_second[0],
        edge_second[1],
        attn_first,
        attn_second[:, :, 0:3],
        attn_second[:, :, 3],
        mlp_first,
        mlp_second,
        vecs_first,
        vecs_second,
        keep_share * (new_edge - teacher_edge),
        keep_share * (new_attn - teacher_attn),
        keep_share * (new_mlp - teacher_mlp),
        keep_share * (new_vecs - teacher_vecs),
        new_edge.astype(jnp.bfloat16),
        new_attn.astype(jnp.bfloat16),
        new_mlp.astype(jnp.bfloat16),
        new_vecs.astype(jnp.bfloat16),
    )


MESH = pl.DeviceIdType.MESH
ORDERS = (("z", "x", "y"), ("x", "y", "z"), ("y", "z", "x"))
LOW = jnp.bfloat16
ALL = slice(None)


def coords():
    d = lax.axis_index(DP)
    t = lax.axis_index(TENSOR)
    return dict(a=t // 2, z=t % 2, y=d // 4, x=(d // 2) % 2, c=d % 2)


def ident(co):
    return (co["y"] * 4 + co["x"] * 2 + co["c"], co["a"] * 2 + co["z"])


def flip(co, k):
    co = dict(co)
    co[k] = 1 - co[k]
    return ident(co)


def place(co, full, rows):
    return tuple(ALL if k in full else co[k] for k in "azyxc") + (rows,)


ANY = pl.BlockSpec(memory_space=pl.ANY)
DMA = pltpu.SemaphoreType.DMA


def shape_of(shape, kind=LOW):
    return jax.ShapeDtypeStruct(shape, kind)


def dot(left, right):
    return jnp.dot(left, right, preferred_element_type=jnp.float32)


def dot_nt(left, right):
    return lax.dot_general(
        left, right, (((1,), (1,)), ((), ())), preferred_element_type=jnp.float32
    )


def dot_tn(left, right):
    return lax.dot_general(
        left, right, (((0,), (0,)), ((), ())), preferred_element_type=jnp.float32
    )


def pack_heads(block):
    q, k, v, o = (block[..., i, :] for i in range(4))
    two = 2 * HEAD
    pieces = [q[..., :two], k[..., :two], v[..., :two], q[..., two:], v[..., two:], k[..., two:]]
    pieces += [o[..., HEAD:two], o[..., :HEAD], o[..., two:]]
    return jnp.concatenate(pieces, axis=-1)


def unpack_heads(packed):
    cut = lambda *spots: jnp.concatenate(
        [packed[..., HEAD * a : HEAD * b] for a, b in spots], axis=-1
    )
    kinds = [cut((0, 2), (6, 7)), cut((2, 4), (8, 9)), cut((4, 6), (7, 8))]
    kinds.append(cut((10, 11), (9, 10), (11, 12)))
    return jnp.stack(kinds, axis=-2)


def norm_block(values, gain, shift):
    average = jnp.mean(values, axis=-1, keepdims=True)
    centered = values - average
    spread = jnp.mean(centered * centered, axis=-1, keepdims=True)
    return centered * lax.rsqrt(spread + norm_epsilon) * gain + shift


def matrix(value):
    return value.reshape(-1, value.shape[-1])


def low_lanes(shape):
    return lax.broadcasted_iota(jnp.int32, shape, len(shape) - 1) % 128 < HEAD


def forward_kernel(*refs):
    (attn_mine, attn_other, mlp_mine, mlp_other, edge_mine, edge_other) = refs[:6]
    vec_mine, vec_other, patch = refs[6:9]
    (o_attn, o_mlp, o_head, o_vec, o_x, o_mid, o_normed, o_qkv, o_peer, o_ctx) = refs[9:19]
    (o_hid, o_act, o_slope, o_lse, o_last, o_final, o_pixels, o_dlow, o_sums, o_mask) = refs[19:29]
    (w_attn, w_mlp, w_edge, w_vec, pixels, embed_w, head_w, gains, x, mid) = refs[29:39]
    (normed, qkv, peer, ctx, hid, act, slope, lse, work, target, stat, sums, turned) = refs[39:52]
    early, final_stat = refs[52:54]
    local_sem, send_sem, recv_sem, patch_sem, peer_sem, stat_sem, save_sem, core_sem = refs[54:]
    co = coords()
    me = ident(co)
    column = co["y"] * 2 + co["x"]
    teaching = co["a"] == 1
    rows_here = x.shape[0]
    width = x.shape[1]
    layers = attn_mine.shape[0]
    last_row = 4 * layers
    barrier = pltpu.get_barrier_semaphore()
    for k in range(1, 8):
        to = (column * 2 + (co["c"] + k // 4) % 2, (me[1] + k % 4) % 4)
        pl.semaphore_signal(barrier, inc=1, device_id=to, device_id_type=MESH)
    for k in "xy":
        pl.semaphore_signal(barrier, inc=1, device_id=flip(co, k), device_id_type=MESH)
    pl.semaphore_wait(barrier, 9)

    items = [(edge_mine, edge_other, w_edge, 0), (vec_mine, vec_other, w_vec, 0)]
    for l in range(layers):
        items.append((attn_mine.at[l], attn_other.at[l], w_attn.at[l], 3 * l + 1))
        for k in range(2):
            items.append(
                (mlp_mine.at[l, k], mlp_other.at[l, k], w_mlp.at[l, k], 3 * l + 2 + k)
            )
    sent = []
    table = {}

    def remote(source, to_ref, i, j, k, to):
        copy = pltpu.make_async_remote_copy(
            src_ref=source,
            dst_ref=to_ref,
            send_sem=send_sem.at[i, j, k],
            recv_sem=recv_sem.at[i, j, k],
            device_id=to,
            device_id_type=MESH,
        )
        copy.start()
        sent.append(copy)
        return copy

    def begin(slot):
        for i, (mine, other, full, at) in enumerate(items):
            if at == slot:
                spot = full.at[place(co, "", ALL)]
                copy = pltpu.make_async_copy(mine, spot, local_sem.at[i])
                copy.start()
                table[i, -1] = (copy, remote(other, spot, i, 0, 4, flip(co, "a")))

    def step(wave, s):
        for i, (mine, other, full, at) in enumerate(items):
            if wave - at != s:
                continue
            if s == 0:
                table[i, -1][0].wait()
                table[i, -1][1].wait_recv()
            size = mine.shape[0] // 3
            copies = []
            for p in range(3):
                if s > 0:
                    table[i, s - 1][p].wait_recv()
                if s < 4:
                    order = ORDERS[p] + ("c",)
                    full_dims = ("a",) + order[:s]
                    ref = full.at[place(co, full_dims, pl.ds(p * size, size))]
                    copies.append(remote(ref, ref, i, p, s, flip(co, order[s])))
            table[i, s] = copies

    saves = {}
    counter = iter(range(48))

    def save(name, source, to_ref):
        copy = pltpu.make_async_copy(source, to_ref, save_sem.at[next(counter)])
        copy.start()
        saves[name] = copy

    shared = {}
    core_counter = iter(range(16))
    own_rows, peer_rows = pl.ds(0, rows_here), pl.ds(rows_here, rows_here)

    def to_core(name, source, to_ref):
        n = next(core_counter)
        shared[name] = pltpu.make_async_remote_copy(
            src_ref=source,
            dst_ref=to_ref,
            send_sem=core_sem.at[0, n],
            recv_sem=core_sem.at[1, n],
            device_id=flip(co, "c"),
            device_id_type=MESH,
        )
        shared[name].start()

    def share(name, source, to_ref, lead):
        save(name, source, to_ref.at[lead + (own_rows,)])
        to_core(name, source, to_ref.at[lead + (peer_rows,)])

    turns = []

    def turn(name, columns, to_ref):
        spot = turned.at[len(turns) % 2]
        if len(turns) >= 2:
            wait_saves(turns[-2])
        turns.append(name)
        for n in range(2):
            spot[n] = jnp.transpose(columns(n)).astype(LOW).reshape(spot.shape[1:])
        save(name, spot.at[:, :, co["c"]], to_ref.at[:, :, :, own_rows])
        to_core(name, spot.at[:, :, 1 - co["c"]], to_ref.at[:, :, :, peer_rows])

    def columns_of(ref):
        return lambda n: ref[:, n * rows_here : (n + 1) * rows_here].astype(jnp.float32)

    def by_rows(size, body):
        def run(n, _):
            body(pl.ds(pl.multiple_of(n * size, size), size))
            return 0

        lax.fori_loop(0, rows_here // size, run, 0)

    def gain(row):
        return gains[row : row + 1, :]

    def norm_into(source, out, row):
        def body(span):
            out[span, :] = norm_block(source[span, :], gain(row), gain(row + 1)).astype(LOW)

        by_rows(64, body)

    def embed():
        owned = [
            w_vec[t // 2, t % 2, d // 4, d // 2 % 2, d % 2] for d in range(8) for t in range(4)
        ]
        gains[...] = jnp.transpose(jnp.concatenate(owned))[: gains.shape[0]]
        save("vec", gains, o_vec)
        half = edge_mine.shape[0] // 2
        for d in range(8):
            for a in range(2):
                at = (d // 4, d // 2 % 2, d % 2)
                left = w_edge[(a, 0) + at].astype(jnp.float32)
                right = w_edge[(a, 1) + at].astype(jnp.float32)
                spot = pl.ds((2 * d + a) * 2 * half, 2 * half)
                embed_w[spot, :] = jnp.concatenate([left[:half], right[:half]]).astype(LOW)
                head_w[spot, :] = jnp.concatenate([left[half:], right[half:]]).astype(LOW)
        save("head", head_w, o_head)
        for q in range(2):
            origin = (column * 2 + co["z"], co["c"] * 2 + q)
            same = jnp.logical_and(origin[0] == me[0], origin[1] == me[1])

            @pl.when(same)
            def _():
                pltpu.make_async_copy(patch, pixels.at[q], patch_sem.at[2]).wait()

            @pl.when(jnp.logical_not(same))
            def _():
                pltpu.make_async_remote_copy(
                    src_ref=patch,
                    dst_ref=pixels.at[q],
                    send_sem=patch_sem.at[3],
                    recv_sem=patch_sem.at[q],
                    device_id=me,
                    device_id_type=MESH,
                ).wait_recv()

        save("mask", pixels.at[:, :, width:], o_mask)
        quarter = pixels.shape[1]

        def pixel_columns(n):
            cols = pixels[:, :, n * rows_here : (n + 1) * rows_here].astype(jnp.float32)
            return cols.reshape(rows_here, rows_here)

        turn("pixels", pixel_columns, o_pixels)
        for q in range(2):
            hide = pixels[q, :, width : width + 1].astype(jnp.float32)
            hide = jnp.where(teaching, 0.0, hide)
            rows = pl.ds(q * quarter, quarter)
            x[rows, :] = (
                dot(pixels[q, :, :width], embed_w[...]) * (1.0 - hide) + hide * gain(last_row + 2)
            )

    def peer_copy(l, t):
        return pltpu.make_async_remote_copy(
            src_ref=qkv.at[t, :, 128:640],
            dst_ref=peer.at[l, t],
            send_sem=peer_sem.at[0, l, t],
            recv_sem=peer_sem.at[1, l, t],
            device_id=flip(co, "c"),
            device_id_type=MESH,
        )

    settled = []

    def wait_saves(*names):
        for name in names:
            if name in saves:
                saves.pop(name).wait()
                if name in shared:
                    shared[name].wait_send()
                    settled.append(shared.pop(name))

    def project(l):
        save(("x", l), x, o_x.at[l])
        norm_into(x, normed, 4 * l)
        for t in range(4):
            weight = matrix(w_attn[l, t // 2, t % 2])
            qkv[t] = dot(normed[...], weight).astype(LOW)
            peer_copy(l, t).start()
            save(("qkv", l, t), qkv.at[t], o_qkv.at[l, t])
        turn(("normed", l), columns_of(normed), o_normed.at[l])

    def attend(l, first, last):
        if first == 0:
            for t in range(4):
                peer_copy(l, t).wait_recv()
            lse[...] = jnp.zeros_like(lse)
        size = rows_here

        def body(n, _):
            t = n // (rows_here // size)
            span = pl.ds(pl.multiple_of(n % (rows_here // size) * size, size), size)
            low = low_lanes((size, 128))
            lane = lax.broadcasted_iota(jnp.int32, (size, 128), 1)
            zero = jnp.zeros((size, 128), LOW)
            outs = []
            total = lse[span, :]
            for j in range(3):
                q_at = 0 if j < 2 else 384
                k_at = 128 if j < 2 else 512
                v_at = 256 if j < 2 else 384
                query = qkv[t, span, q_at : q_at + 128] * jnp.asarray(HEAD**-0.5, LOW)
                query = jnp.where(low, query, zero) if j != 1 else jnp.where(low, zero, query)
                scores = jnp.concatenate(
                    [
                        dot_nt(query, qkv[t, :, k_at : k_at + 128]),
                        dot_nt(query, peer[l, t, :, k_at - 128 : k_at]),
                    ],
                    axis=1,
                )
                peak = jnp.max(scores, axis=1, keepdims=True)
                raised = jnp.exp(scores - peak)
                summed = jnp.sum(raised, axis=1, keepdims=True)
                weights = raised.astype(LOW)
                out = dot(weights[:, :rows_here], qkv[t, :, v_at : v_at + 128])
                out = out + dot(weights[:, rows_here:], peer[l, t, :, v_at - 128 : v_at])
                outs.append(out / summed)
                total = jnp.where(lane == 3 * t + j, peak + jnp.log(summed), total)
            lse[span, :] = total
            ctx[t, span, :128] = jnp.where(low, 0.0, outs[1]).astype(LOW)
            ctx[t, span, 128:] = jnp.where(low, outs[0], outs[2]).astype(LOW)
            return 0

        each = rows_here // size
        lax.fori_loop(first * each, last * each, body, 0)
        if last == 4:
            save(("lse", l), lse, o_lse.at[l])
            share(("ctx", l), ctx, o_ctx.at[l], (ALL,))
            save(("peer", l), peer.at[l], o_peer.at[l])

    def out_project(l):
        mid[...] = x[...]

        def body(t, _):
            weight = matrix(w_attn[l, t // 2, t % 2, :, :, :, :, 512:])
            mid[...] += dot_nt(ctx[t], weight)
            return 0

        lax.fori_loop(0, 4, body, 0)
        save(("mid", l), mid, o_mid.at[l])
        norm_into(mid, hid, 4 * l + 2)
        turn(("hid", l), columns_of(hid), o_hid.at[l])

    def expand(l, first, last):
        def body(n, _):
            t = n // 3
            cols = pl.ds(pl.multiple_of(n % 3 * 256, 256), 256)
            weight = matrix(w_mlp[l, 0, t // 2, t % 2, :, :, :, :, cols])
            upward = dot(hid[...], weight)
            share = 0.5 + 0.5 * lax.erf(upward * 0.5**0.5)
            act[t, :, cols] = (upward * share).astype(LOW)
            bell = jnp.exp(-0.5 * upward * upward) * (2.0 * jnp.pi) ** -0.5
            slope[t, :, cols] = (share + upward * bell).astype(LOW)
            return 0

        lax.fori_loop(3 * first, 3 * last, body, 0)
        if last == 4:
            share(("act", l), act, o_act.at[l], (ALL,))
            save(("slope", l), slope, o_slope.at[l])

    def contract(l, first, last):
        if first == 0:
            if l < layers - 1:
                wait_saves(("x", l))
            x[...] = mid[...]

        def body(t, _):
            x[...] += dot_nt(act[t], matrix(w_mlp[l, 1, t // 2, t % 2]))
            return 0

        lax.fori_loop(first, last, body, 0)

    def stat_copy(l):
        return pltpu.make_async_remote_copy(
            src_ref=stat.at[l, 0],
            dst_ref=stat.at[l, 1],
            send_sem=stat_sem.at[0, l],
            recv_sem=stat_sem.at[1, l],
            device_id=flip(co, "c"),
            device_id_type=MESH,
        )

    def to_student(n, source, to_ref):
        return pltpu.make_async_remote_copy(
            src_ref=source,
            dst_ref=to_ref,
            send_sem=stat_sem.at[0, layers + n],
            recv_sem=stat_sem.at[1, layers + n],
            device_id=flip(co, "a"),
            device_id_type=MESH,
        )

    spans = [pl.ds(n * (rows_here // 2), rows_here // 2) for n in range(2)]

    def target_copies():
        copies = [to_student(n, target.at[span], target.at[span]) for n, span in enumerate(spans)]
        return copies + [to_student(2, early, early), to_student(3, final_stat, final_stat)]

    def column_sums(ref, spot):
        spot[...] = jnp.zeros_like(spot)

        def body(span):
            value = ref[span, :]
            spot[0:1] += jnp.sum(value, axis=0, keepdims=True)
            spot[1:2] += jnp.sum(value * value, axis=0, keepdims=True)

        by_rows(64, body)

    def normalizer(l):
        stat_copy(l).start()
        stat_copy(l).wait()
        both = (stat[l, 0] + stat[l, 1]) / (2 * rows_here)
        average = both[0:1]
        spread = both[1:2] - average * average
        return average, lax.rsqrt(spread + inst_epsilon) / layers

    def teach(l):
        @pl.when(teaching)
        def _():
            column_sums(x, stat.at[l, 0])
            average, scale = normalizer(l)

            def mix(span):
                value = (x[span, :] - average) * scale
                if l > 0:
                    value = value + work[span, :]
                work[span, :] = value
                if l == layers - 2:
                    early[span, :] = value.astype(LOW)

            by_rows(64, mix)
            if l == layers - 2:
                target_copies()[2].start()

    def center_last():
        @pl.when(teaching)
        def _():
            column_sums(mid, final_stat)
            final_stat[2:3] = final_stat[0:1] / rows_here

    def contract_last():
        l = layers - 1

        @pl.when(teaching)
        def _():
            center = final_stat[2:3]
            for n, span in enumerate(spans):
                value = mid[span, :]
                for t in range(4):
                    value = value + dot_nt(act[t, span], matrix(w_mlp[l, 1, t // 2, t % 2]))
                x[span, :] = value
                target[span, :] = (value - center).astype(LOW)
                target_copies()[n].start()
            column_sums(x, stat.at[l, 0])
            average, scale = normalizer(l)
            final_stat[0:1] = scale
            final_stat[1:2] = (center - average) * scale
            copies = target_copies()
            copies[3].start()
            for copy in copies:
                copy.wait_send()

        @pl.when(jnp.logical_not(teaching))
        def _():
            contract(l, 0, 4)

    def finish():
        save("last", x, o_last)
        sums[...] = jnp.zeros_like(sums)
        norm_into(x, normed, last_row)
        turn("final", columns_of(normed), o_final)

        @pl.when(jnp.logical_not(teaching))
        def _():
            work[...] = dot(normed[...], head_w[...]) + gain(last_row + 3)
            copies = target_copies()
            copies[2].wait_recv()

            def add_early(span):
                work[span, :] = work[span, :] - early[span, :].astype(jnp.float32)

            by_rows(64, add_early)
            copies[0].wait_recv()
            copies[1].wait_recv()
            copies[3].wait_recv()

            def body(n, _):
                span = pl.ds(pl.multiple_of(n * 64, 64), 64)
                part = pl.ds(pl.multiple_of(n % 3 * 64, 64), 64)
                masked = pixels[n // 3, part, width : width + 1].astype(jnp.float32)
                aim = target[span, :].astype(jnp.float32) * final_stat[0:1] + final_stat[1:2]
                offset = work[span, :] - aim
                size = jnp.abs(offset)
                loss = jnp.where(size < 1.0, 0.5 * offset * offset, size - 0.5) * masked
                pull = jnp.clip(offset, -1.0, 1.0) * masked * width**-0.5
                sums[0:1] += jnp.sum(pull, axis=0, keepdims=True)
                sums[1:2] += jnp.sum(loss, axis=0, keepdims=True)
                target[span, :] = pull.astype(LOW)
                return 0

            lax.fori_loop(0, rows_here // 64, body, 0)

        share("dlow", target, o_dlow, ())
        save("sums", sums, o_sums)

    for r in range(2):
        to = (column * 2 + co["a"], 2 * r + co["c"])
        same = jnp.logical_and(to[0] == me[0], to[1] == me[1])
        spot = pixels.at[co["z"]]

        @pl.when(same)
        def _():
            pltpu.make_async_copy(patch, spot, patch_sem.at[2]).start()

        @pl.when(jnp.logical_not(same))
        def _():
            pltpu.make_async_remote_copy(
                src_ref=patch,
                dst_ref=spot,
                send_sem=patch_sem.at[3 + r],
                recv_sem=patch_sem.at[co["z"]],
                device_id=to,
                device_id_type=MESH,
            ).start()

    def save_weights(slot):
        def run():
            l, k = (slot - 1) // 3, (slot - 1) % 3
            if k == 0:
                save(("attn", l), w_attn.at[l], o_attn.at[l])
            else:
                save(("mlp", l, k), w_mlp.at[l, k - 1], o_mlp.at[l, k - 1])

        return run

    plan = {0: [embed]}
    for l in range(layers):
        repeat = l > 0

        def start(l=l):
            if l > 0:
                for t in range(4):
                    peer_copy(l - 1, t).wait_send()
                wait_saves(*[("qkv", l - 1, t) for t in range(4)])
            project(l)

        def begin_attend(l=l):
            if l > 0:
                wait_saves(("lse", l - 1), ("ctx", l - 1))
            attend(l, 0, 2)

        def begin_out(l=l):
            if l > 0:
                wait_saves(("mid", l - 1))
            out_project(l)

        def begin_expand(l=l):
            if l > 0:
                wait_saves(("act", l - 1), ("slope", l - 1))
            expand(l, 0, 2)

        plan[3 * l + 1] = [
            save_weights(3 * l + 1),
            start,
            begin_attend,
            lambda l=l: attend(l, 2, 4),
            begin_out,
        ]
        plan[3 * l + 2] = [
            save_weights(3 * l + 2),
            begin_expand,
            lambda l=l: expand(l, 2, 4),
        ]
        plan[3 * l + 3] = [
            save_weights(3 * l + 3),
            lambda l=l: contract(l, 0, 2),
            lambda l=l: contract(l, 2, 4),
            lambda l=l: teach(l),
        ]
    plan[3 * layers - 1].append(center_last)
    wait_last = lambda: wait_saves(("x", layers - 1))
    plan[3 * layers] = [wait_last, contract_last, save_weights(3 * layers)]
    final_slot = 3 * layers
    begin(0)
    begin(1)
    for wave in range(final_slot + 5):
        begin(wave + 2)
        step(wave, 4)
        todo = list(plan.get(wave - 4, []))
        for s in range(4):
            step(wave, s)
            if todo:
                todo.pop(0)()
        while todo:
            todo.pop(0)()
    finish()
    wait_saves(*list(saves))
    for copy in settled:
        copy.wait_recv()
    for t in range(4):
        peer_copy(layers - 1, t).wait_send()
    for r in range(2):
        to = (column * 2 + co["a"], 2 * r + co["c"])
        same = jnp.logical_and(to[0] == me[0], to[1] == me[1])

        @pl.when(jnp.logical_not(same))
        def _():
            pltpu.make_async_remote_copy(
                src_ref=patch,
                dst_ref=pixels.at[0],
                send_sem=patch_sem.at[3 + r],
                recv_sem=patch_sem.at[0],
                device_id=me,
                device_id_type=MESH,
            ).wait_send()

    for copy in sent:
        copy.wait_send()


def forward_all(*parts):
    layers, rows, width = parts[0].shape
    cube = (2, 2, 2, 2, 2)
    here = 2 * parts[8].shape[0]
    f32 = jnp.float32
    attn = (layers,) + cube + (rows, width)
    mlp = (layers, 2) + cube + (rows, width)
    tall = (here, width)
    turned = (2, 2, rows, 2 * here)
    quarter = parts[8].shape[0]
    outs = (
        shape_of(attn),
        shape_of(mlp),
        shape_of((width, width)),
        shape_of((16, width), f32),
        shape_of((layers,) + tall, f32),
        shape_of((layers,) + tall, f32),
        shape_of((layers,) + turned),
        shape_of((layers, 4) + tall),
        shape_of((layers, 4, here, 512)),
        shape_of((layers, 4, 2 * here, 256)),
        shape_of((layers,) + turned),
        shape_of((layers, 4, 2 * here, width)),
        shape_of((layers, 4) + tall),
        shape_of((layers, here, 128), f32),
        shape_of(tall, f32),
        shape_of(turned),
        shape_of(turned),
        shape_of((2 * here, width)),
        shape_of((8, width), f32),
        shape_of((2, quarter, 128)),
    )
    scratch = [
        pltpu.VMEM(attn, LOW),
        pltpu.VMEM(mlp, LOW),
        pltpu.VMEM(cube + parts[4].shape, LOW),
        pltpu.VMEM(cube + parts[6].shape, f32),
        pltpu.VMEM((2,) + parts[8].shape, LOW),
        pltpu.VMEM((width, width), LOW),
        pltpu.VMEM((width, width), LOW),
        pltpu.VMEM((16, width), f32),
        pltpu.VMEM(tall, f32),
        pltpu.VMEM(tall, f32),
        pltpu.VMEM(tall, LOW),
        pltpu.VMEM((4,) + tall, LOW),
        pltpu.VMEM((layers, 4, here, 512), LOW),
        pltpu.VMEM((4, here, 256), LOW),
        pltpu.VMEM(tall, LOW),
        pltpu.VMEM((4,) + tall, LOW),
        pltpu.VMEM((4,) + tall, LOW),
        pltpu.VMEM((here, 128), f32),
        pltpu.VMEM(tall, f32),
        pltpu.VMEM(tall, LOW),
        pltpu.VMEM((layers, 2, 8, width), f32),
        pltpu.VMEM((8, width), f32),
        pltpu.VMEM((2, 2, 2, 2, rows, here), LOW),
        pltpu.VMEM(tall, LOW),
        pltpu.VMEM((8, width), f32),
    ]
    count = 2 + 3 * layers
    sems = [
        DMA((count,)),
        DMA((count, 3, 5)),
        DMA((count, 3, 5)),
        DMA((5,)),
        DMA((2, layers, 4)),
        DMA((2, layers + 4)),
        DMA((48,)),
        DMA((2, 16)),
    ]
    return pl.pallas_call(
        forward_kernel,
        out_shape=outs,
        in_specs=[ANY] * 9,
        out_specs=(ANY,) * len(outs),
        scratch_shapes=scratch + sems,
        compiler_params=pltpu.CompilerParams(
            collective_id=0, has_side_effects=True, vmem_limit_bytes=60 * 2**20
        ),
    )(*parts)


def backward_kernel(*refs):
    (w_attn, w_mlp, h_head, h_gains, h_x, h_mid, h_normed, h_qkv, h_peer, h_ctx) = refs[:10]
    (h_hid, h_act, h_slope, h_lse, h_last, h_final, h_pixels, h_dlow, h_sums, h_mask) = refs[10:20]
    o_attn, o_mlp, o_head, o_patch, o_vec = refs[20:25]
    (head, gains, x, normed_t, hid_t, qkv, peer, ctx, lse, attn, act) = refs[25:36]
    (down, up, slope, tall_t, tall, mask, sums, g, acc, low_g, turned, dffn_t) = refs[36:48]
    (datt_t, dup, dctx, dqkv, dkv_out, dkv_in, query, pull, score_row, vec_grad) = refs[48:58]
    vec_turned = refs[58]
    rest = refs[59:]
    co = coords()
    layers = w_attn.shape[0]
    last_row = 4 * layers
    here, width = g.shape
    other_core = flip(co, "c")
    own_rows, peer_rows = pl.ds(0, here), pl.ds(here, here)
    barrier = pltpu.get_barrier_semaphore()
    for k in "azyxc":
        pl.semaphore_signal(barrier, inc=1, device_id=flip(co, k), device_id_type=MESH)

    kinds = {}
    spot = 0
    for name, parts in (("D", 3), ("U", 3), ("A", 3), ("H", 2), ("P", 2), ("V", 3)):
        kinds[name] = dict(mine=rest[spot], part=[], parts=parts, name=name)
        spot += 1
        for p in range(parts):
            kinds[name]["part"].append(rest[spot : spot + 3])
            spot += 3
    items = {}
    targets = [("H", 0, o_head)]
    for l in reversed(range(layers)):
        targets += [("D", l, o_mlp.at[l, 1]), ("U", l, o_mlp.at[l, 0]), ("A", l, o_attn.at[l])]
    targets += [("P", 0, o_patch), ("V", 0, o_vec)]
    for n, (name, l, target) in enumerate(targets):
        items[name, l] = dict(kinds[name], n=n, l=l, target=target, last=rest[spot], sent=[])
        spot += 1
    load_sem, send_sem, recv_sem, out_sem, core_sem, credit = rest[spot:]
    own = {q: co[q] for q in "zyx"}

    def pick(fixed, span):
        return tuple(fixed.get(k, ALL) for k in "azyx") + (span,)

    def span_of(item, p):
        size = item["mine"].shape[4] // item["parts"]
        return pl.ds(p * size, size)

    def part_copy(item, p, s):
        order = ORDERS[p][::-1]
        k = order[s]
        fixed = {q: co[q] for q in order[:s]}
        return pltpu.make_async_remote_copy(
            src_ref=item["mine"].at[pick({**fixed, k: 1 - co[k]}, span_of(item, p))],
            dst_ref=item["part"][p][s].at[pick({q: 0 for q in order[: s + 1]}, ALL)],
            send_sem=send_sem.at[item["n"], p, s],
            recv_sem=recv_sem.at[item["n"], p, s],
            device_id=flip(co, k),
            device_id_type=MESH,
        )

    def last_hop(item, p):
        return pltpu.make_async_remote_copy(
            src_ref=item["mine"].at[pick({**own, "a": 1}, span_of(item, p))],
            dst_ref=item["last"].at[span_of(item, p)],
            send_sem=send_sem.at[item["n"], p, 3],
            recv_sem=recv_sem.at[item["n"], p, 3],
            device_id=flip(co, "a"),
            device_id_type=MESH,
        )

    def out_copy(item):
        return pltpu.make_async_copy(
            item["mine"].at[pick({**own, "a": 0}, ALL)], item["target"], out_sem.at[item["n"]]
        )

    def begin(item, s):
        if s == 0 and item["name"] in "DUA" and item["l"] < layers - 1:
            for q in range(3):
                pl.semaphore_wait(credit.at["DUA".index(item["name"]), q], 1)
        for p in range(item["parts"]):
            begin_part(item, p, s)

    def begin_part(item, p, s):
        copy = part_copy(item, p, s)
        copy.start()
        item["sent"].append(copy)

    def gather_part(item, p, s):
        part_copy(item, p, s).wait_recv()
        done = ORDERS[p][::-1][: s + 1]
        left = [k for k in "azyx" if k not in done]
        mine, part, span = item["mine"], item["part"][p][s], span_of(item, p)

        def body(n, _):
            at = {}
            for k in reversed(left):
                at[k] = n % 2
                n = n // 2
            there = tuple(0 if k in done else at[k] for k in "azyx")
            spot = tuple(co[k] if k in done else at[k] for k in "azyx") + (span,)
            mine[spot] = mine[spot] + part[there]
            return 0

        lax.fori_loop(0, 2 ** len(left), body, 0)

    def advance(name, l, s):
        item = items[name, l]
        for p in range(item["parts"]):
            gather_part(item, p, s)
            if s < 2:
                begin_part(item, p, s + 1)
            else:
                last_hop(item, p).start()
        if s < 2:
            return
        if name in "DUA" and l > 0:
            for q, k in enumerate("zyx"):
                pl.semaphore_signal(
                    credit.at["DUA".index(name), q],
                    inc=1,
                    device_id=flip(co, k),
                    device_id_type=MESH,
                )
        out_copy(item).start()

    def settle(name, l):
        item = items[name, l]
        for copy in item["sent"]:
            copy.wait_send()
        for p in range(item["parts"]):
            last_hop(item, p).wait_send()
        out_copy(item).wait()

    loads = {}
    counter = iter(range(96))

    def load_copy(n, ends):
        return pltpu.make_async_copy(*ends(), load_sem.at[n])

    def fetch(name, ends):
        loads[name] = (next(counter), ends)
        load_copy(*loads[name]).start()

    def need(*names):
        for name in names:
            load_copy(*loads.pop(name)).wait()

    core_counter = iter(range(48))
    core = {}

    def to_core(name, source, to_ref):
        n = next(core_counter)
        core[name] = pltpu.make_async_remote_copy(
            src_ref=source,
            dst_ref=to_ref,
            send_sem=core_sem.at[0, n],
            recv_sem=core_sem.at[1, n],
            device_id=other_core,
            device_id_type=MESH,
        )
        core[name].start()

    def by_rows(size, body):
        def run(n, _):
            body(pl.ds(pl.multiple_of(n * size, size), size))
            return 0

        lax.fori_loop(0, here // size, run, 0)

    def turn(name, source, to_ref):
        for n in range(2):
            cols = source[:, n * here : (n + 1) * here].astype(jnp.float32)
            turned[n] = jnp.transpose(cols).astype(LOW).reshape(turned.shape[1:])
        to_ref[:, :, :, :here] = turned[:, :, co["c"]]
        to_core(name, turned.at[:, :, 1 - co["c"]], to_ref.at[:, :, :, here:])

    def norm_back(values, row):
        gain = gains[row : row + 1, :]

        def body(span):
            value = values[span, :]
            average = jnp.mean(value, axis=-1, keepdims=True)
            centered = value - average
            spread = jnp.mean(centered * centered, axis=-1, keepdims=True)
            scale = lax.rsqrt(spread + norm_epsilon)
            hat = centered * scale
            dy = acc[span, :]
            vec_grad[row : row + 1, :] += jnp.sum(dy * hat, axis=0, keepdims=True)
            vec_grad[row + 1 : row + 2, :] += jnp.sum(dy, axis=0, keepdims=True)
            u = dy * gain
            mean_u = jnp.mean(u, axis=-1, keepdims=True)
            mean_uh = jnp.mean(u * hat, axis=-1, keepdims=True)
            g[span, :] += scale * (u - mean_u - hat * mean_uh)

        by_rows(64, body)

    def attend_back(t):
        low = low_lanes((here, 128))
        zero = jnp.zeros((here, 128), LOW)
        scale = jnp.asarray(HEAD**-0.5, LOW)
        first = qkv[t, :, 0:128] * scale
        query[0] = jnp.where(low, first, zero)
        query[1] = jnp.where(low, zero, first)
        query[2] = jnp.where(low, qkv[t, :, 384:512] * scale, zero)
        pull[0] = jnp.where(low, dctx[:, 128:256], zero)
        pull[1] = jnp.where(low, zero, dctx[:, 0:128])
        pull[2] = jnp.where(low, zero, dctx[:, 128:256])
        one = ctx[t, own_rows, 0:128].astype(jnp.float32)
        two = ctx[t, own_rows, 128:256].astype(jnp.float32)
        lane = lax.broadcasted_iota(jnp.int32, (here, 128), 1)
        dots = jnp.zeros((here, 128), jnp.float32)
        for j, value in enumerate((two, one, two)):
            row_sum = jnp.sum(value * pull[j].astype(jnp.float32), axis=1, keepdims=True)
            dots = jnp.where(lane == j, row_sum, dots)
        dots = jnp.transpose(dots)
        score_row[0:8, :] = dots[0:8]
        logs = jnp.transpose(lse[...])
        log_rows = jnp.zeros((8, here), jnp.float32)
        for u in range(4):
            log_rows = jnp.where(t == u, logs[3 * u : 3 * u + 8], log_rows)
        score_row[8:16, :] = log_rows
        pair = (2 * here, 128)
        groups = (
            (128, 256, query[0:2].reshape(pair), pull[0:2].reshape(pair), (0, 1)),
            (512, 384, query[2], pull[2], (2,)),
        )
        half = lax.broadcasted_iota(jnp.int32, (128, here), 0) < HEAD
        grads = [None, None]
        for source, shift in ((peer, 128), (qkv, 0)):
            outs = []
            for i, (k_at, v_at, asked, pulled, heads) in enumerate(groups):
                key = source[t, :, k_at - shift : k_at - shift + 128]
                value = source[t, :, v_at - shift : v_at - shift + 128]
                logs = jnp.concatenate([score_row[8 + j : 9 + j, :] for j in heads], axis=1)
                dots = jnp.concatenate([score_row[j : j + 1, :] for j in heads], axis=1)
                probs = jnp.exp(dot_nt(key, asked) - logs)
                grad_scores = (probs * (dot_nt(value, pulled) - dots)).astype(LOW)
                outs.append(dot(grad_scores, asked))
                outs.append(dot(probs.astype(LOW), pulled))
                back = dot(jnp.transpose(key.astype(jnp.float32)).astype(LOW), grad_scores)
                grads[i] = back if grads[i] is None else grads[i] + back
            for i, out in zip((0, 1, 3, 2), outs):
                cols = slice(128 * i, 128 * i + 128)
                if shift:
                    dkv_out[t, :, cols] = out.astype(LOW)
                else:
                    dqkv[t, own_rows, 128 * i + 128 : 128 * i + 256] = out.astype(LOW)
        first = jnp.where(half, grads[0][:, :here], grads[0][:, here:])
        dqkv[t, own_rows, 0:128] = (jnp.transpose(first) * HEAD**-0.5).astype(LOW)
        second = jnp.transpose(grads[1]) * HEAD**-0.5
        keep = dqkv[t, own_rows, 384:512].astype(jnp.float32)
        dqkv[t, own_rows, 384:512] = jnp.where(low, second, keep).astype(LOW)

    def blocks(value):
        return value.reshape(2, 2, -1, value.shape[-1])

    steps = [(l, t) for l in reversed(range(layers)) for t in range(4)]

    def fetch_act(n):
        if n < len(steps):
            l, t = steps[n]
            fetch(("act", l, t), lambda: (h_act.at[l, t], act.at[n % 2]))

    def fetch_mlp(n):
        if n < len(steps):
            l, t = steps[n]
            fetch(("up", l, t), lambda: (w_mlp.at[l, 0, t // 2, t % 2], up.at[n % 2]))
            fetch(("down", l, t), lambda: (w_mlp.at[l, 1, t // 2, t % 2], down.at[n % 2]))
            fetch(("slope", l, t), lambda: (h_slope.at[l, t], slope.at[n % 2]))

    def fetch_late(l):
        fetch(("qkv", l), lambda: (h_qkv.at[l], qkv))
        fetch(("peer", l), lambda: (h_peer.at[l], peer))
        fetch(("ctx", l), lambda: (h_ctx.at[l], ctx))
        fetch(("lse", l), lambda: (h_lse.at[l], lse))
        fetch(("attn", l), lambda: (w_attn.at[l], attn))
        fetch(("normed", l), lambda: (h_normed.at[l], normed_t))

    def fetch_hid(l):
        fetch(("hid", l), lambda: (h_hid.at[l], hid_t))
        fetch(("mid", l), lambda: (h_mid.at[l], x))

    def edge_blocks(mine, value):
        size = value.shape[2] // 4
        for t in range(4):
            block = value[:, :, size * t : size * (t + 1)]
            pad = jnp.zeros((2, 2, mine.shape[4] - size, width), jnp.float32)
            mine[t // 2, t % 2] = jnp.concatenate([block, pad], axis=2).astype(LOW)

    def head_back():
        fetch("dlow", lambda: (h_dlow, tall))
        fetch("head", lambda: (h_head, head))
        fetch("last", lambda: (h_last, x))
        fetch("gains", lambda: (h_gains, gains))
        fetch("final", lambda: (h_final, tall_t))
        vec_grad[...] = jnp.zeros_like(vec_grad)
        dqkv[...] = jnp.zeros_like(dqkv)
        g[...] = jnp.zeros_like(g)
        need("dlow", "head")
        acc[...] = dot_nt(tall[own_rows, :], head[...])
        fetch_mlp(0)
        fetch_act(0)
        fetch_act(1)
        fetch_mlp(1)
        need("last", "gains")
        norm_back(x, last_row)
        fetch_hid(layers - 1)
        need("final")
        value = blocks(dot(matrix(tall_t[...]), tall[...]))

        edge_blocks(items["H", 0]["mine"], value)
        fetch_late(layers - 1)
        fetch("sums", lambda: (h_sums, sums))
        fetch("mask", lambda: (h_mask, mask))
        fetch("pixels", lambda: (h_pixels, tall_t))

    def student():
        begin(items["H", 0], 0)
        for l in reversed(range(layers)):
            top = l == layers - 1
            low_g[...] = g[...].astype(LOW)
            if not top:
                core["datt", l + 1].wait_send()
            turn(("dffn", l), low_g, dffn_t)

            def widen(t, l=l):
                n = steps.index((l, t))
                need(("down", l, t), ("slope", l, t), ("up", l, t))
                pulled = dot(low_g[...], matrix(down[n % 2])) * slope[n % 2].astype(jnp.float32)
                dup[t, own_rows, :] = pulled.astype(LOW)
                to_core(("dup", l, t), dup.at[t, own_rows], dup.at[t, peer_rows])
                back = dot_nt(dup[t, own_rows, :], matrix(up[n % 2]))
                acc[...] = back if t == 0 else acc[...] + back
                fetch_mlp(n + 2)

            if not top:
                for t in range(4):
                    core["dup", l + 1, t].wait_send()
            widen(0)
            if top:
                advance("H", 0, 0)
            core["dffn", l].wait_recv()
            if not top:
                settle("D", l + 1)
            for t in range(4):
                n = steps.index((l, t))
                need(("act", l, t))
                value = dot(matrix(dffn_t[...]), act[n % 2])
                items["D", l]["mine"][t // 2, t % 2] = blocks(value).astype(LOW)
                fetch_act(n + 2)
            if not top:
                advance("A", l + 1, 0)
            begin(items["D", l], 0)
            widen(1)
            if top:
                advance("H", 0, 1)
            widen(2)
            widen(3)
            need(("mid", l))
            norm_back(x, 4 * l + 2)
            fetch(("x", l), lambda l=l: (h_x.at[l], x))
            need(("hid", l))
            if not top:
                settle("U", l + 1)
            for t in range(4):
                core["dup", l, t].wait_recv()
                value = dot(matrix(hid_t[...]), dup[t])
                items["U", l]["mine"][t // 2, t % 2] = blocks(value).astype(LOW)
            advance("D", l, 0)
            begin(items["U", l], 0)
            if top:
                advance("H", 0, 2)
            else:
                advance("A", l + 1, 1)
            low_g[...] = g[...].astype(LOW)
            core["dffn", l].wait_send()
            turn(("datt", l), low_g, datt_t)
            need(("attn", l), ("qkv", l), ("peer", l), ("ctx", l), ("lse", l))
            if not top:
                for t in range(4):
                    core["dkv", l + 1, t].wait_send()
                    core["dqkv", l + 1, t].wait_send()
            for t in range(4):
                weight = matrix(attn[t // 2, t % 2, :, :, :, :, 512:])
                dctx[...] = dot(low_g[...], weight).astype(LOW)
                attend_back(t)
                to_core(("dkv", l, t), dkv_out.at[t], dkv_in.at[t])
                if t == 0 and not top:
                    advance("A", l + 1, 2)
                if t == 1:
                    advance("D", l, 1)
                if t == 2:
                    advance("U", l, 0)
                if t == 3:
                    advance("D", l, 2)
            for t in range(4):
                core["dkv", l, t].wait_recv()
                for i in range(4):
                    cols = slice(128 * i + 128, 128 * i + 256)
                    total = dqkv[t, own_rows, cols].astype(jnp.float32)
                    total = total + dkv_in[t, :, 128 * i : 128 * i + 128].astype(jnp.float32)
                    dqkv[t, own_rows, cols] = total.astype(LOW)
                to_core(("dqkv", l, t), dqkv.at[t, own_rows], dqkv.at[t, peer_rows])
                weight = matrix(attn[t // 2, t % 2, :, :, :, :, :640])
                back = dot_nt(dqkv[t, own_rows, :], weight)
                acc[...] = back if t == 0 else acc[...] + back
            need(("normed", l))
            core["datt", l].wait_recv()
            advance("U", l, 1)
            if not top:
                settle("A", l + 1)
            for t in range(4):
                core["dqkv", l, t].wait_recv()
                inward = dot(matrix(normed_t[...]), dqkv[t])
                outward = dot(matrix(datt_t[...]), ctx[t])
                joint = inward[:, 512:640] + outward[:, :128]
                value = jnp.concatenate([inward[:, :512], joint, outward[:, 128:]], axis=1)
                items["A", l]["mine"][t // 2, t % 2] = blocks(value).astype(LOW)
            begin(items["A", l], 0)
            advance("U", l, 2)
            need(("x", l))
            norm_back(x, 4 * l)
            if l > 0:
                fetch_hid(l - 1)
                fetch_late(l - 1)
        need("mask", "sums", "pixels")

        def embed_back(n, _):
            span = pl.ds(pl.multiple_of(n * 64, 64), 64)
            part = pl.ds(pl.multiple_of(n % 3 * 64, 64), 64)
            hide = mask[n // 3, part, 0:1].astype(jnp.float32)
            value = g[span, :]
            tall[span, :] = (value * (1.0 - hide)).astype(LOW)
            vec_grad[last_row + 2 : last_row + 3, :] += jnp.sum(value * hide, axis=0, keepdims=True)
            return 0

        lax.fori_loop(0, here // 64, embed_back, 0)
        to_core("embed", tall.at[own_rows], tall.at[peer_rows])
        vec_grad[last_row + 3 : last_row + 4, :] = sums[0:1, :]
        loss = jnp.sum(sums[1:2, :], axis=1, keepdims=True) * width**-0.5
        vec_grad[last_row + 4 : last_row + 5, :] = jnp.broadcast_to(loss, (1, width))
        full = jnp.concatenate([vec_grad[...], jnp.zeros((112, width), jnp.float32)])
        full = jnp.transpose(full)
        size = width // 32
        for d in range(8):
            for t in range(4):
                row = (4 * d + t) * size
                vec_turned[d % 2, t // 2, t % 2, d // 4, d // 2 % 2] = full[row : row + size]
        vec = items["V", 0]
        vec_in = vec_turned.at[2]
        to_core("vec", vec_turned.at[1 - co["c"]], vec_in)
        core["embed"].wait_recv()
        edge_blocks(items["P", 0]["mine"], blocks(dot(matrix(tall_t[...]), tall[...])))
        begin(items["P", 0], 0)
        core["vec"].wait_recv()
        vec["mine"][...] = vec_turned[co["c"]] + vec_turned[2]
        begin(vec, 0)
        for s in range(3):
            advance("A", 0, s)
            advance("P", 0, s)
            advance("V", 0, s)
        for name, l, unused in targets:
            if l == 0:
                settle(name, l)
        core["embed"].wait_send()
        core["vec"].wait_send()
        core["datt", 0].wait_send()
        for t in range(4):
            for name in ("dup", "dkv", "dqkv"):
                core[name, 0, t].wait_send()

    @pl.when(co["a"] == 0)
    def _():
        head_back()

    pl.semaphore_wait(barrier, 5)

    @pl.when(co["a"] == 0)
    def _():
        student()

    @pl.when(co["a"] == 1)
    def _():
        for name, l, target in targets:
            item = items[name, l]
            for p in range(item["parts"]):
                last_hop(item, p).wait_recv()
            copy = pltpu.make_async_copy(item["last"], target, out_sem.at[item["n"]])
            copy.start()
        for name, l, target in targets:
            item = items[name, l]
            pltpu.make_async_copy(item["last"], target, out_sem.at[item["n"]]).wait()


def backward_all(*parts):
    w_attn, w_mlp = parts[:2]
    layers, rows, width = w_attn.shape[0], w_attn.shape[-2], w_attn.shape[-1]
    here = parts[4].shape[1]
    f32 = jnp.float32
    tall = (here, width)
    turned = (2, 2, rows, 2 * here)
    weight = (2, 2, 2, rows, width)
    edge = 32
    small = width // 32
    scratch = [
        ((width, width), LOW),
        ((16, width), f32),
        (tall, f32),
        (turned, LOW),
        (turned, LOW),
        ((4,) + tall, LOW),
        ((4, here, 512), LOW),
        ((4, 2 * here, 256), LOW),
        ((here, 128), f32),
        ((2, 2) + weight, LOW),
        ((2, 2 * here, width), LOW),
        ((2,) + weight, LOW),
        ((2,) + weight, LOW),
        ((2,) + tall, LOW),
        (turned, LOW),
        ((2 * here, width), LOW),
        (parts[19].shape, LOW),
        ((8, width), f32),
        (tall, f32),
        (tall, f32),
        (tall, LOW),
        ((2, 2, 2, rows, here), LOW),
        (turned, LOW),
        (turned, LOW),
        ((4, 2 * here, width), LOW),
        ((here, 256), LOW),
        ((4, 2 * here, 640), LOW),
        ((4, here, 512), LOW),
        ((4, here, 512), LOW),
        ((3, here, 128), LOW),
        ((3, here, 128), LOW),
        ((16, here), f32),
        ((16, width), f32),
        ((3, 2, 2, 2, 2, small, 128), f32),
    ]
    shapes = dict(
        D=(rows, width, LOW, 3),
        U=(rows, width, LOW, 3),
        A=(rows, width, LOW, 3),
        H=(edge, width, LOW, 2),
        P=(edge, width, LOW, 2),
        V=(small, 128, f32, 3),
    )
    for count, cols, kind, pieces in shapes.values():
        scratch.append(((2, 2, 2, 2, count, cols), kind))
        for p in range(pieces):
            order = ORDERS[p][::-1]
            for s in range(3):
                dims = tuple(1 if k in order[: s + 1] else 2 for k in "azyx")
                scratch.append((dims + (count // pieces, cols), kind))
    names = "H" + "DUA" * layers + "PV"
    for name in names:
        count, cols, kind, pieces = shapes[name]
        scratch.append(((count, cols), kind))
    count = len(names)
    return pl.pallas_call(
        backward_kernel,
        out_shape=(
            shape_of((layers, rows, width)),
            shape_of((layers, 2, rows, width)),
            shape_of((edge, width)),
            shape_of((edge, width)),
            shape_of((small, 128), f32),
        ),
        in_specs=[ANY] * len(parts),
        out_specs=(ANY,) * 5,
        scratch_shapes=[pltpu.VMEM(*s) for s in scratch]
        + [
            DMA((96,)),
            DMA((count, 3, 4)),
            DMA((count, 3, 4)),
            DMA((count,)),
            DMA((2, 48)),
            pltpu.SemaphoreType.REGULAR((3, 3)),
        ],
        compiler_params=pltpu.CompilerParams(
            collective_id=1, has_side_effects=True, vmem_limit_bytes=60 * 2**20
        ),
    )(*parts)


def total_kernel(value, out, held, send_sem, recv_sem):
    co = coords()
    d, t = ident(co)
    near = [(d - d % 2 + (d + k // 4) % 2, (t + k) % 4) for k in range(1, 8)]
    far = [((d + 2 * k) % 8, t) for k in range(1, 4)]
    barrier = pltpu.get_barrier_semaphore()
    for to in near + far:
        pl.semaphore_signal(barrier, inc=1, device_id=to, device_id_type=MESH)
    pl.semaphore_wait(barrier, len(near) + len(far))
    total = value[...]
    n = 0
    for s, group in enumerate((near, far)):
        held[0, s] = total
        copies = []
        for to in group:
            copy = pltpu.make_async_remote_copy(
                src_ref=held.at[0, s],
                dst_ref=held.at[1, n],
                send_sem=send_sem.at[n],
                recv_sem=recv_sem.at[n],
                device_id=to,
                device_id_type=MESH,
            )
            copy.start()
            copies.append((copy, n))
            n += 1
        for copy, spot in copies:
            copy.wait()
            total = total + held[1, spot]
    out[...] = total


def total_all(value):
    return pl.pallas_call(
        total_kernel,
        out_shape=shape_of(value.shape, jnp.float32),
        in_specs=[pl.BlockSpec(memory_space=pltpu.VMEM)],
        out_specs=pl.BlockSpec(memory_space=pltpu.VMEM),
        scratch_shapes=[pltpu.VMEM((2, 10) + value.shape, jnp.float32), DMA((10,)), DMA((10,))],
        compiler_params=pltpu.CompilerParams(collective_id=2, has_side_effects=True),
    )(value)


def per_device(
    patches,
    mask,
    edge,
    attn_w,
    mlp_w,
    vecs,
    edge_m,
    edge_v,
    attn_m,
    attn_v,
    mlp_m,
    mlp_v,
    vecs_m,
    vecs_v,
    teacher_edge,
    teacher_attn,
    teacher_mlp,
    teacher_vecs,
):
    layer_count, rows, kinds, block = attn_w.shape
    wide = mlp_w.shape[3]
    width = patches.shape[2]
    quarter = patches.shape[0]
    edge_rows = edge.shape[1]
    vec_count, vec_cols = vecs.shape
    last_row = 4 * layer_count
    teaching = lax.axis_index(TENSOR) >= 2
    dp_size = lax.axis_size(DP)

    def pack(own_edge, own_attn, own_mlp, own_vecs):
        return (
            pack_heads(own_attn.astype(LOW)),
            jnp.swapaxes(own_mlp.astype(LOW), 1, 2),
            own_edge.astype(LOW).reshape(2 * edge_rows, width),
            jnp.pad(own_vecs.T, ((0, 0), (0, 128 - vec_count))),
        )

    student = (edge, attn_w, mlp_w, vecs)
    teacher = (teacher_edge, teacher_attn, teacher_mlp, teacher_vecs)
    mine = pack(*[jnp.where(teaching, right, left) for left, right in zip(student, teacher)])
    other = pack(*[jnp.where(teaching, left, right) for left, right in zip(student, teacher)])
    parts = [part for pair in zip(mine, other) for part in pair]
    marks = jnp.broadcast_to(mask.astype(LOW), (quarter, 128))
    parts.append(jnp.concatenate([patches.reshape(quarter, width), marks], axis=1))
    attn_grad, mlp_grad, head_grad, patch_grad, vecs_grad = backward_all(*forward_all(*parts))
    by_row = Layout(major_to_minor=(0, 1, 2, 3))
    attn_grad = with_layout_constraint(unpack_heads(attn_grad).astype(jnp.float32), by_row)
    mlp_grad = with_layout_constraint(jnp.swapaxes(mlp_grad.astype(jnp.float32), 1, 2), by_row)
    edge_grad = jnp.stack([patch_grad[:edge_rows], head_grad[:edge_rows]]).astype(jnp.float32)
    loss_total = vecs_grad[0, vec_count]
    vecs_grad = vecs_grad[:, :vec_count].T
    edge_first, edge_second, edge_update = direction(edge, edge_grad, edge_m, edge_v)
    attn_first, attn_second, attn_update = direction(attn_w, attn_grad, attn_m, attn_v)
    mlp_first, mlp_second, mlp_update = direction(mlp_w, mlp_grad, mlp_m, mlp_v)
    vecs_first, vecs_second, vecs_update = direction(vecs, vecs_grad, vecs_m, vecs_v)
    squares = jnp.stack(
        [
            matrix_squares(edge, attn_w, mlp_w),
            matrix_squares(edge_update, attn_update, mlp_update),
        ]
    )
    squares = jnp.pad(squares, ((0, 6), (0, 128 - squares.shape[1])))
    norms = jnp.sqrt(total_all(squares)[:2, : 2 + 6 * layer_count])
    trust = norms[0] / (norms[1] + adam_epsilon)
    edge_trust = trust[0:2]
    layer_trust = trust[2:].reshape(layer_count, 6)
    new_edge = edge - learn_rate * edge_trust[:, None, None] * edge_update
    new_attn = attn_w - learn_rate * layer_trust[:, None, 0:4, None] * attn_update
    new_mlp = mlp_w - learn_rate * layer_trust[:, None, 4:6, None] * mlp_update
    new_vecs = vecs - learn_rate * vecs_update
    keep_share = 1.0 - teacher_decay
    token_total = 4 * quarter * dp_size
    return (
        loss_total / token_total,
        norms,
        new_edge,
        new_attn,
        new_mlp,
        new_vecs,
        edge_first,
        edge_second[0],
        edge_second[1],
        attn_first,
        attn_second[:, :, 0:3],
        attn_second[:, :, 3],
        mlp_first,
        mlp_second,
        vecs_first,
        vecs_second,
        keep_share * (new_edge - teacher_edge),
        keep_share * (new_attn - teacher_attn),
        keep_share * (new_mlp - teacher_mlp),
        keep_share * (new_vecs - teacher_vecs),
        new_edge.astype(LOW),
        new_attn.astype(LOW),
        new_mlp.astype(LOW),
        new_vecs.astype(LOW),
    )


def solution(mesh):
    placed = (
        P(TENSOR, DP, None),
        P(TENSOR, DP),
        P(None, (DP, TENSOR), None),
        P(None, DP, None, TENSOR),
        P(None, DP, None, TENSOR),
        P(None, (DP, TENSOR)),
        P(None, (DP, TENSOR), None),
        P(None, (DP, TENSOR), None),
        P(None, DP, None, TENSOR),
        P(None, DP, None, TENSOR),
        P(None, DP, None, TENSOR),
        P(None, DP, None, TENSOR),
        P(None, (DP, TENSOR)),
        P(None, (DP, TENSOR)),
        P(None, (DP, TENSOR), None),
        P(None, DP, None, TENSOR),
        P(None, DP, None, TENSOR),
        P(None, (DP, TENSOR)),
    )
    planned = dict(mesh.shape) == {DP: 8, TENSOR: 4}
    return jax.shard_map(
        per_device if planned else per_device_general,
        mesh=mesh,
        in_specs=placed,
        out_specs=(
            P(),
            P(),
            P(None, (DP, TENSOR), None),
            P(None, DP, None, TENSOR),
            P(None, DP, None, TENSOR),
            P(None, (DP, TENSOR)),
            P(None, (DP, TENSOR), None),
            P((DP, TENSOR), None),
            P((DP, TENSOR), None),
            P(None, DP, None, TENSOR),
            P(None, DP, None, TENSOR),
            P(None, DP, TENSOR),
            P(None, DP, None, TENSOR),
            P(None, DP, None, TENSOR),
            P(None, (DP, TENSOR)),
            P(None, (DP, TENSOR)),
            P(None, (DP, TENSOR), None),
            P(None, DP, None, TENSOR),
            P(None, DP, None, TENSOR),
            P(None, (DP, TENSOR)),
            P(None, (DP, TENSOR), None),
            P(None, DP, None, TENSOR),
            P(None, DP, None, TENSOR),
            P(None, (DP, TENSOR)),
        ),
        check_vma=False,
    )
```

```python
import jax
import jax.numpy as jnp
from jax import lax
from jax.experimental import pallas as pl
from jax.experimental.layout import Layout, with_layout_constraint
from jax.experimental.pallas import tpu as pltpu
from jax.sharding import PartitionSpec as P

HEAD = 64
DP = "dp"
TENSOR = "tensor"


norm_epsilon = 1e-06
inst_epsilon = 1e-05
first_decay = 0.9
second_decay = 0.999
adam_epsilon = 1e-06
weight_decay = 0.01
learn_rate = 0.3
teacher_decay = 0.999
step_count = 10


def norm_rows(values, gain, shift):
    average = jnp.mean(values, axis=-1, keepdims=True)
    centered = values - average
    spread = jnp.mean(centered * centered, axis=-1, keepdims=True)
    return centered * lax.rsqrt(spread + norm_epsilon) * gain + shift


def exact_gelu(values):
    return jax.nn.gelu(values, approximate=False)


def fetch_edges(edge_part, vector_part):
    return (
        lax.all_gather(edge_part, (DP, TENSOR), axis=1, tiled=True),
        lax.all_gather(vector_part, (DP, TENSOR), axis=1, tiled=True),
    )


def fetch_layer(attn_part, mlp_part):
    return (
        lax.all_gather(attn_part.astype(jnp.bfloat16), DP, axis=0, tiled=True),
        lax.all_gather(mlp_part.astype(jnp.bfloat16), DP, axis=0, tiled=True),
    )


def fetch_again(attn_part, mlp_part):
    return (
        lax.all_gather(attn_part.astype(jnp.bfloat16), DP, axis=0, tiled=True),
        lax.all_gather(mlp_part.astype(jnp.bfloat16), DP, axis=0, tiled=True),
    )


def gather_rows(local_part):
    return lax.all_gather(local_part, TENSOR, axis=0, tiled=True)


def gather_grads(local_part):
    return lax.all_gather(local_part, TENSOR, axis=0, tiled=True)


def project_term(full_rows, weight):
    return jnp.einsum("sck,dk->scd", full_rows, weight, preferred_element_type=jnp.float32)


def scatter_rows(full_rows, weight):
    return lax.psum_scatter(
        project_term(full_rows, weight).astype(jnp.bfloat16),
        TENSOR,
        scatter_dimension=0,
        tiled=True,
    ).astype(jnp.float32)


def scatter_grads(full_rows, weight):
    return lax.psum_scatter(
        project_term(full_rows, weight).astype(jnp.bfloat16),
        TENSOR,
        scatter_dimension=0,
        tiled=True,
    ).astype(jnp.float32)


def attend_forward(parts):
    queries, keys_in, values_in = parts
    scores = jnp.einsum(
        "shd,thd->hst", queries, keys_in, preferred_element_type=jnp.float32
    ) * HEAD ** (-0.5)
    peak = jnp.max(scores, axis=-1, keepdims=True)
    raised = jnp.exp(scores - peak)
    summed = jnp.sum(raised, axis=-1, keepdims=True)
    weights = (raised / summed).astype(jnp.bfloat16)
    context = jnp.einsum("hst,thd->shd", weights, values_in, preferred_element_type=jnp.float32)
    return (context.astype(jnp.bfloat16), (peak + jnp.log(summed))[..., 0])


def attend_backward(parts):
    queries, keys_in, values_in, log_total, grad_context = parts
    scale = HEAD ** (-0.5)
    scores = (
        jnp.einsum("shd,thd->hst", queries, keys_in, preferred_element_type=jnp.float32) * scale
    )
    probs = jnp.exp(scores - log_total[..., None])
    probs_low = probs.astype(jnp.bfloat16)
    grad_values = jnp.einsum(
        "hst,shd->thd", probs_low, grad_context, preferred_element_type=jnp.float32
    )
    grad_probs = jnp.einsum(
        "shd,thd->hst", grad_context, values_in, preferred_element_type=jnp.float32
    )
    grad_scores = (
        probs * (grad_probs - jnp.sum(probs * grad_probs, axis=-1, keepdims=True))
    ).astype(jnp.bfloat16)
    grad_queries = (
        jnp.einsum("hst,thd->shd", grad_scores, keys_in, preferred_element_type=jnp.float32) * scale
    )
    grad_keys = (
        jnp.einsum("hst,shd->thd", grad_scores, queries, preferred_element_type=jnp.float32) * scale
    )
    return (grad_queries, grad_keys, grad_values)


def run_block(stream, attn_full, mlp_full, gains):
    model_width = stream.shape[2]
    head_width = attn_full.shape[2]
    normed = norm_rows(stream, gains[0], gains[1]).astype(jnp.bfloat16)
    normed_full = gather_rows(normed)
    seq_len = normed_full.shape[0]
    clip_count = normed_full.shape[1]
    weight_in = attn_full[:, 0:3].reshape(model_width, 3 * head_width)
    joined = jnp.einsum(
        "scd,dk->sck", normed_full, weight_in, preferred_element_type=jnp.float32
    ).astype(jnp.bfloat16)
    split_heads = jnp.moveaxis(
        joined.reshape(seq_len, clip_count, 3, head_width // HEAD, HEAD), 1, 0
    )
    context, log_total = lax.map(
        attend_forward, (split_heads[:, :, 0], split_heads[:, :, 1], split_heads[:, :, 2])
    )
    context_rows = jnp.moveaxis(context, 0, 1).reshape(seq_len, clip_count, head_width)
    middle = stream + scatter_rows(context_rows, attn_full[:, 3])
    hidden = norm_rows(middle, gains[2], gains[3]).astype(jnp.bfloat16)
    hidden_full = gather_rows(hidden)
    upward = jnp.einsum(
        "scd,df->scf", hidden_full, mlp_full[:, 0], preferred_element_type=jnp.float32
    )
    active = exact_gelu(upward).astype(jnp.bfloat16)
    result = middle + scatter_rows(active, mlp_full[:, 1])
    return (
        result,
        (
            stream,
            normed_full,
            split_heads,
            log_total,
            context_rows,
            middle,
            hidden_full,
            upward,
            active,
        ),
    )


def back_block(grad_stream, saved, attn_full, mlp_full, gains):
    (
        stream,
        normed_full,
        split_heads,
        log_total,
        context_rows,
        middle,
        hidden_full,
        upward,
        active,
    ) = saved
    model_width = stream.shape[2]
    head_width = attn_full.shape[2]
    seq_len = normed_full.shape[0]
    clip_count = normed_full.shape[1]
    grad_ffn = gather_grads(grad_stream.astype(jnp.bfloat16))
    grad_down = jnp.einsum("scd,scf->df", grad_ffn, active, preferred_element_type=jnp.float32)
    grad_active = jnp.einsum(
        "scd,df->scf", grad_ffn, mlp_full[:, 1], preferred_element_type=jnp.float32
    )
    unused, gelu_pull = jax.vjp(exact_gelu, upward)
    grad_upward = gelu_pull(grad_active)[0].astype(jnp.bfloat16)
    grad_up = jnp.einsum(
        "scd,scf->df", hidden_full, grad_upward, preferred_element_type=jnp.float32
    )
    grad_hidden = scatter_grads(grad_upward, mlp_full[:, 0])
    unused, second_pull = jax.vjp(norm_rows, middle, gains[2], gains[3])
    grad_middle_norm, grad_gain_two, grad_shift_two = second_pull(grad_hidden)
    grad_middle = grad_stream + grad_middle_norm
    grad_attn = gather_grads(grad_middle.astype(jnp.bfloat16))
    grad_outward = jnp.einsum(
        "scd,sck->dk", grad_attn, context_rows, preferred_element_type=jnp.float32
    )
    grad_context = jnp.einsum(
        "scd,dk->sck", grad_attn, attn_full[:, 3], preferred_element_type=jnp.float32
    ).astype(jnp.bfloat16)
    grad_context = jnp.moveaxis(
        grad_context.reshape(seq_len, clip_count, head_width // HEAD, HEAD), 1, 0
    )
    grad_queries, grad_keys, grad_values = lax.map(
        attend_backward,
        (split_heads[:, :, 0], split_heads[:, :, 1], split_heads[:, :, 2], log_total, grad_context),
    )
    grad_joined = jnp.moveaxis(jnp.stack((grad_queries, grad_keys, grad_values), axis=2), 0, 1)
    grad_joined = grad_joined.reshape(seq_len, clip_count, 3 * head_width).astype(jnp.bfloat16)
    weight_in = attn_full[:, 0:3].reshape(model_width, 3 * head_width)
    grad_inward = jnp.einsum(
        "scd,sck->dk", normed_full, grad_joined, preferred_element_type=jnp.float32
    ).reshape(model_width, 3, head_width)
    grad_normed = scatter_grads(grad_joined, weight_in)
    unused, first_pull = jax.vjp(norm_rows, stream, gains[0], gains[1])
    grad_stream_norm, grad_gain_one, grad_shift_one = first_pull(grad_normed)
    attn_grad = jnp.concatenate([grad_inward, grad_outward[:, None]], axis=1)
    mlp_grad = jnp.stack([grad_up, grad_down], axis=1)
    layer_attn, layer_mlp = (
        lax.psum_scatter(attn_grad, DP, scatter_dimension=0, tiled=True),
        lax.psum_scatter(mlp_grad, DP, scatter_dimension=0, tiled=True),
    )
    vector_grads = jnp.stack([grad_gain_one, grad_shift_one, grad_gain_two, grad_shift_two])
    return (grad_middle + grad_stream_norm, layer_attn, layer_mlp, vector_grads)


def direction(weight, grad, first, second):
    bias_one = 1.0 - first_decay**step_count
    bias_two = 1.0 - second_decay**step_count
    first_new = first_decay * first + (1.0 - first_decay) * grad
    second_new = second_decay * second + (1.0 - second_decay) * grad * grad
    update = (
        first_new / bias_one / (jnp.sqrt(second_new / bias_two) + adam_epsilon)
        + weight_decay * weight
    )
    return (first_new, second_new, update)


def matrix_squares(edge_part, attn_part, mlp_part):
    layer_part = jnp.concatenate(
        [jnp.sum(attn_part * attn_part, axis=(1, 3)), jnp.sum(mlp_part * mlp_part, axis=(1, 3))],
        axis=1,
    )
    return jnp.concatenate([jnp.sum(edge_part * edge_part, axis=(1, 2)), layer_part.reshape(-1)])


def per_device_general(
    patches,
    mask,
    edge,
    attn_w,
    mlp_w,
    vecs,
    edge_m,
    edge_v,
    attn_m,
    attn_v,
    mlp_m,
    mlp_v,
    vecs_m,
    vecs_v,
    teacher_edge,
    teacher_attn,
    teacher_mlp,
    teacher_vecs,
):
    layer_count = attn_w.shape[0]
    local_count = patches.shape[0]
    clip_count = patches.shape[1]
    model_width = patches.shape[2]
    last_row = 4 * layer_count
    student_edge, student_vecs = fetch_edges(edge, vecs)
    teach_edge, teach_vecs = fetch_edges(teacher_edge, teacher_vecs)
    seq_total = local_count * lax.axis_size(TENSOR)
    stream = jnp.einsum(
        "scp,pd->scd",
        patches,
        teach_edge[0].astype(jnp.bfloat16),
        preferred_element_type=jnp.float32,
    )
    summed = jnp.zeros_like(stream)
    for layer_index in range(layer_count):
        attn_full, mlp_full = fetch_layer(teacher_attn[layer_index], teacher_mlp[layer_index])
        stream, unused = run_block(
            stream, attn_full, mlp_full, teach_vecs[4 * layer_index : 4 * layer_index + 4]
        )
        first_sum, square_sum = lax.psum(
            (jnp.sum(stream, axis=0), jnp.sum(stream * stream, axis=0)), TENSOR
        )
        average = first_sum / seq_total
        spread = square_sum / seq_total - average * average
        summed = summed + (stream - average) * lax.rsqrt(spread + inst_epsilon)
    target = summed / layer_count
    masked = mask.astype(jnp.float32)[..., None]
    embedded = jnp.einsum(
        "scp,pd->scd",
        patches,
        student_edge[0].astype(jnp.bfloat16),
        preferred_element_type=jnp.float32,
    )
    stream = embedded * (1.0 - masked) + masked * student_vecs[last_row + 2]
    saved_list = []
    weight_list = []
    for layer_index in range(layer_count):
        attn_full, mlp_full = fetch_layer(attn_w[layer_index], mlp_w[layer_index])
        stream, saved = run_block(
            stream, attn_full, mlp_full, student_vecs[4 * layer_index : 4 * layer_index + 4]
        )
        saved_list.append(saved)
        weight_list.append((attn_full, mlp_full))
    final_low = norm_rows(stream, student_vecs[last_row], student_vecs[last_row + 1]).astype(
        jnp.bfloat16
    )
    head_low = student_edge[1].astype(jnp.bfloat16)
    predicted = (
        jnp.einsum("scd,de->sce", final_low, head_low, preferred_element_type=jnp.float32)
        + student_vecs[last_row + 3]
    )
    offset = predicted - target
    size_abs = jnp.abs(offset)
    loss_part = (
        jnp.sum(jnp.where(size_abs < 1.0, 0.5 * offset * offset, size_abs - 0.5) * masked)
        / model_width**0.5
    )
    grad_pred = jnp.clip(offset, -1.0, 1.0) * masked / model_width**0.5
    grad_low = grad_pred.astype(jnp.bfloat16)
    grad_head = jnp.einsum("scd,sce->de", final_low, grad_low, preferred_element_type=jnp.float32)
    grad_bias = jnp.sum(grad_pred, axis=(0, 1))
    grad_final = jnp.einsum("sce,de->scd", grad_low, head_low, preferred_element_type=jnp.float32)
    unused, final_pull = jax.vjp(
        norm_rows, stream, student_vecs[last_row], student_vecs[last_row + 1]
    )
    grad_stream, grad_final_gain, grad_final_shift = final_pull(grad_final)
    attn_grads = []
    mlp_grads = []
    vector_rows = []
    for layer_index in reversed(range(layer_count)):
        attn_full, mlp_full = fetch_again(attn_w[layer_index], mlp_w[layer_index])
        grad_stream, layer_attn, layer_mlp, vector_grads = back_block(
            grad_stream,
            saved_list[layer_index],
            attn_full,
            mlp_full,
            student_vecs[4 * layer_index : 4 * layer_index + 4],
        )
        attn_grads.insert(0, layer_attn)
        mlp_grads.insert(0, layer_mlp)
        vector_rows.insert(0, vector_grads)
    grad_embed = (grad_stream * (1.0 - masked)).astype(jnp.bfloat16)
    grad_mask_vec = jnp.sum(grad_stream * masked, axis=(0, 1))
    grad_patch = jnp.einsum("scp,scd->pd", patches, grad_embed, preferred_element_type=jnp.float32)
    vector_grad = jnp.concatenate(
        vector_rows + [jnp.stack([grad_final_gain, grad_final_shift, grad_mask_vec, grad_bias])],
        axis=0,
    )
    edge_grad, vecs_grad = (
        lax.psum_scatter(
            jnp.stack([grad_patch, grad_head]), (DP, TENSOR), scatter_dimension=1, tiled=True
        ),
        lax.psum_scatter(vector_grad, (DP, TENSOR), scatter_dimension=1, tiled=True),
    )
    attn_grad = jnp.stack(attn_grads)
    mlp_grad = jnp.stack(mlp_grads)
    edge_first, edge_second, edge_update = direction(edge, edge_grad, edge_m, edge_v)
    attn_first, attn_second, attn_update = direction(attn_w, attn_grad, attn_m, attn_v)
    mlp_first, mlp_second, mlp_update = direction(mlp_w, mlp_grad, mlp_m, mlp_v)
    vecs_first, vecs_second, vecs_update = direction(vecs, vecs_grad, vecs_m, vecs_v)
    weight_sq, update_sq, loss_total = lax.psum(
        (
            matrix_squares(edge, attn_w, mlp_w),
            matrix_squares(edge_update, attn_update, mlp_update),
            loss_part,
        ),
        (DP, TENSOR),
    )
    weight_norm = jnp.sqrt(weight_sq)
    update_norm = jnp.sqrt(update_sq)
    trust = weight_norm / (update_norm + adam_epsilon)
    edge_trust = trust[0:2]
    layer_trust = trust[2:].reshape(layer_count, 6)
    new_edge = edge - learn_rate * edge_trust[:, None, None] * edge_update
    new_attn = attn_w - learn_rate * layer_trust[:, None, 0:4, None] * attn_update
    new_mlp = mlp_w - learn_rate * layer_trust[:, None, 4:6, None] * mlp_update
    new_vecs = vecs - learn_rate * vecs_update
    keep_share = 1.0 - teacher_decay
    token_total = seq_total * clip_count * lax.axis_size(DP)
    return (
        loss_total / token_total,
        jnp.stack([weight_norm, update_norm]),
        new_edge,
        new_attn,
        new_mlp,
        new_vecs,
        edge_first,
        edge_second[0],
        edge_second[1],
        attn_first,
        attn_second[:, :, 0:3],
        attn_second[:, :, 3],
        mlp_first,
        mlp_second,
        vecs_first,
        vecs_second,
        keep_share * (new_edge - teacher_edge),
        keep_share * (new_attn - teacher_attn),
        keep_share * (new_mlp - teacher_mlp),
        keep_share * (new_vecs - teacher_vecs),
        new_edge.astype(jnp.bfloat16),
        new_attn.astype(jnp.bfloat16),
        new_mlp.astype(jnp.bfloat16),
        new_vecs.astype(jnp.bfloat16),
    )


MESH = pl.DeviceIdType.MESH
ORDERS = (("z", "x", "y"), ("x", "y", "z"), ("y", "z", "x"))
LOW = jnp.bfloat16
ALL = slice(None)


def coords():
    d = lax.axis_index(DP)
    t = lax.axis_index(TENSOR)
    return dict(a=t // 2, z=t % 2, y=d // 4, x=(d // 2) % 2, c=d % 2)


def ident(co):
    return (co["y"] * 4 + co["x"] * 2 + co["c"], co["a"] * 2 + co["z"])


def flip(co, k):
    co = dict(co)
    co[k] = 1 - co[k]
    return ident(co)


def place(co, full, rows):
    return tuple(ALL if k in full else co[k] for k in "azyxc") + (rows,)


ANY = pl.BlockSpec(memory_space=pl.ANY)
DMA = pltpu.SemaphoreType.DMA


def shape_of(shape, kind=LOW):
    return jax.ShapeDtypeStruct(shape, kind)


def dot(left, right):
    return jnp.dot(left, right, preferred_element_type=jnp.float32)


def dot_nt(left, right):
    return lax.dot_general(
        left, right, (((1,), (1,)), ((), ())), preferred_element_type=jnp.float32
    )


def dot_tn(left, right):
    return lax.dot_general(
        left, right, (((0,), (0,)), ((), ())), preferred_element_type=jnp.float32
    )


def pack_heads(block):
    q, k, v, o = (block[..., i, :] for i in range(4))
    two = 2 * HEAD
    pieces = [q[..., :two], k[..., :two], v[..., :two], q[..., two:], v[..., two:], k[..., two:]]
    pieces += [o[..., HEAD:two], o[..., :HEAD], o[..., two:]]
    return jnp.concatenate(pieces, axis=-1)


def unpack_heads(packed):
    cut = lambda *spots: jnp.concatenate(
        [packed[..., HEAD * a : HEAD * b] for a, b in spots], axis=-1
    )
    kinds = [cut((0, 2), (6, 7)), cut((2, 4), (8, 9)), cut((4, 6), (7, 8))]
    kinds.append(cut((10, 11), (9, 10), (11, 12)))
    return jnp.stack(kinds, axis=-2)


def norm_block(values, gain, shift):
    average = jnp.mean(values, axis=-1, keepdims=True)
    centered = values - average
    spread = jnp.mean(centered * centered, axis=-1, keepdims=True)
    return centered * lax.rsqrt(spread + norm_epsilon) * gain + shift


def matrix(value):
    return value.reshape(-1, value.shape[-1])


def low_lanes(shape):
    return lax.broadcasted_iota(jnp.int32, shape, len(shape) - 1) % 128 < HEAD


def forward_kernel(*refs):
    (attn_mine, attn_other, mlp_mine, mlp_other, edge_mine, edge_other) = refs[:6]
    vec_mine, vec_other, patch = refs[6:9]
    (o_attn, o_mlp, o_head, o_vec, o_x, o_mid, o_normed, o_qkv, o_peer, o_ctx) = refs[9:19]
    (o_hid, o_act, o_slope, o_lse, o_last, o_final, o_pixels, o_dlow, o_sums, o_mask) = refs[19:29]
    (w_attn, w_mlp, w_edge, w_vec, pixels, embed_w, head_w, gains, x, mid) = refs[29:39]
    (normed, qkv, peer, ctx, hid, act, slope, lse, work, target, stat, sums, turned) = refs[39:52]
    early, final_stat = refs[52:54]
    local_sem, send_sem, recv_sem, patch_sem, peer_sem, stat_sem, save_sem, core_sem = refs[54:]
    co = coords()
    me = ident(co)
    column = co["y"] * 2 + co["x"]
    teaching = co["a"] == 1
    rows_here = x.shape[0]
    width = x.shape[1]
    layers = attn_mine.shape[0]
    last_row = 4 * layers
    barrier = pltpu.get_barrier_semaphore()
    for k in range(1, 8):
        to = (column * 2 + (co["c"] + k // 4) % 2, (me[1] + k % 4) % 4)
        pl.semaphore_signal(barrier, inc=1, device_id=to, device_id_type=MESH)
    for k in "xy":
        pl.semaphore_signal(barrier, inc=1, device_id=flip(co, k), device_id_type=MESH)
    pl.semaphore_wait(barrier, 9)

    items = [(edge_mine, edge_other, w_edge, 0), (vec_mine, vec_other, w_vec, 0)]
    for l in range(layers):
        items.append((attn_mine.at[l], attn_other.at[l], w_attn.at[l], 3 * l + 1))
        for k in range(2):
            items.append(
                (mlp_mine.at[l, k], mlp_other.at[l, k], w_mlp.at[l, k], 3 * l + 2 + k)
            )
    sent = []
    table = {}

    def remote(source, to_ref, i, j, k, to):
        copy = pltpu.make_async_remote_copy(
            src_ref=source,
            dst_ref=to_ref,
            send_sem=send_sem.at[i, j, k],
            recv_sem=recv_sem.at[i, j, k],
            device_id=to,
            device_id_type=MESH,
        )
        copy.start()
        sent.append(copy)
        return copy

    def begin(slot):
        for i, (mine, other, full, at) in enumerate(items):
            if at == slot:
                spot = full.at[place(co, "", ALL)]
                copy = pltpu.make_async_copy(mine, spot, local_sem.at[i])
                copy.start()
                table[i, -1] = (copy, remote(other, spot, i, 0, 4, flip(co, "a")))

    def step(wave, s):
        for i, (mine, other, full, at) in enumerate(items):
            if wave - at != s:
                continue
            if s == 0:
                table[i, -1][0].wait()
                table[i, -1][1].wait_recv()
            size = mine.shape[0] // 3
            copies = []
            for p in range(3):
                if s > 0:
                    table[i, s - 1][p].wait_recv()
                if s < 4:
                    order = ORDERS[p] + ("c",)
                    full_dims = ("a",) + order[:s]
                    ref = full.at[place(co, full_dims, pl.ds(p * size, size))]
                    copies.append(remote(ref, ref, i, p, s, flip(co, order[s])))
            table[i, s] = copies

    saves = {}
    counter = iter(range(48))

    def save(name, source, to_ref):
        copy = pltpu.make_async_copy(source, to_ref, save_sem.at[next(counter)])
        copy.start()
        saves[name] = copy

    shared = {}
    core_counter = iter(range(16))
    own_rows, peer_rows = pl.ds(0, rows_here), pl.ds(rows_here, rows_here)

    def to_core(name, source, to_ref):
        n = next(core_counter)
        shared[name] = pltpu.make_async_remote_copy(
            src_ref=source,
            dst_ref=to_ref,
            send_sem=core_sem.at[0, n],
            recv_sem=core_sem.at[1, n],
            device_id=flip(co, "c"),
            device_id_type=MESH,
        )
        shared[name].start()

    def share(name, source, to_ref, lead):
        save(name, source, to_ref.at[lead + (own_rows,)])
        to_core(name, source, to_ref.at[lead + (peer_rows,)])

    turns = []

    def turn(name, columns, to_ref):
        spot = turned.at[len(turns) % 2]
        if len(turns) >= 2:
            wait_saves(turns[-2])
        turns.append(name)
        for n in range(2):
            spot[n] = jnp.transpose(columns(n)).astype(LOW).reshape(spot.shape[1:])
        save(name, spot.at[:, :, co["c"]], to_ref.at[:, :, :, own_rows])
        to_core(name, spot.at[:, :, 1 - co["c"]], to_ref.at[:, :, :, peer_rows])

    def columns_of(ref):
        return lambda n: ref[:, n * rows_here : (n + 1) * rows_here].astype(jnp.float32)

    def by_rows(size, body):
        def run(n, _):
            body(pl.ds(pl.multiple_of(n * size, size), size))
            return 0

        lax.fori_loop(0, rows_here // size, run, 0)

    def gain(row):
        return gains[row : row + 1, :]

    def norm_into(source, out, row):
        def body(span):
            out[span, :] = norm_block(source[span, :], gain(row), gain(row + 1)).astype(LOW)

        by_rows(64, body)

    def embed():
        owned = [
            w_vec[t // 2, t % 2, d // 4, d // 2 % 2, d % 2] for d in range(8) for t in range(4)
        ]
        gains[...] = jnp.transpose(jnp.concatenate(owned))[: gains.shape[0]]
        save("vec", gains, o_vec)
        half = edge_mine.shape[0] // 2
        for d in range(8):
            for a in range(2):
                at = (d // 4, d // 2 % 2, d % 2)
                left = w_edge[(a, 0) + at].astype(jnp.float32)
                right = w_edge[(a, 1) + at].astype(jnp.float32)
                spot = pl.ds((2 * d + a) * 2 * half, 2 * half)
                embed_w[spot, :] = jnp.concatenate([left[:half], right[:half]]).astype(LOW)
                head_w[spot, :] = jnp.concatenate([left[half:], right[half:]]).astype(LOW)
        save("head", head_w, o_head)
        for q in range(2):
            origin = (column * 2 + co["z"], co["c"] * 2 + q)
            same = jnp.logical_and(origin[0] == me[0], origin[1] == me[1])

            @pl.when(same)
            def _():
                pltpu.make_async_copy(patch, pixels.at[q], patch_sem.at[2]).wait()

            @pl.when(jnp.logical_not(same))
            def _():
                pltpu.make_async_remote_copy(
                    src_ref=patch,
                    dst_ref=pixels.at[q],
                    send_sem=patch_sem.at[3],
                    recv_sem=patch_sem.at[q],
                    device_id=me,
                    device_id_type=MESH,
                ).wait_recv()

        save("mask", pixels.at[:, :, width:], o_mask)
        quarter = pixels.shape[1]

        def pixel_columns(n):
            cols = pixels[:, :, n * rows_here : (n + 1) * rows_here].astype(jnp.float32)
            return cols.reshape(rows_here, rows_here)

        turn("pixels", pixel_columns, o_pixels)
        for q in range(2):
            hide = pixels[q, :, width : width + 1].astype(jnp.float32)
            hide = jnp.where(teaching, 0.0, hide)
            rows = pl.ds(q * quarter, quarter)
            x[rows, :] = (
                dot(pixels[q, :, :width], embed_w[...]) * (1.0 - hide) + hide * gain(last_row + 2)
            )

    def peer_copy(l, t):
        return pltpu.make_async_remote_copy(
            src_ref=qkv.at[t, :, 128:640],
            dst_ref=peer.at[l, t],
            send_sem=peer_sem.at[0, l, t],
            recv_sem=peer_sem.at[1, l, t],
            device_id=flip(co, "c"),
            device_id_type=MESH,
        )

    settled = []

    def wait_saves(*names):
        for name in names:
            if name in saves:
                saves.pop(name).wait()
                if name in shared:
                    shared[name].wait_send()
                    settled.append(shared.pop(name))

    def project(l):
        save(("x", l), x, o_x.at[l])
        norm_into(x, normed, 4 * l)
        for t in range(4):
            weight = matrix(w_attn[l, t // 2, t % 2])
            qkv[t] = dot(normed[...], weight).astype(LOW)
            peer_copy(l, t).start()
            save(("qkv", l, t), qkv.at[t], o_qkv.at[l, t])
        turn(("normed", l), columns_of(normed), o_normed.at[l])

    def attend(l, first, last):
        if first == 0:
            for t in range(4):
                peer_copy(l, t).wait_recv()
            lse[...] = jnp.zeros_like(lse)
        size = rows_here

        def body(n, _):
            t = n // (rows_here // size)
            span = pl.ds(pl.multiple_of(n % (rows_here // size) * size, size), size)
            low = low_lanes((size, 128))
            lane = lax.broadcasted_iota(jnp.int32, (size, 128), 1)
            zero = jnp.zeros((size, 128), LOW)
            outs = []
            total = lse[span, :]
            for j in range(3):
                q_at = 0 if j < 2 else 384
                k_at = 128 if j < 2 else 512
                v_at = 256 if j < 2 else 384
                query = qkv[t, span, q_at : q_at + 128] * jnp.asarray(HEAD**-0.5, LOW)
                query = jnp.where(low, query, zero) if j != 1 else jnp.where(low, zero, query)
                scores = jnp.concatenate(
                    [
                        dot_nt(query, qkv[t, :, k_at : k_at + 128]),
                        dot_nt(query, peer[l, t, :, k_at - 128 : k_at]),
                    ],
                    axis=1,
                )
                peak = jnp.max(scores, axis=1, keepdims=True)
                raised = jnp.exp(scores - peak)
                summed = jnp.sum(raised, axis=1, keepdims=True)
                weights = raised.astype(LOW)
                out = dot(weights[:, :rows_here], qkv[t, :, v_at : v_at + 128])
                out = out + dot(weights[:, rows_here:], peer[l, t, :, v_at - 128 : v_at])
                outs.append(out / summed)
                total = jnp.where(lane == 3 * t + j, peak + jnp.log(summed), total)
            lse[span, :] = total
            ctx[t, span, :128] = jnp.where(low, 0.0, outs[1]).astype(LOW)
            ctx[t, span, 128:] = jnp.where(low, outs[0], outs[2]).astype(LOW)
            return 0

        each = rows_here // size
        lax.fori_loop(first * each, last * each, body, 0)
        if last == 4:
            save(("lse", l), lse, o_lse.at[l])
            share(("ctx", l), ctx, o_ctx.at[l], (ALL,))
            save(("peer", l), peer.at[l], o_peer.at[l])

    def out_project(l):
        mid[...] = x[...]

        def body(t, _):
            weight = matrix(w_attn[l, t // 2, t % 2, :, :, :, :, 512:])
            mid[...] += dot_nt(ctx[t], weight)
            return 0

        lax.fori_loop(0, 4, body, 0)
        save(("mid", l), mid, o_mid.at[l])
        norm_into(mid, hid, 4 * l + 2)
        turn(("hid", l), columns_of(hid), o_hid.at[l])

    def expand(l, first, last):
        def body(n, _):
            t = n // 3
            cols = pl.ds(pl.multiple_of(n % 3 * 256, 256), 256)
            weight = matrix(w_mlp[l, 0, t // 2, t % 2, :, :, :, :, cols])
            upward = dot(hid[...], weight)
            share = 0.5 + 0.5 * lax.erf(upward * 0.5**0.5)
            act[t, :, cols] = (upward * share).astype(LOW)
            bell = jnp.exp(-0.5 * upward * upward) * (2.0 * jnp.pi) ** -0.5
            slope[t, :, cols] = (share + upward * bell).astype(LOW)
            return 0

        lax.fori_loop(3 * first, 3 * last, body, 0)
        if last == 4:
            share(("act", l), act, o_act.at[l], (ALL,))
            save(("slope", l), slope, o_slope.at[l])

    def contract(l, first, last):
        if first == 0:
            if l < layers - 1:
                wait_saves(("x", l))
            x[...] = mid[...]

        def body(t, _):
            x[...] += dot_nt(act[t], matrix(w_mlp[l, 1, t // 2, t % 2]))
            return 0

        lax.fori_loop(first, last, body, 0)

    def stat_copy(l):
        return pltpu.make_async_remote_copy(
            src_ref=stat.at[l, 0],
            dst_ref=stat.at[l, 1],
            send_sem=stat_sem.at[0, l],
            recv_sem=stat_sem.at[1, l],
            device_id=flip(co, "c"),
            device_id_type=MESH,
        )

    def to_student(n, source, to_ref):
        return pltpu.make_async_remote_copy(
            src_ref=source,
            dst_ref=to_ref,
            send_sem=stat_sem.at[0, layers + n],
            recv_sem=stat_sem.at[1, layers + n],
            device_id=flip(co, "a"),
            device_id_type=MESH,
        )

    spans = [pl.ds(n * (rows_here // 2), rows_here // 2) for n in range(2)]

    def target_copies():
        copies = [to_student(n, target.at[span], target.at[span]) for n, span in enumerate(spans)]
        return copies + [to_student(2, early, early), to_student(3, final_stat, final_stat)]

    def column_sums(ref, spot):
        spot[...] = jnp.zeros_like(spot)

        def body(span):
            value = ref[span, :]
            spot[0:1] += jnp.sum(value, axis=0, keepdims=True)
            spot[1:2] += jnp.sum(value * value, axis=0, keepdims=True)

        by_rows(64, body)

    def normalizer(l):
        stat_copy(l).start()
        stat_copy(l).wait()
        both = (stat[l, 0] + stat[l, 1]) / (2 * rows_here)
        average = both[0:1]
        spread = both[1:2] - average * average
        return average, lax.rsqrt(spread + inst_epsilon) / layers

    def teach(l):
        @pl.when(teaching)
        def _():
            column_sums(x, stat.at[l, 0])
            average, scale = normalizer(l)

            def mix(span):
                value = (x[span, :] - average) * scale
                if l > 0:
                    value = value + work[span, :]
                work[span, :] = value
                if l == layers - 2:
                    early[span, :] = value.astype(LOW)

            by_rows(64, mix)
            if l == layers - 2:
                target_copies()[2].start()

    def center_last():
        @pl.when(teaching)
        def _():
            column_sums(mid, final_stat)
            final_stat[2:3] = final_stat[0:1] / rows_here

    def contract_last():
        l = layers - 1

        @pl.when(teaching)
        def _():
            center = final_stat[2:3]
            for n, span in enumerate(spans):
                value = mid[span, :]
                for t in range(4):
                    value = value + dot_nt(act[t, span], matrix(w_mlp[l, 1, t // 2, t % 2]))
                x[span, :] = value
                target[span, :] = (value - center).astype(LOW)
                target_copies()[n].start()
            column_sums(x, stat.at[l, 0])
            average, scale = normalizer(l)
            final_stat[0:1] = scale
            final_stat[1:2] = (center - average) * scale
            copies = target_copies()
            copies[3].start()
            for copy in copies:
                copy.wait_send()

        @pl.when(jnp.logical_not(teaching))
        def _():
            contract(l, 0, 4)

    def finish():
        save("last", x, o_last)
        sums[...] = jnp.zeros_like(sums)
        norm_into(x, normed, last_row)
        turn("final", columns_of(normed), o_final)

        @pl.when(jnp.logical_not(teaching))
        def _():
            work[...] = dot(normed[...], head_w[...]) + gain(last_row + 3)
            copies = target_copies()
            copies[2].wait_recv()

            def add_early(span):
                work[span, :] = work[span, :] - early[span, :].astype(jnp.float32)

            by_rows(64, add_early)
            copies[0].wait_recv()
            copies[1].wait_recv()
            copies[3].wait_recv()

            def body(n, _):
                span = pl.ds(pl.multiple_of(n * 64, 64), 64)
                part = pl.ds(pl.multiple_of(n % 3 * 64, 64), 64)
                masked = pixels[n // 3, part, width : width + 1].astype(jnp.float32)
                aim = target[span, :].astype(jnp.float32) * final_stat[0:1] + final_stat[1:2]
                offset = work[span, :] - aim
                size = jnp.abs(offset)
                loss = jnp.where(size < 1.0, 0.5 * offset * offset, size - 0.5) * masked
                pull = jnp.clip(offset, -1.0, 1.0) * masked * width**-0.5
                sums[0:1] += jnp.sum(pull, axis=0, keepdims=True)
                sums[1:2] += jnp.sum(loss, axis=0, keepdims=True)
                target[span, :] = pull.astype(LOW)
                return 0

            lax.fori_loop(0, rows_here // 64, body, 0)

        share("dlow", target, o_dlow, ())
        save("sums", sums, o_sums)

    for r in range(2):
        to = (column * 2 + co["a"], 2 * r + co["c"])
        same = jnp.logical_and(to[0] == me[0], to[1] == me[1])
        spot = pixels.at[co["z"]]

        @pl.when(same)
        def _():
            pltpu.make_async_copy(patch, spot, patch_sem.at[2]).start()

        @pl.when(jnp.logical_not(same))
        def _():
            pltpu.make_async_remote_copy(
                src_ref=patch,
                dst_ref=spot,
                send_sem=patch_sem.at[3 + r],
                recv_sem=patch_sem.at[co["z"]],
                device_id=to,
                device_id_type=MESH,
            ).start()

    def save_weights(slot):
        def run():
            l, k = (slot - 1) // 3, (slot - 1) % 3
            if k == 0:
                save(("attn", l), w_attn.at[l], o_attn.at[l])
            else:
                save(("mlp", l, k), w_mlp.at[l, k - 1], o_mlp.at[l, k - 1])

        return run

    plan = {0: [embed]}
    for l in range(layers):
        repeat = l > 0

        def start(l=l):
            if l > 0:
                for t in range(4):
                    peer_copy(l - 1, t).wait_send()
                wait_saves(*[("qkv", l - 1, t) for t in range(4)])
            project(l)

        def begin_attend(l=l):
            if l > 0:
                wait_saves(("lse", l - 1), ("ctx", l - 1))
            attend(l, 0, 2)

        def begin_out(l=l):
            if l > 0:
                wait_saves(("mid", l - 1))
            out_project(l)

        def begin_expand(l=l):
            if l > 0:
                wait_saves(("act", l - 1), ("slope", l - 1))
            expand(l, 0, 2)

        plan[3 * l + 1] = [
            save_weights(3 * l + 1),
            start,
            begin_attend,
            lambda l=l: attend(l, 2, 4),
            begin_out,
        ]
        plan[3 * l + 2] = [
            save_weights(3 * l + 2),
            begin_expand,
            lambda l=l: expand(l, 2, 4),
        ]
        plan[3 * l + 3] = [
            save_weights(3 * l + 3),
            lambda l=l: contract(l, 0, 2),
            lambda l=l: contract(l, 2, 4),
            lambda l=l: teach(l),
        ]
    plan[3 * layers - 1].append(center_last)
    wait_last = lambda: wait_saves(("x", layers - 1))
    plan[3 * layers] = [wait_last, contract_last, save_weights(3 * layers)]
    final_slot = 3 * layers
    begin(0)
    begin(1)
    for wave in range(final_slot + 5):
        begin(wave + 2)
        step(wave, 4)
        todo = list(plan.get(wave - 4, []))
        for s in range(4):
            step(wave, s)
            if todo:
                todo.pop(0)()
        while todo:
            todo.pop(0)()
    finish()
    wait_saves(*list(saves))
    for copy in settled:
        copy.wait_recv()
    for t in range(4):
        peer_copy(layers - 1, t).wait_send()
    for r in range(2):
        to = (column * 2 + co["a"], 2 * r + co["c"])
        same = jnp.logical_and(to[0] == me[0], to[1] == me[1])

        @pl.when(jnp.logical_not(same))
        def _():
            pltpu.make_async_remote_copy(
                src_ref=patch,
                dst_ref=pixels.at[0],
                send_sem=patch_sem.at[3 + r],
                recv_sem=patch_sem.at[0],
                device_id=me,
                device_id_type=MESH,
            ).wait_send()

    for copy in sent:
        copy.wait_send()


def forward_all(*parts):
    layers, rows, width = parts[0].shape
    cube = (2, 2, 2, 2, 2)
    here = 2 * parts[8].shape[0]
    f32 = jnp.float32
    attn = (layers,) + cube + (rows, width)
    mlp = (layers, 2) + cube + (rows, width)
    tall = (here, width)
    turned = (2, 2, rows, 2 * here)
    quarter = parts[8].shape[0]
    outs = (
        shape_of(attn),
        shape_of(mlp),
        shape_of((width, width)),
        shape_of((16, width), f32),
        shape_of((layers,) + tall, f32),
        shape_of((layers,) + tall, f32),
        shape_of((layers,) + turned),
        shape_of((layers, 4) + tall),
        shape_of((layers, 4, here, 512)),
        shape_of((layers, 4, 2 * here, 256)),
        shape_of((layers,) + turned),
        shape_of((layers, 4, 2 * here, width)),
        shape_of((layers, 4) + tall),
        shape_of((layers, here, 128), f32),
        shape_of(tall, f32),
        shape_of(turned),
        shape_of(turned),
        shape_of((2 * here, width)),
        shape_of((8, width), f32),
        shape_of((2, quarter, 128)),
    )
    scratch = [
        pltpu.VMEM(attn, LOW),
        pltpu.VMEM(mlp, LOW),
        pltpu.VMEM(cube + parts[4].shape, LOW),
        pltpu.VMEM(cube + parts[6].shape, f32),
        pltpu.VMEM((2,) + parts[8].shape, LOW),
        pltpu.VMEM((width, width), LOW),
        pltpu.VMEM((width, width), LOW),
        pltpu.VMEM((16, width), f32),
        pltpu.VMEM(tall, f32),
        pltpu.VMEM(tall, f32),
        pltpu.VMEM(tall, LOW),
        pltpu.VMEM((4,) + tall, LOW),
        pltpu.VMEM((layers, 4, here, 512), LOW),
        pltpu.VMEM((4, here, 256), LOW),
        pltpu.VMEM(tall, LOW),
        pltpu.VMEM((4,) + tall, LOW),
        pltpu.VMEM((4,) + tall, LOW),
        pltpu.VMEM((here, 128), f32),
        pltpu.VMEM(tall, f32),
        pltpu.VMEM(tall, LOW),
        pltpu.VMEM((layers, 2, 8, width), f32),
        pltpu.VMEM((8, width), f32),
        pltpu.VMEM((2, 2, 2, 2, rows, here), LOW),
        pltpu.VMEM(tall, LOW),
        pltpu.VMEM((8, width), f32),
    ]
    count = 2 + 3 * layers
    sems = [
        DMA((count,)),
        DMA((count, 3, 5)),
        DMA((count, 3, 5)),
        DMA((5,)),
        DMA((2, layers, 4)),
        DMA((2, layers + 4)),
        DMA((48,)),
        DMA((2, 16)),
    ]
    return pl.pallas_call(
        forward_kernel,
        out_shape=outs,
        in_specs=[ANY] * 9,
        out_specs=(ANY,) * len(outs),
        scratch_shapes=scratch + sems,
        compiler_params=pltpu.CompilerParams(
            collective_id=0, has_side_effects=True, vmem_limit_bytes=60 * 2**20
        ),
    )(*parts)


def backward_kernel(*refs):
    (w_attn, w_mlp, h_head, h_gains, h_x, h_mid, h_normed, h_qkv, h_peer, h_ctx) = refs[:10]
    (h_hid, h_act, h_slope, h_lse, h_last, h_final, h_pixels, h_dlow, h_sums, h_mask) = refs[10:20]
    o_attn, o_mlp, o_head, o_patch, o_vec = refs[20:25]
    (head, gains, x, normed_t, hid_t, qkv, peer, ctx, lse, attn, act) = refs[25:36]
    (down, up, slope, tall_t, tall, mask, sums, g, acc, low_g, turned, dffn_t) = refs[36:48]
    (datt_t, dup, dctx, dqkv, dkv_out, dkv_in, query, pull, score_row, vec_grad) = refs[48:58]
    vec_turned = refs[58]
    rest = refs[59:]
    co = coords()
    layers = w_attn.shape[0]
    last_row = 4 * layers
    here, width = g.shape
    other_core = flip(co, "c")
    own_rows, peer_rows = pl.ds(0, here), pl.ds(here, here)
    barrier = pltpu.get_barrier_semaphore()
    for k in "azyxc":
        pl.semaphore_signal(barrier, inc=1, device_id=flip(co, k), device_id_type=MESH)

    kinds = {}
    spot = 0
    for name, parts in (("D", 3), ("U", 3), ("A", 3), ("H", 2), ("P", 2), ("V", 3)):
        kinds[name] = dict(mine=rest[spot], part=[], parts=parts, name=name)
        spot += 1
        for p in range(parts):
            kinds[name]["part"].append(rest[spot : spot + 3])
            spot += 3
    items = {}
    targets = [("H", 0, o_head)]
    for l in reversed(range(layers)):
        targets += [("D", l, o_mlp.at[l, 1]), ("U", l, o_mlp.at[l, 0]), ("A", l, o_attn.at[l])]
    targets += [("P", 0, o_patch), ("V", 0, o_vec)]
    for n, (name, l, target) in enumerate(targets):
        items[name, l] = dict(kinds[name], n=n, l=l, target=target, last=rest[spot], sent=[])
        spot += 1
    load_sem, send_sem, recv_sem, out_sem, core_sem, credit = rest[spot:]
    own = {q: co[q] for q in "zyx"}

    def pick(fixed, span):
        return tuple(fixed.get(k, ALL) for k in "azyx") + (span,)

    def span_of(item, p):
        size = item["mine"].shape[4] // item["parts"]
        return pl.ds(p * size, size)

    def part_copy(item, p, s):
        order = ORDERS[p][::-1]
        k = order[s]
        fixed = {q: co[q] for q in order[:s]}
        return pltpu.make_async_remote_copy(
            src_ref=item["mine"].at[pick({**fixed, k: 1 - co[k]}, span_of(item, p))],
            dst_ref=item["part"][p][s].at[pick({q: 0 for q in order[: s + 1]}, ALL)],
            send_sem=send_sem.at[item["n"], p, s],
            recv_sem=recv_sem.at[item["n"], p, s],
            device_id=flip(co, k),
            device_id_type=MESH,
        )

    def last_hop(item, p):
        return pltpu.make_async_remote_copy(
            src_ref=item["mine"].at[pick({**own, "a": 1}, span_of(item, p))],
            dst_ref=item["last"].at[span_of(item, p)],
            send_sem=send_sem.at[item["n"], p, 3],
            recv_sem=recv_sem.at[item["n"], p, 3],
            device_id=flip(co, "a"),
            device_id_type=MESH,
        )

    def out_copy(item):
        return pltpu.make_async_copy(
            item["mine"].at[pick({**own, "a": 0}, ALL)], item["target"], out_sem.at[item["n"]]
        )

    def begin(item, s):
        if s == 0 and item["name"] in "DUA" and item["l"] < layers - 1:
            for q in range(3):
                pl.semaphore_wait(credit.at["DUA".index(item["name"]), q], 1)
        for p in range(item["parts"]):
            begin_part(item, p, s)

    def begin_part(item, p, s):
        copy = part_copy(item, p, s)
        copy.start()
        item["sent"].append(copy)

    def gather_part(item, p, s):
        part_copy(item, p, s).wait_recv()
        done = ORDERS[p][::-1][: s + 1]
        left = [k for k in "azyx" if k not in done]
        mine, part, span = item["mine"], item["part"][p][s], span_of(item, p)

        def body(n, _):
            at = {}
            for k in reversed(left):
                at[k] = n % 2
                n = n // 2
            there = tuple(0 if k in done else at[k] for k in "azyx")
            spot = tuple(co[k] if k in done else at[k] for k in "azyx") + (span,)
            mine[spot] = mine[spot] + part[there]
            return 0

        lax.fori_loop(0, 2 ** len(left), body, 0)

    def advance(name, l, s):
        item = items[name, l]
        for p in range(item["parts"]):
            gather_part(item, p, s)
            if s < 2:
                begin_part(item, p, s + 1)
            else:
                last_hop(item, p).start()
        if s < 2:
            return
        if name in "DUA" and l > 0:
            for q, k in enumerate("zyx"):
                pl.semaphore_signal(
                    credit.at["DUA".index(name), q],
                    inc=1,
                    device_id=flip(co, k),
                    device_id_type=MESH,
                )
        out_copy(item).start()

    def settle(name, l):
        item = items[name, l]
        for copy in item["sent"]:
            copy.wait_send()
        for p in range(item["parts"]):
            last_hop(item, p).wait_send()
        out_copy(item).wait()

    loads = {}
    counter = iter(range(96))

    def load_copy(n, ends):
        return pltpu.make_async_copy(*ends(), load_sem.at[n])

    def fetch(name, ends):
        loads[name] = (next(counter), ends)
        load_copy(*loads[name]).start()

    def need(*names):
        for name in names:
            load_copy(*loads.pop(name)).wait()

    core_counter = iter(range(48))
    core = {}

    def to_core(name, source, to_ref):
        n = next(core_counter)
        core[name] = pltpu.make_async_remote_copy(
            src_ref=source,
            dst_ref=to_ref,
            send_sem=core_sem.at[0, n],
            recv_sem=core_sem.at[1, n],
            device_id=other_core,
            device_id_type=MESH,
        )
        core[name].start()

    def by_rows(size, body):
        def run(n, _):
            body(pl.ds(pl.multiple_of(n * size, size), size))
            return 0

        lax.fori_loop(0, here // size, run, 0)

    def turn(name, source, to_ref):
        for n in range(2):
            cols = source[:, n * here : (n + 1) * here].astype(jnp.float32)
            turned[n] = jnp.transpose(cols).astype(LOW).reshape(turned.shape[1:])
        to_ref[:, :, :, :here] = turned[:, :, co["c"]]
        to_core(name, turned.at[:, :, 1 - co["c"]], to_ref.at[:, :, :, here:])

    def norm_back(values, row):
        gain = gains[row : row + 1, :]

        def body(span):
            value = values[span, :]
            average = jnp.mean(value, axis=-1, keepdims=True)
            centered = value - average
            spread = jnp.mean(centered * centered, axis=-1, keepdims=True)
            scale = lax.rsqrt(spread + norm_epsilon)
            hat = centered * scale
            dy = acc[span, :]
            vec_grad[row : row + 1, :] += jnp.sum(dy * hat, axis=0, keepdims=True)
            vec_grad[row + 1 : row + 2, :] += jnp.sum(dy, axis=0, keepdims=True)
            u = dy * gain
            mean_u = jnp.mean(u, axis=-1, keepdims=True)
            mean_uh = jnp.mean(u * hat, axis=-1, keepdims=True)
            g[span, :] += scale * (u - mean_u - hat * mean_uh)

        by_rows(128, body)

    def attend_back(t):
        low = low_lanes((here, 128))
        zero = jnp.zeros((here, 128), LOW)
        scale = jnp.asarray(HEAD**-0.5, LOW)
        first = qkv[t, :, 0:128] * scale
        query[0] = jnp.where(low, first, zero)
        query[1] = jnp.where(low, zero, first)
        query[2] = jnp.where(low, qkv[t, :, 384:512] * scale, zero)
        pull[0] = jnp.where(low, dctx[:, 128:256], zero)
        pull[1] = jnp.where(low, zero, dctx[:, 0:128])
        pull[2] = jnp.where(low, zero, dctx[:, 128:256])
        one = ctx[t, own_rows, 0:128].astype(jnp.float32)
        two = ctx[t, own_rows, 128:256].astype(jnp.float32)
        lane = lax.broadcasted_iota(jnp.int32, (here, 128), 1)
        dots = jnp.zeros((here, 128), jnp.float32)
        for j, value in enumerate((two, one, two)):
            row_sum = jnp.sum(value * pull[j].astype(jnp.float32), axis=1, keepdims=True)
            dots = jnp.where(lane == j, row_sum, dots)
        dots = jnp.transpose(dots)
        score_row[0:8, :] = dots[0:8]
        logs = jnp.transpose(lse[...])
        log_rows = jnp.zeros((8, here), jnp.float32)
        for u in range(4):
            log_rows = jnp.where(t == u, logs[3 * u : 3 * u + 8], log_rows)
        score_row[8:16, :] = log_rows
        pair = (2 * here, 128)
        groups = (
            (128, 256, query[0:2].reshape(pair), pull[0:2].reshape(pair), (0, 1)),
            (512, 384, query[2], pull[2], (2,)),
        )
        half = lax.broadcasted_iota(jnp.int32, (128, here), 0) < HEAD
        grads = [None, None]
        for source, shift in ((peer, 128), (qkv, 0)):
            outs = []
            for i, (k_at, v_at, asked, pulled, heads) in enumerate(groups):
                key = source[t, :, k_at - shift : k_at - shift + 128]
                value = source[t, :, v_at - shift : v_at - shift + 128]
                logs = jnp.concatenate([score_row[8 + j : 9 + j, :] for j in heads], axis=1)
                dots = jnp.concatenate([score_row[j : j + 1, :] for j in heads], axis=1)
                probs = jnp.exp(dot_nt(key, asked) - logs)
                grad_scores = (probs * (dot_nt(value, pulled) - dots)).astype(LOW)
                outs.append(dot(grad_scores, asked))
                outs.append(dot(probs.astype(LOW), pulled))
                back = dot(jnp.transpose(key.astype(jnp.float32)).astype(LOW), grad_scores)
                grads[i] = back if grads[i] is None else grads[i] + back
            for i, out in zip((0, 1, 3, 2), outs):
                cols = slice(128 * i, 128 * i + 128)
                if shift:
                    dkv_out[t, :, cols] = out.astype(LOW)
                else:
                    dqkv[t, own_rows, 128 * i + 128 : 128 * i + 256] = out.astype(LOW)
        first = jnp.where(half, grads[0][:, :here], grads[0][:, here:])
        dqkv[t, own_rows, 0:128] = (jnp.transpose(first) * HEAD**-0.5).astype(LOW)
        second = jnp.transpose(grads[1]) * HEAD**-0.5
        keep = dqkv[t, own_rows, 384:512].astype(jnp.float32)
        dqkv[t, own_rows, 384:512] = jnp.where(low, second, keep).astype(LOW)

    def blocks(value):
        return value.reshape(2, 2, -1, value.shape[-1])

    steps = [(l, t) for l in reversed(range(layers)) for t in range(4)]

    def fetch_act(n):
        if n < len(steps):
            l, t = steps[n]
            fetch(("act", l, t), lambda: (h_act.at[l, t], act.at[n % 2]))

    def fetch_mlp(n):
        if n < len(steps):
            l, t = steps[n]
            fetch(("up", l, t), lambda: (w_mlp.at[l, 0, t // 2, t % 2], up.at[n % 2]))
            fetch(("down", l, t), lambda: (w_mlp.at[l, 1, t // 2, t % 2], down.at[n % 2]))
            fetch(("slope", l, t), lambda: (h_slope.at[l, t], slope.at[n % 2]))

    def fetch_late(l):
        fetch(("qkv", l), lambda: (h_qkv.at[l], qkv))
        fetch(("peer", l), lambda: (h_peer.at[l], peer))
        fetch(("ctx", l), lambda: (h_ctx.at[l], ctx))
        fetch(("lse", l), lambda: (h_lse.at[l], lse))
        fetch(("attn", l), lambda: (w_attn.at[l], attn))
        fetch(("normed", l), lambda: (h_normed.at[l], normed_t))

    def fetch_hid(l):
        fetch(("hid", l), lambda: (h_hid.at[l], hid_t))
        fetch(("mid", l), lambda: (h_mid.at[l], x))

    def edge_blocks(mine, value):
        size = value.shape[2] // 4
        for t in range(4):
            block = value[:, :, size * t : size * (t + 1)]
            pad = jnp.zeros((2, 2, mine.shape[4] - size, width), jnp.float32)
            mine[t // 2, t % 2] = jnp.concatenate([block, pad], axis=2).astype(LOW)

    def head_back():
        fetch("dlow", lambda: (h_dlow, tall))
        fetch("head", lambda: (h_head, head))
        fetch("last", lambda: (h_last, x))
        fetch("gains", lambda: (h_gains, gains))
        fetch("final", lambda: (h_final, tall_t))
        vec_grad[...] = jnp.zeros_like(vec_grad)
        dqkv[...] = jnp.zeros_like(dqkv)
        g[...] = jnp.zeros_like(g)
        need("dlow", "head")
        acc[...] = dot_nt(tall[own_rows, :], head[...])
        fetch_mlp(0)
        fetch_act(0)
        fetch_act(1)
        fetch_mlp(1)
        need("last", "gains")
        norm_back(x, last_row)
        fetch_hid(layers - 1)
        need("final")
        value = blocks(dot(matrix(tall_t[...]), tall[...]))

        edge_blocks(items["H", 0]["mine"], value)
        fetch_late(layers - 1)
        fetch("sums", lambda: (h_sums, sums))
        fetch("mask", lambda: (h_mask, mask))
        fetch("pixels", lambda: (h_pixels, tall_t))

    def student():
        begin(items["H", 0], 0)
        for l in reversed(range(layers)):
            top = l == layers - 1
            low_g[...] = g[...].astype(LOW)
            if not top:
                core["datt", l + 1].wait_send()
            turn(("dffn", l), low_g, dffn_t)

            def widen(t, l=l):
                n = steps.index((l, t))
                need(("down", l, t), ("slope", l, t), ("up", l, t))
                pulled = dot(low_g[...], matrix(down[n % 2])) * slope[n % 2].astype(jnp.float32)
                dup[t, own_rows, :] = pulled.astype(LOW)
                to_core(("dup", l, t), dup.at[t, own_rows], dup.at[t, peer_rows])
                back = dot_nt(dup[t, own_rows, :], matrix(up[n % 2]))
                acc[...] = back if t == 0 else acc[...] + back
                fetch_mlp(n + 2)

            if not top:
                for t in range(4):
                    core["dup", l + 1, t].wait_send()
            widen(0)
            if top:
                advance("H", 0, 0)
            core["dffn", l].wait_recv()
            if not top:
                settle("D", l + 1)
            for t in range(4):
                n = steps.index((l, t))
                need(("act", l, t))
                value = dot(matrix(dffn_t[...]), act[n % 2])
                items["D", l]["mine"][t // 2, t % 2] = blocks(value).astype(LOW)
                fetch_act(n + 2)
            if not top:
                advance("A", l + 1, 0)
            begin(items["D", l], 0)
            widen(1)
            if top:
                advance("H", 0, 1)
            widen(2)
            widen(3)
            need(("mid", l))
            norm_back(x, 4 * l + 2)
            fetch(("x", l), lambda l=l: (h_x.at[l], x))
            need(("hid", l))
            if not top:
                settle("U", l + 1)
            for t in range(4):
                core["dup", l, t].wait_recv()
                value = dot(matrix(hid_t[...]), dup[t])
                items["U", l]["mine"][t // 2, t % 2] = blocks(value).astype(LOW)
            advance("D", l, 0)
            begin(items["U", l], 0)
            if top:
                advance("H", 0, 2)
            else:
                advance("A", l + 1, 1)
            low_g[...] = g[...].astype(LOW)
            core["dffn", l].wait_send()
            turn(("datt", l), low_g, datt_t)
            need(("attn", l), ("qkv", l), ("peer", l), ("ctx", l), ("lse", l))
            if not top:
                for t in range(4):
                    core["dkv", l + 1, t].wait_send()
                    core["dqkv", l + 1, t].wait_send()
            for t in range(4):
                weight = matrix(attn[t // 2, t % 2, :, :, :, :, 512:])
                dctx[...] = dot(low_g[...], weight).astype(LOW)
                attend_back(t)
                to_core(("dkv", l, t), dkv_out.at[t], dkv_in.at[t])
                if t == 0 and not top:
                    advance("A", l + 1, 2)
                if t == 1:
                    advance("D", l, 1)
                if t == 2:
                    advance("U", l, 0)
                if t == 3:
                    advance("D", l, 2)
            for t in range(4):
                core["dkv", l, t].wait_recv()
                for i in range(4):
                    cols = slice(128 * i + 128, 128 * i + 256)
                    total = dqkv[t, own_rows, cols].astype(jnp.float32)
                    total = total + dkv_in[t, :, 128 * i : 128 * i + 128].astype(jnp.float32)
                    dqkv[t, own_rows, cols] = total.astype(LOW)
                to_core(("dqkv", l, t), dqkv.at[t, own_rows], dqkv.at[t, peer_rows])
                weight = matrix(attn[t // 2, t % 2, :, :, :, :, :640])
                back = dot_nt(dqkv[t, own_rows, :], weight)
                acc[...] = back if t == 0 else acc[...] + back
            need(("normed", l))
            core["datt", l].wait_recv()
            advance("U", l, 1)
            if not top:
                settle("A", l + 1)
            for t in range(4):
                core["dqkv", l, t].wait_recv()
                inward = dot(matrix(normed_t[...]), dqkv[t])
                outward = dot(matrix(datt_t[...]), ctx[t])
                joint = inward[:, 512:640] + outward[:, :128]
                value = jnp.concatenate([inward[:, :512], joint, outward[:, 128:]], axis=1)
                items["A", l]["mine"][t // 2, t % 2] = blocks(value).astype(LOW)
            begin(items["A", l], 0)
            advance("U", l, 2)
            need(("x", l))
            norm_back(x, 4 * l)
            if l > 0:
                fetch_hid(l - 1)
                fetch_late(l - 1)
        need("mask", "sums", "pixels")

        def embed_back(n, _):
            span = pl.ds(pl.multiple_of(n * 64, 64), 64)
            part = pl.ds(pl.multiple_of(n % 3 * 64, 64), 64)
            hide = mask[n // 3, part, 0:1].astype(jnp.float32)
            value = g[span, :]
            tall[span, :] = (value * (1.0 - hide)).astype(LOW)
            vec_grad[last_row + 2 : last_row + 3, :] += jnp.sum(value * hide, axis=0, keepdims=True)
            return 0

        lax.fori_loop(0, here // 64, embed_back, 0)
        to_core("embed", tall.at[own_rows], tall.at[peer_rows])
        vec_grad[last_row + 3 : last_row + 4, :] = sums[0:1, :]
        loss = jnp.sum(sums[1:2, :], axis=1, keepdims=True) * width**-0.5
        vec_grad[last_row + 4 : last_row + 5, :] = jnp.broadcast_to(loss, (1, width))
        full = jnp.concatenate([vec_grad[...], jnp.zeros((112, width), jnp.float32)])
        full = jnp.transpose(full)
        size = width // 32
        for d in range(8):
            for t in range(4):
                row = (4 * d + t) * size
                vec_turned[d % 2, t // 2, t % 2, d // 4, d // 2 % 2] = full[row : row + size]
        vec = items["V", 0]
        vec_in = vec_turned.at[2]
        to_core("vec", vec_turned.at[1 - co["c"]], vec_in)
        core["embed"].wait_recv()
        edge_blocks(items["P", 0]["mine"], blocks(dot(matrix(tall_t[...]), tall[...])))
        begin(items["P", 0], 0)
        core["vec"].wait_recv()
        vec["mine"][...] = vec_turned[co["c"]] + vec_turned[2]
        begin(vec, 0)
        for s in range(3):
            advance("A", 0, s)
            advance("P", 0, s)
            advance("V", 0, s)
        for name, l, unused in targets:
            if l == 0:
                settle(name, l)
        core["embed"].wait_send()
        core["vec"].wait_send()
        core["datt", 0].wait_send()
        for t in range(4):
            for name in ("dup", "dkv", "dqkv"):
                core[name, 0, t].wait_send()

    @pl.when(co["a"] == 0)
    def _():
        head_back()

    pl.semaphore_wait(barrier, 5)

    @pl.when(co["a"] == 0)
    def _():
        student()

    @pl.when(co["a"] == 1)
    def _():
        for name, l, target in targets:
            item = items[name, l]
            for p in range(item["parts"]):
                last_hop(item, p).wait_recv()
            copy = pltpu.make_async_copy(item["last"], target, out_sem.at[item["n"]])
            copy.start()
        for name, l, target in targets:
            item = items[name, l]
            pltpu.make_async_copy(item["last"], target, out_sem.at[item["n"]]).wait()


def backward_all(*parts):
    w_attn, w_mlp = parts[:2]
    layers, rows, width = w_attn.shape[0], w_attn.shape[-2], w_attn.shape[-1]
    here = parts[4].shape[1]
    f32 = jnp.float32
    tall = (here, width)
    turned = (2, 2, rows, 2 * here)
    weight = (2, 2, 2, rows, width)
    edge = 32
    small = width // 32
    scratch = [
        ((width, width), LOW),
        ((16, width), f32),
        (tall, f32),
        (turned, LOW),
        (turned, LOW),
        ((4,) + tall, LOW),
        ((4, here, 512), LOW),
        ((4, 2 * here, 256), LOW),
        ((here, 128), f32),
        ((2, 2) + weight, LOW),
        ((2, 2 * here, width), LOW),
        ((2,) + weight, LOW),
        ((2,) + weight, LOW),
        ((2,) + tall, LOW),
        (turned, LOW),
        ((2 * here, width), LOW),
        (parts[19].shape, LOW),
        ((8, width), f32),
        (tall, f32),
        (tall, f32),
        (tall, LOW),
        ((2, 2, 2, rows, here), LOW),
        (turned, LOW),
        (turned, LOW),
        ((4, 2 * here, width), LOW),
        ((here, 256), LOW),
        ((4, 2 * here, 640), LOW),
        ((4, here, 512), LOW),
        ((4, here, 512), LOW),
        ((3, here, 128), LOW),
        ((3, here, 128), LOW),
        ((16, here), f32),
        ((16, width), f32),
        ((3, 2, 2, 2, 2, small, 128), f32),
    ]
    shapes = dict(
        D=(rows, width, LOW, 3),
        U=(rows, width, LOW, 3),
        A=(rows, width, LOW, 3),
        H=(edge, width, LOW, 2),
        P=(edge, width, LOW, 2),
        V=(small, 128, f32, 3),
    )
    for count, cols, kind, pieces in shapes.values():
        scratch.append(((2, 2, 2, 2, count, cols), kind))
        for p in range(pieces):
            order = ORDERS[p][::-1]
            for s in range(3):
                dims = tuple(1 if k in order[: s + 1] else 2 for k in "azyx")
                scratch.append((dims + (count // pieces, cols), kind))
    names = "H" + "DUA" * layers + "PV"
    for name in names:
        count, cols, kind, pieces = shapes[name]
        scratch.append(((count, cols), kind))
    count = len(names)
    return pl.pallas_call(
        backward_kernel,
        out_shape=(
            shape_of((layers, rows, width)),
            shape_of((layers, 2, rows, width)),
            shape_of((edge, width)),
            shape_of((edge, width)),
            shape_of((small, 128), f32),
        ),
        in_specs=[ANY] * len(parts),
        out_specs=(ANY,) * 5,
        scratch_shapes=[pltpu.VMEM(*s) for s in scratch]
        + [
            DMA((96,)),
            DMA((count, 3, 4)),
            DMA((count, 3, 4)),
            DMA((count,)),
            DMA((2, 48)),
            pltpu.SemaphoreType.REGULAR((3, 3)),
        ],
        compiler_params=pltpu.CompilerParams(
            collective_id=1, has_side_effects=True, vmem_limit_bytes=60 * 2**20
        ),
    )(*parts)


def total_kernel(value, out, held, send_sem, recv_sem):
    co = coords()
    d, t = ident(co)
    near = [(d - d % 2 + (d + k // 4) % 2, (t + k) % 4) for k in range(1, 8)]
    far = [((d + 2 * k) % 8, t) for k in range(1, 4)]
    barrier = pltpu.get_barrier_semaphore()
    for to in near + far:
        pl.semaphore_signal(barrier, inc=1, device_id=to, device_id_type=MESH)
    pl.semaphore_wait(barrier, len(near) + len(far))
    total = value[...]
    n = 0
    for s, group in enumerate((near, far)):
        held[0, s] = total
        copies = []
        for to in group:
            copy = pltpu.make_async_remote_copy(
                src_ref=held.at[0, s],
                dst_ref=held.at[1, n],
                send_sem=send_sem.at[n],
                recv_sem=recv_sem.at[n],
                device_id=to,
                device_id_type=MESH,
            )
            copy.start()
            copies.append((copy, n))
            n += 1
        for copy, spot in copies:
            copy.wait()
            total = total + held[1, spot]
    out[...] = total


def total_all(value):
    return pl.pallas_call(
        total_kernel,
        out_shape=shape_of(value.shape, jnp.float32),
        in_specs=[pl.BlockSpec(memory_space=pltpu.VMEM)],
        out_specs=pl.BlockSpec(memory_space=pltpu.VMEM),
        scratch_shapes=[pltpu.VMEM((2, 10) + value.shape, jnp.float32), DMA((10,)), DMA((10,))],
        compiler_params=pltpu.CompilerParams(collective_id=2, has_side_effects=True),
    )(value)


def per_device(
    patches,
    mask,
    edge,
    attn_w,
    mlp_w,
    vecs,
    edge_m,
    edge_v,
    attn_m,
    attn_v,
    mlp_m,
    mlp_v,
    vecs_m,
    vecs_v,
    teacher_edge,
    teacher_attn,
    teacher_mlp,
    teacher_vecs,
):
    layer_count, rows, kinds, block = attn_w.shape
    wide = mlp_w.shape[3]
    width = patches.shape[2]
    quarter = patches.shape[0]
    edge_rows = edge.shape[1]
    vec_count, vec_cols = vecs.shape
    last_row = 4 * layer_count
    teaching = lax.axis_index(TENSOR) >= 2
    dp_size = lax.axis_size(DP)

    def pack(own_edge, own_attn, own_mlp, own_vecs):
        return (
            pack_heads(own_attn.astype(LOW)),
            jnp.swapaxes(own_mlp.astype(LOW), 1, 2),
            own_edge.astype(LOW).reshape(2 * edge_rows, width),
            jnp.pad(own_vecs.T, ((0, 0), (0, 128 - vec_count))),
        )

    student = (edge, attn_w, mlp_w, vecs)
    teacher = (teacher_edge, teacher_attn, teacher_mlp, teacher_vecs)
    mine = pack(*[jnp.where(teaching, right, left) for left, right in zip(student, teacher)])
    other = pack(*[jnp.where(teaching, left, right) for left, right in zip(student, teacher)])
    parts = [part for pair in zip(mine, other) for part in pair]
    marks = jnp.broadcast_to(mask.astype(LOW), (quarter, 128))
    parts.append(jnp.concatenate([patches.reshape(quarter, width), marks], axis=1))
    attn_grad, mlp_grad, head_grad, patch_grad, vecs_grad = backward_all(*forward_all(*parts))
    by_row = Layout(major_to_minor=(0, 1, 2, 3))
    attn_grad = with_layout_constraint(unpack_heads(attn_grad).astype(jnp.float32), by_row)
    mlp_grad = with_layout_constraint(jnp.swapaxes(mlp_grad.astype(jnp.float32), 1, 2), by_row)
    edge_grad = jnp.stack([patch_grad[:edge_rows], head_grad[:edge_rows]]).astype(jnp.float32)
    loss_total = vecs_grad[0, vec_count]
    vecs_grad = vecs_grad[:, :vec_count].T
    edge_first, edge_second, edge_update = direction(edge, edge_grad, edge_m, edge_v)
    attn_first, attn_second, attn_update = direction(attn_w, attn_grad, attn_m, attn_v)
    mlp_first, mlp_second, mlp_update = direction(mlp_w, mlp_grad, mlp_m, mlp_v)
    vecs_first, vecs_second, vecs_update = direction(vecs, vecs_grad, vecs_m, vecs_v)
    squares = jnp.stack(
        [
            matrix_squares(edge, attn_w, mlp_w),
            matrix_squares(edge_update, attn_update, mlp_update),
        ]
    )
    squares = jnp.pad(squares, ((0, 6), (0, 128 - squares.shape[1])))
    norms = jnp.sqrt(total_all(squares)[:2, : 2 + 6 * layer_count])
    trust = norms[0] / (norms[1] + adam_epsilon)
    edge_trust = trust[0:2]
    layer_trust = trust[2:].reshape(layer_count, 6)
    new_edge = edge - learn_rate * edge_trust[:, None, None] * edge_update
    new_attn = attn_w - learn_rate * layer_trust[:, None, 0:4, None] * attn_update
    new_mlp = mlp_w - learn_rate * layer_trust[:, None, 4:6, None] * mlp_update
    new_vecs = vecs - learn_rate * vecs_update
    keep_share = 1.0 - teacher_decay
    token_total = 4 * quarter * dp_size
    return (
        loss_total / token_total,
        norms,
        new_edge,
        new_attn,
        new_mlp,
        new_vecs,
        edge_first,
        edge_second[0],
        edge_second[1],
        attn_first,
        attn_second[:, :, 0:3],
        attn_second[:, :, 3],
        mlp_first,
        mlp_second,
        vecs_first,
        vecs_second,
        keep_share * (new_edge - teacher_edge),
        keep_share * (new_attn - teacher_attn),
        keep_share * (new_mlp - teacher_mlp),
        keep_share * (new_vecs - teacher_vecs),
        new_edge.astype(LOW),
        new_attn.astype(LOW),
        new_mlp.astype(LOW),
        new_vecs.astype(LOW),
    )


def solution(mesh):
    placed = (
        P(TENSOR, DP, None),
        P(TENSOR, DP),
        P(None, (DP, TENSOR), None),
        P(None, DP, None, TENSOR),
        P(None, DP, None, TENSOR),
        P(None, (DP, TENSOR)),
        P(None, (DP, TENSOR), None),
        P(None, (DP, TENSOR), None),
        P(None, DP, None, TENSOR),
        P(None, DP, None, TENSOR),
        P(None, DP, None, TENSOR),
        P(None, DP, None, TENSOR),
        P(None, (DP, TENSOR)),
        P(None, (DP, TENSOR)),
        P(None, (DP, TENSOR), None),
        P(None, DP, None, TENSOR),
        P(None, DP, None, TENSOR),
        P(None, (DP, TENSOR)),
    )
    planned = dict(mesh.shape) == {DP: 8, TENSOR: 4}
    return jax.shard_map(
        per_device if planned else per_device_general,
        mesh=mesh,
        in_specs=placed,
        out_specs=(
            P(),
            P(),
            P(None, (DP, TENSOR), None),
            P(None, DP, None, TENSOR),
            P(None, DP, None, TENSOR),
            P(None, (DP, TENSOR)),
            P(None, (DP, TENSOR), None),
            P((DP, TENSOR), None),
            P((DP, TENSOR), None),
            P(None, DP, None, TENSOR),
            P(None, DP, None, TENSOR),
            P(None, DP, TENSOR),
            P(None, DP, None, TENSOR),
            P(None, DP, None, TENSOR),
            P(None, (DP, TENSOR)),
            P(None, (DP, TENSOR)),
            P(None, (DP, TENSOR), None),
            P(None, DP, None, TENSOR),
            P(None, DP, None, TENSOR),
            P(None, (DP, TENSOR)),
            P(None, (DP, TENSOR), None),
            P(None, DP, None, TENSOR),
            P(None, DP, None, TENSOR),
            P(None, (DP, TENSOR)),
        ),
        check_vma=False,
    )
```
